32 devices in a mesh: dp: 16 (over z, y, core), expert: 2 (over x).
Axes of the slice: x: 2, y: 2, z: 4, core: 2. Of those that a mesh axis runs over, the one named last changes fastest.
Arguments:
- tokens: bfloat16 [31520, 512], P(('dp', 'expert')), may hold values from -6 to 6
- choices: int32 [31520, 2], P(('dp', 'expert')), may hold values from 0 to 31, all different within a row; in each aligned block of 985 rows (0 to 984, 985 to 1969, ...) at most 128 rows name the same one
- ln1_gain: float32 [512], P('dp'), may hold values from 0.5 to 1.5
- ln1_bias: float32 [512], P('dp'), may hold values from -4 to 4
- w_qkv: float32 [512, 1536], P('dp'), may hold values from -0.25 to 0.25
- w_proj: float32 [512, 512], P('dp'), may hold values from -0.5 to 0.5
- ln2_gain: float32 [512], P('dp'), may hold values from 0.5 to 1.5
- ln2_bias: float32 [512], P('dp'), may hold values from -4 to 4
- w_router: float32 [512, 32], P('dp'), may hold values from -0.1875 to 0.1875
- w_expert_in: float32 [32, 512, 2048], P('expert', 'dp'), may hold values from -0.25 to 0.25
- w_expert_out: float32 [32, 2048, 512], P('expert', 'dp'), may hold values from -2 to 2
- cotangent: bfloat16 [31520, 512], P(('dp', 'expert')), may hold values from -6 to 6
Outputs:
- output: bfloat16 [31520, 512], P(('dp', 'expert'))
- input_grad: float32 [31520, 512], P(('dp', 'expert'))
- ln1_gain_grad: float32 [512], P('dp')
- ln1_bias_grad: float32 [512], P('dp')
- qkv_grad: float32 [512, 1536], P('dp')
- proj_grad: float32 [512, 512], P('dp')
- ln2_gain_grad: float32 [512], P('dp')
- ln2_bias_grad: float32 [512], P('dp')
- router_grad: float32 [512, 32], P('dp')
- expert_in_grad: float32 [32, 512, 2048], P('expert', 'dp')
- expert_out_grad: float32 [32, 2048, 512], P('expert', 'dp')
The draws below stay inside these ranges and needn't reach their ends.
Inputs may be any that keep to these rules, and one draw needn't show every extreme that they name: `choices`: each token names two different experts. Among the 985 tokens of one device no expert is named more than 128 times, and on some device some expert is named exactly 128 times.
All inputs are finite; a program needn't handle non-finite values.
Results may differ from the reference program's by a relative error of at most 0.025.
Values may be sent and summed in bfloat16 or wider, within the bound.
A program may use at most 256 MiB of HBM per device.

```python
import math
from functools import partial
import jax
import jax.numpy as jnp
import numpy as np
from jax import lax

D = 512
HEADS = 8
FF = 2048
EXPERTS = 32
SEQ = 197
CAP = 128
TOK_DEV = 985
TOKENS = 31520


def shard_levels(stream_key, extent, shards, low, top_value):
    level, own = 1.0, jax.random.fold_in(stream_key, 6)
    for axis_at, parts in shards:
        draws = jnp.exp(jax.random.uniform(jax.random.fold_in(own, axis_at), (parts,), jnp.float32, low / len(shards), top_value / len(shards)))
        level = level * jnp.repeat(draws, extent[axis_at] // parts).reshape([-1 if axis == axis_at else 1 for axis in range(len(extent))])
    return level


def shared_out(own_key, own, number, rows, count, top, reach, slope):
    ranking = jax.random.permutation(own_key, count)
    heavy_load, common = portions_of(count, rows * top, reach, slope, True), portions_of(count, rows * top, reach, slope, False)
    places = jnp.arange(count)

    def named(sizes, rotation):
        used = int((sizes > 0).sum())
        fixed = max(1, used // 4)
        shifted = fixed + (places - fixed + rotation * (used - fixed)) % max(1, count - fixed)
        return jnp.zeros((count,), jnp.int32).at[ranking[jnp.where(places < fixed, places, shifted)]].set(jnp.asarray(sizes, jnp.int32))

    sizes = jnp.where(number % 4 == 0, named(heavy_load, number // 4), named(common, number - number // 4 - 1))
    mixed = jax.random.permutation(jax.random.fold_in(own, 3), count)
    giver, receiver = mixed[0:count // 2 * 2:2], mixed[1:count // 2 * 2:2]
    margin = jnp.minimum(sizes[giver] - 1, reach - sizes[receiver]) // 2
    margin = jnp.where((giver == ranking[0]) | (receiver == ranking[0]) | (sizes[receiver] == 0), 0, jnp.maximum(margin, 0))
    shifted = jax.random.randint(jax.random.fold_in(own, 4), (count // 2,), 0, 1 << 20) % (margin + 1)
    sizes = sizes.at[giver].add(-shifted).at[receiver].add(shifted)
    items = jnp.searchsorted(jnp.cumsum(sizes), jnp.arange(rows * top), side="right").astype(jnp.int32)
    table = items.reshape(top, rows).T
    table = table[jax.random.permutation(jax.random.fold_in(own, 1), rows)]
    rotation = jax.random.randint(jax.random.fold_in(own, 2), (rows, 1), 0, top)
    return jnp.take_along_axis(table, (jnp.arange(top)[None, :] + rotation) % top, axis=1)


def portions_of(amount, total, most, slope, full):
    weights = [(1 << 20) // math.isqrt(grade ** slope) + 1 for grade in range(1, amount + 1)]
    largest = most if full else min(most, max(-(-total // amount), total * weights[0] // sum(weights)))
    least = 1 if total - largest >= amount - 1 else 0
    given, rest = [largest] + [least] * (amount - 1), total - largest - least * (amount - 1)
    while rest > 0:
        movable = [i for i in range(1, amount) if given[i] < largest] or [i for i in range(1, amount) if given[i] < most]
        pool, left = sum([weights[i] for i in movable]), rest
        for i in movable:
            extra = min(most - given[i], max(1, left * weights[i] // pool), rest)
            given[i] = given[i] + extra
            rest = rest - extra
    return np.array(given)


def normal_values(key, extent, scale, most, cuts=(), kind=jnp.bfloat16):
    loudness = shard_levels(key, extent, cuts, -0.22, 0.18) if cuts else 1.0
    array = jax.random.normal(key, extent, jnp.float32) * scale * loudness
    return jnp.minimum(jnp.maximum(array, -most), most).astype(kind)


def setup_inputs(seed: int = 0) -> dict:
    key_list = jax.random.split(jax.random.key(seed), 13)
    tokens = normal_values(key_list[0], (TOKENS, D), 1.0, 6.0, ((0, 32),))
    choices_keys = jax.random.split(jax.random.fold_in(key_list[1], 1), TOKENS // TOK_DEV)
    choices_turns = jax.random.permutation(jax.random.fold_in(key_list[1], 3), TOKENS // TOK_DEV)
    choices = jax.vmap(lambda own, number: shared_out(jax.random.fold_in(key_list[1], 2), own, number, TOK_DEV, EXPERTS, 2, CAP, 1))(choices_keys, choices_turns).reshape((TOKENS, 2))
    ln1_gain = jnp.clip(1.0 + 0.1 * jax.random.normal(key_list[2], (D,), jnp.float32), 0.5, 1.5)
    ln1_bias = normal_values(key_list[3], (D,), 0.3, 4.0, ((0, 16),), jnp.float32)
    w_qkv = normal_values(key_list[4], (D, 3 * D), D ** -0.5, 0.25, ((0, 16),), jnp.float32)
    w_proj = normal_values(key_list[5], (D, D), (D // 4) ** -0.5, 0.5, ((0, 16),), jnp.float32)
    ln2_gain = jnp.clip(1.0 + 0.1 * jax.random.normal(key_list[6], (D,), jnp.float32), 0.5, 1.5)
    ln2_bias = normal_values(key_list[7], (D,), 0.3, 4.0, ((0, 16),), jnp.float32)
    w_router = normal_values(key_list[8], (D, EXPERTS), (2 * D) ** -0.5, 0.1875, ((0, 16),), jnp.float32)
    w_expert_in = normal_values(key_list[9], (EXPERTS, D, FF), D ** -0.5, 0.25, ((0, 2), (1, 16)), jnp.float32)
    w_expert_out = normal_values(key_list[10], (EXPERTS, FF, D), (4 * FF // (EXPERTS * EXPERTS)) ** -0.5, 2.0, ((0, 2), (1, 16)), jnp.float32)
    cotangent = normal_values(key_list[11], (TOKENS, D), 1.0, 6.0, ((0, 32),))
    return dict(tokens=tokens, choices=choices, ln1_gain=ln1_gain, ln1_bias=ln1_bias, w_qkv=w_qkv, w_proj=w_proj, ln2_gain=ln2_gain, ln2_bias=ln2_bias, w_router=w_router, w_expert_in=w_expert_in, w_expert_out=w_expert_out, cotangent=cotangent)


@jax.custom_vjp
def low(v):
    return lax.optimization_barrier(v.astype(jnp.bfloat16)).astype(jnp.float32)

@jax.custom_vjp
def low_back(v):
    return v

def low_keep(v):
    return (low(v), None)

def low_pass(kept, grad):
    return (grad,)

def back_keep(v):
    return (v, None)

def back_low(kept, grad):
    return (low(grad),)
low.defvjp(low_keep, low_pass)
low_back.defvjp(back_keep, back_low)
epsilon = 1e-06
highest = lax.Precision.HIGHEST

def layer_norm(values, gain_vec, offset):
    center = values - lax.optimization_barrier(jnp.mean(values, axis=-1, keepdims=True))
    spread = lax.optimization_barrier(jnp.mean(center * center, axis=-1, keepdims=True))
    return center * lax.rsqrt(spread + epsilon) * gain_vec + offset

def attend_block(row_block, gain_vec, offset, qkv_weight, proj_weight):
    images = row_block.shape[0] // SEQ
    normed = low(layer_norm(row_block, gain_vec, offset))
    mixed_rows = low(low_back(jnp.dot(normed, qkv_weight, precision=highest)))
    head_rows = mixed_rows.reshape(images, SEQ, 3, HEADS, D // HEADS)
    queries = head_rows[:, :, 0]
    key_rows = head_rows[:, :, 1]
    value_rows = head_rows[:, :, 2]
    scores = low_back(jnp.einsum('ishd,ithd->ihst', queries, key_rows, precision=highest) * (D // HEADS) ** (-0.5))
    weights = low(jax.nn.softmax(scores, axis=-1))
    context = jnp.einsum('ihst,ithd->ishd', weights, value_rows, precision=highest)
    context = low(low_back(context.reshape(images * SEQ, D)))
    return low_back(jnp.dot(context, proj_weight, precision=highest))

def expert_apply(operands):
    row_block, first_weight, second_weight = operands
    inner_rows = low_back(jnp.dot(row_block, first_weight, precision=highest))
    hidden = low(jax.nn.gelu(inner_rows))
    return low(low_back(jnp.dot(hidden, second_weight, precision=highest)))

def forward(destination, pick_table, inputs, gain_one, bias_one, qkv_weight, proj_weight, gain_two, bias_two, router_weight, expert_first, expert_second):
    gain_one = low(gain_one)
    bias_one = low(bias_one)
    qkv_weight = low(qkv_weight)
    proj_weight = low(proj_weight)
    gain_two = low(gain_two)
    bias_two = low(bias_two)
    router_weight = low(router_weight)
    expert_first = low(expert_first)
    expert_second = low(expert_second)
    blocks = TOKENS // TOK_DEV

    def attend_rows(row_block):
        return attend_block(row_block, gain_one, bias_one, qkv_weight, proj_weight)
    attended = lax.map(jax.checkpoint(attend_rows), inputs.reshape(blocks, TOK_DEV, D))
    resid = inputs + attended.reshape(TOKENS, D)
    normed = low(layer_norm(resid, gain_two, bias_two))
    logits = low_back(jnp.dot(normed, router_weight, precision=highest))
    router_probs = jax.nn.softmax(logits, axis=-1)
    gate_values = lax.optimization_barrier(jnp.sum(router_probs[:, None, :] * pick_table, axis=-1))
    repeated = jnp.repeat(normed, 2, axis=0)
    buffer_rows = jnp.zeros((blocks * EXPERTS * CAP, D), jnp.float32).at[destination].set(repeated)
    expert_rows = buffer_rows.reshape(blocks, EXPERTS, CAP, D).transpose(1, 0, 2, 3).reshape(EXPERTS, blocks * CAP, D)
    expert_rows = low_back(expert_rows)
    returned = lax.map(jax.checkpoint(expert_apply), (expert_rows, expert_first, expert_second))
    back_rows = returned.reshape(EXPERTS, blocks, CAP, D).transpose(1, 0, 2, 3).reshape(blocks * EXPERTS * CAP, D)
    picked = back_rows[destination].reshape(TOKENS, 2, D)
    return resid + lax.optimization_barrier(jnp.sum(gate_values[:, :, None] * picked, axis=1))

def reference(tokens, choices, ln1_gain, ln1_bias, w_qkv, w_proj, ln2_gain, ln2_bias, w_router, w_expert_in, w_expert_out, cotangent):
    blocks = TOKENS // TOK_DEV
    pick_int = (choices[:, :, None] == jnp.arange(EXPERTS, dtype=jnp.int32)[None, None, :]).astype(jnp.int32)
    pick_table = pick_int.astype(jnp.float32)
    flat_picks = pick_int.reshape(blocks, 2 * TOK_DEV, EXPERTS)
    running = jnp.cumsum(flat_picks, axis=1)
    slot_index = lax.optimization_barrier(jnp.sum((running - 1) * flat_picks, axis=-1)).astype(jnp.int32)
    block_index = jnp.arange(blocks, dtype=jnp.int32)[:, None]
    destination = ((block_index * EXPERTS + choices.reshape(blocks, 2 * TOK_DEV)) * CAP + slot_index).reshape(-1).astype(jnp.int32)
    output, pullback = jax.vjp(partial(forward, destination, pick_table), tokens.astype(jnp.float32), ln1_gain.astype(jnp.float32), ln1_bias.astype(jnp.float32), w_qkv.astype(jnp.float32), w_proj.astype(jnp.float32), ln2_gain.astype(jnp.float32), ln2_bias.astype(jnp.float32), w_router.astype(jnp.float32), w_expert_in.astype(jnp.float32), w_expert_out.astype(jnp.float32))
    grads = pullback(cotangent.astype(jnp.float32))
    return (output.astype(jnp.bfloat16), grads[0], grads[1], grads[2], grads[3], grads[4], grads[5], grads[6], grads[7], grads[8], grads[9])
```

```python
import jax
import jax.numpy as jnp
from jax import lax
from jax.sharding import Mesh
from jax.sharding import PartitionSpec as P

D = 512
HEADS = 8
EXPERTS = 32
SEQ = 197
CAP = 128


epsilon = 1e-06


def norm_forward(values, gain_vec, offset):
    center = values - jnp.mean(values, axis=-1, keepdims=True)
    factor = lax.rsqrt(jnp.mean(center * center, axis=-1, keepdims=True) + epsilon)
    normed = center * factor
    return (normed, factor, normed * gain_vec + offset)


def norm_backward(normed, factor, gain_vec, upstream):
    scaled = upstream * gain_vec
    inner_part = (
        scaled
        - jnp.mean(scaled, axis=-1, keepdims=True)
        - normed * jnp.mean(scaled * normed, axis=-1, keepdims=True)
    )
    return (factor * inner_part, jnp.sum(upstream * normed, axis=0), jnp.sum(upstream, axis=0))


def column_product(left, right):
    return lax.dot_general(
        left, right, (((0,), (0,)), ((), ())), preferred_element_type=jnp.float32
    )


def times_transposed(left, right):
    return lax.dot_general(
        left, right, (((1,), (1,)), ((), ())), preferred_element_type=jnp.float32
    )


def body(
    tokens,
    choices,
    ln1_gain,
    ln1_bias,
    w_qkv,
    w_proj,
    ln2_gain,
    ln2_bias,
    w_router,
    w_expert_in,
    w_expert_out,
    cotangent,
):
    low_type = jnp.bfloat16
    full_type = jnp.float32
    gathered = (
        lax.all_gather(ln1_gain.astype(low_type), ("replica", "part"), axis=0, tiled=True),
        lax.all_gather(ln1_bias.astype(low_type), ("replica", "part"), axis=0, tiled=True),
        lax.all_gather(w_qkv.astype(low_type), ("replica", "part"), axis=0, tiled=True),
        lax.all_gather(w_proj.astype(low_type), ("replica", "part"), axis=0, tiled=True),
        lax.all_gather(ln2_gain.astype(low_type), ("replica", "part"), axis=0, tiled=True),
        lax.all_gather(ln2_bias.astype(low_type), ("replica", "part"), axis=0, tiled=True),
        lax.all_gather(w_router.astype(low_type), ("replica", "part"), axis=0, tiled=True),
    )
    gain_one = gathered[0].astype(full_type)
    bias_one = gathered[1].astype(full_type)
    qkv_weight = gathered[2]
    proj_weight = gathered[3]
    gain_two = gathered[4].astype(full_type)
    bias_two = gathered[5].astype(full_type)
    router_weight = gathered[6]
    replicas, parts, groups = (lax.axis_size(name) for name in ("replica", "part", "expert"))
    own = w_expert_in.shape[0] // parts

    def spread(master):
        pieces = master.astype(low_type).reshape(parts, own, *master.shape[1:])
        pieces = jnp.concatenate([pieces] * replicas, axis=0)
        pieces = lax.all_to_all(pieces, ("replica", "part"), split_axis=0, concat_axis=0, tiled=True)
        return pieces.transpose(1, 0, 2, 3).reshape(own, -1, master.shape[2])

    def collect(grad):
        pieces = grad.astype(low_type).reshape(own, replicas * parts, -1, grad.shape[2])
        pieces = lax.all_to_all(
            pieces.transpose(1, 0, 2, 3),
            ("replica", "part"),
            split_axis=0,
            concat_axis=0,
            tiled=True,
        )
        pieces = pieces.reshape(replicas, parts * own, -1, grad.shape[2])
        return jnp.sum(pieces.astype(full_type), axis=0)

    def to_experts(rows):
        rows = rows.reshape(parts * groups, own * CAP, D)
        rows = lax.all_to_all(rows, ("part", "expert"), split_axis=0, concat_axis=0, tiled=True)
        rows = rows.reshape(parts * groups, own, CAP, D).transpose(1, 0, 2, 3)
        return rows.reshape(own, parts * groups * CAP, D)

    def to_tokens(rows):
        rows = rows.reshape(own, parts * groups, CAP, D).transpose(1, 0, 2, 3)
        rows = rows.reshape(parts * groups, own * CAP, D)
        rows = lax.all_to_all(rows, ("part", "expert"), split_axis=0, concat_axis=0, tiled=True)
        return rows.reshape(EXPERTS * CAP, D)

    expert_first = spread(w_expert_in)
    expert_second = spread(w_expert_out)
    images = tokens.shape[0] // SEQ
    head_size = D // HEADS
    qk_factor = head_size ** (-0.5)
    inputs = tokens.astype(full_type)
    normed_one, factor_one, hidden_one = norm_forward(inputs, gain_one, bias_one)
    attn_in = hidden_one.astype(low_type)
    mixed_rows = jnp.dot(attn_in, qkv_weight, preferred_element_type=full_type).astype(low_type)
    head_rows = mixed_rows.reshape(images, SEQ, 3, HEADS, head_size)
    queries = head_rows[:, :, 0]
    key_rows = head_rows[:, :, 1]
    value_rows = head_rows[:, :, 2]

    def attention_probs():
        scores = (
            jnp.einsum("ishd,ithd->ihst", queries, key_rows, preferred_element_type=full_type)
            * qk_factor
        )
        return jax.nn.softmax(scores, axis=-1)

    attn_probs = attention_probs()
    context = (
        jnp.einsum(
            "ihst,ithd->ishd",
            attn_probs.astype(low_type),
            value_rows,
            preferred_element_type=full_type,
        )
        .reshape(images * SEQ, D)
        .astype(low_type)
    )
    resid = inputs + jnp.dot(context, proj_weight, preferred_element_type=full_type)
    normed_two, factor_two, hidden_two = norm_forward(resid, gain_two, bias_two)
    router_in = hidden_two.astype(low_type)
    logits = jnp.dot(router_in, router_weight, preferred_element_type=full_type)
    router_probs = jax.nn.softmax(logits, axis=-1)
    pick_table = choices[:, :, None] == jnp.arange(EXPERTS, dtype=jnp.int32)[None, None, :]
    pick_float = pick_table.astype(full_type)
    gate_values = jnp.sum(router_probs[:, None, :] * pick_float, axis=-1)
    flat_picks = pick_table.astype(jnp.int32).reshape(-1, EXPERTS)
    running = jnp.cumsum(flat_picks, axis=0)
    slot_index = jnp.sum((running - 1) * flat_picks, axis=-1)
    flat_choices = choices.reshape(-1)
    group = flat_choices // (parts * own)
    inside = flat_choices % (parts * own)
    place = ((inside // own) * groups + group) * own + inside % own
    destination = place * CAP + slot_index
    repeated = jnp.repeat(router_in, 2, axis=0)
    outgoing = (
        jnp.zeros((EXPERTS * CAP, D), low_type)
        .at[destination]
        .set(repeated)
    )
    received = to_experts(outgoing)
    inner_rows = jnp.einsum(
        "erd,edf->erf", received, expert_first, preferred_element_type=full_type
    )
    hidden = jax.nn.gelu(inner_rows).astype(low_type)
    returned = jnp.einsum(
        "erf,efd->erd", hidden, expert_second, preferred_element_type=full_type
    ).astype(low_type)
    combined = to_tokens(returned)
    picked = combined[destination].reshape(-1, 2, D).astype(full_type)
    output = resid + jnp.sum(gate_values[:, :, None] * picked, axis=1)
    upstream = cotangent.astype(full_type)
    grad_gates = jnp.sum(upstream[:, None, :] * picked, axis=-1)
    grad_picked = (gate_values[:, :, None] * upstream[:, None, :]).astype(low_type).reshape(-1, D)
    grad_outgoing = (
        jnp.zeros((EXPERTS * CAP, D), low_type)
        .at[destination]
        .set(grad_picked)
    )
    grad_returned = to_experts(grad_outgoing)
    grad_hidden = jnp.einsum(
        "erd,efd->erf", grad_returned, expert_second, preferred_element_type=full_type
    )
    gelu_value, gelu_pull = jax.vjp(jax.nn.gelu, inner_rows)
    grad_inner = gelu_pull(grad_hidden)[0].astype(low_type)
    grad_second = jnp.einsum(
        "erf,erd->efd", hidden, grad_returned, preferred_element_type=full_type
    )
    grad_first = jnp.einsum("erd,erf->edf", received, grad_inner, preferred_element_type=full_type)
    grad_received = jnp.einsum(
        "erf,edf->erd", grad_inner, expert_first, preferred_element_type=full_type
    ).astype(low_type)
    grad_back = to_tokens(grad_received)
    grad_router_in = jnp.sum(grad_back[destination].reshape(-1, 2, D).astype(full_type), axis=1)
    expert_in_grad, expert_out_grad = (collect(grad_first), collect(grad_second))
    grad_probs = jnp.sum(grad_gates[:, :, None] * pick_float, axis=1)
    grad_logits = (
        router_probs * (grad_probs - jnp.sum(router_probs * grad_probs, axis=-1, keepdims=True))
    ).astype(low_type)
    router_grad = column_product(router_in, grad_logits)
    grad_router_in = grad_router_in + times_transposed(grad_logits, router_weight)
    grad_resid_two, gain_two_grad, bias_two_grad = norm_backward(
        normed_two, factor_two, gain_two, grad_router_in
    )
    grad_resid = upstream + grad_resid_two
    grad_attended = grad_resid.astype(low_type)
    proj_grad = column_product(context, grad_attended)
    grad_context = (
        times_transposed(grad_attended, proj_weight)
        .astype(low_type)
        .reshape(images, SEQ, HEADS, head_size)
    )
    probs_again = attention_probs()
    grad_weights = jnp.einsum(
        "ishd,ithd->ihst", grad_context, value_rows, preferred_element_type=full_type
    )
    grad_scores = (
        probs_again * (grad_weights - jnp.sum(probs_again * grad_weights, axis=-1, keepdims=True))
    ).astype(low_type)
    grad_queries = (
        jnp.einsum("ihst,ithd->ishd", grad_scores, key_rows, preferred_element_type=full_type)
        * qk_factor
    )
    grad_keys = (
        jnp.einsum("ihst,ishd->ithd", grad_scores, queries, preferred_element_type=full_type)
        * qk_factor
    )
    grad_values = jnp.einsum(
        "ihst,ishd->ithd",
        probs_again.astype(low_type),
        grad_context,
        preferred_element_type=full_type,
    )
    grad_mixed = (
        jnp.stack([grad_queries, grad_keys, grad_values], axis=2)
        .reshape(images * SEQ, 3 * D)
        .astype(low_type)
    )
    qkv_grad = column_product(attn_in, grad_mixed)
    grad_hidden_one = times_transposed(grad_mixed, qkv_weight)
    grad_input_one, gain_one_grad, bias_one_grad = norm_backward(
        normed_one, factor_one, gain_one, grad_hidden_one
    )
    input_grad = grad_resid + grad_input_one
    dense_grads = (
        gain_one_grad,
        bias_one_grad,
        qkv_grad,
        proj_grad,
        gain_two_grad,
        bias_two_grad,
        router_grad,
    )
    summed = (
        lax.psum(dense_grads[0].astype(jnp.bfloat16), "expert").astype(jnp.float32),
        lax.psum(dense_grads[1].astype(jnp.bfloat16), "expert").astype(jnp.float32),
        lax.psum(dense_grads[2].astype(jnp.bfloat16), "expert").astype(jnp.float32),
        lax.psum(dense_grads[3].astype(jnp.bfloat16), "expert").astype(jnp.float32),
        lax.psum(dense_grads[4].astype(jnp.bfloat16), "expert").astype(jnp.float32),
        lax.psum(dense_grads[5].astype(jnp.bfloat16), "expert").astype(jnp.float32),
        lax.psum(dense_grads[6].astype(jnp.bfloat16), "expert").astype(jnp.float32),
    )
    shares = (
        lax.psum_scatter(
            summed[0].astype(jnp.bfloat16), ("replica", "part"), scatter_dimension=0, tiled=True
        ).astype(jnp.float32),
        lax.psum_scatter(
            summed[1].astype(jnp.bfloat16), ("replica", "part"), scatter_dimension=0, tiled=True
        ).astype(jnp.float32),
        lax.psum_scatter(
            summed[2].astype(jnp.bfloat16), ("replica", "part"), scatter_dimension=0, tiled=True
        ).astype(jnp.float32),
        lax.psum_scatter(
            summed[3].astype(jnp.bfloat16), ("replica", "part"), scatter_dimension=0, tiled=True
        ).astype(jnp.float32),
        lax.psum_scatter(
            summed[4].astype(jnp.bfloat16), ("replica", "part"), scatter_dimension=0, tiled=True
        ).astype(jnp.float32),
        lax.psum_scatter(
            summed[5].astype(jnp.bfloat16), ("replica", "part"), scatter_dimension=0, tiled=True
        ).astype(jnp.float32),
        lax.psum_scatter(
            summed[6].astype(jnp.bfloat16), ("replica", "part"), scatter_dimension=0, tiled=True
        ).astype(jnp.float32),
    )
    return (
        output.astype(low_type),
        input_grad,
        shares[0],
        shares[1],
        shares[2],
        shares[3],
        shares[4],
        shares[5],
        shares[6],
        expert_in_grad,
        expert_out_grad,
    )


def solution(mesh):
    dp, groups = mesh.shape["dp"], mesh.shape["expert"]
    parts = min(EXPERTS // groups, dp // 2)
    mesh = Mesh(mesh.devices.reshape(dp // parts, parts, groups), ("replica", "part", "expert"))
    placed = (
        P(("replica", "part", "expert"), None),
        P(("replica", "part", "expert"), None),
        P(("replica", "part")),
        P(("replica", "part")),
        P(("replica", "part"), None),
        P(("replica", "part"), None),
        P(("replica", "part")),
        P(("replica", "part")),
        P(("replica", "part"), None),
        P("expert", ("replica", "part"), None),
        P("expert", ("replica", "part"), None),
        P(("replica", "part", "expert"), None),
    )
    return jax.shard_map(
        body,
        mesh=mesh,
        in_specs=placed,
        out_specs=(
            P(("replica", "part", "expert"), None),
            P(("replica", "part", "expert"), None),
            P(("replica", "part")),
            P(("replica", "part")),
            P(("replica", "part"), None),
            P(("replica", "part"), None),
            P(("replica", "part")),
            P(("replica", "part")),
            P(("replica", "part"), None),
            P("expert", ("replica", "part"), None),
            P("expert", ("replica", "part"), None),
        ),
        check_vma=False,
    )
```

```python
from functools import partial

import jax
import jax.numpy as jnp
import numpy as np
from jax import lax
from jax.experimental import pallas as pl
from jax.experimental.pallas import tpu as pltpu
from jax.sharding import Mesh
from jax.sharding import PartitionSpec as P

D = 512
HEADS = 8
EXPERTS = 32
SEQ = 197
CAP = 128
ROWS = 208
HEAD = D // HEADS
LANES = 128
QKV = 3 * D
PACKED = QKV + D + LANES
epsilon = 1e-06
low = jnp.bfloat16
full = jnp.float32
BIG = 56 * 1024 * 1024


def dot(left, right):
    return jnp.dot(left, right, preferred_element_type=full)


def dot_rt(left, right):
    return lax.dot_general(left, right, (((1,), (1,)), ((), ())), preferred_element_type=full)


def dot_lt(left, right):
    return lax.dot_general(left, right, (((0,), (0,)), ((), ())), preferred_element_type=full)


def lanes_of(shape):
    return lax.broadcasted_iota(jnp.int32, shape, len(shape) - 1)


def normed_rows(values):
    center = values - jnp.mean(values, axis=-1, keepdims=True)
    factor = lax.rsqrt(jnp.mean(center * center, axis=-1, keepdims=True) + epsilon)
    return center * factor, factor


def norm_back(normed, factor, gain_vec, upstream):
    scaled = upstream * gain_vec
    return factor * (
        scaled
        - jnp.mean(scaled, axis=-1, keepdims=True)
        - normed * jnp.mean(scaled * normed, axis=-1, keepdims=True)
    )


def norm_vectors(weights_ref):
    rows = weights_ref[:, QKV + D :].astype(full).T
    return [rows[EXPERTS + i : EXPERTS + i + 1] for i in range(4)]


def halves(pair):
    first = lanes_of(pair.shape) < HEAD
    zero = jnp.zeros_like(pair)
    return jnp.where(first, pair, zero), jnp.where(first, zero, pair)


def head_probs(query, key_pair):
    scores = dot_rt(query, key_pair) * (HEAD**-0.5)
    scores = jnp.where(lanes_of(scores.shape) < SEQ, scores, -1e30)
    grown = jnp.exp(scores - jnp.max(scores, axis=-1, keepdims=True))
    return grown / jnp.sum(grown, axis=-1, keepdims=True)


def attend_kernel(x_ref, w_ref, qkv_ref, ctx_ref, r_ref, h_ref, probs_ref):
    gain_one, bias_one, gain_two, bias_two = norm_vectors(w_ref)
    x = x_ref[0].astype(full)
    normed, _ = normed_rows(x)
    attn_in = (normed * gain_one + bias_one).astype(low)
    qkv_ref[0] = dot(attn_in, w_ref[:, :QKV]).astype(low)
    for pair in range(HEADS // 2):
        at = pair * LANES
        query = halves(qkv_ref[0, :, at : at + LANES])
        key = qkv_ref[0, :, D + at : D + at + LANES]
        value = halves(qkv_ref[0, :, 2 * D + at : 2 * D + at + LANES])
        total = None
        for i in range(2):
            part = dot(head_probs(query[i], key).astype(low), value[i])
            total = part if total is None else total + part
        ctx_ref[0, :, at : at + LANES] = total.astype(low)
    r = x + dot(ctx_ref[0], w_ref[:, QKV : QKV + D])
    r_ref[0] = r
    normed, _ = normed_rows(r)
    h = (normed * gain_two + bias_two).astype(low)
    h_ref[0] = h
    logits = dot(h, w_ref[:, QKV + D :])
    logits = jnp.where(lanes_of(logits.shape) < EXPERTS, logits, -1e30)
    grown = jnp.exp(logits - jnp.max(logits, axis=-1, keepdims=True))
    probs_ref[0] = grown / jnp.sum(grown, axis=-1, keepdims=True)


def image_spec(width):
    return pl.BlockSpec((1, ROWS, width), lambda i: (i, 0, 0))


def whole_spec(shape):
    return pl.BlockSpec(shape, lambda *_: (0,) * len(shape))


def params(n):
    return pltpu.CompilerParams(
        dimension_semantics=("arbitrary",) * n, vmem_limit_bytes=BIG
    )


def attend(x, weights):
    images = x.shape[0]
    shapes = ((QKV, low), (D, low), (D, full), (D, low), (LANES, full))
    return pl.pallas_call(
        attend_kernel,
        grid=(images,),
        in_specs=[image_spec(D), whole_spec(weights.shape)],
        out_specs=[image_spec(width) for width, _ in shapes],
        out_shape=[jax.ShapeDtypeStruct((images, ROWS, w), t) for w, t in shapes],
        compiler_params=params(1),
        cost_estimate=pl.CostEstimate(
            flops=8 * 10**9, bytes_accessed=12 * 10**6, transcendentals=2 * 10**6
        ),
        name="attend",
    )(x, weights)


def attend_back_kernel(
    images, x_ref, w_ref, qkv_ref, ctx_ref, r_ref, h_ref, probs_ref, dprobs_ref, dh_ref, dy_ref,
    dx_ref, grads_ref, dqkv_ref, qkv_acc, proj_acc, router_acc, norm_acc,
):
    step = pl.program_id(0)

    @pl.when(step == 0)
    def _():
        qkv_acc[...] = jnp.zeros_like(qkv_acc)
        proj_acc[...] = jnp.zeros_like(proj_acc)
        router_acc[...] = jnp.zeros_like(router_acc)
        norm_acc[...] = jnp.zeros_like(norm_acc)

    gain_one, bias_one, gain_two, _ = norm_vectors(w_ref)
    probs, dprobs = probs_ref[0], dprobs_ref[0]
    dlogits = (probs * (dprobs - jnp.sum(probs * dprobs, axis=-1, keepdims=True))).astype(low)
    router_acc[...] += dot_lt(h_ref[0], dlogits)
    dh = dh_ref[0] + dot_rt(dlogits, w_ref[:, QKV + D :])
    normed, factor = normed_rows(r_ref[0])
    norm_acc[2:3] += jnp.sum(dh * normed, axis=0, keepdims=True)
    norm_acc[3:4] += jnp.sum(dh, axis=0, keepdims=True)
    dr = dy_ref[0].astype(full) + norm_back(normed, factor, gain_two, dh)
    dattended = dr.astype(low)
    proj_acc[...] += dot_lt(ctx_ref[0], dattended)
    dctx = dot_rt(dattended, w_ref[:, QKV : QKV + D]).astype(low)
    for pair in range(HEADS // 2):
        at = pair * LANES
        query = halves(qkv_ref[0, :, at : at + LANES])
        key = qkv_ref[0, :, D + at : D + at + LANES]
        keys = halves(key)
        value = qkv_ref[0, :, 2 * D + at : 2 * D + at + LANES]
        dhead = halves(dctx[:, at : at + LANES])
        dq = dk = dv = None
        for i in range(2):
            p = head_probs(query[i], key)
            dp = dot_rt(dhead[i], value)
            ds = (p * (dp - jnp.sum(p * dp, axis=-1, keepdims=True))).astype(low)
            parts = dot(ds, keys[i]), dot_lt(ds, query[i]), dot_lt(p.astype(low), dhead[i])
            dq, dk, dv = parts if dq is None else (dq + parts[0], dk + parts[1], dv + parts[2])
        dqkv_ref[:, at : at + LANES] = (dq * HEAD**-0.5).astype(low)
        dqkv_ref[:, D + at : D + at + LANES] = (dk * HEAD**-0.5).astype(low)
        dqkv_ref[:, 2 * D + at : 2 * D + at + LANES] = dv.astype(low)
    normed, factor = normed_rows(x_ref[0].astype(full))
    attn_in = (normed * gain_one + bias_one).astype(low)
    qkv_acc[...] += dot_lt(attn_in, dqkv_ref[...])
    da = dot_rt(dqkv_ref[...], w_ref[:, :QKV])
    norm_acc[0:1] += jnp.sum(da * normed, axis=0, keepdims=True)
    norm_acc[1:2] += jnp.sum(da, axis=0, keepdims=True)
    dx_ref[0] = dr + norm_back(normed, factor, gain_one, da)

    @pl.when(step == images - 1)
    def _():
        grads_ref[:, :QKV] = qkv_acc[...].astype(low)
        grads_ref[:, QKV : QKV + D] = proj_acc[...].astype(low)
        columns = norm_acc[...].T
        moved = pltpu.roll(columns, EXPERTS, 1)
        lane = lanes_of(moved.shape)
        tile = jnp.where(lane < EXPERTS, router_acc[...], moved)
        grads_ref[:, QKV + D :] = tile.astype(low)


def attend_back(x, weights, qkv, ctx, r, h, probs, dprobs, dh, dy):
    images = x.shape[0]
    widths = (D, None, QKV, D, D, D, LANES, LANES, D, D)
    return pl.pallas_call(
        partial(attend_back_kernel, images),
        grid=(images,),
        in_specs=[whole_spec(weights.shape) if w is None else image_spec(w) for w in widths],
        out_specs=[image_spec(D), whole_spec((D, PACKED))],
        out_shape=[
            jax.ShapeDtypeStruct((images, ROWS, D), full),
            jax.ShapeDtypeStruct((D, PACKED), low),
        ],
        scratch_shapes=[
            pltpu.VMEM((ROWS, QKV), low),
            pltpu.VMEM((D, QKV), full),
            pltpu.VMEM((D, D), full),
            pltpu.VMEM((D, LANES), full),
            pltpu.VMEM((LANES, D), full),
        ],
        compiler_params=params(1),
        cost_estimate=pl.CostEstimate(
            flops=20 * 10**9, bytes_accessed=16 * 10**6, transcendentals=2 * 10**6
        ),
        name="attend_back",
    )(x, weights, qkv, ctx, r, h, probs, dprobs, dh, dy)


def dispatch_kernel(own, keys_ref, rows_ref, out_ref):
    slots = lax.broadcasted_iota(jnp.int32, (CAP, keys_ref.shape[2]), 0).astype(full)
    picks = [(keys_ref[0, i : i + 1] == slots).astype(low) for i in range(own)]
    picks = jnp.concatenate(picks, axis=0)
    out_ref[0] = dot(picks, rows_ref[...]).astype(low)


def dispatch(keys, rows):
    peers, own, tokens = keys.shape
    return pl.pallas_call(
        partial(dispatch_kernel, own),
        grid=(peers,),
        in_specs=[pl.BlockSpec((1, own, tokens), lambda i: (i, 0, 0)), whole_spec(rows.shape)],
        out_specs=pl.BlockSpec((1, own * CAP, D), lambda i: (i, 0, 0)),
        out_shape=jax.ShapeDtypeStruct((peers, own * CAP, D), low),
        compiler_params=params(1),
        cost_estimate=pl.CostEstimate(
            flops=2 * EXPERTS * CAP * tokens * D, bytes_accessed=5 * 10**6, transcendentals=0
        ),
        name="dispatch",
    )(keys, rows)


def chooser(own, step):
    shape = (LANES, own * CAP)
    expert = lax.broadcasted_iota(jnp.int32, shape, 0)
    slot = lax.broadcasted_iota(jnp.int32, shape, 1)
    return (expert == step * own + slot // CAP).astype(low)


def combine_kernel(own, peers, keys_ref, probs_ref, dy_ref, r_ref, y_ref, out_ref, dprobs_ref, acc):
    step = pl.program_id(0)
    spread = chooser(own, step)
    y = y_ref[0]

    @pl.when(step == 0)
    def _():
        acc[...] = jnp.zeros_like(acc)
        dprobs_ref[...] = jnp.zeros_like(dprobs_ref)

    for at in range(0, acc.shape[0], ROWS):
        rows = slice(at, at + ROWS)
        slot = lanes_of((ROWS, own * CAP)) % CAP
        here = dot(keys_ref[rows], spread) == slot.astype(full)
        gate = dot(probs_ref[rows].astype(low), spread)
        acc[rows] += dot(jnp.where(here, gate, 0.0).astype(low), y)
        agreed = jnp.where(here, dot_rt(dy_ref[rows], y), 0.0)
        lane = lanes_of((ROWS, LANES))
        change = dprobs_ref[rows]
        for i in range(own):
            column = jnp.sum(agreed[:, i * CAP : (i + 1) * CAP], axis=-1, keepdims=True)
            change = jnp.where(lane == step * own + i, column, change)
        dprobs_ref[rows] = change

    @pl.when(step == peers - 1)
    def _():
        out_ref[...] = (r_ref[...] + acc[...]).astype(low)


def combine(keys, probs, dy, r, y):
    peers, width, _ = y.shape
    tokens = keys.shape[0]
    return pl.pallas_call(
        partial(combine_kernel, width // CAP, peers),
        grid=(peers,),
        in_specs=[whole_spec(a.shape) for a in (keys, probs, dy, r)]
        + [pl.BlockSpec((1, width, D), lambda i: (i, 0, 0))],
        out_specs=[whole_spec((tokens, D)), whole_spec((tokens, LANES))],
        out_shape=[
            jax.ShapeDtypeStruct((tokens, D), low),
            jax.ShapeDtypeStruct((tokens, LANES), full),
        ],
        scratch_shapes=[pltpu.VMEM((tokens, D), full)],
        compiler_params=params(1),
        cost_estimate=pl.CostEstimate(
            flops=12 * 10**9, bytes_accessed=10 * 10**6, transcendentals=0
        ),
        name="combine",
    )(keys, probs, dy, r, y)


def gather_kernel(own, keys_ref, rows_ref, out_ref):
    step = pl.program_id(0)
    spread = chooser(own, step)

    @pl.when(step == 0)
    def _():
        out_ref[...] = jnp.zeros_like(out_ref)

    for at in range(0, out_ref.shape[0], ROWS):
        rows = slice(at, at + ROWS)
        slot = lanes_of((ROWS, own * CAP)) % CAP
        here = dot(keys_ref[rows], spread) == slot.astype(full)
        out_ref[rows] += dot(here.astype(low), rows_ref[0])


def gather(keys, back):
    peers, width, _ = back.shape
    tokens = keys.shape[0]
    return pl.pallas_call(
        partial(gather_kernel, width // CAP),
        grid=(peers,),
        in_specs=[whole_spec(keys.shape), pl.BlockSpec((1, width, D), lambda i: (i, 0, 0))],
        out_specs=whole_spec((tokens, D)),
        out_shape=jax.ShapeDtypeStruct((tokens, D), full),
        compiler_params=params(1),
        cost_estimate=pl.CostEstimate(
            flops=6 * 10**9, bytes_accessed=7 * 10**6, transcendentals=0
        ),
        name="gather",
    )(keys, back)


GELU = 0.7978845608028654
CUBE = 0.044715


def gelu_pair(u):
    square = u * u
    bent = jnp.tanh(u * (GELU * CUBE * square + GELU))
    half = 0.5 * bent + 0.5
    value = u * half
    return value, half + value * (1.0 - bent) * (3.0 * GELU * CUBE * square + GELU)


def first_kernel(chunk, h_ref, dy_ref, w_ref, wr_ref, sel_ref, g_ref, slope_ref, dye_ref, dw_ref, dye_t):
    rows = h_ref.shape[0] * CAP
    sources = chunk // CAP
    tile = w_ref.shape[3]

    @pl.when(pl.program_id(1) == 0)
    def _():
        for at in range(0, rows, chunk):
            source = slice(at // CAP, at // CAP + sources)
            h = h_ref[source, 0].reshape(chunk, D)
            logits = dot(h, wr_ref[...])
            logits = jnp.where(lanes_of(logits.shape) < EXPERTS, logits, -1e30)
            grown = jnp.exp(logits - jnp.max(logits, axis=-1, keepdims=True))
            mine = jnp.sum(grown * sel_ref[0], axis=-1, keepdims=True)
            gate = mine / jnp.sum(grown, axis=-1, keepdims=True)
            dye = dy_ref[source, 0].reshape(chunk, D).astype(full) * gate
            dye_ref[source, 0] = dye.astype(low).reshape(sources, CAP, D)
            dye_t[:, at : at + chunk] = dye.T.astype(low)

    w = w_ref[:, 0].reshape(D, tile)
    for at in range(0, rows, chunk):
        source = slice(at // CAP, at // CAP + sources)
        u = dot(h_ref[source, 0].reshape(chunk, D), w)
        value, slope = gelu_pair(u)
        g_ref[0, at : at + chunk] = value.astype(low)
        slope_ref[0, at : at + chunk] = slope.astype(low)
    grad = dot(dye_t[...], g_ref[0]).T
    dw_ref[:, 0] = grad.astype(low).reshape(dw_ref.shape[0], dw_ref.shape[2], D)


def expert_first(h, dy, w_in, w_router, select, tile):
    sources, own, _, _ = h.shape
    owners, _, depth, hidden = w_in.shape
    rows = sources * CAP
    per = hidden // owners
    token_spec = pl.BlockSpec((sources, 1, CAP, D), lambda e, f: (0, e, 0, 0))
    hidden_spec = pl.BlockSpec((1, rows, tile), lambda e, f: (e, 0, f))
    return pl.pallas_call(
        partial(first_kernel, 2 * CAP),
        grid=(own, hidden // tile),
        in_specs=[
            token_spec,
            token_spec,
            pl.BlockSpec((owners, 1, depth, tile), lambda e, f: (0, e, 0, f)),
            whole_spec(w_router.shape),
            pl.BlockSpec((1, 1, LANES), lambda e, f: (e, 0, 0)),
        ],
        out_specs=[
            hidden_spec,
            hidden_spec,
            token_spec,
            pl.BlockSpec((tile // per, 1, per, D), lambda e, f: (f, e, 0, 0)),
        ],
        out_shape=[
            jax.ShapeDtypeStruct((own, rows, hidden), low),
            jax.ShapeDtypeStruct((own, rows, hidden), low),
            jax.ShapeDtypeStruct(h.shape, low),
            jax.ShapeDtypeStruct((owners, own, per, D), low),
        ],
        scratch_shapes=[pltpu.VMEM((D, rows), low)],
        compiler_params=params(2),
        cost_estimate=pl.CostEstimate(
            flops=4 * own * rows * D * hidden,
            bytes_accessed=50 * 10**6,
            transcendentals=own * rows * hidden,
        ),
        name="expert_first",
    )(h, dy, w_in, w_router, select)


def second_kernel(g_ref, w_ref, y_ref):
    hidden = g_ref.shape[2]
    y = dot(g_ref[0], w_ref[:, 0].reshape(hidden, D)).astype(low)
    y_ref[:, 0] = y.reshape(y_ref.shape[0], CAP, D)


def expert_second(g, w_out):
    own, rows, hidden = g.shape
    owners, _, per, _ = w_out.shape
    block = 4
    return pl.pallas_call(
        second_kernel,
        grid=(own, rows // (block * CAP)),
        in_specs=[
            pl.BlockSpec((1, block * CAP, hidden), lambda e, i: (e, i, 0)),
            pl.BlockSpec((owners, 1, per, D), lambda e, i: (0, e, 0, 0)),
        ],
        out_specs=pl.BlockSpec((block, 1, CAP, D), lambda e, i: (i, e, 0, 0)),
        out_shape=jax.ShapeDtypeStruct((rows // CAP, own, CAP, D), low),
        compiler_params=params(2),
        cost_estimate=pl.CostEstimate(
            flops=2 * own * rows * D * hidden, bytes_accessed=26 * 10**6, transcendentals=0
        ),
        name="expert_second",
    )(g, w_out)


def back_kernel(chunk, steps, h_ref, dye_ref, slope_ref, w_in_ref, w_out_ref, dbuf_ref, dw_ref, h_t, du_ref, acc):
    rows = h_ref.shape[0] * CAP
    sources = chunk // CAP
    tile = slope_ref.shape[2]
    step = pl.program_id(1)

    @pl.when(step == 0)
    def _():
        acc[...] = jnp.zeros_like(acc)
        for at in range(0, rows, chunk):
            source = slice(at // CAP, at // CAP + sources)
            h_t[:, at : at + chunk] = h_ref[source, 0].reshape(chunk, D).T

    w_in = w_in_ref[:, 0].reshape(D, tile)
    w_out = w_out_ref[:, 0].reshape(tile, D)
    for at in range(0, rows, chunk):
        source = slice(at // CAP, at // CAP + sources)
        dg = dot_rt(dye_ref[source, 0].reshape(chunk, D), w_out)
        du = (dg * slope_ref[0, at : at + chunk].astype(full)).astype(low)
        du_ref[at : at + chunk] = du
        acc[at : at + chunk] += dot_rt(du, w_in)
    grad = dot(h_t[...], du_ref[...]).astype(low)
    dw_ref[:, 0] = grad.reshape(dw_ref.shape[0], dw_ref.shape[2], tile)

    @pl.when(step == steps - 1)
    def _():
        dbuf_ref[:, 0] = acc[...].astype(low).reshape(rows // CAP, CAP, D)


def expert_back(h, dye, slope, w_in, w_out, tile):
    sources, own, _, _ = h.shape
    owners, _, depth, hidden = w_in.shape
    rows = sources * CAP
    per = hidden // owners
    token_spec = pl.BlockSpec((sources, 1, CAP, D), lambda e, f: (0, e, 0, 0))
    in_spec = pl.BlockSpec((owners, 1, depth, tile), lambda e, f: (0, e, 0, f))
    return pl.pallas_call(
        partial(back_kernel, 2 * CAP, hidden // tile),
        grid=(own, hidden // tile),
        in_specs=[
            token_spec,
            token_spec,
            pl.BlockSpec((1, rows, tile), lambda e, f: (e, 0, f)),
            in_spec,
            pl.BlockSpec((tile // per, 1, per, D), lambda e, f: (f, e, 0, 0)),
        ],
        out_specs=[token_spec, in_spec],
        out_shape=[
            jax.ShapeDtypeStruct(h.shape, low),
            jax.ShapeDtypeStruct(w_in.shape, low),
        ],
        scratch_shapes=[
            pltpu.VMEM((D, rows), low),
            pltpu.VMEM((rows, tile), low),
            pltpu.VMEM((rows, D), full),
        ],
        compiler_params=params(2),
        cost_estimate=pl.CostEstimate(
            flops=6 * own * rows * D * hidden, bytes_accessed=40 * 10**6, transcendentals=0
        ),
        name="expert_back",
    )(h, dye, slope, w_in, w_out)


ALL = ("replica", "part")


def body(
    tokens,
    choices,
    ln1_gain,
    ln1_bias,
    w_qkv,
    w_proj,
    ln2_gain,
    ln2_bias,
    w_router,
    w_expert_in,
    w_expert_out,
    cotangent,
):
    replicas, parts, groups = (lax.axis_size(name) for name in ("replica", "part", "expert"))
    owners = replicas * parts
    peers = parts * groups
    own = EXPERTS // peers
    images = tokens.shape[0] // SEQ
    count = images * ROWS
    tile = 512 * 16 // peers

    order = np.arange(EXPERTS).reshape(groups, parts, own).transpose(1, 0, 2).reshape(-1)
    small_rows = w_router.shape[0]
    placed_router = (
        w_router.reshape(small_rows, groups, parts, own).transpose(0, 2, 1, 3).reshape(small_rows, EXPERTS)
    )
    vectors = jnp.stack([ln1_gain, ln1_bias, ln2_gain, ln2_bias], axis=1)
    packed = jnp.concatenate(
        [w_qkv, w_proj, placed_router, vectors, jnp.zeros((small_rows, LANES - EXPERTS - 4), full)],
        axis=1,
    ).astype(low)
    weights = lax.all_gather(packed, ALL, axis=0, tiled=True)

    def spread(master):
        pieces = master.astype(low).reshape(parts, own, *master.shape[1:])
        pieces = jnp.concatenate([pieces] * replicas, axis=0)
        return lax.all_to_all(pieces, ALL, split_axis=0, concat_axis=0, tiled=True)

    def collect(grad):
        pieces = lax.all_to_all(grad, ALL, split_axis=0, concat_axis=0, tiled=True)
        pieces = pieces.reshape(replicas, parts * own, *grad.shape[2:])
        return jnp.sum(pieces.astype(full), axis=0)

    def exchange(rows):
        rows = rows.reshape(peers, own * CAP, D)
        rows = lax.all_to_all(rows, ("part", "expert"), split_axis=0, concat_axis=0, tiled=True)
        return rows.reshape(peers, own, CAP, D)

    def padded(rows, fill=0):
        rows = rows.reshape(images, SEQ, rows.shape[1])
        return jnp.pad(rows, ((0, 0), (0, ROWS - SEQ), (0, 0)), constant_values=fill)

    x = padded(tokens)
    dy = padded(cotangent)
    picks = padded(choices, -1).reshape(count, 2)
    named = (picks[:, :, None] == order[None, None, :]).any(axis=1)
    earlier = np.tril(np.ones((count, count)), -1).astype(low)
    slots = dot(earlier, named.astype(low))
    keys = jnp.where(named, slots, -1.0)
    key_rows = keys.T.reshape(peers, own, count)
    key_columns = jnp.pad(keys, ((0, 0), (0, LANES - EXPERTS)), constant_values=-1).astype(low)

    dy_rows = dy.reshape(count, D)
    dy_slots = exchange(dispatch(key_rows, dy_rows))
    first_weight = spread(w_expert_in)
    qkv, ctx, r, h, probs = attend(x, weights)
    h_slots = exchange(dispatch(key_rows, h.reshape(count, D)))
    second_weight = spread(w_expert_out)
    mine = (lax.axis_index("part") * groups + lax.axis_index("expert")) * own + jnp.arange(own)
    select = (mine[:, None, None] == jnp.arange(LANES)[None, None, :]).astype(full)
    g, slope, dye, dw_second = expert_first(
        h_slots, dy_slots, first_weight, weights[:, QKV + D :], select, tile
    )
    y = exchange(expert_second(g, second_weight))
    dbuf, dw_first = expert_back(h_slots, dye, slope, first_weight, second_weight, tile)
    dbuf = exchange(dbuf)
    expert_out_grad = collect(dw_second)
    expert_in_grad = collect(dw_first)
    output, dprobs = combine(
        key_columns,
        probs.reshape(count, LANES),
        dy_rows,
        r.reshape(count, D),
        y.reshape(peers, own * CAP, D),
    )
    dh = gather(key_columns, dbuf.reshape(peers, own * CAP, D))
    dx, grads = attend_back(
        x, weights, qkv, ctx, r, h, probs,
        dprobs.reshape(images, ROWS, LANES), dh.reshape(images, ROWS, D), dy,
    )
    grads = grads.reshape(owners, small_rows, PACKED)
    grads = lax.all_to_all(grads, ALL, split_axis=0, concat_axis=0, tiled=True)
    grads = jnp.sum(grads.astype(full), axis=0).astype(low)
    grads = lax.psum(grads, "expert").astype(full)
    router_grad = (
        grads[:, QKV + D : QKV + D + EXPERTS]
        .reshape(small_rows, parts, groups, own)
        .transpose(0, 2, 1, 3)
        .reshape(small_rows, EXPERTS)
    )
    norms = [grads[:, QKV + D + EXPERTS + i] for i in range(4)]

    def unpadded(rows):
        return rows.reshape(images, ROWS, D)[:, :SEQ].reshape(images * SEQ, D)

    return (
        unpadded(output),
        unpadded(dx),
        norms[0],
        norms[1],
        grads[:, :QKV],
        grads[:, QKV : QKV + D],
        norms[2],
        norms[3],
        router_grad,
        expert_in_grad,
        expert_out_grad,
    )


def solution(mesh):
    dp, groups = mesh.shape["dp"], mesh.shape["expert"]
    parts = min(EXPERTS // groups, dp // 2)
    mesh = Mesh(mesh.devices.reshape(dp // parts, parts, groups), ("replica", "part", "expert"))
    rows = P(("replica", "part", "expert"), None)
    vector, matrix = P(ALL), P(ALL, None)
    experts = P("expert", ALL, None)
    return jax.shard_map(
        body,
        mesh=mesh,
        in_specs=(
            rows, rows, vector, vector, matrix, matrix, vector, vector, matrix, experts, experts, rows,
        ),
        out_specs=(
            rows, rows, vector, vector, matrix, matrix, vector, vector, matrix, experts, experts,
        ),
        check_vma=False,
    )
```

```python
from functools import partial

import jax
import jax.numpy as jnp
from jax import lax
from jax.experimental import pallas as pl
from jax.experimental.pallas import tpu as pltpu
from jax.sharding import Mesh
from jax.sharding import PartitionSpec as P

D = 512
HEADS = 8
EXPERTS = 32
SEQ = 197
CAP = 128
ROWS = 208
HEAD = D // HEADS
LANES = 128
QKV = 3 * D
PACKED = QKV + D + LANES
epsilon = 1e-06
low = jnp.bfloat16
full = jnp.float32
MESH = pl.DeviceIdType.MESH
BIG = 63 * 1024 * 1024


def dot(left, right):
    return jnp.dot(left, right, preferred_element_type=full)


def dot_rt(left, right):
    return lax.dot_general(left, right, (((1,), (1,)), ((), ())), preferred_element_type=full)


def dot_lt(left, right):
    return lax.dot_general(left, right, (((0,), (0,)), ((), ())), preferred_element_type=full)


def lanes_of(shape):
    return lax.broadcasted_iota(jnp.int32, shape, len(shape) - 1)


def normed_rows(values):
    center = values - jnp.mean(values, axis=-1, keepdims=True)
    factor = lax.rsqrt(jnp.mean(center * center, axis=-1, keepdims=True) + epsilon)
    return center * factor, factor


def norm_back(normed, factor, gain_vec, upstream):
    scaled = upstream * gain_vec
    return factor * (
        scaled
        - jnp.mean(scaled, axis=-1, keepdims=True)
        - normed * jnp.mean(scaled * normed, axis=-1, keepdims=True)
    )


def norm_vectors(weights_ref):
    rows = weights_ref[:, QKV + D :].astype(full).T
    return [rows[EXPERTS + i : EXPERTS + i + 1] for i in range(4)]


def halves(pair):
    first = lanes_of(pair.shape) < HEAD
    zero = jnp.zeros_like(pair)
    return jnp.where(first, pair, zero), jnp.where(first, zero, pair)


def head_probs(query, key_pair):
    scores = dot_rt(query, key_pair) * (HEAD**-0.5)
    scores = jnp.where(lanes_of(scores.shape) < SEQ, scores, -1e30)
    grown = jnp.exp(scores - jnp.max(scores, axis=-1, keepdims=True))
    return grown / jnp.sum(grown, axis=-1, keepdims=True)


def attend_kernel(x_ref, w_ref, order_ref, qkv_ref, ctx_ref, r_ref, h_ref, probs_ref):
    gain_one, bias_one, gain_two, bias_two = norm_vectors(w_ref)
    x = x_ref[0].astype(full)
    normed, _ = normed_rows(x)
    attn_in = (normed * gain_one + bias_one).astype(low)
    qkv_ref[0] = dot(attn_in, w_ref[:, :QKV]).astype(low)
    for pair in range(HEADS // 2):
        at = pair * LANES
        query = halves(qkv_ref[0, :, at : at + LANES])
        key = qkv_ref[0, :, D + at : D + at + LANES]
        value = halves(qkv_ref[0, :, 2 * D + at : 2 * D + at + LANES])
        total = None
        for i in range(2):
            part = dot(head_probs(query[i], key).astype(low), value[i])
            total = part if total is None else total + part
        ctx_ref[0, :, at : at + LANES] = total.astype(low)
    r = x + dot(ctx_ref[0], w_ref[:, QKV : QKV + D])
    r_ref[0] = r
    normed, _ = normed_rows(r)
    h = (normed * gain_two + bias_two).astype(low)
    h_ref[0] = h
    logits = dot(h, dot(w_ref[:, QKV + D :], order_ref[...]).astype(low))
    logits = jnp.where(lanes_of(logits.shape) < EXPERTS, logits, -1e30)
    grown = jnp.exp(logits - jnp.max(logits, axis=-1, keepdims=True))
    probs_ref[0] = grown / jnp.sum(grown, axis=-1, keepdims=True)


def image_spec(width):
    return pl.BlockSpec((1, ROWS, width), lambda i: (i, 0, 0))


def whole_spec(shape):
    return pl.BlockSpec(shape, lambda *_: (0,) * len(shape))


def params(n):
    return pltpu.CompilerParams(
        dimension_semantics=("arbitrary",) * n, vmem_limit_bytes=BIG
    )


def attend(x, weights, order):
    images = x.shape[0]
    shapes = ((QKV, low), (D, low), (D, full), (D, low), (LANES, full))
    return pl.pallas_call(
        attend_kernel,
        grid=(images,),
        in_specs=[image_spec(D), whole_spec(weights.shape), whole_spec(order.shape)],
        out_specs=[image_spec(width) for width, _ in shapes],
        out_shape=[jax.ShapeDtypeStruct((images, ROWS, w), t) for w, t in shapes],
        compiler_params=params(1),
        cost_estimate=pl.CostEstimate(
            flops=8 * 10**9, bytes_accessed=12 * 10**6, transcendentals=2 * 10**6
        ),
        name="attend",
    )(x, weights, order)


def attend_back_kernel(
    images, x_ref, w_ref, order_ref, qkv_ref, ctx_ref, r_ref, h_ref, probs_ref, dprobs_ref, dh_ref, dy_ref,
    dx_ref, grads_ref, dqkv_ref, qkv_acc, proj_acc, router_acc, norm_acc,
):
    step = pl.program_id(0)

    @pl.when(step == 0)
    def _():
        qkv_acc[...] = jnp.zeros_like(qkv_acc)
        proj_acc[...] = jnp.zeros_like(proj_acc)
        router_acc[...] = jnp.zeros_like(router_acc)
        norm_acc[...] = jnp.zeros_like(norm_acc)

    gain_one, bias_one, gain_two, _ = norm_vectors(w_ref)
    probs, dprobs = probs_ref[0], dprobs_ref[0]
    dlogits = (probs * (dprobs - jnp.sum(probs * dprobs, axis=-1, keepdims=True))).astype(low)
    router_acc[...] += dot_lt(h_ref[0], dlogits)
    router = dot(w_ref[:, QKV + D :], order_ref[...]).astype(low)
    dh = dh_ref[0] + dot_rt(dlogits, router)
    normed, factor = normed_rows(r_ref[0])
    norm_acc[2:3] += jnp.sum(dh * normed, axis=0, keepdims=True)
    norm_acc[3:4] += jnp.sum(dh, axis=0, keepdims=True)
    dr = dy_ref[0].astype(full) + norm_back(normed, factor, gain_two, dh)
    dattended = dr.astype(low)
    proj_acc[...] += dot_lt(ctx_ref[0], dattended)
    dctx = dot_rt(dattended, w_ref[:, QKV : QKV + D]).astype(low)
    for pair in range(HEADS // 2):
        at = pair * LANES
        query = halves(qkv_ref[0, :, at : at + LANES])
        key = qkv_ref[0, :, D + at : D + at + LANES]
        keys = halves(key)
        value = qkv_ref[0, :, 2 * D + at : 2 * D + at + LANES]
        dhead = halves(dctx[:, at : at + LANES])
        dq = dk = dv = None
        for i in range(2):
            p = head_probs(query[i], key)
            dp = dot_rt(dhead[i], value)
            ds = (p * (dp - jnp.sum(p * dp, axis=-1, keepdims=True))).astype(low)
            parts = dot(ds, keys[i]), dot_lt(ds, query[i]), dot_lt(p.astype(low), dhead[i])
            dq, dk, dv = parts if dq is None else (dq + parts[0], dk + parts[1], dv + parts[2])
        dqkv_ref[:, at : at + LANES] = (dq * HEAD**-0.5).astype(low)
        dqkv_ref[:, D + at : D + at + LANES] = (dk * HEAD**-0.5).astype(low)
        dqkv_ref[:, 2 * D + at : 2 * D + at + LANES] = dv.astype(low)
    normed, factor = normed_rows(x_ref[0].astype(full))
    attn_in = (normed * gain_one + bias_one).astype(low)
    qkv_acc[...] += dot_lt(attn_in, dqkv_ref[...])
    da = dot_rt(dqkv_ref[...], w_ref[:, :QKV])
    norm_acc[0:1] += jnp.sum(da * normed, axis=0, keepdims=True)
    norm_acc[1:2] += jnp.sum(da, axis=0, keepdims=True)
    dx_ref[0] = dr + norm_back(normed, factor, gain_one, da)

    @pl.when(step == images - 1)
    def _():
        grads_ref[:, :QKV] = qkv_acc[...].astype(low)
        grads_ref[:, QKV : QKV + D] = proj_acc[...].astype(low)
        columns = norm_acc[...].T
        moved = pltpu.roll(columns, EXPERTS, 1)
        lane = lanes_of(moved.shape)
        tile = jnp.where(lane < EXPERTS, router_acc[...], moved)
        grads_ref[:, QKV + D :] = dot_rt(tile.astype(low), order_ref[...]).astype(low)


def attend_back(x, weights, order, qkv, ctx, r, h, probs, dprobs, dh, dy):
    images = x.shape[0]
    widths = (D, None, None, QKV, D, D, D, LANES, LANES, D, D)
    arrays = (x, weights, order, qkv, ctx, r, h, probs, dprobs, dh, dy)
    return pl.pallas_call(
        partial(attend_back_kernel, images),
        grid=(images,),
        in_specs=[
            whole_spec(a.shape) if w is None else image_spec(w) for a, w in zip(arrays, widths)
        ],
        out_specs=[image_spec(D), whole_spec((D, PACKED))],
        out_shape=[
            jax.ShapeDtypeStruct((images, ROWS, D), full),
            jax.ShapeDtypeStruct((D, PACKED), low),
        ],
        scratch_shapes=[
            pltpu.VMEM((ROWS, QKV), low),
            pltpu.VMEM((D, QKV), full),
            pltpu.VMEM((D, D), full),
            pltpu.VMEM((D, LANES), full),
            pltpu.VMEM((LANES, D), full),
        ],
        compiler_params=params(1),
        cost_estimate=pl.CostEstimate(
            flops=20 * 10**9, bytes_accessed=16 * 10**6, transcendentals=2 * 10**6
        ),
        name="attend_back",
    )(*arrays)


def position(groups):
    return lax.axis_index("part") * groups + lax.axis_index("expert")


def peer_of(groups, k):
    peer = position(groups) ^ k
    return lax.axis_index("replica"), peer // groups, peer % groups


def greet(peers, groups):
    barrier = pltpu.get_barrier_semaphore()
    for k in range(1, peers):
        pl.semaphore_signal(barrier, inc=1, device_id=peer_of(groups, k), device_id_type=MESH)
    pl.semaphore_wait(barrier, peers - 1)


def swap(source, target, sends, receives, groups, k):
    return pltpu.make_async_remote_copy(
        src_ref=source.at[k],
        dst_ref=target.at[k],
        send_sem=sends.at[k],
        recv_sem=receives.at[k],
        device_id=peer_of(groups, k),
        device_id_type=MESH,
    )


def dispatch_kernel(groups, keys_ref, rows_ref, out_ref, blocks, sends, receives, local):
    peers, own, tokens = keys_ref.shape
    slots = lax.broadcasted_iota(jnp.int32, (CAP, tokens), 0).astype(full)
    greet(peers, groups)

    def build(k):
        picks = [(keys_ref[k, i : i + 1] == slots).astype(low) for i in range(own)]
        picks = jnp.concatenate(picks, axis=0) if own > 1 else picks[0]
        blocks[k] = dot(picks, rows_ref[...]).astype(low).reshape(own, CAP, D)

    copies = [swap(blocks, out_ref, sends, receives, groups, k) for k in range(1, peers)]
    for k in range(1, peers):
        build(k)
        copies[k - 1].start()
    build(0)
    mine = pltpu.make_async_copy(blocks.at[0], out_ref.at[0], local)
    mine.start()
    for copy in copies:
        copy.wait()
    mine.wait()


def dispatch(keys, rows, groups, number):
    peers, own, tokens = keys.shape
    shape = (peers, own, CAP, D)
    return pl.pallas_call(
        partial(dispatch_kernel, groups),
        in_specs=[pl.BlockSpec(memory_space=pltpu.VMEM)] * 2,
        out_specs=pl.BlockSpec(memory_space=pl.ANY),
        out_shape=jax.ShapeDtypeStruct(shape, low),
        scratch_shapes=[
            pltpu.VMEM(shape, low),
            pltpu.SemaphoreType.DMA((peers,)),
            pltpu.SemaphoreType.DMA((peers,)),
            pltpu.SemaphoreType.DMA,
        ],
        compiler_params=pltpu.CompilerParams(
            vmem_limit_bytes=BIG, collective_id=number, has_side_effects=True
        ),
        cost_estimate=pl.CostEstimate(
            flops=60 * 10**9, bytes_accessed=5 * 10**6, transcendentals=0
        ),
        name=f"dispatch_{number}",
    )(keys, rows)


def exchange_kernel(groups, blocks_ref, out_ref, sends, receives, local):
    peers = blocks_ref.shape[0]
    greet(peers, groups)
    copies = [swap(blocks_ref, out_ref, sends, receives, groups, k) for k in range(1, peers)]
    for copy in copies:
        copy.start()
    mine = pltpu.make_async_copy(blocks_ref.at[0], out_ref.at[0], local)
    mine.start()
    for copy in copies:
        copy.wait()
    mine.wait()


def exchange(blocks, groups, number):
    peers = blocks.shape[0]
    return pl.pallas_call(
        partial(exchange_kernel, groups),
        in_specs=[pl.BlockSpec(memory_space=pl.ANY)],
        out_specs=pl.BlockSpec(memory_space=pl.ANY),
        out_shape=jax.ShapeDtypeStruct(blocks.shape, low),
        scratch_shapes=[
            pltpu.SemaphoreType.DMA((peers,)),
            pltpu.SemaphoreType.DMA((peers,)),
            pltpu.SemaphoreType.DMA,
        ],
        compiler_params=pltpu.CompilerParams(collective_id=number, has_side_effects=True),
        cost_estimate=pl.CostEstimate(
            flops=60 * 10**9, bytes_accessed=10 * 10**6, transcendentals=0
        ),
        name=f"exchange_{number}",
    )(blocks)


def chooser(own, k):
    shape = (LANES, own * CAP)
    expert = lax.broadcasted_iota(jnp.int32, shape, 0)
    slot = lax.broadcasted_iota(jnp.int32, shape, 1)
    return (expert == k * own + slot // CAP).astype(low)


def combine_kernel(keys_ref, probs_ref, r_ref, y_ref, out_ref):
    peers, own, _, _ = y_ref.shape

    @pl.loop(0, r_ref.shape[0] // ROWS)
    def _(i):
        rows = pl.ds(pl.multiple_of(i * ROWS, ROWS), ROWS)
        slot = (lanes_of((ROWS, own * CAP)) % CAP).astype(full)
        probs = probs_ref[rows].astype(low)
        total = r_ref[rows]
        for k in range(peers):
            spread = chooser(own, k)
            here = dot(keys_ref[rows], spread) == slot
            gate = jnp.where(here, dot(probs, spread), 0.0)
            total = total + dot(gate.astype(low), y_ref[k].reshape(own * CAP, D))
        out_ref[rows] = total.astype(low)


def combine(keys, probs, r, y):
    tokens = keys.shape[0]
    return pl.pallas_call(
        combine_kernel,
        out_shape=jax.ShapeDtypeStruct((tokens, D), low),
        compiler_params=pltpu.CompilerParams(vmem_limit_bytes=BIG),
        cost_estimate=pl.CostEstimate(
            flops=6 * 10**9, bytes_accessed=10 * 10**6, transcendentals=0
        ),
        name="combine",
    )(keys, probs, r, y)


def gather_kernel(keys_ref, back_ref, dh_ref, dprobs_ref):
    peers, own, _, _ = back_ref.shape
    width = own * CAP

    @pl.loop(0, dh_ref.shape[0] // ROWS)
    def _(i):
        rows = pl.ds(pl.multiple_of(i * ROWS, ROWS), ROWS)
        slot = (lanes_of((ROWS, width)) % CAP).astype(full)
        lane = lanes_of((ROWS, LANES))
        total = jnp.zeros((ROWS, D), full)
        dprobs = jnp.zeros((ROWS, LANES), full)
        for k in range(peers):
            here = dot(keys_ref[rows], chooser(own, k)) == slot
            total = total + dot(here.astype(low), back_ref[k, :, :CAP].reshape(width, D))
            dgate = back_ref[k, :, CAP : CAP + 1].astype(full)
            dgate = dgate[:, :, :CAP] + dgate[:, :, CAP : 2 * CAP]
            agreed = [
                jnp.where(here[:, e * CAP : (e + 1) * CAP], dgate[e], 0.0) for e in range(own)
            ]
            for e in range(own):
                column = jnp.sum(agreed[e], axis=-1, keepdims=True)
                dprobs = jnp.where(lane == k * own + e, column, dprobs)
        dh_ref[rows] = total
        dprobs_ref[rows] = dprobs


def gather(keys, back):
    tokens = keys.shape[0]
    return pl.pallas_call(
        gather_kernel,
        out_shape=[
            jax.ShapeDtypeStruct((tokens, D), full),
            jax.ShapeDtypeStruct((tokens, LANES), full),
        ],
        compiler_params=pltpu.CompilerParams(vmem_limit_bytes=BIG),
        cost_estimate=pl.CostEstimate(
            flops=6 * 10**9, bytes_accessed=7 * 10**6, transcendentals=0
        ),
        name="gather",
    )(keys, back)


GELU = 0.7978845608028654
CUBE = 0.044715


def gelu_pair(u):
    square = u * u
    bent = jnp.tanh(u * (GELU * CUBE * square + GELU))
    half = 0.5 * bent + 0.5
    value = u * half
    return value, half + value * (1.0 - bent) * (3.0 * GELU * CUBE * square + GELU)


def first_kernel(h_ref, dy_ref, w_ref, wr_ref, sel_ref, g_ref, slope_ref, dw_ref, gates, dye_t):
    sources = h_ref.shape[0]
    tile = w_ref.shape[3]

    @pl.when(pl.program_id(1) == 0)
    def _():
        for k in range(sources):
            rows = slice(k * CAP, (k + 1) * CAP)
            logits = dot(h_ref[k, 0], wr_ref[...])
            logits = jnp.where(lanes_of(logits.shape) < EXPERTS, logits, -1e30)
            grown = jnp.exp(logits - jnp.max(logits, axis=-1, keepdims=True))
            mine = jnp.sum(grown * sel_ref[0], axis=-1, keepdims=True)
            gate = mine / jnp.sum(grown, axis=-1, keepdims=True)
            gates[rows] = jnp.broadcast_to(gate, (CAP, LANES))
            dye_t[:, rows] = (dy_ref[k, 0].astype(full) * gate).T.astype(low)

    w = w_ref[:, 0].reshape(D, tile)
    for k in range(0, sources, 2):
        rows = slice(k * CAP, (k + 2) * CAP)
        value, slope = gelu_pair(dot(h_ref[k : k + 2, 0].reshape(2 * CAP, D), w))
        g_ref[0, rows] = value.astype(low)
        slope_ref[0, rows] = (slope * gates[rows, :1]).astype(low)
    grad = dot(dye_t[...], g_ref[0]).T
    dw_ref[:, 0] = grad.astype(low).reshape(dw_ref.shape[0], dw_ref.shape[2], D)


def slot_spec(sources):
    return pl.BlockSpec((sources, 1, CAP, D), lambda e, f: (0, e, 0, 0))


def expert_first(h, dy, w_in, w_router, select, tile):
    sources = h.shape[0]
    owners, own, depth, hidden = w_in.shape
    rows = sources * CAP
    per = hidden // owners
    hidden_spec = pl.BlockSpec((1, rows, tile), lambda e, f: (e, 0, f))
    return pl.pallas_call(
        first_kernel,
        grid=(own, hidden // tile),
        in_specs=[
            slot_spec(sources),
            slot_spec(sources),
            pl.BlockSpec((owners, 1, depth, tile), lambda e, f: (0, e, 0, f)),
            whole_spec(w_router.shape),
            pl.BlockSpec((1, 1, LANES), lambda e, f: (e, 0, 0)),
        ],
        out_specs=[
            hidden_spec,
            hidden_spec,
            pl.BlockSpec((tile // per, 1, per, D), lambda e, f: (f, e, 0, 0)),
        ],
        out_shape=[
            jax.ShapeDtypeStruct((own, rows, hidden), low),
            jax.ShapeDtypeStruct((own, rows, hidden), low),
            jax.ShapeDtypeStruct((owners, own, per, D), low),
        ],
        scratch_shapes=[pltpu.VMEM((rows, LANES), full), pltpu.VMEM((D, rows), low)],
        compiler_params=params(2),
        cost_estimate=pl.CostEstimate(
            flops=4 * own * rows * D * hidden,
            bytes_accessed=50 * 10**6,
            transcendentals=own * rows * hidden,
        ),
        name="expert_first",
    )(h, dy, w_in, w_router, select)


def rest_kernel(
    groups, own, steps, dy_ref, h_ref, g_ref, slope_ref, w_in_ref, w_out_ref,
    back_ref, dw_ref, y_ref, du, acc, dgates, dgate_rows, h_t, staged, sends, receives, local,
):
    sources = dy_ref.shape[0]
    tile = slope_ref.shape[2]
    at = pl.program_id(0)
    phase, expert, step = at // (own * steps), at // steps % own, at % steps
    w_in = w_in_ref[:, 0].reshape(D, tile)
    w_out = w_out_ref[:, 0].reshape(tile, D)
    chunk = 2 * CAP

    def copy(k, e):
        return pltpu.make_async_remote_copy(
            src_ref=staged.at[k, e],
            dst_ref=back_ref.at[k, e],
            send_sem=sends.at[k, e],
            recv_sem=receives.at[k, e],
            device_id=peer_of(groups, k),
            device_id_type=MESH,
        )

    def mine(e):
        return pltpu.make_async_copy(staged.at[0, e], back_ref.at[0, e], local.at[e])

    @pl.when(at == 0)
    def _():
        greet(sources, groups)

    @pl.when((phase != 1) & (step == 0))
    def _():
        acc[...] = jnp.zeros_like(acc)

    @pl.when(phase == 0)
    def _():
        @pl.when(step == 0)
        def _():
            dgates[...] = jnp.zeros_like(dgates)

        for k in range(0, sources, 2):
            rows = slice(k * CAP, (k + 2) * CAP)
            dg = dot_rt(dy_ref[k : k + 2, 0].reshape(chunk, D), w_out)
            change = (dg * slope_ref[0, rows].astype(full)).astype(low)
            du[expert * steps + step, rows] = change
            acc[rows] += dot_rt(change, w_in)
            agreed = dg * g_ref[0, rows].astype(full)
            dgates[rows] += sum(agreed[:, i : i + LANES] for i in range(0, tile, LANES))

        @pl.when(step == steps - 1)
        def _():
            sums = dgates[...]
            high = sums.astype(low)
            rest = (sums - high.astype(full)).astype(low)
            ones = jnp.ones((16, LANES), low)
            dgate_rows[...] = dot_rt(ones, high) + dot_rt(ones, rest)
            for k in range(sources):
                rows = slice(k * CAP, (k + 1) * CAP)
                staged[k, expert, :CAP] = acc[rows].astype(low)
                row = dgate_rows[:, rows]
                high = row.astype(low)
                staged[k, expert, CAP:, :CAP] = high
                staged[k, expert, CAP:, CAP : 2 * CAP] = (row - high.astype(full)).astype(low)
                staged[k, expert, CAP:, 2 * CAP :] = jnp.zeros((16, D - 2 * CAP), low)

        for e in range(own):
            @pl.when((step == steps - 1) & (expert == e))
            def _():
                for k in range(1, sources):
                    copy(k, e).start()
                mine(e).start()

    @pl.when(phase == 1)
    def _():
        @pl.when(step == 0)
        def _():
            for k in range(sources):
                h_t[:, k * CAP : (k + 1) * CAP] = h_ref[k, 0].T

        grad = dot(h_t[...], du[expert * steps + step]).astype(low)
        dw_ref[:, 0] = grad.reshape(dw_ref.shape[0], dw_ref.shape[2], tile)

    @pl.when(phase == 2)
    def _():
        for k in range(0, sources, 2):
            rows = slice(k * CAP, (k + 2) * CAP)
            acc[rows] += dot(g_ref[0, rows], w_out)

        @pl.when(step == steps - 1)
        def _():
            y_ref[:, 0] = acc[...].astype(low).reshape(sources, CAP, D)

    @pl.when(at == 3 * own * steps - 1)
    def _():
        for e in range(own):
            for k in range(1, sources):
                copy(k, e).wait()
            mine(e).wait()


def expert_rest(dy, h, g, slope, w_in, w_out, tile, groups, number):
    sources, own, _, _ = dy.shape
    owners, _, depth, hidden = w_in.shape
    rows = sources * CAP
    per = hidden // owners
    steps = hidden // tile
    last = own * steps - 1

    def during(phases):
        def find(at):
            if 0 in phases and 2 in phases:
                inside = jnp.where(at // (last + 1) == 1, last, at % (last + 1))
            else:
                inside = jnp.clip(at - phases[0] * (last + 1), 0, last)
            return inside // steps, inside % steps

        return find

    def spec(shape, phases, index, buffers=2):
        return pl.BlockSpec(
            shape, lambda at: index(*during(phases)(at)), pipeline_mode=pl.Buffered(buffers)
        )

    token, hidden_at = (sources, 1, CAP, D), (1, rows, tile)
    whole_expert = lambda e, f: (0, e, 0, 0)
    in_tile = lambda e, f: (0, e, 0, f)
    return pl.pallas_call(
        partial(rest_kernel, groups, own, steps),
        grid=(3 * own * steps,),
        in_specs=[
            spec(token, (0,), whole_expert, 1),
            spec(token, (1,), whole_expert, 1),
            spec(hidden_at, (0, 2), lambda e, f: (e, 0, f)),
            spec(hidden_at, (0,), lambda e, f: (e, 0, f)),
            spec((owners, 1, depth, tile), (0,), in_tile),
            spec((tile // per, 1, per, D), (0, 2), lambda e, f: (f, e, 0, 0)),
        ],
        out_specs=[
            pl.BlockSpec(memory_space=pl.ANY),
            spec((owners, 1, depth, tile), (1,), in_tile),
            spec(token, (2,), whole_expert),
        ],
        out_shape=[
            jax.ShapeDtypeStruct((sources, own, CAP + 16, D), low),
            jax.ShapeDtypeStruct(w_in.shape, low),
            jax.ShapeDtypeStruct(dy.shape, low),
        ],
        scratch_shapes=[
            pltpu.VMEM((own * steps, rows, tile), low),
            pltpu.VMEM((rows, D), full),
            pltpu.VMEM((rows, LANES), full),
            pltpu.VMEM((16, rows), full),
            pltpu.VMEM((D, rows), low),
            pltpu.VMEM((sources, own, CAP + 16, D), low),
            pltpu.SemaphoreType.DMA((sources, own)),
            pltpu.SemaphoreType.DMA((sources, own)),
            pltpu.SemaphoreType.DMA((own,)),
        ],
        compiler_params=pltpu.CompilerParams(
            dimension_semantics=("arbitrary",),
            vmem_limit_bytes=BIG,
            collective_id=number,
            has_side_effects=True,
        ),
        cost_estimate=pl.CostEstimate(
            flops=8 * own * rows * D * hidden, bytes_accessed=60 * 10**6, transcendentals=0
        ),
        name="expert_rest",
    )(dy, h, g, slope, w_in, w_out)


ALL = ("replica", "part")


def body(
    tokens,
    choices,
    ln1_gain,
    ln1_bias,
    w_qkv,
    w_proj,
    ln2_gain,
    ln2_bias,
    w_router,
    w_expert_in,
    w_expert_out,
    cotangent,
):
    replicas, parts, groups = (lax.axis_size(name) for name in ("replica", "part", "expert"))
    owners = replicas * parts
    peers = parts * groups
    own = EXPERTS // peers
    images = tokens.shape[0] // SEQ
    count = images * ROWS
    tile = 512 * 16 // peers

    small_rows = w_router.shape[0]
    placed_router = (
        w_router.reshape(small_rows, groups, parts, own).transpose(0, 2, 1, 3).reshape(small_rows, EXPERTS)
    )
    vectors = jnp.stack([ln1_gain, ln1_bias, ln2_gain, ln2_bias], axis=1)
    packed = jnp.concatenate(
        [w_qkv, w_proj, placed_router, vectors, jnp.zeros((small_rows, LANES - EXPERTS - 4), full)],
        axis=1,
    ).astype(low)
    weights = lax.all_gather(packed, ALL, axis=0, tiled=True)

    def spread(master):
        pieces = master.astype(low).reshape(parts, own, *master.shape[1:])
        pieces = jnp.concatenate([pieces] * replicas, axis=0)
        return lax.all_to_all(pieces, ALL, split_axis=0, concat_axis=0, tiled=True)

    def collect(grad):
        pieces = lax.all_to_all(grad, ALL, split_axis=0, concat_axis=0, tiled=True)
        pieces = pieces.reshape(replicas, parts * own, *grad.shape[2:])
        return jnp.sum(pieces.astype(full), axis=0)

    me = position(groups)

    def padded(rows, fill=0):
        rows = rows.reshape(images, SEQ, rows.shape[1])
        return jnp.pad(rows, ((0, 0), (0, ROWS - SEQ), (0, 0)), constant_values=fill)

    x = padded(tokens)
    dy = padded(cotangent)
    picks = padded(choices, -1).reshape(count, 2)
    column = jnp.arange(EXPERTS)
    place = (me ^ (column // own)) * own + column % own
    expert = (place // own % groups) * (parts * own) + place // (groups * own) * own + place % own
    lane = jnp.arange(LANES)
    order = jnp.where(lane < EXPERTS, jnp.pad(place, (0, LANES - EXPERTS)), lane)
    order = (lane[:, None] == order[None, :]).astype(low)
    named = (picks[:, :, None] == expert[None, None, :]).any(axis=1)
    row = jnp.arange(count)
    slots = dot((row[None, :] < row[:, None]).astype(low), named.astype(low))
    keys = jnp.where(named, slots, -1.0)
    key_rows = keys.T.reshape(peers, own, count)
    key_columns = jnp.pad(keys, ((0, 0), (0, LANES - EXPERTS)), constant_values=-1).astype(low)

    first_weight = spread(w_expert_in)
    dy_slots = dispatch(key_rows, dy.reshape(count, D), groups, 0)
    qkv, ctx, r, h, probs = attend(x, weights, order)
    w_expert_out, h = lax.optimization_barrier((w_expert_out, h))
    second_weight = spread(w_expert_out)
    h_slots = dispatch(key_rows, h.reshape(count, D), groups, 1)
    select = ((me * own + jnp.arange(own))[:, None, None] == lane[None, None, :]).astype(full)
    g, slope, dw_second = expert_first(
        h_slots, dy_slots, first_weight, weights[:, QKV + D :], select, tile
    )
    back, dw_first, y = expert_rest(
        dy_slots, h_slots, g, slope, first_weight, second_weight, tile, groups, 2
    )
    y = exchange(y, groups, 3)
    expert_out_grad = collect(dw_second)
    expert_in_grad = collect(dw_first)
    dh, dprobs = gather(key_columns, back)
    dx, grads = attend_back(
        x, weights, order, qkv, ctx, r, h, probs,
        dprobs.reshape(images, ROWS, LANES), dh.reshape(images, ROWS, D), dy,
    )
    output = combine(key_columns, probs.reshape(count, LANES), r.reshape(count, D), y)
    grads = lax.psum_scatter(grads, ALL, scatter_dimension=0, tiled=True)
    grads = lax.psum(grads, "expert").astype(full)
    router_grad = (
        grads[:, QKV + D : QKV + D + EXPERTS]
        .reshape(small_rows, parts, groups, own)
        .transpose(0, 2, 1, 3)
        .reshape(small_rows, EXPERTS)
    )
    norms = [grads[:, QKV + D + EXPERTS + i] for i in range(4)]

    def unpadded(rows):
        return rows.reshape(images, ROWS, D)[:, :SEQ].reshape(images * SEQ, D)

    return (
        unpadded(output),
        unpadded(dx),
        norms[0],
        norms[1],
        grads[:, :QKV],
        grads[:, QKV : QKV + D],
        norms[2],
        norms[3],
        router_grad,
        expert_in_grad,
        expert_out_grad,
    )


def solution(mesh):
    dp, groups = mesh.shape["dp"], mesh.shape["expert"]
    parts = min(EXPERTS // groups, dp // 2)
    mesh = Mesh(mesh.devices.reshape(dp // parts, parts, groups), ("replica", "part", "expert"))
    rows = P(("replica", "part", "expert"), None)
    vector, matrix = P(ALL), P(ALL, None)
    experts = P("expert", ALL, None)
    return jax.shard_map(
        body,
        mesh=mesh,
        in_specs=(
            rows, rows, vector, vector, matrix, matrix, vector, vector, matrix, experts, experts, rows,
        ),
        out_specs=(
            rows, rows, vector, vector, matrix, matrix, vector, vector, matrix, experts, experts,
        ),
        check_vma=False,
    )
```

```python
from functools import partial

import jax
import jax.numpy as jnp
from jax import lax
from jax.experimental import pallas as pl
from jax.experimental.pallas import tpu as pltpu
from jax.sharding import Mesh
from jax.sharding import PartitionSpec as P

D = 512
HEADS = 8
EXPERTS = 32
SEQ = 197
CAP = 128
ROWS = 208
HEAD = D // HEADS
LANES = 128
QKV = 3 * D
SENT = D + LANES
PACKED = QKV + D + LANES
epsilon = 1e-06
low = jnp.bfloat16
full = jnp.float32
MESH = pl.DeviceIdType.MESH
BIG = 63 * 1024 * 1024


def dot(left, right):
    return jnp.dot(left, right, preferred_element_type=full)


def dot_rt(left, right):
    return lax.dot_general(left, right, (((1,), (1,)), ((), ())), preferred_element_type=full)


def dot_lt(left, right):
    return lax.dot_general(left, right, (((0,), (0,)), ((), ())), preferred_element_type=full)


def lanes_of(shape):
    return lax.broadcasted_iota(jnp.int32, shape, len(shape) - 1)


def normed_rows(values):
    center = values - jnp.mean(values, axis=-1, keepdims=True)
    factor = lax.rsqrt(jnp.mean(center * center, axis=-1, keepdims=True) + epsilon)
    return center * factor, factor


def norm_back(normed, factor, gain_vec, upstream):
    scaled = upstream * gain_vec
    return factor * (
        scaled
        - jnp.mean(scaled, axis=-1, keepdims=True)
        - normed * jnp.mean(scaled * normed, axis=-1, keepdims=True)
    )


def norm_vectors(weights_ref):
    rows = weights_ref[:, QKV + D :].astype(full).T
    return [rows[EXPERTS + i : EXPERTS + i + 1] for i in range(4)]


def halves(pair):
    first = lanes_of(pair.shape) < HEAD
    zero = jnp.zeros_like(pair)
    return jnp.where(first, pair, zero), jnp.where(first, zero, pair)


def head_probs(query, key_pair):
    scores = dot_rt(query, key_pair) * (HEAD**-0.5)
    scores = jnp.where(lanes_of(scores.shape) < SEQ, scores, -1e30)
    grown = jnp.exp(scores - jnp.max(scores, axis=-1, keepdims=True))
    return grown / jnp.sum(grown, axis=-1, keepdims=True)


def attend_kernel(x_ref, w_ref, order_ref, qkv_ref, ctx_ref, r_ref, sent_ref, probs_ref):
    gain_one, bias_one, gain_two, bias_two = norm_vectors(w_ref)
    x = x_ref[0].astype(full)
    normed, _ = normed_rows(x)
    attn_in = (normed * gain_one + bias_one).astype(low)
    qkv_ref[0] = dot(attn_in, w_ref[:, :QKV]).astype(low)
    for pair in range(HEADS // 2):
        at = pair * LANES
        query = halves(qkv_ref[0, :, at : at + LANES])
        key = qkv_ref[0, :, D + at : D + at + LANES]
        value = halves(qkv_ref[0, :, 2 * D + at : 2 * D + at + LANES])
        total = None
        for i in range(2):
            part = dot(head_probs(query[i], key).astype(low), value[i])
            total = part if total is None else total + part
        ctx_ref[0, :, at : at + LANES] = total.astype(low)
    r = x + dot(ctx_ref[0], w_ref[:, QKV : QKV + D])
    r_ref[0] = r
    normed, _ = normed_rows(r)
    h = (normed * gain_two + bias_two).astype(low)
    sent_ref[0, :, :D] = h
    logits = dot(h, dot(w_ref[:, QKV + D :], order_ref[...]).astype(low))
    logits = jnp.where(lanes_of(logits.shape) < EXPERTS, logits, -1e30)
    grown = jnp.exp(logits - jnp.max(logits, axis=-1, keepdims=True))
    probs = grown / jnp.sum(grown, axis=-1, keepdims=True)
    probs_ref[0] = probs
    sent_ref[0, :, D:] = pltpu.roll(probs, LANES - EXPERTS // 2, 1).astype(low)


def image_spec(width):
    return pl.BlockSpec((1, ROWS, width), lambda i: (i, 0, 0))


def whole_spec(shape):
    return pl.BlockSpec(shape, lambda *_: (0,) * len(shape))


def params(n):
    return pltpu.CompilerParams(
        dimension_semantics=("arbitrary",) * n, vmem_limit_bytes=BIG
    )


def attend(x, weights, order):
    images = x.shape[0]
    shapes = ((QKV, low), (D, low), (D, full), (SENT, low), (LANES, full))
    return pl.pallas_call(
        attend_kernel,
        grid=(images,),
        in_specs=[image_spec(D), whole_spec(weights.shape), whole_spec(order.shape)],
        out_specs=[image_spec(width) for width, _ in shapes],
        out_shape=[jax.ShapeDtypeStruct((images, ROWS, w), t) for w, t in shapes],
        compiler_params=params(1),
        cost_estimate=pl.CostEstimate(
            flops=8 * 10**9, bytes_accessed=12 * 10**6, transcendentals=2 * 10**6
        ),
        name="attend",
    )(x, weights, order)


def attend_back_kernel(
    images, x_ref, w_ref, order_ref, qkv_ref, ctx_ref, r_ref, h_ref, probs_ref, dprobs_ref, dh_ref, dy_ref,
    dx_ref, grads_ref, dqkv_ref, qkv_acc, proj_acc, router_acc, norm_acc,
):
    step = pl.program_id(0)

    @pl.when(step == 0)
    def _():
        qkv_acc[...] = jnp.zeros_like(qkv_acc)
        proj_acc[...] = jnp.zeros_like(proj_acc)
        router_acc[...] = jnp.zeros_like(router_acc)
        norm_acc[...] = jnp.zeros_like(norm_acc)

    gain_one, bias_one, gain_two, _ = norm_vectors(w_ref)
    probs, dprobs = probs_ref[0], dprobs_ref[0]
    dlogits = (probs * (dprobs - jnp.sum(probs * dprobs, axis=-1, keepdims=True))).astype(low)
    router_acc[...] += dot_lt(h_ref[0], dlogits)
    router = dot(w_ref[:, QKV + D :], order_ref[...]).astype(low)
    dh = dh_ref[0] + dot_rt(dlogits, router)
    normed, factor = normed_rows(r_ref[0])
    norm_acc[2:3] += jnp.sum(dh * normed, axis=0, keepdims=True)
    norm_acc[3:4] += jnp.sum(dh, axis=0, keepdims=True)
    dr = dy_ref[0].astype(full) + norm_back(normed, factor, gain_two, dh)
    dattended = dr.astype(low)
    proj_acc[...] += dot_lt(ctx_ref[0], dattended)
    dctx = dot_rt(dattended, w_ref[:, QKV : QKV + D]).astype(low)
    for pair in range(HEADS // 2):
        at = pair * LANES
        query = halves(qkv_ref[0, :, at : at + LANES])
        key = qkv_ref[0, :, D + at : D + at + LANES]
        keys = halves(key)
        value = qkv_ref[0, :, 2 * D + at : 2 * D + at + LANES]
        dhead = halves(dctx[:, at : at + LANES])
        dq = dk = dv = None
        for i in range(2):
            p = head_probs(query[i], key)
            dp = dot_rt(dhead[i], value)
            ds = (p * (dp - jnp.sum(p * dp, axis=-1, keepdims=True))).astype(low)
            parts = dot(ds, keys[i]), dot_lt(ds, query[i]), dot_lt(p.astype(low), dhead[i])
            dq, dk, dv = parts if dq is None else (dq + parts[0], dk + parts[1], dv + parts[2])
        dqkv_ref[:, at : at + LANES] = (dq * HEAD**-0.5).astype(low)
        dqkv_ref[:, D + at : D + at + LANES] = (dk * HEAD**-0.5).astype(low)
        dqkv_ref[:, 2 * D + at : 2 * D + at + LANES] = dv.astype(low)
    normed, factor = normed_rows(x_ref[0].astype(full))
    attn_in = (normed * gain_one + bias_one).astype(low)
    qkv_acc[...] += dot_lt(attn_in, dqkv_ref[...])
    da = dot_rt(dqkv_ref[...], w_ref[:, :QKV])
    norm_acc[0:1] += jnp.sum(da * normed, axis=0, keepdims=True)
    norm_acc[1:2] += jnp.sum(da, axis=0, keepdims=True)
    dx_ref[0] = dr + norm_back(normed, factor, gain_one, da)

    @pl.when(step == images - 1)
    def _():
        grads_ref[:, :QKV] = qkv_acc[...].astype(low)
        grads_ref[:, QKV : QKV + D] = proj_acc[...].astype(low)
        columns = norm_acc[...].T
        moved = pltpu.roll(columns, EXPERTS, 1)
        lane = lanes_of(moved.shape)
        tile = jnp.where(lane < EXPERTS, router_acc[...], moved)
        grads_ref[:, QKV + D :] = dot_rt(tile.astype(low), order_ref[...]).astype(low)


def attend_back(x, weights, order, qkv, ctx, r, h, probs, dprobs, dh, dy):
    images = x.shape[0]
    widths = (D, None, None, QKV, D, D, D, LANES, LANES, D, D)
    arrays = (x, weights, order, qkv, ctx, r, h, probs, dprobs, dh, dy)
    return pl.pallas_call(
        partial(attend_back_kernel, images),
        grid=(images,),
        in_specs=[
            whole_spec(a.shape) if w is None else image_spec(w) for a, w in zip(arrays, widths)
        ],
        out_specs=[image_spec(D), whole_spec((D, PACKED))],
        out_shape=[
            jax.ShapeDtypeStruct((images, ROWS, D), full),
            jax.ShapeDtypeStruct((D, PACKED), low),
        ],
        scratch_shapes=[
            pltpu.VMEM((ROWS, QKV), low),
            pltpu.VMEM((D, QKV), full),
            pltpu.VMEM((D, D), full),
            pltpu.VMEM((D, LANES), full),
            pltpu.VMEM((LANES, D), full),
        ],
        compiler_params=params(1),
        cost_estimate=pl.CostEstimate(
            flops=20 * 10**9, bytes_accessed=16 * 10**6, transcendentals=2 * 10**6
        ),
        name="attend_back",
    )(*arrays)


def device(offset):
    names = ("replica", "part", "expert")
    return tuple(lax.axis_index(name) ^ o for name, o in zip(names, offset))


def near(groups, j):
    return (0, j // groups, j % groups)


def greet(offsets):
    barrier = pltpu.get_barrier_semaphore()
    for offset in offsets:
        pl.semaphore_signal(barrier, inc=1, device_id=device(offset), device_id_type=MESH)
    pl.semaphore_wait(barrier, len(offsets))


def remote(source, target, send, receive, offset):
    return pltpu.make_async_remote_copy(
        src_ref=source,
        dst_ref=target,
        send_sem=send,
        recv_sem=receive,
        device_id=device(offset),
        device_id_type=MESH,
    )


def owners_like(replicas, parts):
    return [(r, p, 0) for r in range(replicas) for p in range(0, parts, 2) if (r, p) != (0, 0)]


def owner(parts, offset=(0, 0, 0)):
    return (lax.axis_index("replica") ^ offset[0]) * parts + (lax.axis_index("part") ^ offset[1])


CORE = (0, 1, 0)


def dispatch_kernel(sizes, keys_ref, rows_ref, *refs):
    replicas, parts, groups = sizes
    opening = replicas > 0
    if opening:
        shard_ref, out_ref, weights_ref, *refs = refs
    else:
        out_ref, other_ref, *refs = refs
    blocks, other, hop, sends, receives, local, *refs = refs
    _, count, own, tokens = keys_ref.shape
    mirror = (0, parts // 2, 0)
    owners = owners_like(replicas, parts)
    greet(sorted({near(groups, j) for j in range(1, count)} | {mirror, *owners}))
    slots = lax.broadcasted_iota(jnp.int32, (CAP, tokens), 0).astype(full)
    copies = [remote(rows_ref, other, hop.at[0], hop.at[1], mirror)]
    copies[0].start()
    if opening:
        early, late, here = refs
        mine = owner(parts)
        gathers = [
            remote(shard_ref, weights_ref.at[mine], early.at[0, i], early.at[1, i], o)
            for i, o in enumerate(owners)
        ]
        passes = [remote(shard_ref, weights_ref.at[mine], late.at[0, 0], late.at[1, 0], CORE)]
        for i, o in enumerate(owners):
            slot = weights_ref.at[owner(parts, o)]
            passes.append(remote(slot, slot, late.at[0, i + 1], late.at[1, i + 1], CORE))
        for copy in gathers:
            copy.start()
        passes[0].start()
        kept = pltpu.make_async_copy(shard_ref, weights_ref.at[mine], here)
        kept.start()

    def build(s, source_ref):
        for j in [*range(1, count), 0]:
            picks = [(keys_ref[s, j, i : i + 1] == slots).astype(low) for i in range(own)]
            picks = jnp.concatenate(picks, axis=0) if own > 1 else picks[0]
            rows = dot(picks, source_ref[:, :D]).astype(low)
            blocks[j, s] = rows.reshape(own, CAP, D)
            if j:
                copy = remote(
                    blocks.at[j, s], out_ref.at[j, s], sends.at[j, s], receives.at[j, s],
                    near(groups, j),
                )
            else:
                copy = pltpu.make_async_copy(blocks.at[0, s], out_ref.at[0, s], local.at[s])
            copy.start()
            copies.append(copy)

    build(0, rows_ref)
    if opening:
        for i, copy in enumerate(gathers):
            copy.wait_recv()
            passes[i + 1].start()
    copies[0].wait_recv()
    build(1, other)
    if not opening:
        keep = pltpu.make_async_copy(other, other_ref, local.at[2])
        keep.start()
        keep.wait()
    copies[0].wait_send()
    for copy in copies[1:]:
        copy.wait()
    if opening:
        for copy in gathers:
            copy.wait_send()
        for copy in passes:
            copy.wait()
        kept.wait()


def dispatch(keys, rows, sizes, number, shard=None):
    replicas, parts, groups = sizes
    _, count, own, tokens = keys.shape
    shape = (count, 2, own, CAP, D)
    owners = replicas * parts
    opening = shard is not None
    second = (owners, *shard.shape) if opening else rows.shape
    semaphores = [(2,), (count, 2), (count, 2), (3,)]
    if opening:
        semaphores += [(2, owners // 2 - 1), (2, owners // 2), ()]
    inner = pl.BlockSpec(memory_space=pltpu.VMEM)
    outer = pl.BlockSpec(memory_space=pl.ANY)
    return pl.pallas_call(
        partial(dispatch_kernel, sizes if opening else (0, parts, groups)),
        in_specs=[inner, inner] + [inner] * opening,
        out_specs=[outer, outer],
        out_shape=[jax.ShapeDtypeStruct(shape, low), jax.ShapeDtypeStruct(second, low)],
        scratch_shapes=[pltpu.VMEM(shape, low), pltpu.VMEM(rows.shape, low)]
        + [pltpu.SemaphoreType.DMA(n) for n in semaphores],
        compiler_params=pltpu.CompilerParams(
            vmem_limit_bytes=BIG, collective_id=number, has_side_effects=True
        ),
        cost_estimate=pl.CostEstimate(
            flops=60 * 10**9, bytes_accessed=5 * 10**6, transcendentals=0
        ),
        name=f"dispatch_{number}",
    )(keys, rows, *([shard] if opening else []))


def chooser(own, j):
    shape = (LANES, own * CAP)
    expert = lax.broadcasted_iota(jnp.int32, shape, 0)
    slot = lax.broadcasted_iota(jnp.int32, shape, 1)
    return (expert == j * own + slot // CAP).astype(low)


def gather_kernel(sizes, keys_ref, back_ref, dh_ref, dprobs_ref, sent, got, sends, receives):
    _, parts, groups = sizes
    count, _, own, _, _ = back_ref.shape
    tokens = dh_ref.shape[0]
    width = own * CAP
    half = count * own
    mirror = (0, parts // 2, 0)
    greet([mirror])

    def rows_of(i):
        return pl.ds(pl.multiple_of(i * ROWS, ROWS), ROWS)

    def hop(i):
        rows = rows_of(i)
        return remote(sent.at[rows], got.at[rows], sends.at[i], receives.at[i], mirror)

    def summed(s, rows):
        slot = (lanes_of((ROWS, width)) % CAP).astype(full)
        lane = lanes_of((ROWS, LANES))
        keys = keys_ref[s, rows]
        total = jnp.zeros((ROWS, D), full)
        dprobs = jnp.zeros((ROWS, LANES), full)
        for j in range(count):
            here = dot(keys, chooser(own, j)) == slot
            total = total + dot(here.astype(low), back_ref[j, s, :, :CAP].reshape(width, D))
            dgate = back_ref[j, s, :, CAP : CAP + 1].astype(full)
            dgate = dgate[:, :, :CAP] + dgate[:, :, CAP : 2 * CAP]
            for e in range(own):
                agreed = jnp.where(here[:, e * CAP : (e + 1) * CAP], dgate[e], 0.0)
                column = jnp.sum(agreed, axis=-1, keepdims=True)
                dprobs = jnp.where(lane == j * own + e, column, dprobs)
        return total, dprobs

    @pl.loop(0, tokens // ROWS)
    def _(i):
        rows = rows_of(i)
        total, dprobs = summed(1, rows)
        sent[rows, :D] = total.astype(low)
        high = dprobs.astype(low)
        rest = pltpu.roll(dprobs - high.astype(full), half, 1)
        sent[rows, D:] = (high.astype(full) + rest).astype(low)
        hop(i).start()

    @pl.loop(0, tokens // ROWS)
    def _(i):
        rows = rows_of(i)
        dh_ref[rows], dprobs_ref[rows] = summed(0, rows)

    @pl.loop(0, tokens // ROWS)
    def _(i):
        rows = rows_of(i)
        hop(i).wait()
        dh_ref[rows] += got[rows, :D].astype(full)
        pair = got[rows, D:].astype(full)
        lane = lanes_of(pair.shape)
        theirs = pair + pltpu.roll(pair, half, 1)
        mine = (lane >= half) & (lane < 2 * half)
        dprobs_ref[rows] += jnp.where(mine, theirs, 0.0)


def gather(keys, back, sizes, number):
    tokens = keys.shape[1]
    steps = tokens // ROWS
    inner = pl.BlockSpec(memory_space=pltpu.VMEM)
    return pl.pallas_call(
        partial(gather_kernel, sizes),
        in_specs=[inner, inner],
        out_specs=[inner, inner],
        out_shape=[
            jax.ShapeDtypeStruct((tokens, D), full),
            jax.ShapeDtypeStruct((tokens, LANES), full),
        ],
        scratch_shapes=[
            pltpu.VMEM((tokens, SENT), low),
            pltpu.VMEM((tokens, SENT), low),
            pltpu.SemaphoreType.DMA((steps,)),
            pltpu.SemaphoreType.DMA((steps,)),
        ],
        compiler_params=pltpu.CompilerParams(
            vmem_limit_bytes=BIG, collective_id=number, has_side_effects=True
        ),
        cost_estimate=pl.CostEstimate(
            flops=30 * 10**9, bytes_accessed=7 * 10**6, transcendentals=0
        ),
        name="gather",
    )(keys, back)


def close_kernel(
    sizes, keys_ref, probs_ref, r_ref, theirs_ref, y_ref, grads_ref, out_ref, total_ref,
    ys, acc, sent, got, kept, first, second, third,
    y_sends, y_receives, y_local, hops, core_sems, kept_sems, owner_sems, expert_sems,
):
    replicas, parts, groups = sizes
    count, _, own, _, _ = y_ref.shape
    tokens = r_ref.shape[0]
    width = own * CAP
    mirror = (0, parts // 2, 0)
    owners = owners_like(replicas, parts)
    across = [(0, 0, g) for g in range(1, groups)]
    greet(sorted({near(groups, j) for j in range(1, count)} | {mirror, CORE, *owners, *across}))
    core = lax.axis_index("part") % 2
    pairs = replicas * parts // 2

    def swap(j, s):
        if j == 0:
            return pltpu.make_async_copy(y_ref.at[0, s], ys.at[0, s], y_local.at[s])
        return remote(
            y_ref.at[j, s], ys.at[j, s], y_sends.at[j, s], y_receives.at[j, s], near(groups, j)
        )

    swaps = [[swap(j, s) for j in range(count)] for s in range(2)]
    to_core = [
        remote(grads_ref.at[2 * i + 1 - core], first.at[i], core_sems.at[0, i], core_sems.at[1, i], CORE)
        for i in range(pairs)
    ]
    own_rows = [
        pltpu.make_async_copy(grads_ref.at[2 * i + core], kept.at[i], kept_sems.at[i])
        for i in range(pairs)
    ]
    for copy in to_core + own_rows + swaps[1] + swaps[0]:
        copy.start()
    for i in range(pairs):
        own_rows[i].wait()
        to_core[i].wait()
        kept[i] = (kept[i].astype(full) + first[i].astype(full)).astype(low)
    to_owner = [
        remote(kept.at[owner(parts, o) // 2], second.at[i], owner_sems.at[0, i], owner_sems.at[1, i], o)
        for i, o in enumerate(owners)
    ]
    for copy in to_owner:
        copy.start()

    def rows_of(i):
        return pl.ds(pl.multiple_of(i * ROWS, ROWS), ROWS)

    def weighted(s, rows, probs):
        slot = (lanes_of((ROWS, width)) % CAP).astype(full)
        keys = keys_ref[s, rows]
        total = jnp.zeros((ROWS, D), full)
        for j in range(count):
            spread = chooser(own, j)
            gate = jnp.where(dot(keys, spread) == slot, dot(probs, spread), 0.0)
            total = total + dot(gate.astype(low), ys[j, s].reshape(width, D))
        return total

    def hop(i):
        rows = rows_of(i)
        return remote(sent.at[rows], got.at[rows], hops.at[0, i], hops.at[1, i], mirror)

    for copy in swaps[1]:
        copy.wait()

    @pl.loop(0, tokens // ROWS)
    def _(i):
        rows = rows_of(i)
        sent[rows] = weighted(1, rows, theirs_ref[rows, D:]).astype(low)
        hop(i).start()

    total = kept[owner(parts) // 2].astype(full)
    for i, copy in enumerate(to_owner):
        copy.wait()
        total = total + second[i].astype(full)
    me = lax.axis_index("expert")
    third[me] = total.astype(low)
    to_others = [
        remote(third.at[me], third.at[me], expert_sems.at[0, i], expert_sems.at[1, i], o)
        for i, o in enumerate(across)
    ]
    for copy in to_others:
        copy.start()
    for copy in swaps[0]:
        copy.wait()

    @pl.loop(0, tokens // ROWS)
    def _(i):
        rows = rows_of(i)
        acc[rows] = r_ref[rows] + weighted(0, rows, probs_ref[rows].astype(low))

    for copy in to_others:
        copy.wait()
    total = third[0].astype(full)
    for g in range(1, groups):
        total = total + third[g].astype(full)
    total_ref[...] = total

    @pl.loop(0, tokens // ROWS)
    def _(i):
        rows = rows_of(i)
        hop(i).wait()
        out_ref[rows] = (acc[rows] + got[rows].astype(full)).astype(low)


def close(keys, probs, r, theirs, y, grads, sizes, number):
    replicas, parts, groups = sizes
    tokens = r.shape[0]
    steps = tokens // ROWS
    count = y.shape[0]
    pairs = replicas * parts // 2
    shard = grads.shape[1:]
    inner = pl.BlockSpec(memory_space=pltpu.VMEM)
    outer = pl.BlockSpec(memory_space=pl.ANY)
    semaphores = [
        (count, 2), (count, 2), (2,), (2, steps), (2, pairs), (pairs,), (2, pairs - 1), (2, groups - 1),
    ]
    return pl.pallas_call(
        partial(close_kernel, sizes),
        in_specs=[inner] * 4 + [outer] * 2,
        out_specs=[inner, inner],
        out_shape=[jax.ShapeDtypeStruct((tokens, D), low), jax.ShapeDtypeStruct(shard, full)],
        scratch_shapes=[
            pltpu.VMEM(y.shape, low),
            pltpu.VMEM((tokens, D), full),
            pltpu.VMEM((tokens, D), low),
            pltpu.VMEM((tokens, D), low),
            pltpu.VMEM((pairs, *shard), low),
            pltpu.VMEM((pairs, *shard), low),
            pltpu.VMEM((pairs - 1, *shard), low),
            pltpu.VMEM((groups, *shard), low),
        ]
        + [pltpu.SemaphoreType.DMA(n) for n in semaphores],
        compiler_params=pltpu.CompilerParams(
            vmem_limit_bytes=BIG, collective_id=number, has_side_effects=True
        ),
        cost_estimate=pl.CostEstimate(
            flops=60 * 10**9, bytes_accessed=10 * 10**6, transcendentals=0
        ),
        name="close",
    )(keys, probs, r, theirs, y, grads)


GELU = 0.7978845608028654
CUBE = 0.044715


def gelu_pair(u):
    square = u * u
    bent = jnp.tanh(u * (GELU * CUBE * square + GELU))
    half = 0.5 * bent + 0.5
    value = u * half
    return value, half + value * (1.0 - bent) * (3.0 * GELU * CUBE * square + GELU)


def first_kernel(h_ref, dy_ref, w_ref, wr_ref, sel_ref, g_ref, slope_ref, dw_ref, gates, dye_t):
    sources = h_ref.shape[0]
    tile = w_ref.shape[3]

    @pl.when(pl.program_id(1) == 0)
    def _():
        for k in range(sources):
            rows = slice(k * CAP, (k + 1) * CAP)
            logits = dot(h_ref[k, 0], wr_ref[...])
            logits = jnp.where(lanes_of(logits.shape) < EXPERTS, logits, -1e30)
            grown = jnp.exp(logits - jnp.max(logits, axis=-1, keepdims=True))
            mine = jnp.sum(grown * sel_ref[0], axis=-1, keepdims=True)
            gate = mine / jnp.sum(grown, axis=-1, keepdims=True)
            gates[rows] = jnp.broadcast_to(gate, (CAP, LANES))
            dye_t[:, rows] = (dy_ref[k, 0].astype(full) * gate).T.astype(low)

    w = w_ref[:, 0].reshape(D, tile)
    for k in range(0, sources, 2):
        rows = slice(k * CAP, (k + 2) * CAP)
        value, slope = gelu_pair(dot(h_ref[k : k + 2, 0].reshape(2 * CAP, D), w))
        g_ref[0, rows] = value.astype(low)
        slope_ref[0, rows] = (slope * gates[rows, :1]).astype(low)
    grad = dot(dye_t[...], g_ref[0]).T
    dw_ref[:, 0] = grad.astype(low).reshape(dw_ref.shape[0], dw_ref.shape[2], D)


def slot_spec(sources):
    return pl.BlockSpec((sources, 1, CAP, D), lambda e, f: (0, e, 0, 0))


def expert_first(h, dy, w_in, w_router, select, tile):
    sources = h.shape[0]
    owners, own, depth, hidden = w_in.shape
    rows = sources * CAP
    per = hidden // owners
    hidden_spec = pl.BlockSpec((1, rows, tile), lambda e, f: (e, 0, f))
    return pl.pallas_call(
        first_kernel,
        grid=(own, hidden // tile),
        in_specs=[
            slot_spec(sources),
            slot_spec(sources),
            pl.BlockSpec((owners, 1, depth, tile), lambda e, f: (0, e, 0, f)),
            whole_spec(w_router.shape),
            pl.BlockSpec((1, 1, LANES), lambda e, f: (e, 0, 0)),
        ],
        out_specs=[
            hidden_spec,
            hidden_spec,
            pl.BlockSpec((tile // per, 1, per, D), lambda e, f: (f, e, 0, 0)),
        ],
        out_shape=[
            jax.ShapeDtypeStruct((own, rows, hidden), low),
            jax.ShapeDtypeStruct((own, rows, hidden), low),
            jax.ShapeDtypeStruct((owners, own, per, D), low),
        ],
        scratch_shapes=[pltpu.VMEM((rows, LANES), full), pltpu.VMEM((D, rows), low)],
        compiler_params=params(2),
        cost_estimate=pl.CostEstimate(
            flops=4 * own * rows * D * hidden,
            bytes_accessed=50 * 10**6,
            transcendentals=own * rows * hidden,
        ),
        name="expert_first",
    )(h, dy, w_in, w_router, select)


def rest_kernel(
    groups, own, steps, dy_ref, h_ref, g_ref, slope_ref, w_in_ref, w_out_ref,
    back_ref, dw_ref, y_ref, du, acc, dgates, dgate_rows, h_t, staged, sends, receives, local,
):
    sources = dy_ref.shape[0]
    tile = slope_ref.shape[2]
    at = pl.program_id(0)
    phase, expert, step = at // (own * steps), at // steps % own, at % steps
    w_in = w_in_ref[:, 0].reshape(D, tile)
    w_out = w_out_ref[:, 0].reshape(tile, D)
    chunk = 2 * CAP

    def copy(k, e):
        return pltpu.make_async_remote_copy(
            src_ref=staged.at[k, e],
            dst_ref=back_ref.at[k, e],
            send_sem=sends.at[k, e],
            recv_sem=receives.at[k, e],
            device_id=device(near(groups, k // 2)),
            device_id_type=MESH,
        )

    def mine(k, e):
        return pltpu.make_async_copy(staged.at[k, e], back_ref.at[k, e], local.at[k, e])

    @pl.when(at == 0)
    def _():
        greet([near(groups, j) for j in range(1, sources // 2)])

    @pl.when((phase != 1) & (step == 0))
    def _():
        acc[...] = jnp.zeros_like(acc)

    @pl.when(phase == 0)
    def _():
        @pl.when(step == 0)
        def _():
            dgates[...] = jnp.zeros_like(dgates)

        for k in range(0, sources, 2):
            rows = slice(k * CAP, (k + 2) * CAP)
            dg = dot_rt(dy_ref[k : k + 2, 0].reshape(chunk, D), w_out)
            change = (dg * slope_ref[0, rows].astype(full)).astype(low)
            du[expert * steps + step, rows] = change
            acc[rows] += dot_rt(change, w_in)
            agreed = dg * g_ref[0, rows].astype(full)
            dgates[rows] += sum(agreed[:, i : i + LANES] for i in range(0, tile, LANES))

        @pl.when(step == steps - 1)
        def _():
            sums = dgates[...]
            high = sums.astype(low)
            rest = (sums - high.astype(full)).astype(low)
            ones = jnp.ones((16, LANES), low)
            dgate_rows[...] = dot_rt(ones, high) + dot_rt(ones, rest)
            for k in range(sources):
                rows = slice(k * CAP, (k + 1) * CAP)
                staged[k, expert, :CAP] = acc[rows].astype(low)
                row = dgate_rows[:, rows]
                high = row.astype(low)
                staged[k, expert, CAP:, :CAP] = high
                staged[k, expert, CAP:, CAP : 2 * CAP] = (row - high.astype(full)).astype(low)
                staged[k, expert, CAP:, 2 * CAP :] = jnp.zeros((16, D - 2 * CAP), low)

        for e in range(own):
            @pl.when((step == steps - 1) & (expert == e))
            def _():
                for k in range(2, sources):
                    copy(k, e).start()
                mine(0, e).start()
                mine(1, e).start()

    @pl.when(phase == 1)
    def _():
        @pl.when(step == 0)
        def _():
            for k in range(sources):
                h_t[:, k * CAP : (k + 1) * CAP] = h_ref[k, 0].T

        grad = dot(h_t[...], du[expert * steps + step]).astype(low)
        dw_ref[:, 0] = grad.reshape(dw_ref.shape[0], dw_ref.shape[2], tile)

    @pl.when(phase == 2)
    def _():
        for k in range(0, sources, 2):
            rows = slice(k * CAP, (k + 2) * CAP)
            acc[rows] += dot(g_ref[0, rows], w_out)

        @pl.when(step == steps - 1)
        def _():
            y_ref[:, 0] = acc[...].astype(low).reshape(sources, CAP, D)

    @pl.when(at == 3 * own * steps - 1)
    def _():
        for e in range(own):
            for k in range(2, sources):
                copy(k, e).wait()
            mine(0, e).wait()
            mine(1, e).wait()


def expert_rest(dy, h, g, slope, w_in, w_out, tile, groups, number):
    sources, own, _, _ = dy.shape
    owners, _, depth, hidden = w_in.shape
    rows = sources * CAP
    per = hidden // owners
    steps = hidden // tile
    last = own * steps - 1

    def during(phases):
        def find(at):
            if 0 in phases and 2 in phases:
                inside = jnp.where(at // (last + 1) == 1, last, at % (last + 1))
            else:
                inside = jnp.clip(at - phases[0] * (last + 1), 0, last)
            return inside // steps, inside % steps

        return find

    def spec(shape, phases, index, buffers=2):
        return pl.BlockSpec(
            shape, lambda at: index(*during(phases)(at)), pipeline_mode=pl.Buffered(buffers)
        )

    token, hidden_at = (sources, 1, CAP, D), (1, rows, tile)
    whole_expert = lambda e, f: (0, e, 0, 0)
    in_tile = lambda e, f: (0, e, 0, f)
    return pl.pallas_call(
        partial(rest_kernel, groups, own, steps),
        grid=(3 * own * steps,),
        in_specs=[
            spec(token, (0,), whole_expert, 1),
            spec(token, (1,), whole_expert, 1),
            spec(hidden_at, (0, 2), lambda e, f: (e, 0, f)),
            spec(hidden_at, (0,), lambda e, f: (e, 0, f)),
            spec((owners, 1, depth, tile), (0,), in_tile),
            spec((tile // per, 1, per, D), (0, 2), lambda e, f: (f, e, 0, 0)),
        ],
        out_specs=[
            pl.BlockSpec(memory_space=pl.ANY),
            spec((owners, 1, depth, tile), (1,), in_tile),
            spec(token, (2,), whole_expert),
        ],
        out_shape=[
            jax.ShapeDtypeStruct((sources, own, CAP + 16, D), low),
            jax.ShapeDtypeStruct(w_in.shape, low),
            jax.ShapeDtypeStruct(dy.shape, low),
        ],
        scratch_shapes=[
            pltpu.VMEM((own * steps, rows, tile), low),
            pltpu.VMEM((rows, D), full),
            pltpu.VMEM((rows, LANES), full),
            pltpu.VMEM((16, rows), full),
            pltpu.VMEM((D, rows), low),
            pltpu.VMEM((sources, own, CAP + 16, D), low),
            pltpu.SemaphoreType.DMA((sources, own)),
            pltpu.SemaphoreType.DMA((sources, own)),
            pltpu.SemaphoreType.DMA((2, own)),
        ],
        compiler_params=pltpu.CompilerParams(
            dimension_semantics=("arbitrary",),
            vmem_limit_bytes=BIG,
            collective_id=number,
            has_side_effects=True,
        ),
        cost_estimate=pl.CostEstimate(
            flops=8 * own * rows * D * hidden, bytes_accessed=60 * 10**6, transcendentals=0
        ),
        name="expert_rest",
    )(dy, h, g, slope, w_in, w_out)


ALL = ("replica", "part")


def body(
    tokens,
    choices,
    ln1_gain,
    ln1_bias,
    w_qkv,
    w_proj,
    ln2_gain,
    ln2_bias,
    w_router,
    w_expert_in,
    w_expert_out,
    cotangent,
):
    replicas, parts, groups = (lax.axis_size(name) for name in ("replica", "part", "expert"))
    owners = replicas * parts
    peers = parts * groups
    own = EXPERTS // peers
    images = tokens.shape[0] // SEQ
    count = images * ROWS
    tile = 512 * 16 // peers

    small_rows = w_router.shape[0]
    placed_router = (
        w_router.reshape(small_rows, groups, parts, own).transpose(0, 2, 1, 3).reshape(small_rows, EXPERTS)
    )
    vectors = jnp.stack([ln1_gain, ln1_bias, ln2_gain, ln2_bias], axis=1)
    packed = jnp.concatenate(
        [w_qkv, w_proj, placed_router, vectors, jnp.zeros((small_rows, LANES - EXPERTS - 4), full)],
        axis=1,
    ).astype(low)
    def spread(master):
        pieces = master.astype(low).reshape(parts, own, *master.shape[1:])
        pieces = jnp.concatenate([pieces] * replicas, axis=0)
        return lax.all_to_all(pieces, ALL, split_axis=0, concat_axis=0, tiled=True)

    def collect(grad):
        pieces = lax.all_to_all(grad, ALL, split_axis=0, concat_axis=0, tiled=True)
        pieces = pieces.reshape(replicas, parts * own, *grad.shape[2:])
        return jnp.sum(pieces.astype(full), axis=0)

    me = lax.axis_index("part") * groups + lax.axis_index("expert")
    sizes = (replicas, parts, groups)

    def padded(rows, fill=0):
        rows = rows.reshape(images, SEQ, rows.shape[1])
        return jnp.pad(rows, ((0, 0), (0, ROWS - SEQ), (0, 0)), constant_values=fill)

    x = padded(tokens)
    dy = padded(cotangent)
    half = parts // 2
    flips = [(i, i ^ half) for i in range(parts)]
    picks = jnp.stack([choices, lax.ppermute(choices, "part", flips)]).reshape(2 * images, SEQ, 2)
    picks = jnp.pad(picks, ((0, 0), (0, ROWS - SEQ), (0, 0)), constant_values=-1)
    picks = picks.reshape(2, count, 2)
    column = jnp.arange(EXPERTS)
    place = (me ^ (column // own)) * own + column % own
    expert = (place // own % groups) * (parts * own) + place // (groups * own) * own + place % own
    lane = jnp.arange(LANES)
    order = jnp.where(lane < EXPERTS, jnp.pad(place, (0, LANES - EXPERTS)), lane)
    order = (lane[:, None] == order[None, :]).astype(low)
    expert = expert[: EXPERTS // 2]
    named = (picks[:, :, :, None] == expert).any(axis=2)
    row = jnp.arange(count)
    earlier = (row[None, :] < row[:, None]).astype(low)
    slots = jnp.einsum("tu,sue->ste", earlier, named.astype(low), preferred_element_type=full)
    keys = jnp.where(named, slots, -1.0)
    key_rows = keys.transpose(0, 2, 1).reshape(2, peers // 2, own, count)
    key_columns = jnp.pad(
        keys, ((0, 0), (0, 0), (0, LANES - EXPERTS // 2)), constant_values=-1
    ).astype(low)

    first_weight = spread(w_expert_in)
    dy_slots, weights = dispatch(key_rows, dy.reshape(count, D), sizes, 0, packed)
    weights = weights.reshape(D, PACKED)
    qkv, ctx, r, sent, probs = attend(x, weights, order)
    w_expert_out, sent = lax.optimization_barrier((w_expert_out, sent))
    second_weight = spread(w_expert_out)
    h_slots, theirs = dispatch(key_rows, sent.reshape(count, SENT), sizes, 1)
    dy_slots = dy_slots.reshape(peers, own, CAP, D)
    h_slots = h_slots.reshape(peers, own, CAP, D)
    select = ((me * own + jnp.arange(own))[:, None, None] == lane[None, None, :]).astype(full)
    g, slope, dw_second = expert_first(
        h_slots, dy_slots, first_weight, weights[:, QKV + D :], select, tile
    )
    back, dw_first, y = expert_rest(
        dy_slots, h_slots, g, slope, first_weight, second_weight, tile, groups, 2
    )
    back = back.reshape(peers // 2, 2, own, CAP + 16, D)
    y = y.reshape(peers // 2, 2, own, CAP, D)
    expert_out_grad = collect(dw_second)
    expert_in_grad = collect(dw_first)
    dh, dprobs = gather(key_columns, back, sizes, 3)
    dx, grads = attend_back(
        x, weights, order, qkv, ctx, r, sent, probs,
        dprobs.reshape(images, ROWS, LANES), dh.reshape(images, ROWS, D), dy,
    )
    output, grads = close(
        key_columns, probs.reshape(count, LANES), r.reshape(count, D), theirs, y,
        grads.reshape(owners, small_rows, PACKED), sizes, 4,
    )
    router_grad = (
        grads[:, QKV + D : QKV + D + EXPERTS]
        .reshape(small_rows, parts, groups, own)
        .transpose(0, 2, 1, 3)
        .reshape(small_rows, EXPERTS)
    )
    norms = [grads[:, QKV + D + EXPERTS + i] for i in range(4)]

    def unpadded(rows):
        return rows.reshape(images, ROWS, D)[:, :SEQ].reshape(images * SEQ, D)

    return (
        unpadded(output),
        unpadded(dx),
        norms[0],
        norms[1],
        grads[:, :QKV],
        grads[:, QKV : QKV + D],
        norms[2],
        norms[3],
        router_grad,
        expert_in_grad,
        expert_out_grad,
    )


def solution(mesh):
    dp, groups = mesh.shape["dp"], mesh.shape["expert"]
    parts = min(EXPERTS // groups, dp // 2)
    mesh = Mesh(mesh.devices.reshape(dp // parts, parts, groups), ("replica", "part", "expert"))
    rows = P(("replica", "part", "expert"), None)
    vector, matrix = P(ALL), P(ALL, None)
    experts = P("expert", ALL, None)
    return jax.shard_map(
        body,
        mesh=mesh,
        in_specs=(
            rows, rows, vector, vector, matrix, matrix, vector, vector, matrix, experts, experts, rows,
        ),
        out_specs=(
            rows, rows, vector, vector, matrix, matrix, vector, vector, matrix, experts, experts,
        ),
        check_vma=False,
    )
```

```python
from functools import partial

import jax
import jax.numpy as jnp
from jax import lax
from jax.experimental import pallas as pl
from jax.experimental.pallas import tpu as pltpu
from jax.sharding import Mesh
from jax.sharding import PartitionSpec as P

D = 512
HEADS = 8
EXPERTS = 32
SEQ = 197
CAP = 128
ROWS = 208
HEAD = D // HEADS
LANES = 128
QKV = 3 * D
SENT = D + LANES
PACKED = QKV + D + LANES
epsilon = 1e-06
low = jnp.bfloat16
full = jnp.float32
MESH = pl.DeviceIdType.MESH
BIG = 63 * 1024 * 1024


def dot(left, right):
    return jnp.dot(left, right, preferred_element_type=full)


def dot_rt(left, right):
    return lax.dot_general(left, right, (((1,), (1,)), ((), ())), preferred_element_type=full)


def dot_lt(left, right):
    return lax.dot_general(left, right, (((0,), (0,)), ((), ())), preferred_element_type=full)


def lanes_of(shape):
    return lax.broadcasted_iota(jnp.int32, shape, len(shape) - 1)


def normed_rows(values):
    center = values - jnp.mean(values, axis=-1, keepdims=True)
    factor = lax.rsqrt(jnp.mean(center * center, axis=-1, keepdims=True) + epsilon)
    return center * factor, factor


def norm_back(normed, factor, gain_vec, upstream):
    scaled = upstream * gain_vec
    return factor * (
        scaled
        - jnp.mean(scaled, axis=-1, keepdims=True)
        - normed * jnp.mean(scaled * normed, axis=-1, keepdims=True)
    )


def norm_vectors(weights_ref):
    rows = weights_ref[:, QKV + D :].astype(full).T
    return [rows[EXPERTS + i : EXPERTS + i + 1] for i in range(4)]


def halves(pair):
    first = lanes_of(pair.shape) < HEAD
    zero = jnp.zeros_like(pair)
    return jnp.where(first, pair, zero), jnp.where(first, zero, pair)


def head_probs(query, key_pair):
    scores = dot_rt(query, key_pair) * (HEAD**-0.5)
    scores = jnp.where(lanes_of(scores.shape) < SEQ, scores, -1e30)
    grown = jnp.exp(scores - jnp.max(scores, axis=-1, keepdims=True))
    return grown / jnp.sum(grown, axis=-1, keepdims=True)


def attend_kernel(
    sizes, x_ref, w_ref, order_ref, master_ref, _, qkv_ref, ctx_ref, r_ref, sent_ref, probs_ref, first_ref, flow
):
    def moved():
        return outward(sizes, wide_part, master_ref, first_ref, flow, GROUPS - 1, 0)

    @pl.when(pl.program_id(0) == 0)
    def _():
        greet(all_owners(*sizes[:2]))
        start(moved())

    gain_one, bias_one, gain_two, bias_two = norm_vectors(w_ref)
    x = x_ref[0].astype(full)
    normed, _ = normed_rows(x)
    attn_in = (normed * gain_one + bias_one).astype(low)
    qkv_ref[0] = dot(attn_in, w_ref[:, :QKV]).astype(low)
    for pair in range(HEADS // 2):
        at = pair * LANES
        query = halves(qkv_ref[0, :, at : at + LANES])
        key = qkv_ref[0, :, D + at : D + at + LANES]
        value = halves(qkv_ref[0, :, 2 * D + at : 2 * D + at + LANES])
        total = None
        for i in range(2):
            part = dot(head_probs(query[i], key).astype(low), value[i])
            total = part if total is None else total + part
        ctx_ref[0, :, at : at + LANES] = total.astype(low)
    r = x + dot(ctx_ref[0], w_ref[:, QKV : QKV + D])
    r_ref[0] = r
    normed, _ = normed_rows(r)
    h = (normed * gain_two + bias_two).astype(low)
    sent_ref[0, :, :D] = h
    logits = dot(h, dot(w_ref[:, QKV + D :], order_ref[...]).astype(low))
    logits = jnp.where(lanes_of(logits.shape) < EXPERTS, logits, -1e30)
    grown = jnp.exp(logits - jnp.max(logits, axis=-1, keepdims=True))
    probs = grown / jnp.sum(grown, axis=-1, keepdims=True)
    probs_ref[0] = probs
    sent_ref[0, :, D:] = pltpu.roll(probs, LANES - EXPERTS // 2, 1).astype(low)

    @pl.when(pl.program_id(0) == pl.num_programs(0) - 1)
    def _():
        wait(moved())


def image_spec(width):
    return pl.BlockSpec((1, ROWS, width), lambda i: (i, 0, 0))


def whole_spec(shape):
    return pl.BlockSpec(shape, lambda *_: (0,) * len(shape))


def params(n):
    return pltpu.CompilerParams(
        dimension_semantics=("arbitrary",) * n, vmem_limit_bytes=BIG
    )


def remote_params(n, number):
    return pltpu.CompilerParams(
        dimension_semantics=("arbitrary",) * n,
        vmem_limit_bytes=BIG,
        collective_id=number,
        has_side_effects=True,
    )


def attend(x, weights, order, master, first, sizes, number):
    images = x.shape[0]
    shapes = ((QKV, low), (D, low), (D, full), (SENT, low), (LANES, full))
    outer = pl.BlockSpec(memory_space=pl.ANY)
    return pl.pallas_call(
        partial(attend_kernel, sizes),
        grid=(images,),
        in_specs=[image_spec(D), whole_spec(weights.shape), whole_spec(order.shape), outer, outer],
        out_specs=[image_spec(width) for width, _ in shapes] + [outer],
        out_shape=[jax.ShapeDtypeStruct((images, ROWS, w), t) for w, t in shapes]
        + [jax.ShapeDtypeStruct(first.shape, low)],
        input_output_aliases={4: 5},
        scratch_shapes=[flow_semaphores(sizes, 1)],
        compiler_params=remote_params(1, number),
        cost_estimate=pl.CostEstimate(
            flops=8 * 10**9, bytes_accessed=12 * 10**6, transcendentals=2 * 10**6
        ),
        name="attend",
    )(x, weights, order, master, first)


def device(offset):
    names = ("replica", "part", "expert")
    return tuple(lax.axis_index(name) ^ o for name, o in zip(names, offset))


def near(groups, j):
    return (0, j // groups, j % groups)


def greet(offsets):
    barrier = pltpu.get_barrier_semaphore()
    for offset in offsets:
        pl.semaphore_signal(barrier, inc=1, device_id=device(offset), device_id_type=MESH)
    pl.semaphore_wait(barrier, len(offsets))


def remote(source, target, send, receive, offset):
    return pltpu.make_async_remote_copy(
        src_ref=source,
        dst_ref=target,
        send_sem=send,
        recv_sem=receive,
        device_id=device(offset),
        device_id_type=MESH,
    )


def owners_like(replicas, parts):
    return [(r, p, 0) for r in range(replicas) for p in range(0, parts, 2) if (r, p) != (0, 0)]


def owner(parts, offset=(0, 0, 0)):
    return (lax.axis_index("replica") ^ offset[0]) * parts + (lax.axis_index("part") ^ offset[1])


CORE = (0, 1, 0)
GROUPS = 4


def all_owners(replicas, parts):
    return [(r, p, 0) for r in range(replicas) for p in range(parts) if (r, p) != (0, 0)]


def wide_part(ref, at, g):
    width = ref.shape[-1] // GROUPS
    return ref.at[at, ..., pl.ds(g * width, width)]


def narrow_part(ref, at, g):
    width = ref.shape[-1] // (2 * GROUPS)
    return ref.at[at, ..., pl.ds(g * width, width)]


def tall_part(ref, at, g):
    depth = ref.shape[-2] // GROUPS
    return ref.at[at, ..., pl.ds(g * depth, depth), :]


def outward(sizes, part_of, source, target, semaphores, g, slot):
    _, parts, _ = sizes
    own = target.shape[1]
    here = owner(parts)

    def block(p):
        return part_of(source, pl.ds((lax.axis_index("part") ^ p) * own, own), g)

    copies = [
        remote(block(o[1]), part_of(target, here, g), semaphores.at[0, slot, i], semaphores.at[1, slot, i], o)
        for i, o in enumerate(all_owners(*sizes[:2]))
    ]
    last = semaphores.at[0, slot, len(copies)]
    return copies + [pltpu.make_async_copy(block(0), part_of(target, here, g), last)]


def across(sizes, part_of, source, target, semaphores, g, slot):
    replicas, parts, _ = sizes

    def rows(r):
        return pl.ds((lax.axis_index("replica") ^ r) * parts, parts)

    return [
        remote(
            part_of(source, rows(r), g), part_of(target, r - 1, g),
            semaphores.at[0, slot, r], semaphores.at[1, slot, r], (r, 0, 0),
        )
        for r in range(1, replicas)
    ]


def homeward(sizes, part_of, source, target, semaphores, g, slot):
    _, parts, _ = sizes
    here = lax.axis_index("part")
    copies = [
        remote(
            part_of(source, here ^ p, g), part_of(target, here, g),
            semaphores.at[0, slot, p], semaphores.at[1, slot, p], (0, p, 0),
        )
        for p in range(1, parts)
    ]
    last = semaphores.at[0, slot, 0]
    return copies + [pltpu.make_async_copy(part_of(source, here, g), part_of(target, here, g), last)]


def partners(sizes):
    replicas, parts, _ = sizes
    return {(0, p, 0) for p in range(1, parts)} | {(r, 0, 0) for r in range(1, replicas)}


def mine_of(sizes, dw_ref):
    return dw_ref.at[pl.ds(lax.axis_index("replica") * sizes[1], sizes[1])]


def pieces_of(sizes, dw):
    return jax.ShapeDtypeStruct((sizes[0] - 1, sizes[1], *dw.shape[1:]), low)


def start(copies):
    for copy in copies:
        copy.start()


def wait(copies):
    for copy in copies:
        copy.wait()


def flow_semaphores(sizes, slots):
    return pltpu.SemaphoreType.DMA((2, slots, sizes[0] * sizes[1]))


def swap_slots(groups, keys_ref, blocks, out_ref, sends, receives, local):
    _, count, own, tokens = keys_ref.shape
    slots = lax.broadcasted_iota(jnp.int32, (CAP, tokens), 0).astype(full)

    def build(s, source_ref):
        copies = []
        for j in [*range(1, count), 0]:
            picks = [(keys_ref[s, j, i : i + 1] == slots).astype(low) for i in range(own)]
            picks = jnp.concatenate(picks, axis=0) if own > 1 else picks[0]
            rows = dot(picks, source_ref[:, :D]).astype(low)
            blocks[j, s] = rows.reshape(own, CAP, D)
            if j:
                copy = remote(
                    blocks.at[j, s], out_ref.at[j, s], sends.at[j, s], receives.at[j, s],
                    near(groups, j),
                )
            else:
                copy = pltpu.make_async_copy(blocks.at[0, s], out_ref.at[0, s], local.at[s])
            copy.start()
            copies.append(copy)
        return copies

    return build


def open_kernel(
    sizes, keys_ref, rows_ref, shard_ref, master_ref, out_ref, weights_ref, first_ref,
    blocks, other, hop, sends, receives, local, flow, early, late, here,
):
    replicas, parts, groups = sizes
    count = keys_ref.shape[1]
    mirror = (0, parts // 2, 0)
    owners = owners_like(replicas, parts)
    greet(
        sorted({near(groups, j) for j in range(1, count)} | {mirror, *all_owners(replicas, parts)})
    )
    hops = remote(rows_ref, other, hop.at[0], hop.at[1], mirror)
    hops.start()
    mine = weights_ref.at[owner(parts)]
    gathers = [
        remote(shard_ref, mine, early.at[0, i], early.at[1, i], o) for i, o in enumerate(owners)
    ]
    passes = [remote(shard_ref, mine, late.at[0, 0], late.at[1, 0], CORE)]
    for i, o in enumerate(owners):
        slot = weights_ref.at[owner(parts, o)]
        passes.append(remote(slot, slot, late.at[0, i + 1], late.at[1, i + 1], CORE))
    start(gathers)
    passes[0].start()
    kept = pltpu.make_async_copy(shard_ref, mine, here)
    kept.start()
    parts_of = [
        outward(sizes, wide_part, master_ref, first_ref, flow, g, g) for g in range(GROUPS - 1)
    ]
    start(parts_of[0])
    build = swap_slots(groups, keys_ref, blocks, out_ref, sends, receives, local)
    copies = build(0, rows_ref)
    start(parts_of[1])
    for i, copy in enumerate(gathers):
        copy.wait_recv()
        passes[i + 1].start()
    hops.wait_recv()
    copies += build(1, other)
    start(parts_of[2])
    hops.wait_send()
    wait(copies)
    for copy in gathers:
        copy.wait_send()
    wait(passes)
    kept.wait()
    for group in parts_of:
        wait(group)


def dispatch_kernel(
    sizes, keys_ref, rows_ref, master_ref, out_ref, other_ref, second_ref,
    blocks, other, hop, sends, receives, local, flow,
):
    replicas, parts, groups = sizes
    count = keys_ref.shape[1]
    mirror = (0, parts // 2, 0)
    greet(
        sorted({near(groups, j) for j in range(1, count)} | {mirror, *all_owners(replicas, parts)})
    )
    hops = remote(rows_ref, other, hop.at[0], hop.at[1], mirror)
    hops.start()
    build = swap_slots(groups, keys_ref, blocks, out_ref, sends, receives, local)
    copies = build(0, rows_ref)
    more = [outward(sizes, tall_part, master_ref, second_ref, flow, g, g) for g in range(3)]
    start(more[0])
    start(more[1])
    hops.wait()
    copies += build(1, other)
    start(more[2])
    keep = pltpu.make_async_copy(other, other_ref, local.at[2])
    keep.start()
    keep.wait()
    wait(copies)
    for group in more:
        wait(group)


def dispatch(keys, rows, sizes, number, master, shard=None):
    replicas, parts, groups = sizes
    _, count, own, tokens = keys.shape
    shape = (count, 2, own, CAP, D)
    owners = replicas * parts
    opening = number == 0
    inner = pl.BlockSpec(memory_space=pltpu.VMEM)
    outer = pl.BlockSpec(memory_space=pl.ANY)
    whole = jax.ShapeDtypeStruct((owners, own, *master.shape[1:]), low)
    outs = [jax.ShapeDtypeStruct(shape, low)]
    semaphores = [(2,), (count, 2), (count, 2), (3,)]
    scratch = [pltpu.VMEM(shape, low), pltpu.VMEM(rows.shape, low)]
    scratch += [pltpu.SemaphoreType.DMA(n) for n in semaphores] + [flow_semaphores(sizes, 3)]
    if opening:
        arrays = (keys, rows, shard, master)
        outs += [jax.ShapeDtypeStruct((owners, *shard.shape), low), whole]
        more = [(2, owners // 2 - 1), (2, owners // 2), ()]
        scratch += [pltpu.SemaphoreType.DMA(n) for n in more]
    else:
        arrays = (keys, rows, master)
        outs += [jax.ShapeDtypeStruct(rows.shape, low), whole]
    return pl.pallas_call(
        partial(open_kernel if opening else dispatch_kernel, sizes),
        in_specs=[inner, inner] + [outer] * (len(arrays) - 2),
        out_specs=[outer] * len(outs),
        out_shape=outs,
        scratch_shapes=scratch,
        compiler_params=pltpu.CompilerParams(
            vmem_limit_bytes=BIG, collective_id=number, has_side_effects=True
        ),
        cost_estimate=pl.CostEstimate(
            flops=60 * 10**9, bytes_accessed=5 * 10**6, transcendentals=0
        ),
        name="open" if opening else "dispatch",
    )(*arrays)


def chooser(own, j):
    shape = (LANES, own * CAP)
    expert = lax.broadcasted_iota(jnp.int32, shape, 0)
    slot = lax.broadcasted_iota(jnp.int32, shape, 1)
    return (expert == j * own + slot // CAP).astype(low)


def attend_back(i, weights, held, acc, dqkv, dx_ref):
    w_ref, order_ref = weights
    x_ref, qkv_ref, ctx_ref, r_ref, h_ref, probs_ref, dy_ref, dh_ref, dprobs_ref = held
    qkv_acc, proj_acc, router_acc, norm_acc = acc
    rows = pl.ds(pl.multiple_of(i * ROWS, ROWS), ROWS)
    gain_one, bias_one, gain_two, _ = norm_vectors(w_ref)
    probs, dprobs = probs_ref[i], dprobs_ref[rows]
    dlogits = (probs * (dprobs - jnp.sum(probs * dprobs, axis=-1, keepdims=True))).astype(low)
    router_acc[...] += dot_lt(h_ref[i], dlogits)
    router = dot(w_ref[:, QKV + D :], order_ref[...]).astype(low)
    dh = dh_ref[rows] + dot_rt(dlogits, router)
    normed, factor = normed_rows(r_ref[i])
    norm_acc[2:3] += jnp.sum(dh * normed, axis=0, keepdims=True)
    norm_acc[3:4] += jnp.sum(dh, axis=0, keepdims=True)
    dr = dy_ref[i].astype(full) + norm_back(normed, factor, gain_two, dh)
    dattended = dr.astype(low)
    proj_acc[...] += dot_lt(ctx_ref[i], dattended)
    dctx = dot_rt(dattended, w_ref[:, QKV : QKV + D]).astype(low)
    for pair in range(HEADS // 2):
        at = pair * LANES
        query = halves(qkv_ref[i, :, at : at + LANES])
        key = qkv_ref[i, :, D + at : D + at + LANES]
        keys = halves(key)
        value = qkv_ref[i, :, 2 * D + at : 2 * D + at + LANES]
        dhead = halves(dctx[:, at : at + LANES])
        dq = dk = dv = None
        for e in range(2):
            p = head_probs(query[e], key)
            dp = dot_rt(dhead[e], value)
            ds = (p * (dp - jnp.sum(p * dp, axis=-1, keepdims=True))).astype(low)
            terms = dot(ds, keys[e]), dot_lt(ds, query[e]), dot_lt(p.astype(low), dhead[e])
            dq, dk, dv = terms if dq is None else (dq + terms[0], dk + terms[1], dv + terms[2])
        dqkv[:, at : at + LANES] = (dq * HEAD**-0.5).astype(low)
        dqkv[:, D + at : D + at + LANES] = (dk * HEAD**-0.5).astype(low)
        dqkv[:, 2 * D + at : 2 * D + at + LANES] = dv.astype(low)
    normed, factor = normed_rows(x_ref[i].astype(full))
    attn_in = (normed * gain_one + bias_one).astype(low)
    qkv_acc[...] += dot_lt(attn_in, dqkv[...])
    da = dot_rt(dqkv[...], w_ref[:, :QKV])
    norm_acc[0:1] += jnp.sum(da * normed, axis=0, keepdims=True)
    norm_acc[1:2] += jnp.sum(da, axis=0, keepdims=True)
    dx_ref[i] = dr + norm_back(normed, factor, gain_one, da)


def close_kernel(
    sizes, keys_ref, back_ref, w_ref, order_ref, x_ref, qkv_ref, ctx_ref, r_ref, sent_ref, probs_ref, dy_ref,
    theirs_ref, y_ref, dw_one_ref, dw_two_ref, got_two_ref,
    dx_ref, out_ref, total_ref, one_ref, two_ref,
    xs, qkvs, ctxs, rs, hs, ps, dys, their_probs, ys, dh, dprobs, sent, got, sent_two, got_two,
    mine_one, others_one, mine_two, others_two,
    dqkv, qkv_acc, proj_acc, router_acc, norm_acc, grads, kept, first, second, third,
    loads, y_sends, y_receives, hops, hops_two, flow, home_one, home_two,
    core_sems, owner_sems, expert_sems,
):
    replicas, parts, groups = sizes
    count, _, own, _, _ = y_ref.shape
    images = x_ref.shape[0]
    width = own * CAP
    half = count * own
    mirror = (0, parts // 2, 0)
    owners = owners_like(replicas, parts)
    sideways = [(0, 0, g) for g in range(1, groups)]
    peers = {near(groups, j) for j in range(1, count)} | {mirror, *sideways, *owners}
    greet(sorted(peers | partners(sizes)))

    pairs_of = [
        (r_ref, rs), (theirs_ref.at[:, D:], their_probs), (x_ref, xs), (qkv_ref, qkvs), (ctx_ref, ctxs),
        (sent_ref.at[:, :, :D], hs), (probs_ref, ps), (dy_ref, dys),
        (mine_of(sizes, dw_two_ref), mine_two), (got_two_ref, others_two),
        (mine_of(sizes, dw_one_ref), mine_one), (y_ref.at[0], ys.at[0]),
    ]
    loading = [
        pltpu.make_async_copy(source, target, loads.at[i])
        for i, (source, target) in enumerate(pairs_of)
    ]
    swaps = [
        [
            remote(y_ref.at[j, s], ys.at[j, s], y_sends.at[j, s], y_receives.at[j, s], near(groups, j))
            for j in range(1, count)
        ]
        for s in range(2)
    ]
    eighths = [
        across(sizes, narrow_part, dw_one_ref, others_one, flow, g, g) for g in range(2 * GROUPS)
    ]
    start(swaps[1])
    start(swaps[0])
    start(eighths[0])
    start(eighths[1])
    start(loading)

    def rows_of(i):
        return pl.ds(pl.multiple_of(i * ROWS, ROWS), ROWS)

    def hop(i):
        rows = rows_of(i)
        return remote(sent.at[rows], got.at[rows], hops.at[0, i], hops.at[1, i], mirror)

    def hop_two(i):
        rows = rows_of(i)
        return remote(sent_two.at[rows], got_two.at[rows], hops_two.at[0, i], hops_two.at[1, i], mirror)

    def gathered(s, rows):
        slot = (lanes_of((ROWS, width)) % CAP).astype(full)
        lane = lanes_of((ROWS, LANES))
        keys = keys_ref[s, rows]
        total = jnp.zeros((ROWS, D), full)
        change = jnp.zeros((ROWS, LANES), full)
        for j in range(count):
            here = dot(keys, chooser(own, j)) == slot
            total = total + dot(here.astype(low), back_ref[j, s, :, :CAP].reshape(width, D))
            dgate = back_ref[j, s, :, CAP : CAP + 1].astype(full)
            dgate = dgate[:, :, :CAP] + dgate[:, :, CAP : 2 * CAP]
            for e in range(own):
                agreed = jnp.where(here[:, e * CAP : (e + 1) * CAP], dgate[e], 0.0)
                column = jnp.sum(agreed, axis=-1, keepdims=True)
                change = jnp.where(lane == j * own + e, column, change)
        return total, change

    def weighted(s, rows, probs):
        slot = (lanes_of((ROWS, width)) % CAP).astype(full)
        keys = keys_ref[s, rows]
        total = jnp.zeros((ROWS, D), full)
        for j in range(count):
            spread = chooser(own, j)
            gate = jnp.where(dot(keys, spread) == slot, dot(probs, spread), 0.0)
            total = total + dot(gate.astype(low), ys[j, s].reshape(width, D))
        return total

    @pl.loop(0, images)
    def _(i):
        rows = rows_of(i)
        total, change = gathered(1, rows)
        sent[rows, :D] = total.astype(low)
        high = change.astype(low)
        rest = pltpu.roll(change - high.astype(full), half, 1)
        sent[rows, D:] = (high.astype(full) + rest).astype(low)
        hop(i).start()

    start(eighths[2])

    @pl.loop(0, images)
    def _(i):
        rows = rows_of(i)
        dh[rows], dprobs[rows] = gathered(0, rows)

    wait(loading)
    wait(swaps[1])

    @pl.loop(0, images)
    def _(i):
        rows = rows_of(i)
        sent_two[rows] = weighted(1, rows, their_probs[rows]).astype(low)
        hop_two(i).start()

    start(eighths[3])

    @pl.loop(0, images)
    def _(i):
        rows = rows_of(i)
        hop(i).wait()
        dh[rows] += got[rows, :D].astype(full)
        pair = got[rows, D:].astype(full)
        lane = lanes_of(pair.shape)
        whole = pair + pltpu.roll(pair, half, 1)
        dprobs[rows] += jnp.where((lane >= half) & (lane < 2 * half), whole, 0.0)

    for g in range(GROUPS, 2 * GROUPS):
        start(eighths[g])

    def add(mine, others, columns):
        @pl.loop(0, parts)
        def _(p):
            total = mine[p, :, :, columns].astype(full)
            for r in range(replicas - 1):
                total = total + others[r, p, :, :, columns].astype(full)
            mine[p, :, :, columns] = total.astype(low)

    add(mine_two, others_two, slice(None))
    homes = homeward(sizes, lambda ref, at, g: ref.at[at], mine_two, two_ref, home_two, 0, 0)
    start(homes)
    for ref in (qkv_acc, proj_acc, router_acc, norm_acc):
        ref[...] = jnp.zeros_like(ref)

    @pl.loop(0, images)
    def _(i):
        attend_back(
            i, (w_ref, order_ref), (xs, qkvs, ctxs, rs, hs, ps, dys, dh, dprobs),
            (qkv_acc, proj_acc, router_acc, norm_acc), dqkv, dx_ref,
        )

    columns = norm_acc[...].T
    shifted = pltpu.roll(columns, EXPERTS, 1)
    tile = jnp.where(lanes_of(shifted.shape) < EXPERTS, router_acc[...], shifted)
    router_acc[...] = dot_rt(tile.astype(low), order_ref[...])
    depth = grads.shape[1]
    core = lax.axis_index("part") % 2
    blocks = replicas * parts // 2

    @pl.loop(0, 2 * blocks)
    def _(o):
        rows = pl.ds(pl.multiple_of(o * depth, depth), depth)
        grads[o, :, :QKV] = qkv_acc[rows].astype(low)
        grads[o, :, QKV : QKV + D] = proj_acc[rows].astype(low)
        grads[o, :, QKV + D :] = router_acc[rows].astype(low)

    to_core = [
        remote(grads.at[2 * i + 1 - core], first.at[i], core_sems.at[0, i], core_sems.at[1, i], CORE)
        for i in range(blocks)
    ]
    start(to_core)
    for i in range(blocks):
        to_core[i].wait()
        kept[i] = (grads[2 * i + core].astype(full) + first[i].astype(full)).astype(low)
    to_owner = [
        remote(kept.at[owner(parts, o) // 2], second.at[i], owner_sems.at[0, i], owner_sems.at[1, i], o)
        for i, o in enumerate(owners)
    ]
    start(to_owner)

    each = mine_one.shape[-1] // GROUPS
    for g in range(GROUPS):
        wait(eighths[2 * g])
        wait(eighths[2 * g + 1])
        add(mine_one, others_one, slice(g * each, (g + 1) * each))
        copies = homeward(sizes, wide_part, mine_one, one_ref, home_one, g, g)
        start(copies)
        homes += copies
    wait(swaps[0])

    @pl.loop(0, images)
    def _(i):
        rows = rows_of(i)
        total = rs[i] + weighted(0, rows, ps[i].astype(low))
        hop_two(i).wait()
        out_ref[rows] = (total + got_two[rows].astype(full)).astype(low)

    total = kept[owner(parts) // 2].astype(full)
    for i, copy in enumerate(to_owner):
        copy.wait()
        total = total + second[i].astype(full)
    me = lax.axis_index("expert")
    third[me] = total.astype(low)
    to_others = [
        remote(third.at[me], third.at[me], expert_sems.at[0, i], expert_sems.at[1, i], o)
        for i, o in enumerate(sideways)
    ]
    start(to_others)
    wait(to_others)
    total = third[0].astype(full)
    for g in range(1, groups):
        total = total + third[g].astype(full)
    total_ref[...] = total
    wait(homes)


def close(keys, back, weights, order, x, qkv, ctx, r, sent, probs, dy, theirs, y, dw_one, dw_two, got_two, sizes, number):
    replicas, parts, groups = sizes
    images = x.shape[0]
    tokens = images * ROWS
    count = y.shape[0]
    owners = replicas * parts
    shard = (weights.shape[0] // owners, PACKED)
    one = (parts, *dw_one.shape[1:])
    two = (parts, *dw_two.shape[1:])
    inner = pl.BlockSpec(memory_space=pltpu.VMEM)
    outer = pl.BlockSpec(memory_space=pl.ANY)
    buffers = [
        (x.shape, low), (qkv.shape, low), (ctx.shape, low), (r.shape, full), (x.shape, low),
        (probs.shape, full), (dy.shape, low), ((tokens, LANES), low), (y.shape, low),
        ((tokens, D), full), ((tokens, LANES), full),
        ((tokens, SENT), low), ((tokens, SENT), low), ((tokens, D), low), ((tokens, D), low),
        (one, low), ((replicas - 1, *one), low), (two, low), ((replicas - 1, *two), low),
        ((ROWS, QKV), low), ((D, QKV), full), ((D, D), full), ((D, LANES), full), ((LANES, D), full),
        ((owners, *shard), low), ((owners // 2, *shard), low), ((owners // 2, *shard), low),
        ((owners // 2 - 1, *shard), low), ((groups, *shard), low),
    ]
    semaphores = [
        (12,), (count, 2), (count, 2), (2, images), (2, images), (2, 2 * GROUPS, replicas),
        (2, GROUPS, parts), (2, 1, parts), (2, owners // 2), (2, owners // 2 - 1), (2, groups - 1),
    ]
    arrays = (
        keys, back, weights, order, x, qkv, ctx, r, sent, probs, dy, theirs, y, dw_one, dw_two, got_two,
    )
    return pl.pallas_call(
        partial(close_kernel, sizes),
        in_specs=[inner] * 4 + [outer] * 12,
        out_specs=[inner] * 3 + [outer] * 2,
        out_shape=[
            jax.ShapeDtypeStruct((images, ROWS, D), full),
            jax.ShapeDtypeStruct((tokens, D), low),
            jax.ShapeDtypeStruct(shard, full),
            jax.ShapeDtypeStruct(one, low),
            jax.ShapeDtypeStruct(two, low),
        ],
        scratch_shapes=[pltpu.VMEM(*b) for b in buffers]
        + [pltpu.SemaphoreType.DMA(n) for n in semaphores],
        compiler_params=pltpu.CompilerParams(
            vmem_limit_bytes=BIG, collective_id=number, has_side_effects=True
        ),
        cost_estimate=pl.CostEstimate(
            flops=60 * 10**9, bytes_accessed=30 * 10**6, transcendentals=2 * 10**6
        ),
        name="close",
    )(*arrays)


GELU = 0.7978845608028654
CUBE = 0.044715


def gelu_pair(u):
    square = u * u
    bent = jnp.tanh(u * (GELU * CUBE * square + GELU))
    half = 0.5 * bent + 0.5
    value = u * half
    return value, half + value * (1.0 - bent) * (3.0 * GELU * CUBE * square + GELU)


def first_kernel(
    sizes, h_ref, dy_ref, w_ref, wr_ref, sel_ref, master_ref, _, g_ref, slope_ref, dw_ref, second_ref,
    gates, dye_t, flow,
):
    sources = h_ref.shape[0]
    tile = w_ref.shape[3]
    at = pl.program_id(0) * pl.num_programs(1) + pl.program_id(1)

    def moved(g):
        return outward(sizes, tall_part, master_ref, second_ref, flow, g, g - 3)

    @pl.when(at == 0)
    def _():
        greet(all_owners(*sizes[:2]))
        start(moved(3))

    @pl.when(pl.program_id(1) == 0)
    def _():
        for k in range(sources):
            rows = slice(k * CAP, (k + 1) * CAP)
            logits = dot(h_ref[k, 0], wr_ref[...])
            logits = jnp.where(lanes_of(logits.shape) < EXPERTS, logits, -1e30)
            grown = jnp.exp(logits - jnp.max(logits, axis=-1, keepdims=True))
            mine = jnp.sum(grown * sel_ref[0], axis=-1, keepdims=True)
            gate = mine / jnp.sum(grown, axis=-1, keepdims=True)
            gates[rows] = jnp.broadcast_to(gate, (CAP, LANES))
            dye_t[:, rows] = (dy_ref[k, 0].astype(full) * gate).T.astype(low)

    w = w_ref[:, 0].reshape(D, tile)
    for k in range(0, sources, 2):
        rows = slice(k * CAP, (k + 2) * CAP)
        value, slope = gelu_pair(dot(h_ref[k : k + 2, 0].reshape(2 * CAP, D), w))
        g_ref[0, rows] = value.astype(low)
        slope_ref[0, rows] = (slope * gates[rows, :1]).astype(low)
    grad = dot(dye_t[...], g_ref[0]).T
    dw_ref[:, 0] = grad.astype(low).reshape(dw_ref.shape[0], dw_ref.shape[2], D)

    @pl.when(at == pl.num_programs(0) * pl.num_programs(1) - 1)
    def _():
        wait(moved(3))


def slot_spec(sources):
    return pl.BlockSpec((sources, 1, CAP, D), lambda e, f: (0, e, 0, 0))


def expert_first(h, dy, w_in, w_router, select, master, second, sizes, tile, number):
    sources = h.shape[0]
    owners, own, depth, hidden = w_in.shape
    rows = sources * CAP
    per = hidden // owners
    hidden_spec = pl.BlockSpec((1, rows, tile), lambda e, f: (e, 0, f))
    return pl.pallas_call(
        partial(first_kernel, sizes),
        grid=(own, hidden // tile),
        in_specs=[
            slot_spec(sources),
            slot_spec(sources),
            pl.BlockSpec((owners, 1, depth, tile), lambda e, f: (0, e, 0, f)),
            whole_spec(w_router.shape),
            pl.BlockSpec((1, 1, LANES), lambda e, f: (e, 0, 0)),
            pl.BlockSpec(memory_space=pl.ANY),
            pl.BlockSpec(memory_space=pl.ANY),
        ],
        out_specs=[
            hidden_spec,
            hidden_spec,
            pl.BlockSpec((tile // per, 1, per, D), lambda e, f: (f, e, 0, 0)),
            pl.BlockSpec(memory_space=pl.ANY),
        ],
        out_shape=[
            jax.ShapeDtypeStruct((own, rows, hidden), low),
            jax.ShapeDtypeStruct((own, rows, hidden), low),
            jax.ShapeDtypeStruct((owners, own, per, D), low),
            jax.ShapeDtypeStruct(second.shape, low),
        ],
        input_output_aliases={6: 3},
        scratch_shapes=[
            pltpu.VMEM((rows, LANES), full), pltpu.VMEM((D, rows), low), flow_semaphores(sizes, 2),
        ],
        compiler_params=pltpu.CompilerParams(
            dimension_semantics=("arbitrary",) * 2,
            vmem_limit_bytes=BIG,
            collective_id=number,
            has_side_effects=True,
        ),
        cost_estimate=pl.CostEstimate(
            flops=4 * own * rows * D * hidden,
            bytes_accessed=50 * 10**6,
            transcendentals=own * rows * hidden,
        ),
        name="expert_first",
    )(h, dy, w_in, w_router, select, master, second)


def rest_kernel(
    sizes, own, steps, dy_ref, h_ref, g_ref, slope_ref, w_in_ref, w_out_ref, dw_two_ref,
    back_ref, dw_ref, y_ref, two_ref, du, acc, dgates, dgate_rows, h_t, staged, sends, receives, local, flow,
):
    replicas, parts, groups = sizes

    def moved(g):
        return across(sizes, tall_part, dw_two_ref, two_ref, flow, g, g)

    sources = dy_ref.shape[0]
    tile = slope_ref.shape[2]
    at = pl.program_id(0)
    phase, expert, step = at // (own * steps), at // steps % own, at % steps
    w_in = w_in_ref[:, 0].reshape(D, tile)
    w_out = w_out_ref[:, 0].reshape(tile, D)
    chunk = 2 * CAP

    def copy(k, e):
        return pltpu.make_async_remote_copy(
            src_ref=staged.at[k, e],
            dst_ref=back_ref.at[k, e],
            send_sem=sends.at[k, e],
            recv_sem=receives.at[k, e],
            device_id=device(near(groups, k // 2)),
            device_id_type=MESH,
        )

    def mine(k, e):
        return pltpu.make_async_copy(staged.at[k, e], back_ref.at[k, e], local.at[k, e])

    @pl.when(at == 0)
    def _():
        greet(sorted({near(groups, j) for j in range(1, sources // 2)} | partners(sizes)))
        start(moved(0))
        start(moved(1))

    @pl.when((phase != 1) & (step == 0))
    def _():
        acc[...] = jnp.zeros_like(acc)

    @pl.when(phase == 0)
    def _():
        @pl.when(step == 0)
        def _():
            dgates[...] = jnp.zeros_like(dgates)

        for k in range(0, sources, 2):
            rows = slice(k * CAP, (k + 2) * CAP)
            dg = dot_rt(dy_ref[k : k + 2, 0].reshape(chunk, D), w_out)
            change = (dg * slope_ref[0, rows].astype(full)).astype(low)
            du[expert * steps + step, rows] = change
            acc[rows] += dot_rt(change, w_in)
            agreed = dg * g_ref[0, rows].astype(full)
            dgates[rows] += sum(agreed[:, i : i + LANES] for i in range(0, tile, LANES))

        @pl.when(step == steps - 1)
        def _():
            sums = dgates[...]
            high = sums.astype(low)
            rest = (sums - high.astype(full)).astype(low)
            ones = jnp.ones((16, LANES), low)
            dgate_rows[...] = dot_rt(ones, high) + dot_rt(ones, rest)
            for k in range(sources):
                rows = slice(k * CAP, (k + 1) * CAP)
                staged[k, expert, :CAP] = acc[rows].astype(low)
                row = dgate_rows[:, rows]
                high = row.astype(low)
                staged[k, expert, CAP:, :CAP] = high
                staged[k, expert, CAP:, CAP : 2 * CAP] = (row - high.astype(full)).astype(low)
                staged[k, expert, CAP:, 2 * CAP :] = jnp.zeros((16, D - 2 * CAP), low)

        for e in range(own):
            @pl.when((step == steps - 1) & (expert == e))
            def _():
                for k in range(2, sources):
                    copy(k, e).start()
                mine(0, e).start()
                mine(1, e).start()

    @pl.when(at == own * steps)
    def _():
        start(moved(2))
        start(moved(3))

    @pl.when(phase == 1)
    def _():
        @pl.when(step == 0)
        def _():
            for k in range(sources):
                h_t[:, k * CAP : (k + 1) * CAP] = h_ref[k, 0].T

        grad = dot(h_t[...], du[expert * steps + step]).astype(low)
        dw_ref[:, 0] = grad.reshape(dw_ref.shape[0], dw_ref.shape[2], tile)

    @pl.when(phase == 2)
    def _():
        for k in range(0, sources, 2):
            rows = slice(k * CAP, (k + 2) * CAP)
            acc[rows] += dot(g_ref[0, rows], w_out)

        @pl.when(step == steps - 1)
        def _():
            y_ref[:, 0] = acc[...].astype(low).reshape(sources, CAP, D)

    @pl.when(at == 3 * own * steps - 1)
    def _():
        for e in range(own):
            for k in range(2, sources):
                copy(k, e).wait()
            mine(0, e).wait()
            mine(1, e).wait()
        for g in range(GROUPS):
            wait(moved(g))


def expert_rest(dy, h, g, slope, w_in, w_out, dw_two, tile, sizes, number):
    sources, own, _, _ = dy.shape
    owners, _, depth, hidden = w_in.shape
    rows = sources * CAP
    per = hidden // owners
    steps = hidden // tile
    last = own * steps - 1

    def during(phases):
        def find(at):
            if 0 in phases and 2 in phases:
                inside = jnp.where(at // (last + 1) == 1, last, at % (last + 1))
            else:
                inside = jnp.clip(at - phases[0] * (last + 1), 0, last)
            return inside // steps, inside % steps

        return find

    def spec(shape, phases, index, buffers=2):
        return pl.BlockSpec(
            shape, lambda at: index(*during(phases)(at)), pipeline_mode=pl.Buffered(buffers)
        )

    token, hidden_at = (sources, 1, CAP, D), (1, rows, tile)
    whole_expert = lambda e, f: (0, e, 0, 0)
    in_tile = lambda e, f: (0, e, 0, f)
    return pl.pallas_call(
        partial(rest_kernel, sizes, own, steps),
        grid=(3 * own * steps,),
        in_specs=[
            spec(token, (0,), whole_expert, 1),
            spec(token, (1,), whole_expert, 1),
            spec(hidden_at, (0, 2), lambda e, f: (e, 0, f)),
            spec(hidden_at, (0,), lambda e, f: (e, 0, f)),
            spec((owners, 1, depth, tile), (0,), in_tile),
            spec((tile // per, 1, per, D), (0, 2), lambda e, f: (f, e, 0, 0)),
            pl.BlockSpec(memory_space=pl.ANY),
        ],
        out_specs=[
            pl.BlockSpec(memory_space=pl.ANY),
            spec((owners, 1, depth, tile), (1,), in_tile),
            spec(token, (2,), whole_expert),
            pl.BlockSpec(memory_space=pl.ANY),
        ],
        out_shape=[
            jax.ShapeDtypeStruct((sources, own, CAP + 16, D), low),
            jax.ShapeDtypeStruct(w_in.shape, low),
            jax.ShapeDtypeStruct(dy.shape, low),
            pieces_of(sizes, dw_two),
        ],
        scratch_shapes=[
            pltpu.VMEM((own * steps, rows, tile), low),
            pltpu.VMEM((rows, D), full),
            pltpu.VMEM((rows, LANES), full),
            pltpu.VMEM((16, rows), full),
            pltpu.VMEM((D, rows), low),
            pltpu.VMEM((sources, own, CAP + 16, D), low),
            pltpu.SemaphoreType.DMA((sources, own)),
            pltpu.SemaphoreType.DMA((sources, own)),
            pltpu.SemaphoreType.DMA((2, own)),
            flow_semaphores(sizes, GROUPS),
        ],
        compiler_params=pltpu.CompilerParams(
            dimension_semantics=("arbitrary",),
            vmem_limit_bytes=BIG,
            collective_id=number,
            has_side_effects=True,
        ),
        cost_estimate=pl.CostEstimate(
            flops=8 * own * rows * D * hidden, bytes_accessed=60 * 10**6, transcendentals=0
        ),
        name="expert_rest",
    )(dy, h, g, slope, w_in, w_out, dw_two)


ALL = ("replica", "part")


def body(
    tokens,
    choices,
    ln1_gain,
    ln1_bias,
    w_qkv,
    w_proj,
    ln2_gain,
    ln2_bias,
    w_router,
    w_expert_in,
    w_expert_out,
    cotangent,
):
    replicas, parts, groups = (lax.axis_size(name) for name in ("replica", "part", "expert"))
    owners = replicas * parts
    peers = parts * groups
    own = EXPERTS // peers
    images = tokens.shape[0] // SEQ
    count = images * ROWS
    tile = 512 * 16 // peers

    small_rows = w_router.shape[0]
    placed_router = (
        w_router.reshape(small_rows, groups, parts, own).transpose(0, 2, 1, 3).reshape(small_rows, EXPERTS)
    )
    vectors = jnp.stack([ln1_gain, ln1_bias, ln2_gain, ln2_bias], axis=1)
    packed = jnp.concatenate(
        [w_qkv, w_proj, placed_router, vectors, jnp.zeros((small_rows, LANES - EXPERTS - 4), full)],
        axis=1,
    ).astype(low)
    me = lax.axis_index("part") * groups + lax.axis_index("expert")
    sizes = (replicas, parts, groups)

    def padded(rows, fill=0):
        rows = rows.reshape(images, SEQ, rows.shape[1])
        return jnp.pad(rows, ((0, 0), (0, ROWS - SEQ), (0, 0)), constant_values=fill)

    x = padded(tokens)
    dy = padded(cotangent)
    half = parts // 2
    flips = [(i, i ^ half) for i in range(parts)]
    picks = jnp.stack([choices, lax.ppermute(choices, "part", flips)]).reshape(2 * images, SEQ, 2)
    picks = jnp.pad(picks, ((0, 0), (0, ROWS - SEQ), (0, 0)), constant_values=-1)
    picks = picks.reshape(2, count, 2)
    column = jnp.arange(EXPERTS)
    place = (me ^ (column // own)) * own + column % own
    expert = (place // own % groups) * (parts * own) + place // (groups * own) * own + place % own
    lane = jnp.arange(LANES)
    order = jnp.where(lane < EXPERTS, jnp.pad(place, (0, LANES - EXPERTS)), lane)
    order = (lane[:, None] == order[None, :]).astype(low)
    expert = expert[: EXPERTS // 2]
    named = (picks[:, :, :, None] == expert).any(axis=2)
    row = jnp.arange(count)
    earlier = (row[None, :] < row[:, None]).astype(low)
    slots = jnp.einsum("tu,sue->ste", earlier, named.astype(low), preferred_element_type=full)
    keys = jnp.where(named, slots, -1.0)
    key_rows = keys.transpose(0, 2, 1).reshape(2, peers // 2, own, count)
    key_columns = jnp.pad(
        keys, ((0, 0), (0, 0), (0, LANES - EXPERTS // 2)), constant_values=-1
    ).astype(low)

    first_master, second_master = w_expert_in.astype(low), w_expert_out.astype(low)
    dy_slots, weights, first_weight = dispatch(
        key_rows, dy.reshape(count, D), sizes, 0, first_master, packed
    )
    weights = weights.reshape(D, PACKED)
    qkv, ctx, r, sent, probs, first_weight = attend(
        x, weights, order, first_master, first_weight, sizes, 6
    )
    h_slots, theirs, second_weight = dispatch(
        key_rows, sent.reshape(count, SENT), sizes, 1, second_master
    )
    dy_slots = dy_slots.reshape(peers, own, CAP, D)
    h_slots = h_slots.reshape(peers, own, CAP, D)
    select = ((me * own + jnp.arange(own))[:, None, None] == lane[None, None, :]).astype(full)
    g, slope, dw_second, second_weight = expert_first(
        h_slots, dy_slots, first_weight, weights[:, QKV + D :], select, second_master, second_weight,
        sizes, tile, 5,
    )
    back, dw_first, y, got_second = expert_rest(
        dy_slots, h_slots, g, slope, first_weight, second_weight, dw_second, tile, sizes, 2
    )
    back = back.reshape(peers // 2, 2, own, CAP + 16, D)
    y = y.reshape(peers // 2, 2, own, CAP, D)
    dx, output, grads, first_grad, second_grad = close(
        key_columns, back, weights, order, x, qkv, ctx, r, sent, probs, dy, theirs, y,
        dw_first, dw_second, got_second, sizes, 3,
    )
    expert_in_grad = first_grad.reshape(w_expert_in.shape).astype(full)
    expert_out_grad = second_grad.reshape(w_expert_out.shape).astype(full)
    router_grad = (
        grads[:, QKV + D : QKV + D + EXPERTS]
        .reshape(small_rows, parts, groups, own)
        .transpose(0, 2, 1, 3)
        .reshape(small_rows, EXPERTS)
    )
    norms = [grads[:, QKV + D + EXPERTS + i] for i in range(4)]

    def unpadded(rows):
        return rows.reshape(images, ROWS, D)[:, :SEQ].reshape(images * SEQ, D)

    return (
        unpadded(output),
        unpadded(dx),
        norms[0],
        norms[1],
        grads[:, :QKV],
        grads[:, QKV : QKV + D],
        norms[2],
        norms[3],
        router_grad,
        expert_in_grad,
        expert_out_grad,
    )


def solution(mesh):
    dp, groups = mesh.shape["dp"], mesh.shape["expert"]
    parts = min(EXPERTS // groups, dp // 2)
    mesh = Mesh(mesh.devices.reshape(dp // parts, parts, groups), ("replica", "part", "expert"))
    rows = P(("replica", "part", "expert"), None)
    vector, matrix = P(ALL), P(ALL, None)
    experts = P("expert", ALL, None)
    return jax.shard_map(
        body,
        mesh=mesh,
        in_specs=(
            rows, rows, vector, vector, matrix, matrix, vector, vector, matrix, experts, experts, rows,
        ),
        out_specs=(
            rows, rows, vector, vector, matrix, matrix, vector, vector, matrix, experts, experts,
        ),
        check_vma=False,
    )
```

```python
from functools import partial

import jax
import jax.numpy as jnp
from jax import lax
from jax.experimental import pallas as pl
from jax.experimental.pallas import tpu as pltpu
from jax.sharding import Mesh
from jax.sharding import PartitionSpec as P

D = 512
HEADS = 8
EXPERTS = 32
SEQ = 197
CAP = 128
ROWS = 208
HEAD = D // HEADS
LANES = 128
QKV = 3 * D
PACKED = QKV + D + LANES
epsilon = 1e-06
low = jnp.bfloat16
full = jnp.float32
MESH = pl.DeviceIdType.MESH
BIG = 63 * 1024 * 1024


def dot(left, right):
    return jnp.dot(left, right, preferred_element_type=full)


def dot_rt(left, right):
    return lax.dot_general(left, right, (((1,), (1,)), ((), ())), preferred_element_type=full)


def dot_lt(left, right):
    return lax.dot_general(left, right, (((0,), (0,)), ((), ())), preferred_element_type=full)


def lanes_of(shape):
    return lax.broadcasted_iota(jnp.int32, shape, len(shape) - 1)


def normed_rows(values):
    center = values - jnp.mean(values, axis=-1, keepdims=True)
    factor = lax.rsqrt(jnp.mean(center * center, axis=-1, keepdims=True) + epsilon)
    return center * factor, factor


def norm_back(normed, factor, gain_vec, upstream):
    scaled = upstream * gain_vec
    return factor * (
        scaled
        - jnp.mean(scaled, axis=-1, keepdims=True)
        - normed * jnp.mean(scaled * normed, axis=-1, keepdims=True)
    )


def columns_of(weights_ref, start_at, end):
    return weights_ref[:, :, start_at:end].reshape(D, end - start_at)


def norm_vectors(weights_ref):
    rows = columns_of(weights_ref, QKV + D, PACKED).astype(full).T
    return [rows[EXPERTS + i : EXPERTS + i + 1] for i in range(4)]


def halves(pair):
    first = lanes_of(pair.shape) < HEAD
    zero = jnp.zeros_like(pair)
    return jnp.where(first, pair, zero), jnp.where(first, zero, pair)


def head_probs(query, key_pair):
    scores = dot_rt(query, key_pair) * (HEAD**-0.5)
    scores = jnp.where(lanes_of(scores.shape) < SEQ, scores, -1e30)
    grown = jnp.exp(scores - jnp.max(scores, axis=-1, keepdims=True))
    return grown / jnp.sum(grown, axis=-1, keepdims=True)


def attend(i, weights, order, x_ref, qkv_ref, ctx_ref, r_ref, h_ref, probs_ref):
    gain_one, bias_one, gain_two, bias_two = norm_vectors(weights)
    x = x_ref[i].astype(full)
    normed, _ = normed_rows(x)
    attn_in = (normed * gain_one + bias_one).astype(low)
    qkv_ref[i] = dot(attn_in, columns_of(weights, 0, QKV)).astype(low)
    for pair in range(HEADS // 2):
        at = pair * LANES
        query = halves(qkv_ref[i, :, at : at + LANES])
        key = qkv_ref[i, :, D + at : D + at + LANES]
        value = halves(qkv_ref[i, :, 2 * D + at : 2 * D + at + LANES])
        total = None
        for e in range(2):
            part = dot(head_probs(query[e], key).astype(low), value[e])
            total = part if total is None else total + part
        ctx_ref[i, :, at : at + LANES] = total.astype(low)
    r = x + dot(ctx_ref[i], columns_of(weights, QKV, QKV + D))
    r_ref[i] = r
    normed, _ = normed_rows(r)
    h = (normed * gain_two + bias_two).astype(low)
    h_ref[i] = h
    probs_ref[i] = routed(h, weights, order)


def routed(h, weights, order):
    logits = dot(h, dot(columns_of(weights, QKV + D, PACKED), order).astype(low))
    logits = jnp.where(lanes_of(logits.shape) < EXPERTS, logits, -1e30)
    grown = jnp.exp(logits - jnp.max(logits, axis=-1, keepdims=True))
    return grown / jnp.sum(grown, axis=-1, keepdims=True)


def whole_spec(shape):
    return pl.BlockSpec(shape, lambda *_: (0,) * len(shape))


def remote_params(n, number):
    return pltpu.CompilerParams(
        dimension_semantics=("arbitrary",) * n,
        vmem_limit_bytes=BIG,
        collective_id=number,
        has_side_effects=True,
    )


def device(offset):
    names = ("replica", "part", "expert")
    return tuple(lax.axis_index(name) ^ o for name, o in zip(names, offset))


def near(groups, j):
    return (0, j // groups, j % groups)


def greet(offsets):
    barrier = pltpu.get_barrier_semaphore()
    for offset in offsets:
        pl.semaphore_signal(barrier, inc=1, device_id=device(offset), device_id_type=MESH)
    pl.semaphore_wait(barrier, len(offsets))


def remote(source, target, send, receive, offset):
    return pltpu.make_async_remote_copy(
        src_ref=source,
        dst_ref=target,
        send_sem=send,
        recv_sem=receive,
        device_id=device(offset),
        device_id_type=MESH,
    )


def owners_like(replicas, parts):
    return [(r, p, 0) for r in range(replicas) for p in range(0, parts, 2) if (r, p) != (0, 0)]


def owner(parts, offset=(0, 0, 0)):
    return (lax.axis_index("replica") ^ offset[0]) * parts + (lax.axis_index("part") ^ offset[1])


def in_line(replicas, parts):
    return [o for o in owners_like(replicas, parts) if o[1] % 4 == 0]


CORE = (0, 1, 0)
ROW = (0, 2, 0)
GROUPS = 4
EARLY = 5


def all_owners(replicas, parts):
    return [(r, p, 0) for r in range(replicas) for p in range(parts) if (r, p) != (0, 0)]


def wide_part(ref, at, g):
    width = ref.shape[-1] // GROUPS
    return ref.at[at, ..., pl.ds(g * width, width)]


def narrow_part(ref, at, g):
    width = ref.shape[-1] // (2 * GROUPS)
    return ref.at[at, ..., pl.ds(g * width, width)]


def tall_part(ref, at, g):
    depth = ref.shape[-2] // GROUPS
    return ref.at[at, ..., pl.ds(g * depth, depth), :]


def small_part(ref, at, g):
    depth, width = ref.shape[-2] // GROUPS, ref.shape[-1] // 2
    return ref.at[at, ..., pl.ds(g // 2 * depth, depth), pl.ds(g % 2 * width, width)]


def outward(sizes, part_of, source, target, semaphores, g, slot):
    _, parts, _ = sizes
    own = target.shape[1]
    here = owner(parts)

    def block(p):
        return part_of(source, pl.ds((lax.axis_index("part") ^ p) * own, own), g)

    copies = [
        remote(block(o[1]), part_of(target, here, g), semaphores.at[0, slot, i], semaphores.at[1, slot, i], o)
        for i, o in enumerate(all_owners(*sizes[:2]))
    ]
    last = semaphores.at[0, slot, len(copies)]
    return copies + [pltpu.make_async_copy(block(0), part_of(target, here, g), last)]


def across(sizes, part_of, source, target, semaphores, g, slot):
    replicas, parts, _ = sizes

    def rows(r):
        return pl.ds((lax.axis_index("replica") ^ r) * parts, parts)

    return [
        remote(
            part_of(source, rows(r), g), part_of(target, r - 1, g),
            semaphores.at[0, slot, r], semaphores.at[1, slot, r], (r, 0, 0),
        )
        for r in range(1, replicas)
    ]


def homeward(sizes, part_of, source, target, semaphores, g, slot):
    _, parts, _ = sizes
    here = lax.axis_index("part")
    copies = [
        remote(
            part_of(source, here ^ p, g), part_of(target, here, g),
            semaphores.at[0, slot, p], semaphores.at[1, slot, p], (0, p, 0),
        )
        for p in range(1, parts)
    ]
    last = semaphores.at[0, slot, 0]
    return copies + [pltpu.make_async_copy(part_of(source, here, g), part_of(target, here, g), last)]


def partners(sizes):
    replicas, parts, _ = sizes
    return {(0, p, 0) for p in range(1, parts)} | {(r, 0, 0) for r in range(1, replicas)}


def mine_of(sizes, dw_ref):
    return dw_ref.at[pl.ds(lax.axis_index("replica") * sizes[1], sizes[1])]


def add(sizes, mine, others, rows, columns):
    @pl.loop(0, sizes[1])
    def _(p):
        total = mine[p, :, rows, columns].astype(full)
        for r in range(sizes[0] - 1):
            total = total + others[r, p, :, rows, columns].astype(full)
        mine[p, :, rows, columns] = total.astype(low)


def start(copies):
    for copy in copies:
        copy.start()


def wait(copies):
    for copy in copies:
        copy.wait()


def flow_semaphores(sizes, slots):
    return pltpu.SemaphoreType.DMA((2, slots, sizes[0] * sizes[1]))


def swap_slots(groups, keys_ref, blocks, out_ref, sends, receives, local):
    _, count, own, tokens = keys_ref.shape
    slots = lax.broadcasted_iota(jnp.int32, (CAP, tokens), 0).astype(full)

    def build(s, source):
        copies = []
        for j in [*range(1, count), 0]:
            picks = [(keys_ref[s, j, i : i + 1] == slots).astype(low) for i in range(own)]
            picks = jnp.concatenate(picks, axis=0) if own > 1 else picks[0]
            rows = dot(picks, source).astype(low)
            blocks[j, s] = rows.reshape(own, CAP, D)
            if j:
                copy = remote(
                    blocks.at[j, s], out_ref.at[j, s], sends.at[j, s], receives.at[j, s],
                    near(groups, j),
                )
            else:
                copy = pltpu.make_async_copy(blocks.at[0, s], out_ref.at[0, s], local.at[s])
            copy.start()
            copies.append(copy)
        return copies

    return build


def open_kernel(
    sizes, keys_ref, cotangent_ref, tokens_ref, order_ref, shard_ref, raw_one_ref, raw_two_ref,
    x_out, dy_kept, dy_out, h_out, weights_out, first_ref, second_ref, qkv_out, ctx_out, r_out, h_kept, probs_out, theirs_out,
    master_out,
    x_ref, dy_ref, dy_blocks, h_blocks, weights, other_dy, other_h, qkv, ctx, r, h, probs, theirs,
    raw_one, raw_two, master_one, master_two,
    hop, hops, dy_sends, dy_receives, dy_local, h_sends, h_receives, h_local, early, middle, late, here, keeps,
    raws, flow,
):
    replicas, parts, groups = sizes
    count = keys_ref.shape[1]
    images = x_ref.shape[0]
    mirror = (0, parts // 2, 0)
    owners = owners_like(replicas, parts)
    reading = [
        pltpu.make_async_copy(raw_one_ref, raw_one, raws.at[0]),
        pltpu.make_async_copy(raw_two_ref, raw_two, raws.at[1]),
    ]
    start(reading)
    for padded, rows_ref in ((dy_ref, cotangent_ref), (x_ref, tokens_ref)):
        padded[...] = jnp.zeros_like(padded)
        for i in range(images):
            padded[i, :SEQ] = rows_ref[i * SEQ : (i + 1) * SEQ].astype(full).astype(low)
    greet(
        sorted({near(groups, j) for j in range(1, count)} | {mirror, *all_owners(replicas, parts)})
    )
    swap_dy = remote(dy_ref, other_dy, hop.at[0], hop.at[1], mirror)
    swap_dy.start()
    side = lax.axis_index("expert") % 2
    cut_at = (PACKED // LANES + 1) // 2 * LANES

    def half(ref, which):
        return ref.at[:, : PACKED - cut_at] if which == 0 else ref.at[:, PACKED - cut_at :]

    def halves_of(o, which):
        return half(weights.at[owner(parts, o)], which)

    kept = pltpu.make_async_copy(shard_ref, weights.at[owner(parts)], here)
    kept.start()
    to_core = remote(shard_ref, weights.at[owner(parts)], late.at[0, 0, 0], late.at[1, 0, 0], CORE)
    to_core.start()

    def gathers(which):
        return [
            remote(
                half(shard_ref, which), halves_of((0, 0, 0), which), early.at[0, i], early.at[1, i], o
            )
            for i, o in enumerate(owners)
        ]

    def beside(which):
        return [
            remote(
                halves_of(o, which), halves_of(o, which), middle.at[0, i], middle.at[1, i], (0, 0, 1)
            )
            for i, o in enumerate(owners)
        ]

    def onward(which, slot):
        return [
            remote(
                halves_of(o, which), halves_of(o, which), late.at[0, slot, i + 1], late.at[1, slot, i + 1], CORE
            )
            for i, o in enumerate(owners)
        ]

    for which in range(2):
        @pl.when(side == which)
        def _():
            start(gathers(which))

    one = [outward(sizes, wide_part, master_one, first_ref, flow, g, g) for g in range(GROUPS)]
    two = [
        outward(sizes, small_part, master_two, second_ref, flow, g, GROUPS + g)
        for g in range(EARLY)
    ]
    reading[0].wait()

    @pl.loop(0, raw_one.shape[0])
    def _(e):
        master_one[e] = raw_one[e].astype(low)

    start(one[0])
    build_dy = swap_slots(groups, keys_ref, dy_blocks, dy_out, dy_sends, dy_receives, dy_local)
    build_h = swap_slots(groups, keys_ref, h_blocks, h_out, h_sends, h_receives, h_local)
    copies = build_dy(0, dy_ref[...].reshape(images * ROWS, D))
    start(one[1])
    reading[1].wait()

    @pl.loop(0, raw_two.shape[0])
    def _(e):
        master_two[e] = raw_two[e].astype(low)

    for which in range(2):
        @pl.when(side == which)
        def _():
            for a, b, c in zip(gathers(which), beside(which), onward(which, 0)):
                a.wait_recv()
                b.start()
                c.start()

    swap_dy.wait()
    copies += build_dy(1, other_dy[...].reshape(images * ROWS, D))
    for which in range(2):
        @pl.when(side == which)
        def _():
            for b, c in zip(beside(1 - which), onward(1 - which, 1)):
                b.wait_recv()
                c.start()
            for a, b, c, d in zip(gathers(which), beside(which), onward(which, 0), onward(1 - which, 1)):
                a.wait_send()
                b.wait_send()
                c.wait()
                d.wait()

    to_core.wait()
    kept.wait()

    def hop_of(i):
        return remote(h.at[i], other_h.at[i], hops.at[0, i], hops.at[1, i], mirror)

    @pl.loop(0, images)
    def _(i):
        attend(i, weights, order_ref[...], x_ref, qkv, ctx, r, h, probs)
        hop_of(i).start()

    start(one[2])
    start(one[3])
    keeping = [
        pltpu.make_async_copy(source, target, keeps.at[i])
        for i, (source, target) in enumerate(
            [
                (weights, weights_out), (qkv, qkv_out), (ctx, ctx_out), (r, r_out), (h, h_kept),
                (probs, probs_out), (master_two, master_out), (x_ref, x_out), (dy_ref, dy_kept),
            ]
        )
    ]
    start(keeping)
    copies += build_h(0, h[...].reshape(images * ROWS, D))
    start(two[0])
    start(two[1])

    @pl.loop(0, images)
    def _(i):
        hop_of(i).wait()
        theirs[i] = routed(other_h[i], weights, order_ref[...]).astype(low)

    copies += build_h(1, other_h[...].reshape(images * ROWS, D))
    for group in two[2:]:
        start(group)
    last = pltpu.make_async_copy(theirs, theirs_out, keeps.at[9])
    last.start()
    wait(copies)
    wait(keeping)
    last.wait()
    for group in one + two:
        wait(group)


def forward(keys, cotangent, tokens, order, shard, raw_one, raw_two, sizes, number):
    replicas, parts, groups = sizes
    _, count, own, _ = keys.shape
    images = tokens.shape[0] // SEQ
    owners = replicas * parts
    slots = (count, 2, own, CAP, D)
    rows = lambda width: (images, ROWS, width)
    shapes = [
        (rows(D), low), (rows(D), low), (slots, low), (slots, low), ((owners, *shard.shape), low),
        ((owners, own, *raw_one.shape[1:]), low), ((owners, own, *raw_two.shape[1:]), low),
        (rows(QKV), low), (rows(D), low), (rows(D), full), (rows(D), low), (rows(LANES), full), (rows(LANES), low),
        (raw_two.shape, low),
    ]
    buffers = [
        (rows(D), low), (rows(D), low), (slots, low), (slots, low), ((owners, *shard.shape), low), (rows(D), low),
        (rows(D), low),
        (rows(QKV), low), (rows(D), low), (rows(D), full), (rows(D), low), (rows(LANES), full), (rows(LANES), low),
        (raw_one.shape, full), (raw_two.shape, full), (raw_one.shape, low), (raw_two.shape, low),
    ]
    semaphores = [
        (2,), (2, images), (count, 2), (count, 2), (2,), (count, 2), (count, 2), (2,),
        (2, owners // 2 - 1), (2, owners // 2 - 1), (2, 2, owners // 2), (), (10,), (2,),
        (2, GROUPS + EARLY, owners),
    ]
    inner = pl.BlockSpec(memory_space=pltpu.VMEM)
    outer = pl.BlockSpec(memory_space=pl.ANY)
    return pl.pallas_call(
        partial(open_kernel, sizes),
        in_specs=[inner] * 4 + [outer] * 3,
        out_specs=[outer] * len(shapes),
        out_shape=[jax.ShapeDtypeStruct(*shape) for shape in shapes],
        scratch_shapes=[pltpu.VMEM(*b) for b in buffers]
        + [pltpu.SemaphoreType.DMA(n) for n in semaphores],
        compiler_params=pltpu.CompilerParams(
            vmem_limit_bytes=BIG, collective_id=number, has_side_effects=True
        ),
        cost_estimate=pl.CostEstimate(
            flops=60 * 10**9, bytes_accessed=30 * 10**6, transcendentals=2 * 10**6
        ),
        name="forward",
    )(keys, cotangent, tokens, order, shard, raw_one, raw_two)


def chooser(own, j):
    shape = (LANES, own * CAP)
    expert = lax.broadcasted_iota(jnp.int32, shape, 0)
    slot = lax.broadcasted_iota(jnp.int32, shape, 1)
    return (expert == j * own + slot // CAP).astype(low)


def attend_back(i, weights, held, acc, dqkv, dx_ref):
    w_ref, order_ref = weights
    x_ref, qkv_ref, ctx_ref, r_ref, h_ref, probs_ref, dy_ref, dh_ref, dprobs_ref = held
    qkv_acc, proj_acc, router_acc, norm_acc = acc
    rows = pl.ds(pl.multiple_of(i * ROWS, ROWS), ROWS)
    gain_one, bias_one, gain_two, _ = norm_vectors(w_ref)
    probs, dprobs = probs_ref[i], dprobs_ref[rows]
    dlogits = (probs * (dprobs - jnp.sum(probs * dprobs, axis=-1, keepdims=True))).astype(low)
    router_acc[...] += dot_lt(h_ref[i], dlogits)
    router = dot(columns_of(w_ref, QKV + D, PACKED), order_ref[...]).astype(low)
    dh = dh_ref[rows] + dot_rt(dlogits, router)
    normed, factor = normed_rows(r_ref[i])
    norm_acc[2:3] += jnp.sum(dh * normed, axis=0, keepdims=True)
    norm_acc[3:4] += jnp.sum(dh, axis=0, keepdims=True)
    dr = dy_ref[i].astype(full) + norm_back(normed, factor, gain_two, dh)
    dattended = dr.astype(low)
    proj_acc[...] += dot_lt(ctx_ref[i], dattended)
    dctx = dot_rt(dattended, columns_of(w_ref, QKV, QKV + D)).astype(low)
    for pair in range(HEADS // 2):
        at = pair * LANES
        query = halves(qkv_ref[i, :, at : at + LANES])
        key = qkv_ref[i, :, D + at : D + at + LANES]
        keys = halves(key)
        value = qkv_ref[i, :, 2 * D + at : 2 * D + at + LANES]
        dhead = halves(dctx[:, at : at + LANES])
        dq = dk = dv = None
        for e in range(2):
            p = head_probs(query[e], key)
            dp = dot_rt(dhead[e], value)
            ds = (p * (dp - jnp.sum(p * dp, axis=-1, keepdims=True))).astype(low)
            terms = dot(ds, keys[e]), dot_lt(ds, query[e]), dot_lt(p.astype(low), dhead[e])
            dq, dk, dv = terms if dq is None else (dq + terms[0], dk + terms[1], dv + terms[2])
        dqkv[:, at : at + LANES] = (dq * HEAD**-0.5).astype(low)
        dqkv[:, D + at : D + at + LANES] = (dk * HEAD**-0.5).astype(low)
        dqkv[:, 2 * D + at : 2 * D + at + LANES] = dv.astype(low)
    normed, factor = normed_rows(x_ref[i].astype(full))
    attn_in = (normed * gain_one + bias_one).astype(low)
    qkv_acc[...] += dot_lt(attn_in, dqkv[...])
    da = dot_rt(dqkv[...], columns_of(w_ref, 0, QKV))
    norm_acc[0:1] += jnp.sum(da * normed, axis=0, keepdims=True)
    norm_acc[1:2] += jnp.sum(da, axis=0, keepdims=True)
    dx_ref[i] = dr + norm_back(normed, factor, gain_one, da)


def close_kernel(
    sizes, keys_ref, back_ref, w_ref, order_ref, x_ref, qkv_ref, ctx_ref, r_ref, h_ref, probs_ref, dy_ref,
    theirs_ref, y_ref, dw_one_ref,
    dx_ref, out_ref, total_ref, one_ref,
    xs, qkvs, ctxs, rs, hs, ps, dys, their_probs, ys, dh, dprobs, sent, got, sent_gates, got_gates, sent_two, got_two,
    mine_one, others_one,
    dqkv, qkv_acc, proj_acc, router_acc, norm_acc, grads, kept, first, second, along, third,
    loads, y_sends, y_receives, hops, gate_hops, hops_two, flow, home_one,
    core_sems, row_sems, owner_sems, expert_sems,
):
    replicas, parts, groups = sizes
    count, _, own, _, _ = y_ref.shape
    images = x_ref.shape[0]
    width = own * CAP
    half = count * own
    mirror = (0, parts // 2, 0)
    owners = owners_like(replicas, parts)
    sideways = [(0, 0, g) for g in range(1, groups)]
    peers = {near(groups, j) for j in range(1, count)} | {mirror, *sideways, *owners}
    greet(sorted(peers | partners(sizes)))

    pairs_of = [
        (r_ref, rs), (theirs_ref, their_probs), (x_ref, xs), (qkv_ref, qkvs), (ctx_ref, ctxs),
        (h_ref, hs), (probs_ref, ps), (dy_ref, dys),
        (mine_of(sizes, dw_one_ref), mine_one), (y_ref.at[0], ys.at[0]),
    ]
    loading = [
        pltpu.make_async_copy(source, target, loads.at[i])
        for i, (source, target) in enumerate(pairs_of)
    ]
    swaps = [
        [
            remote(y_ref.at[j, s], ys.at[j, s], y_sends.at[j, s], y_receives.at[j, s], near(groups, j))
            for j in range(1, count)
        ]
        for s in range(2)
    ]
    eighths = [
        across(sizes, narrow_part, dw_one_ref, others_one, flow, g, g) for g in range(2 * GROUPS)
    ]
    start(swaps[1])
    start(swaps[0])
    for g in range(GROUPS):
        start(eighths[g])
    start(loading)

    def rows_of(i):
        return pl.ds(pl.multiple_of(i * ROWS, ROWS), ROWS)

    def hop(i):
        rows = rows_of(i)
        return [
            remote(sent.at[rows], got.at[rows], hops.at[0, i], hops.at[1, i], mirror),
            remote(sent_gates.at[i], got_gates.at[i], gate_hops.at[0, i], gate_hops.at[1, i], mirror),
        ]

    near_lanes = lanes_of((2 * half, LANES))
    near_rows = lax.broadcasted_iota(jnp.int32, (2 * half, LANES), 0)

    def hop_two(i):
        rows = rows_of(i)
        return remote(sent_two.at[rows], got_two.at[rows], hops_two.at[0, i], hops_two.at[1, i], mirror)

    def gathered(s, rows):
        slot = (lanes_of((ROWS, width)) % CAP).astype(full)
        lane = lanes_of((ROWS, LANES))
        keys = keys_ref[s, rows]
        total = jnp.zeros((ROWS, D), full)
        change = jnp.zeros((ROWS, LANES), full)
        for j in range(count):
            here = dot(keys, chooser(own, j)) == slot
            total = total + dot(here.astype(low), back_ref[j, s, :, :CAP].reshape(width, D))
            dgate = back_ref[j, s, :, CAP : CAP + 1].astype(full)
            dgate = dgate[:, :, :CAP] + dgate[:, :, CAP : 2 * CAP]
            for e in range(own):
                agreed = jnp.where(here[:, e * CAP : (e + 1) * CAP], dgate[e], 0.0)
                column = jnp.sum(agreed, axis=-1, keepdims=True)
                change = jnp.where(lane == j * own + e, column, change)
        return total, change

    def weighted(s, rows, probs):
        slot = (lanes_of((ROWS, width)) % CAP).astype(full)
        keys = keys_ref[s, rows]
        total = jnp.zeros((ROWS, D), full)
        for j in range(count):
            spread = chooser(own, j)
            gate = jnp.where(dot(keys, spread) == slot, dot(probs, spread), 0.0)
            total = total + dot(gate.astype(low), ys[j, s].reshape(width, D))
        return total

    @pl.loop(0, images)
    def _(i):
        rows = rows_of(i)
        total, change = gathered(1, rows)
        sent[rows] = total.astype(low)
        high = change.astype(low)
        rest = pltpu.roll(change - high.astype(full), half, 1)
        both = (high.astype(full) + rest).astype(low)
        sent_gates[i] = dot_rt((near_lanes == near_rows).astype(low), both).astype(low)
        start(hop(i))

    for g in range(GROUPS, 2 * GROUPS):
        start(eighths[g])

    @pl.loop(0, images)
    def _(i):
        rows = rows_of(i)
        dh[rows], dprobs[rows] = gathered(0, rows)

    wait(loading)
    wait(swaps[1])

    @pl.loop(0, images)
    def _(i):
        rows = rows_of(i)
        sent_two[rows] = weighted(1, rows, their_probs[i]).astype(low)
        hop_two(i).start()

    @pl.loop(0, images)
    def _(i):
        rows = rows_of(i)
        wait(hop(i))
        dh[rows] += got[rows].astype(full)
        place = (near_lanes == half + near_rows % half).astype(low)
        dprobs[rows] += dot_lt(got_gates[i], place)

    each = mine_one.shape[-1] // GROUPS
    homes = []

    def send_home(g):
        wait(eighths[2 * g])
        wait(eighths[2 * g + 1])
        add(sizes, mine_one, others_one, slice(None), slice(g * each, (g + 1) * each))
        copies = homeward(sizes, wide_part, mine_one, one_ref, home_one, g, g)
        start(copies)
        homes.extend(copies)

    send_home(0)
    send_home(1)
    for ref in (qkv_acc, proj_acc, router_acc, norm_acc):
        ref[...] = jnp.zeros_like(ref)

    @pl.loop(0, images)
    def _(i):
        attend_back(
            i, (w_ref, order_ref), (xs, qkvs, ctxs, rs, hs, ps, dys, dh, dprobs),
            (qkv_acc, proj_acc, router_acc, norm_acc), dqkv, dx_ref,
        )

    columns = norm_acc[...].T
    shifted = pltpu.roll(columns, EXPERTS, 1)
    tile = jnp.where(lanes_of(shifted.shape) < EXPERTS, router_acc[...], shifted)
    router_acc[...] = dot_rt(tile.astype(low), order_ref[...])
    depth = grads.shape[1]
    core = lax.axis_index("part") % 2
    blocks = replicas * parts // 2

    @pl.loop(0, 2 * blocks)
    def _(o):
        rows = pl.ds(pl.multiple_of(o * depth, depth), depth)
        grads[o, :, :QKV] = qkv_acc[rows].astype(low)
        grads[o, :, QKV : QKV + D] = proj_acc[rows].astype(low)
        grads[o, :, QKV + D :] = router_acc[rows].astype(low)

    to_core = [
        remote(grads.at[2 * i + 1 - core], first.at[i], core_sems.at[0, i], core_sems.at[1, i], CORE)
        for i in range(blocks)
    ]
    start(to_core)
    for i in range(blocks):
        to_core[i].wait()
        kept[i] = (grads[2 * i + core].astype(full) + first[i].astype(full)).astype(low)
    side = lax.axis_index("part") // 2 % 2
    to_row = [
        remote(kept.at[2 * i + 1 - side], second.at[i], row_sems.at[0, i], row_sems.at[1, i], ROW)
        for i in range(blocks // 2)
    ]
    start(to_row)
    for i in range(blocks // 2):
        to_row[i].wait()
        at = 2 * i + side
        kept[at] = (kept[at].astype(full) + second[i].astype(full)).astype(low)
    to_owner = [
        remote(kept.at[owner(parts, o) // 2], along.at[i], owner_sems.at[0, i], owner_sems.at[1, i], o)
        for i, o in enumerate(in_line(replicas, parts))
    ]
    start(to_owner)

    for g in range(2, GROUPS):
        send_home(g)
    wait(swaps[0])

    @pl.loop(0, images)
    def _(i):
        rows = rows_of(i)
        total = rs[i] + weighted(0, rows, ps[i].astype(low))
        hop_two(i).wait()
        out_ref[rows] = (total + got_two[rows].astype(full)).astype(low)

    total = kept[owner(parts) // 2].astype(full)
    for i, copy in enumerate(to_owner):
        copy.wait()
        total = total + along[i].astype(full)
    me = lax.axis_index("expert")
    third[me] = total.astype(low)
    to_others = [
        remote(third.at[me], third.at[me], expert_sems.at[0, i], expert_sems.at[1, i], o)
        for i, o in enumerate(sideways)
    ]
    start(to_others)
    wait(to_others)
    total = third[0].astype(full)
    for g in range(1, groups):
        total = total + third[g].astype(full)
    total_ref[...] = total
    wait(homes)


def close(keys, back, weights, order, x, qkv, ctx, r, h, probs, dy, theirs, y, dw_one, sizes, number):
    replicas, parts, groups = sizes
    images = x.shape[0]
    tokens = images * ROWS
    count = y.shape[0]
    owners = replicas * parts
    shard = weights.shape[1:]
    one = (parts, *dw_one.shape[1:])
    line = len(in_line(replicas, parts))
    inner = pl.BlockSpec(memory_space=pltpu.VMEM)
    outer = pl.BlockSpec(memory_space=pl.ANY)
    buffers = [
        (x.shape, low), (qkv.shape, low), (ctx.shape, low), (r.shape, full), (x.shape, low),
        (probs.shape, full), (dy.shape, low), (theirs.shape, low), (y.shape, low),
        ((tokens, D), full), ((tokens, LANES), full),
        ((tokens, D), low), ((tokens, D), low), ((images, EXPERTS, ROWS), low), ((images, EXPERTS, ROWS), low),
        ((tokens, D), low), ((tokens, D), low),
        (one, low), ((replicas - 1, *one), low),
        ((ROWS, QKV), low), ((D, QKV), full), ((D, D), full), ((D, LANES), full), ((LANES, D), full),
        ((owners, *shard), low), ((owners // 2, *shard), low), ((owners // 2, *shard), low),
        ((owners // 4, *shard), low), ((line, *shard), low), ((groups, *shard), low),
    ]
    semaphores = [
        (10,), (count, 2), (count, 2), (2, images), (2, images), (2, images), (2, 2 * GROUPS, replicas),
        (2, GROUPS, parts), (2, owners // 2), (2, owners // 4), (2, line), (2, groups - 1),
    ]
    arrays = (
        keys, back, weights, order, x, qkv, ctx, r, h, probs, dy, theirs, y, dw_one,
    )
    return pl.pallas_call(
        partial(close_kernel, sizes),
        in_specs=[inner] * 4 + [outer] * 10,
        out_specs=[inner] * 3 + [outer],
        out_shape=[
            jax.ShapeDtypeStruct((images, ROWS, D), full),
            jax.ShapeDtypeStruct((tokens, D), low),
            jax.ShapeDtypeStruct(shard, full),
            jax.ShapeDtypeStruct(one, low),
        ],
        scratch_shapes=[pltpu.VMEM(*b) for b in buffers]
        + [pltpu.SemaphoreType.DMA(n) for n in semaphores],
        compiler_params=pltpu.CompilerParams(
            vmem_limit_bytes=BIG, collective_id=number, has_side_effects=True
        ),
        cost_estimate=pl.CostEstimate(
            flops=60 * 10**9, bytes_accessed=30 * 10**6, transcendentals=2 * 10**6
        ),
        name="close",
    )(*arrays)


GELU = 0.7978845608028654
CUBE = 0.044715


def gelu_pair(u):
    square = u * u
    bent = jnp.tanh(u * (GELU * CUBE * square + GELU))
    half = 0.5 * bent + 0.5
    value = u * half
    return value, half + value * (1.0 - bent) * (3.0 * GELU * CUBE * square + GELU)


def first_kernel(
    sizes, h_ref, dy_ref, w_ref, wr_ref, sel_ref, master_ref, _, g_ref, slope_ref, dw_ref, second_ref,
    gates, dye_t, flow,
):
    sources = h_ref.shape[0]
    tile = w_ref.shape[3]
    at = pl.program_id(0) * pl.num_programs(1) + pl.program_id(1)

    def moved(g):
        return outward(sizes, small_part, master_ref, second_ref, flow, g, g - EARLY)

    @pl.when(at == 0)
    def _():
        greet(all_owners(*sizes[:2]))
        for g in range(EARLY, 2 * GROUPS):
            start(moved(g))

    @pl.when(pl.program_id(1) == 0)
    def _():
        for k in range(sources):
            rows = slice(k * CAP, (k + 1) * CAP)
            logits = dot(h_ref[k, 0], wr_ref[...])
            logits = jnp.where(lanes_of(logits.shape) < EXPERTS, logits, -1e30)
            grown = jnp.exp(logits - jnp.max(logits, axis=-1, keepdims=True))
            mine = jnp.sum(grown * sel_ref[0], axis=-1, keepdims=True)
            gate = mine / jnp.sum(grown, axis=-1, keepdims=True)
            gates[rows] = jnp.broadcast_to(gate, (CAP, LANES))
            dye_t[:, rows] = (dy_ref[k, 0].astype(full) * gate).T.astype(low)

    w = w_ref[:, 0].reshape(D, tile)
    for k in range(0, sources, 2):
        rows = slice(k * CAP, (k + 2) * CAP)
        value, slope = gelu_pair(dot(h_ref[k : k + 2, 0].reshape(2 * CAP, D), w))
        g_ref[0, rows] = value.astype(low)
        slope_ref[0, rows] = (slope * gates[rows, :1]).astype(low)
    grad = dot(dye_t[...], g_ref[0]).T
    dw_ref[:, 0] = grad.astype(low).reshape(dw_ref.shape[0], dw_ref.shape[2], D)

    @pl.when(at == pl.num_programs(0) * pl.num_programs(1) - 1)
    def _():
        for g in range(EARLY, 2 * GROUPS):
            wait(moved(g))


def slot_spec(sources):
    return pl.BlockSpec((sources, 1, CAP, D), lambda e, f: (0, e, 0, 0))


def expert_first(h, dy, w_in, w_router, select, master, second, sizes, tile, number):
    sources = h.shape[0]
    owners, own, depth, hidden = w_in.shape
    rows = sources * CAP
    per = hidden // owners
    hidden_spec = pl.BlockSpec((1, rows, tile), lambda e, f: (e, 0, f))
    return pl.pallas_call(
        partial(first_kernel, sizes),
        grid=(own, hidden // tile),
        in_specs=[
            slot_spec(sources),
            slot_spec(sources),
            pl.BlockSpec((owners, 1, depth, tile), lambda e, f: (0, e, 0, f)),
            whole_spec(w_router.shape),
            pl.BlockSpec((1, 1, LANES), lambda e, f: (e, 0, 0)),
            pl.BlockSpec(memory_space=pl.ANY),
            pl.BlockSpec(memory_space=pl.ANY),
        ],
        out_specs=[
            hidden_spec,
            hidden_spec,
            pl.BlockSpec((tile // per, 1, per, D), lambda e, f: (f, e, 0, 0)),
            pl.BlockSpec(memory_space=pl.ANY),
        ],
        out_shape=[
            jax.ShapeDtypeStruct((own, rows, hidden), low),
            jax.ShapeDtypeStruct((own, rows, hidden), low),
            jax.ShapeDtypeStruct((owners, own, per, D), low),
            jax.ShapeDtypeStruct(second.shape, low),
        ],
        input_output_aliases={6: 3},
        scratch_shapes=[
            pltpu.VMEM((rows, LANES), full), pltpu.VMEM((D, rows), low), flow_semaphores(sizes, 2 * GROUPS - EARLY),
        ],
        compiler_params=pltpu.CompilerParams(
            dimension_semantics=("arbitrary",) * 2,
            vmem_limit_bytes=BIG,
            collective_id=number,
            has_side_effects=True,
        ),
        cost_estimate=pl.CostEstimate(
            flops=4 * own * rows * D * hidden,
            bytes_accessed=50 * 10**6,
            transcendentals=own * rows * hidden,
        ),
        name="expert_first",
    )(h, dy, w_in, w_router, select, master, second)


def rest_kernel(
    sizes, own, steps, dy_ref, h_ref, g_ref, slope_ref, w_in_ref, w_out_ref, dw_two_ref,
    back_ref, dw_ref, y_ref, two_ref, du, acc, dgates, dgate_rows, h_t, staged, mine_two, others_two,
    sends, receives, local, flow, home, load,
):
    replicas, parts, groups = sizes

    def moved(g):
        return across(sizes, tall_part, dw_two_ref, others_two, flow, g, g)

    def homes(g):
        return homeward(sizes, tall_part, mine_two, two_ref, home, g, g)

    def send_home(g):
        wait(moved(g))
        depth = mine_two.shape[2] // GROUPS
        add(sizes, mine_two, others_two, slice(g * depth, (g + 1) * depth), slice(None))
        start(homes(g))

    loading = pltpu.make_async_copy(mine_of(sizes, dw_two_ref), mine_two, load)

    sources = dy_ref.shape[0]
    tile = slope_ref.shape[2]
    at = pl.program_id(0)
    phase, expert, step = at // (own * steps), at // steps % own, at % steps
    w_in = w_in_ref[:, 0].reshape(D, tile)
    w_out = w_out_ref[:, 0].reshape(tile, D)
    chunk = 2 * CAP

    def copy(k, e):
        return pltpu.make_async_remote_copy(
            src_ref=staged.at[k, e],
            dst_ref=back_ref.at[k, e],
            send_sem=sends.at[k, e],
            recv_sem=receives.at[k, e],
            device_id=device(near(groups, k // 2)),
            device_id_type=MESH,
        )

    def mine(k, e):
        return pltpu.make_async_copy(staged.at[k, e], back_ref.at[k, e], local.at[k, e])

    @pl.when(at == 0)
    def _():
        greet(sorted({near(groups, j) for j in range(1, sources // 2)} | partners(sizes)))
        loading.start()
        start(moved(0))
        start(moved(1))

    @pl.when((phase != 1) & (step == 0))
    def _():
        acc[...] = jnp.zeros_like(acc)

    @pl.when(phase == 0)
    def _():
        @pl.when(step == 0)
        def _():
            dgates[...] = jnp.zeros_like(dgates)

        for k in range(0, sources, 2):
            rows = slice(k * CAP, (k + 2) * CAP)
            dg = dot_rt(dy_ref[k : k + 2, 0].reshape(chunk, D), w_out)
            change = (dg * slope_ref[0, rows].astype(full)).astype(low)
            du[expert * steps + step, rows] = change
            acc[rows] += dot_rt(change, w_in)
            agreed = dg * g_ref[0, rows].astype(full)
            dgates[rows] += sum(agreed[:, i : i + LANES] for i in range(0, tile, LANES))

        @pl.when(step == steps - 1)
        def _():
            sums = dgates[...]
            high = sums.astype(low)
            rest = (sums - high.astype(full)).astype(low)
            ones = jnp.ones((16, LANES), low)
            dgate_rows[...] = dot_rt(ones, high) + dot_rt(ones, rest)
            for k in range(sources):
                rows = slice(k * CAP, (k + 1) * CAP)
                staged[k, expert, :CAP] = acc[rows].astype(low)
                row = dgate_rows[:, rows]
                high = row.astype(low)
                staged[k, expert, CAP:, :CAP] = high
                staged[k, expert, CAP:, CAP : 2 * CAP] = (row - high.astype(full)).astype(low)
                staged[k, expert, CAP:, 2 * CAP :] = jnp.zeros((16, D - 2 * CAP), low)

        for e in range(own):
            @pl.when((step == steps - 1) & (expert == e))
            def _():
                for k in range(2, sources):
                    copy(k, e).start()
                mine(0, e).start()
                mine(1, e).start()

    @pl.when(at == own * steps)
    def _():
        loading.wait()
        send_home(0)
        start(moved(2))

    @pl.when(at == 2 * own * steps)
    def _():
        send_home(1)
        start(moved(3))

    @pl.when(phase == 1)
    def _():
        @pl.when(step == 0)
        def _():
            for k in range(sources):
                h_t[:, k * CAP : (k + 1) * CAP] = h_ref[k, 0].T

        grad = dot(h_t[...], du[expert * steps + step]).astype(low)
        dw_ref[:, 0] = grad.reshape(dw_ref.shape[0], dw_ref.shape[2], tile)

    @pl.when(phase == 2)
    def _():
        for k in range(0, sources, 2):
            rows = slice(k * CAP, (k + 2) * CAP)
            acc[rows] += dot(g_ref[0, rows], w_out)

        @pl.when(step == steps - 1)
        def _():
            y_ref[:, 0] = acc[...].astype(low).reshape(sources, CAP, D)

    @pl.when(at == 3 * own * steps - 1)
    def _():
        send_home(2)
        send_home(3)
        for e in range(own):
            for k in range(2, sources):
                copy(k, e).wait()
            mine(0, e).wait()
            mine(1, e).wait()
        for g in range(GROUPS):
            wait(homes(g))


def expert_rest(dy, h, g, slope, w_in, w_out, dw_two, tile, sizes, number):
    sources, own, _, _ = dy.shape
    owners, _, depth, hidden = w_in.shape
    rows = sources * CAP
    per = hidden // owners
    steps = hidden // tile
    last = own * steps - 1

    def during(phases):
        def find(at):
            if 0 in phases and 2 in phases:
                inside = jnp.where(at // (last + 1) == 1, last, at % (last + 1))
            else:
                inside = jnp.clip(at - phases[0] * (last + 1), 0, last)
            return inside // steps, inside % steps

        return find

    def spec(shape, phases, index, buffers=2):
        return pl.BlockSpec(
            shape, lambda at: index(*during(phases)(at)), pipeline_mode=pl.Buffered(buffers)
        )

    token, hidden_at = (sources, 1, CAP, D), (1, rows, tile)
    whole_expert = lambda e, f: (0, e, 0, 0)
    in_tile = lambda e, f: (0, e, 0, f)
    return pl.pallas_call(
        partial(rest_kernel, sizes, own, steps),
        grid=(3 * own * steps,),
        in_specs=[
            spec(token, (0,), whole_expert, 1),
            spec(token, (1,), whole_expert, 1),
            spec(hidden_at, (0, 2), lambda e, f: (e, 0, f)),
            spec(hidden_at, (0,), lambda e, f: (e, 0, f)),
            spec((owners, 1, depth, tile), (0,), in_tile),
            spec((tile // per, 1, per, D), (0, 2), lambda e, f: (f, e, 0, 0)),
            pl.BlockSpec(memory_space=pl.ANY),
        ],
        out_specs=[
            pl.BlockSpec(memory_space=pl.ANY),
            spec((owners, 1, depth, tile), (1,), in_tile),
            spec(token, (2,), whole_expert, 1),
            pl.BlockSpec(memory_space=pl.ANY),
        ],
        out_shape=[
            jax.ShapeDtypeStruct((sources, own, CAP + 16, D), low),
            jax.ShapeDtypeStruct(w_in.shape, low),
            jax.ShapeDtypeStruct(dy.shape, low),
            jax.ShapeDtypeStruct((sizes[1], *dw_two.shape[1:]), low),
        ],
        scratch_shapes=[
            pltpu.VMEM((own * steps, rows, tile), low),
            pltpu.VMEM((rows, D), full),
            pltpu.VMEM((rows, LANES), full),
            pltpu.VMEM((16, rows), full),
            pltpu.VMEM((D, rows), low),
            pltpu.VMEM((sources, own, CAP + 16, D), low),
            pltpu.VMEM((sizes[1], *dw_two.shape[1:]), low),
            pltpu.VMEM((sizes[0] - 1, sizes[1], *dw_two.shape[1:]), low),
            pltpu.SemaphoreType.DMA((sources, own)),
            pltpu.SemaphoreType.DMA((sources, own)),
            pltpu.SemaphoreType.DMA((2, own)),
            pltpu.SemaphoreType.DMA((2, GROUPS, sizes[0])),
            pltpu.SemaphoreType.DMA((2, GROUPS, sizes[1])),
            pltpu.SemaphoreType.DMA,
        ],
        compiler_params=pltpu.CompilerParams(
            dimension_semantics=("arbitrary",),
            vmem_limit_bytes=BIG,
            collective_id=number,
            has_side_effects=True,
        ),
        cost_estimate=pl.CostEstimate(
            flops=8 * own * rows * D * hidden, bytes_accessed=60 * 10**6, transcendentals=0
        ),
        name="expert_rest",
    )(dy, h, g, slope, w_in, w_out, dw_two)


def finish_kernel(out_ref, dx_ref, dense_ref, one_ref, two_ref, output, input_grad, qkv, proj, one, two):
    one[...] = one_ref[...].astype(full)
    two[...] = two_ref[...].astype(full)
    images = dx_ref.shape[0]

    @pl.when(pl.program_id(0) == 0)
    def _():
        qkv[...] = dense_ref[:, :QKV]
        proj[...] = dense_ref[:, QKV : QKV + D]
        for i in range(images):
            input_grad[i * SEQ : (i + 1) * SEQ] = dx_ref[i, :SEQ]
            rows = out_ref[i * ROWS : i * ROWS + SEQ].astype(full)
            output[i * SEQ : (i + 1) * SEQ] = rows.astype(low)


def finish(output, dx, dense, one, two):
    images = dx.shape[0]
    tokens = (images * SEQ, D)
    steps = one.shape[0]
    widths = [(dense.shape[0], QKV), (dense.shape[0], D)]
    block = lambda a: pl.BlockSpec((1, *a.shape[1:]), lambda i: (i,) + (0,) * (a.ndim - 1))
    return pl.pallas_call(
        finish_kernel,
        grid=(steps,),
        in_specs=[whole_spec(a.shape) for a in (output, dx, dense)] + [block(one), block(two)],
        out_specs=[whole_spec(a) for a in (tokens, tokens, *widths)] + [block(one), block(two)],
        out_shape=[
            jax.ShapeDtypeStruct(tokens, low),
            jax.ShapeDtypeStruct(tokens, full),
            *(jax.ShapeDtypeStruct(a, full) for a in widths),
            jax.ShapeDtypeStruct(one.shape, full),
            jax.ShapeDtypeStruct(two.shape, full),
        ],
        compiler_params=pltpu.CompilerParams(
            dimension_semantics=("arbitrary",), vmem_limit_bytes=BIG
        ),
        cost_estimate=pl.CostEstimate(flops=0, bytes_accessed=19 * 10**6, transcendentals=0),
        name="finish",
    )(output, dx, dense, one, two)


ALL = ("replica", "part")


def body(
    tokens,
    choices,
    ln1_gain,
    ln1_bias,
    w_qkv,
    w_proj,
    ln2_gain,
    ln2_bias,
    w_router,
    w_expert_in,
    w_expert_out,
    cotangent,
):
    replicas, parts, groups = (lax.axis_size(name) for name in ("replica", "part", "expert"))
    owners = replicas * parts
    peers = parts * groups
    own = EXPERTS // peers
    images = tokens.shape[0] // SEQ
    count = images * ROWS
    tile = 512 * 16 // peers

    small_rows = w_router.shape[0]
    placed_router = (
        w_router.reshape(small_rows, groups, parts, own).transpose(0, 2, 1, 3).reshape(small_rows, EXPERTS)
    )
    vectors = jnp.concatenate([ln1_gain, ln1_bias, ln2_gain, ln2_bias]).reshape(4, small_rows).T
    packed = jnp.concatenate(
        [w_qkv, w_proj, placed_router, vectors, jnp.zeros((small_rows, LANES - EXPERTS - 4), full)],
        axis=1,
    ).astype(low)
    me = lax.axis_index("part") * groups + lax.axis_index("expert")
    sizes = (replicas, parts, groups)

    half = parts // 2
    flips = [(i, i ^ half) for i in range(parts)]
    picks = jnp.stack([choices, lax.ppermute(choices, "part", flips)]).reshape(2 * images, SEQ, 2)
    picks = jnp.pad(picks, ((0, 0), (0, ROWS - SEQ), (0, 0)), constant_values=-1)
    picks = picks.reshape(2, count, 2)
    column = jnp.arange(EXPERTS)
    place = (me ^ (column // own)) * own + column % own
    expert = (place // own % groups) * (parts * own) + place // (groups * own) * own + place % own
    lane = jnp.arange(LANES)
    order = jnp.where(lane < EXPERTS, jnp.pad(place, (0, LANES - EXPERTS)), lane)
    order = (lane[:, None] == order[None, :]).astype(low)
    expert = expert[: EXPERTS // 2]
    named = (picks[:, :, :, None] == expert).any(axis=2)
    row = jnp.arange(count)
    earlier = (row[None, :] < row[:, None]).astype(low)
    slots = jnp.einsum("tu,sue->ste", earlier, named.astype(low), preferred_element_type=full)
    keys = jnp.where(named, slots, -1.0)
    key_rows = keys.transpose(0, 2, 1).reshape(2, peers // 2, own, count)
    key_columns = jnp.pad(
        keys, ((0, 0), (0, 0), (0, LANES - EXPERTS // 2)), constant_values=-1
    ).astype(low)

    (
        x, dy, dy_slots, h_slots, weights, first_weight, second_weight, qkv, ctx, r, h, probs, theirs, second_master,
    ) = forward(key_rows, cotangent, tokens, order, packed, w_expert_in, w_expert_out, sizes, 0)
    dy_slots = dy_slots.reshape(peers, own, CAP, D)
    h_slots = h_slots.reshape(peers, own, CAP, D)
    select = ((me * own + jnp.arange(own))[:, None, None] == lane[None, None, :]).astype(full)
    g, slope, dw_second, second_weight = expert_first(
        h_slots, dy_slots, first_weight, weights[:, :, QKV + D :].reshape(D, LANES), select, second_master, second_weight,
        sizes, tile, 5,
    )
    back, dw_first, y, second_grad = expert_rest(
        dy_slots, h_slots, g, slope, first_weight, second_weight, dw_second, tile, sizes, 2
    )
    back = back.reshape(peers // 2, 2, own, CAP + 16, D)
    y = y.reshape(peers // 2, 2, own, CAP, D)
    dx, output, grads, first_grad = close(
        key_columns, back, weights, order, x, qkv, ctx, r, h, probs, dy, theirs, y,
        dw_first, sizes, 3,
    )
    output, input_grad, qkv_grad, proj_grad, expert_in_grad, expert_out_grad = finish(
        output, dx, grads, first_grad, second_grad
    )
    router_grad = (
        grads[:, QKV + D : QKV + D + EXPERTS]
        .reshape(small_rows, parts, groups, own)
        .transpose(0, 2, 1, 3)
        .reshape(small_rows, EXPERTS)
    )
    norms = [grads[:, QKV + D + EXPERTS + i] for i in range(4)]

    return (
        output,
        input_grad,
        norms[0],
        norms[1],
        qkv_grad,
        proj_grad,
        norms[2],
        norms[3],
        router_grad,
        expert_in_grad.reshape(w_expert_in.shape),
        expert_out_grad.reshape(w_expert_out.shape),
    )


def solution(mesh):
    dp, groups = mesh.shape["dp"], mesh.shape["expert"]
    parts = min(EXPERTS // groups, dp // 2)
    mesh = Mesh(mesh.devices.reshape(dp // parts, parts, groups), ("replica", "part", "expert"))
    rows = P(("replica", "part", "expert"), None)
    vector, matrix = P(ALL), P(ALL, None)
    experts = P("expert", ALL, None)
    return jax.shard_map(
        body,
        mesh=mesh,
        in_specs=(
            rows, rows, vector, vector, matrix, matrix, vector, vector, matrix, experts, experts, rows,
        ),
        out_specs=(
            rows, rows, vector, vector, matrix, matrix, vector, vector, matrix, experts, experts,
        ),
        check_vma=False,
    )
```

```python
from functools import partial

import jax
import jax.numpy as jnp
from jax import lax
from jax.experimental import pallas as pl
from jax.experimental.pallas import tpu as pltpu
from jax.sharding import Mesh
from jax.sharding import PartitionSpec as P

D = 512
HEADS = 8
EXPERTS = 32
SEQ = 197
CAP = 128
ROWS = 208
HEAD = D // HEADS
LANES = 128
QKV = 3 * D
PACKED = QKV + D + LANES
epsilon = 1e-06
low = jnp.bfloat16
full = jnp.float32
MESH = pl.DeviceIdType.MESH
BIG = 63 * 1024 * 1024


def dot(left, right):
    return jnp.dot(left, right, preferred_element_type=full)


def dot_rt(left, right):
    return lax.dot_general(left, right, (((1,), (1,)), ((), ())), preferred_element_type=full)


def dot_lt(left, right):
    return lax.dot_general(left, right, (((0,), (0,)), ((), ())), preferred_element_type=full)


def lanes_of(shape):
    return lax.broadcasted_iota(jnp.int32, shape, len(shape) - 1)


def normed_rows(values):
    center = values - jnp.mean(values, axis=-1, keepdims=True)
    factor = lax.rsqrt(jnp.mean(center * center, axis=-1, keepdims=True) + epsilon)
    return center * factor, factor


def norm_back(normed, factor, gain_vec, upstream):
    scaled = upstream * gain_vec
    return factor * (
        scaled
        - jnp.mean(scaled, axis=-1, keepdims=True)
        - normed * jnp.mean(scaled * normed, axis=-1, keepdims=True)
    )


def columns_of(weights_ref, start_at, end):
    return weights_ref[:, :, start_at:end].reshape(D, end - start_at)


def norm_vectors(weights_ref):
    rows = columns_of(weights_ref, QKV + D, PACKED).astype(full).T
    return [rows[EXPERTS + i : EXPERTS + i + 1] for i in range(4)]


def halves(pair):
    first = lanes_of(pair.shape) < HEAD
    zero = jnp.zeros_like(pair)
    return jnp.where(first, pair, zero), jnp.where(first, zero, pair)


def head_probs(query, key_pair):
    scores = dot_rt(query, key_pair) * (HEAD**-0.5)
    scores = jnp.where(lanes_of(scores.shape) < SEQ, scores, -1e30)
    grown = jnp.exp(scores - jnp.max(scores, axis=-1, keepdims=True))
    return grown / jnp.sum(grown, axis=-1, keepdims=True)


def attend(i, weights, order, x_ref, qkv_ref, ctx_ref, r_ref, h_ref, probs_ref):
    gain_one, bias_one, gain_two, bias_two = norm_vectors(weights)
    x = x_ref[i].astype(full)
    normed, _ = normed_rows(x)
    attn_in = (normed * gain_one + bias_one).astype(low)
    qkv_ref[i] = dot(attn_in, columns_of(weights, 0, QKV)).astype(low)
    for pair in range(HEADS // 2):
        at = pair * LANES
        query = halves(qkv_ref[i, :, at : at + LANES])
        key = qkv_ref[i, :, D + at : D + at + LANES]
        value = halves(qkv_ref[i, :, 2 * D + at : 2 * D + at + LANES])
        total = None
        for e in range(2):
            part = dot(head_probs(query[e], key).astype(low), value[e])
            total = part if total is None else total + part
        ctx_ref[i, :, at : at + LANES] = total.astype(low)
    r = x + dot(ctx_ref[i], columns_of(weights, QKV, QKV + D))
    r_ref[i] = r
    normed, _ = normed_rows(r)
    h = (normed * gain_two + bias_two).astype(low)
    h_ref[i] = h
    probs_ref[i] = routed(h, weights, order)


def routed(h, weights, order):
    logits = dot(h, dot(columns_of(weights, QKV + D, PACKED), order).astype(low))
    logits = jnp.where(lanes_of(logits.shape) < EXPERTS, logits, -1e30)
    grown = jnp.exp(logits - jnp.max(logits, axis=-1, keepdims=True))
    return grown / jnp.sum(grown, axis=-1, keepdims=True)


def whole_spec(shape):
    return pl.BlockSpec(shape, lambda *_: (0,) * len(shape))


def remote_params(n, number):
    return pltpu.CompilerParams(
        dimension_semantics=("arbitrary",) * n,
        vmem_limit_bytes=BIG,
        collective_id=number,
        has_side_effects=True,
    )


def device(offset):
    names = ("replica", "part", "expert")
    return tuple(lax.axis_index(name) ^ o for name, o in zip(names, offset))


def near(groups, j):
    return (0, j // groups, j % groups)


def greet(offsets):
    barrier = pltpu.get_barrier_semaphore()
    for offset in offsets:
        pl.semaphore_signal(barrier, inc=1, device_id=device(offset), device_id_type=MESH)
    pl.semaphore_wait(barrier, len(offsets))


def remote(source, target, send, receive, offset):
    return pltpu.make_async_remote_copy(
        src_ref=source,
        dst_ref=target,
        send_sem=send,
        recv_sem=receive,
        device_id=device(offset),
        device_id_type=MESH,
    )


def owners_like(replicas, parts):
    return [(r, p, 0) for r in range(replicas) for p in range(0, parts, 2) if (r, p) != (0, 0)]


def owner(parts, offset=(0, 0, 0)):
    return (lax.axis_index("replica") ^ offset[0]) * parts + (lax.axis_index("part") ^ offset[1])


def in_line(replicas, parts):
    return [o for o in owners_like(replicas, parts) if o[1] % 4 == 0]


CORE = (0, 1, 0)
ROW = (0, 2, 0)
GROUPS = 4
EARLY = 5


def all_owners(replicas, parts):
    return [(r, p, 0) for r in range(replicas) for p in range(parts) if (r, p) != (0, 0)]


def wide_part(ref, at, g):
    width = ref.shape[-1] // GROUPS
    return ref.at[at, ..., pl.ds(g * width, width)]


def narrow_part(ref, at, g):
    width = ref.shape[-1] // (2 * GROUPS)
    return ref.at[at, ..., pl.ds(g * width, width)]


def tall_part(ref, at, g):
    depth = ref.shape[-2] // GROUPS
    return ref.at[at, ..., pl.ds(g * depth, depth), :]


def small_part(ref, at, g):
    depth, width = ref.shape[-2] // GROUPS, ref.shape[-1] // 2
    return ref.at[at, ..., pl.ds(g // 2 * depth, depth), pl.ds(g % 2 * width, width)]


def outward(sizes, part_of, source, target, semaphores, g, slot):
    _, parts, _ = sizes
    own = target.shape[1]
    here = owner(parts)

    def block(p):
        return part_of(source, pl.ds((lax.axis_index("part") ^ p) * own, own), g)

    copies = [
        remote(block(o[1]), part_of(target, here, g), semaphores.at[0, slot, i], semaphores.at[1, slot, i], o)
        for i, o in enumerate(all_owners(*sizes[:2]))
    ]
    last = semaphores.at[0, slot, len(copies)]
    return copies + [pltpu.make_async_copy(block(0), part_of(target, here, g), last)]


def across(sizes, part_of, source, target, semaphores, g, slot):
    replicas, parts, _ = sizes

    def rows(r):
        return pl.ds((lax.axis_index("replica") ^ r) * parts, parts)

    return [
        remote(
            part_of(source, rows(r), g), part_of(target, r - 1, g),
            semaphores.at[0, slot, r], semaphores.at[1, slot, r], (r, 0, 0),
        )
        for r in range(1, replicas)
    ]


def homeward(sizes, part_of, source, target, semaphores, g, slot):
    _, parts, _ = sizes
    here = lax.axis_index("part")
    copies = [
        remote(
            part_of(source, here ^ p, g), part_of(target, here, g),
            semaphores.at[0, slot, p], semaphores.at[1, slot, p], (0, p, 0),
        )
        for p in range(1, parts)
    ]
    last = semaphores.at[0, slot, 0]
    return copies + [pltpu.make_async_copy(part_of(source, here, g), part_of(target, here, g), last)]


def partners(sizes):
    replicas, parts, _ = sizes
    return {(0, p, 0) for p in range(1, parts)} | {(r, 0, 0) for r in range(1, replicas)}


def mine_of(sizes, dw_ref):
    return dw_ref.at[pl.ds(lax.axis_index("replica") * sizes[1], sizes[1])]


def add(sizes, mine, others, rows, columns):
    @pl.loop(0, sizes[1])
    def _(p):
        total = mine[p, :, rows, columns].astype(full)
        for r in range(sizes[0] - 1):
            total = total + others[r, p, :, rows, columns].astype(full)
        mine[p, :, rows, columns] = total.astype(low)


def start(copies):
    for copy in copies:
        copy.start()


def wait(copies):
    for copy in copies:
        copy.wait()


def flow_semaphores(sizes, slots):
    return pltpu.SemaphoreType.DMA((2, slots, sizes[0] * sizes[1]))


def swap_slots(groups, keys_ref, blocks, out_ref, sends, receives, local):
    _, count, own, tokens = keys_ref.shape
    slots = lax.broadcasted_iota(jnp.int32, (CAP, tokens), 0).astype(full)

    def build(s, source):
        copies = []
        for j in [*range(1, count), 0]:
            picks = [(keys_ref[s, j, i : i + 1] == slots).astype(low) for i in range(own)]
            picks = jnp.concatenate(picks, axis=0) if own > 1 else picks[0]
            rows = dot(picks, source).astype(low)
            blocks[j, s] = rows.reshape(own, CAP, D)
            if j:
                copy = remote(
                    blocks.at[j, s], out_ref.at[j, s], sends.at[j, s], receives.at[j, s],
                    near(groups, j),
                )
            else:
                copy = pltpu.make_async_copy(blocks.at[0, s], out_ref.at[0, s], local.at[s])
            copy.start()
            copies.append(copy)
        return copies

    return build


def open_kernel(
    sizes, keys_ref, cotangent_ref, tokens_ref, order_ref, shard_ref, raw_one_ref, raw_two_ref,
    x_out, dy_kept, dy_out, h_out, weights_out, first_ref, second_ref, qkv_out, ctx_out, r_out, h_kept, probs_out, theirs_out,
    master_out,
    x_ref, dy_ref, dy_blocks, h_blocks, weights, other_dy, other_h, qkv, ctx, r, h, probs, theirs,
    raw_one, raw_two, master_one, master_two,
    hop, hops, dy_sends, dy_receives, dy_local, h_sends, h_receives, h_local, early, middle, late, here, keeps,
    raws, flow,
):
    replicas, parts, groups = sizes
    count = keys_ref.shape[1]
    images = x_ref.shape[0]
    mirror = (0, parts // 2, 0)
    owners = owners_like(replicas, parts)
    reading = [
        pltpu.make_async_copy(raw_one_ref, raw_one, raws.at[0]),
        pltpu.make_async_copy(raw_two_ref, raw_two, raws.at[1]),
    ]
    start(reading)
    for padded, rows_ref in ((dy_ref, cotangent_ref), (x_ref, tokens_ref)):
        padded[...] = jnp.zeros_like(padded)
        for i in range(images):
            padded[i, :SEQ] = rows_ref[i * SEQ : (i + 1) * SEQ].astype(full).astype(low)
    greet(
        sorted({near(groups, j) for j in range(1, count)} | {mirror, *all_owners(replicas, parts)})
    )
    swap_dy = remote(dy_ref, other_dy, hop.at[0], hop.at[1], mirror)
    swap_dy.start()
    side = lax.axis_index("expert") % 2
    cut_at = (PACKED // LANES + 1) // 2 * LANES

    def half(ref, which):
        return ref.at[:, : PACKED - cut_at] if which == 0 else ref.at[:, PACKED - cut_at :]

    def halves_of(o, which):
        return half(weights.at[owner(parts, o)], which)

    kept = pltpu.make_async_copy(shard_ref, weights.at[owner(parts)], here)
    kept.start()
    to_core = remote(shard_ref, weights.at[owner(parts)], late.at[0, 0, 0], late.at[1, 0, 0], CORE)
    to_core.start()

    def gathers(which):
        return [
            remote(
                half(shard_ref, which), halves_of((0, 0, 0), which), early.at[0, i], early.at[1, i], o
            )
            for i, o in enumerate(owners)
        ]

    def beside(which):
        return [
            remote(
                halves_of(o, which), halves_of(o, which), middle.at[0, i], middle.at[1, i], (0, 0, 1)
            )
            for i, o in enumerate(owners)
        ]

    def onward(which, slot):
        return [
            remote(
                halves_of(o, which), halves_of(o, which), late.at[0, slot, i + 1], late.at[1, slot, i + 1], CORE
            )
            for i, o in enumerate(owners)
        ]

    for which in range(2):
        @pl.when(side == which)
        def _():
            start(gathers(which))

    one = [outward(sizes, wide_part, master_one, first_ref, flow, g, g) for g in range(GROUPS)]
    two = [
        outward(sizes, small_part, master_two, second_ref, flow, g, GROUPS + g)
        for g in range(EARLY)
    ]
    reading[0].wait()

    @pl.loop(0, raw_one.shape[0])
    def _(e):
        master_one[e] = raw_one[e].astype(low)

    start(one[0])
    build_dy = swap_slots(groups, keys_ref, dy_blocks, dy_out, dy_sends, dy_receives, dy_local)
    build_h = swap_slots(groups, keys_ref, h_blocks, h_out, h_sends, h_receives, h_local)
    copies = build_dy(0, dy_ref[...].reshape(images * ROWS, D))
    start(one[1])
    reading[1].wait()

    @pl.loop(0, raw_two.shape[0])
    def _(e):
        master_two[e] = raw_two[e].astype(low)

    for which in range(2):
        @pl.when(side == which)
        def _():
            for a, b, c in zip(gathers(which), beside(which), onward(which, 0)):
                a.wait_recv()
                b.start()
                c.start()

    swap_dy.wait()
    copies += build_dy(1, other_dy[...].reshape(images * ROWS, D))
    for which in range(2):
        @pl.when(side == which)
        def _():
            for b, c in zip(beside(1 - which), onward(1 - which, 1)):
                b.wait_recv()
                c.start()
            for a, b, c, d in zip(gathers(which), beside(which), onward(which, 0), onward(1 - which, 1)):
                a.wait_send()
                b.wait_send()
                c.wait()
                d.wait()

    to_core.wait()
    kept.wait()

    def hop_of(i):
        return remote(h.at[i], other_h.at[i], hops.at[0, i], hops.at[1, i], mirror)

    @pl.loop(0, images)
    def _(i):
        attend(i, weights, order_ref[...], x_ref, qkv, ctx, r, h, probs)
        hop_of(i).start()

    start(one[2])
    start(one[3])
    keeping = [
        pltpu.make_async_copy(source, target, keeps.at[i])
        for i, (source, target) in enumerate(
            [
                (weights, weights_out), (qkv, qkv_out), (ctx, ctx_out), (r, r_out), (h, h_kept),
                (probs, probs_out), (master_two, master_out), (x_ref, x_out), (dy_ref, dy_kept),
            ]
        )
    ]
    start(keeping)
    copies += build_h(0, h[...].reshape(images * ROWS, D))
    start(two[0])
    start(two[1])

    @pl.loop(0, images)
    def _(i):
        hop_of(i).wait()
        theirs[i] = routed(other_h[i], weights, order_ref[...]).astype(low)

    copies += build_h(1, other_h[...].reshape(images * ROWS, D))
    for group in two[2:]:
        start(group)
    last = pltpu.make_async_copy(theirs, theirs_out, keeps.at[9])
    last.start()
    wait(copies)
    wait(keeping)
    last.wait()
    for group in one + two:
        wait(group)


def forward(keys, cotangent, tokens, order, shard, raw_one, raw_two, sizes, number):
    replicas, parts, groups = sizes
    _, count, own, _ = keys.shape
    images = tokens.shape[0] // SEQ
    owners = replicas * parts
    slots = (count, 2, own, CAP, D)
    rows = lambda width: (images, ROWS, width)
    shapes = [
        (rows(D), low), (rows(D), low), (slots, low), (slots, low), ((owners, *shard.shape), low),
        ((owners, own, *raw_one.shape[1:]), low), ((owners, own, *raw_two.shape[1:]), low),
        (rows(QKV), low), (rows(D), low), (rows(D), full), (rows(D), low), (rows(LANES), full), (rows(LANES), low),
        (raw_two.shape, low),
    ]
    buffers = [
        (rows(D), low), (rows(D), low), (slots, low), (slots, low), ((owners, *shard.shape), low), (rows(D), low),
        (rows(D), low),
        (rows(QKV), low), (rows(D), low), (rows(D), full), (rows(D), low), (rows(LANES), full), (rows(LANES), low),
        (raw_one.shape, full), (raw_two.shape, full), (raw_one.shape, low), (raw_two.shape, low),
    ]
    semaphores = [
        (2,), (2, images), (count, 2), (count, 2), (2,), (count, 2), (count, 2), (2,),
        (2, owners // 2 - 1), (2, owners // 2 - 1), (2, 2, owners // 2), (), (10,), (2,),
        (2, GROUPS + EARLY, owners),
    ]
    inner = pl.BlockSpec(memory_space=pltpu.VMEM)
    outer = pl.BlockSpec(memory_space=pl.ANY)
    return pl.pallas_call(
        partial(open_kernel, sizes),
        in_specs=[inner] * 4 + [outer] * 3,
        out_specs=[outer] * len(shapes),
        out_shape=[jax.ShapeDtypeStruct(*shape) for shape in shapes],
        scratch_shapes=[pltpu.VMEM(*b) for b in buffers]
        + [pltpu.SemaphoreType.DMA(n) for n in semaphores],
        compiler_params=pltpu.CompilerParams(
            vmem_limit_bytes=BIG, collective_id=number, has_side_effects=True
        ),
        cost_estimate=pl.CostEstimate(
            flops=60 * 10**9, bytes_accessed=30 * 10**6, transcendentals=2 * 10**6
        ),
        name="forward",
    )(keys, cotangent, tokens, order, shard, raw_one, raw_two)


def chooser(own, j):
    shape = (LANES, own * CAP)
    expert = lax.broadcasted_iota(jnp.int32, shape, 0)
    slot = lax.broadcasted_iota(jnp.int32, shape, 1)
    return (expert == j * own + slot // CAP).astype(low)


def attend_back(i, weights, held, acc, dqkv, dx_ref):
    w_ref, order_ref = weights
    x_ref, qkv_ref, ctx_ref, r_ref, h_ref, probs_ref, dy_ref, dh_ref, dprobs_ref = held
    qkv_acc, proj_acc, router_acc, norm_acc = acc
    rows = pl.ds(pl.multiple_of(i * ROWS, ROWS), ROWS)
    gain_one, bias_one, gain_two, _ = norm_vectors(w_ref)
    probs, dprobs = probs_ref[i], dprobs_ref[rows]
    dlogits = (probs * (dprobs - jnp.sum(probs * dprobs, axis=-1, keepdims=True))).astype(low)
    router_acc[...] += dot_lt(h_ref[i], dlogits)
    router = dot(columns_of(w_ref, QKV + D, PACKED), order_ref[...]).astype(low)
    dh = dh_ref[rows] + dot_rt(dlogits, router)
    normed, factor = normed_rows(r_ref[i])
    norm_acc[2:3] += jnp.sum(dh * normed, axis=0, keepdims=True)
    norm_acc[3:4] += jnp.sum(dh, axis=0, keepdims=True)
    dr = dy_ref[i].astype(full) + norm_back(normed, factor, gain_two, dh)
    dattended = dr.astype(low)
    proj_acc[...] += dot_lt(ctx_ref[i], dattended)
    dctx = dot_rt(dattended, columns_of(w_ref, QKV, QKV + D)).astype(low)
    for pair in range(HEADS // 2):
        at = pair * LANES
        query = halves(qkv_ref[i, :, at : at + LANES])
        key = qkv_ref[i, :, D + at : D + at + LANES]
        keys = halves(key)
        value = qkv_ref[i, :, 2 * D + at : 2 * D + at + LANES]
        dhead = halves(dctx[:, at : at + LANES])
        dq = dk = dv = None
        for e in range(2):
            p = head_probs(query[e], key)
            dp = dot_rt(dhead[e], value)
            ds = (p * (dp - jnp.sum(p * dp, axis=-1, keepdims=True))).astype(low)
            terms = dot(ds, keys[e]), dot_lt(ds, query[e]), dot_lt(p.astype(low), dhead[e])
            dq, dk, dv = terms if dq is None else (dq + terms[0], dk + terms[1], dv + terms[2])
        dqkv[:, at : at + LANES] = (dq * HEAD**-0.5).astype(low)
        dqkv[:, D + at : D + at + LANES] = (dk * HEAD**-0.5).astype(low)
        dqkv[:, 2 * D + at : 2 * D + at + LANES] = dv.astype(low)
    normed, factor = normed_rows(x_ref[i].astype(full))
    attn_in = (normed * gain_one + bias_one).astype(low)
    qkv_acc[...] += dot_lt(attn_in, dqkv[...])
    da = dot_rt(dqkv[...], columns_of(w_ref, 0, QKV))
    norm_acc[0:1] += jnp.sum(da * normed, axis=0, keepdims=True)
    norm_acc[1:2] += jnp.sum(da, axis=0, keepdims=True)
    dx_ref[i] = dr + norm_back(normed, factor, gain_one, da)


def close_kernel(
    sizes, keys_ref, back_ref, w_ref, order_ref, x_ref, qkv_ref, ctx_ref, r_ref, h_ref, probs_ref, dy_ref,
    theirs_ref, y_ref, dw_one_ref,
    dx_ref, out_ref, total_ref, one_ref,
    xs, qkvs, ctxs, rs, hs, ps, dys, their_probs, ys, dh, dprobs, sent, got, sent_gates, got_gates, sent_two, got_two,
    mine_one, others_one,
    dqkv, qkv_acc, proj_acc, router_acc, norm_acc, grads, kept, first, second, along, third,
    loads, y_sends, y_receives, hops, gate_hops, hops_two, flow, home_one,
    core_sems, row_sems, owner_sems, expert_sems,
):
    replicas, parts, groups = sizes
    count, _, own, _, _ = y_ref.shape
    images = x_ref.shape[0]
    width = own * CAP
    half = count * own
    mirror = (0, parts // 2, 0)
    owners = owners_like(replicas, parts)
    sideways = [(0, 0, g) for g in range(1, groups)]
    peers = {near(groups, j) for j in range(1, count)} | {mirror, *sideways, *owners}
    greet(sorted(peers | partners(sizes)))

    pairs_of = [
        (r_ref, rs), (theirs_ref, their_probs), (x_ref, xs), (qkv_ref, qkvs), (ctx_ref, ctxs),
        (h_ref, hs), (probs_ref, ps), (dy_ref, dys),
        (mine_of(sizes, dw_one_ref), mine_one), (y_ref.at[0], ys.at[0]),
    ]
    loading = [
        pltpu.make_async_copy(source, target, loads.at[i])
        for i, (source, target) in enumerate(pairs_of)
    ]
    swaps = [
        [
            remote(y_ref.at[j, s], ys.at[j, s], y_sends.at[j, s], y_receives.at[j, s], near(groups, j))
            for j in range(1, count)
        ]
        for s in range(2)
    ]
    eighths = [
        across(sizes, narrow_part, dw_one_ref, others_one, flow, g, g) for g in range(2 * GROUPS)
    ]
    start(swaps[1])
    start(swaps[0])
    for g in range(GROUPS):
        start(eighths[g])
    start(loading)

    def rows_of(i):
        return pl.ds(pl.multiple_of(i * ROWS, ROWS), ROWS)

    def hop(i):
        rows = rows_of(i)
        return [
            remote(sent.at[rows], got.at[rows], hops.at[0, i], hops.at[1, i], mirror),
            remote(sent_gates.at[i], got_gates.at[i], gate_hops.at[0, i], gate_hops.at[1, i], mirror),
        ]

    near_lanes = lanes_of((2 * half, LANES))
    near_rows = lax.broadcasted_iota(jnp.int32, (2 * half, LANES), 0)

    def hop_two(i):
        rows = rows_of(i)
        return remote(sent_two.at[rows], got_two.at[rows], hops_two.at[0, i], hops_two.at[1, i], mirror)

    def gathered(s, rows):
        slot = (lanes_of((ROWS, width)) % CAP).astype(full)
        lane = lanes_of((ROWS, LANES))
        keys = keys_ref[s, rows]
        total = jnp.zeros((ROWS, D), full)
        change = jnp.zeros((ROWS, LANES), full)
        for j in range(count):
            here = dot(keys, chooser(own, j)) == slot
            total = total + dot(here.astype(low), back_ref[j, s, :, :CAP].reshape(width, D))
            dgate = back_ref[j, s, :, CAP : CAP + 1].astype(full)
            dgate = dgate[:, :, :CAP] + dgate[:, :, CAP : 2 * CAP]
            for e in range(own):
                agreed = jnp.where(here[:, e * CAP : (e + 1) * CAP], dgate[e], 0.0)
                column = jnp.sum(agreed, axis=-1, keepdims=True)
                change = jnp.where(lane == j * own + e, column, change)
        return total, change

    def weighted(s, rows, probs):
        slot = (lanes_of((ROWS, width)) % CAP).astype(full)
        keys = keys_ref[s, rows]
        total = jnp.zeros((ROWS, D), full)
        for j in range(count):
            spread = chooser(own, j)
            gate = jnp.where(dot(keys, spread) == slot, dot(probs, spread), 0.0)
            total = total + dot(gate.astype(low), ys[j, s].reshape(width, D))
        return total

    @pl.loop(0, images)
    def _(i):
        rows = rows_of(i)
        total, change = gathered(1, rows)
        sent[rows] = total.astype(low)
        high = change.astype(low)
        rest = pltpu.roll(change - high.astype(full), half, 1)
        both = (high.astype(full) + rest).astype(low)
        sent_gates[i] = dot_rt((near_lanes == near_rows).astype(low), both).astype(low)
        start(hop(i))

    for g in range(GROUPS, 2 * GROUPS):
        start(eighths[g])

    @pl.loop(0, images)
    def _(i):
        rows = rows_of(i)
        dh[rows], dprobs[rows] = gathered(0, rows)

    wait(loading)
    wait(swaps[1])

    @pl.loop(0, images)
    def _(i):
        rows = rows_of(i)
        sent_two[rows] = weighted(1, rows, their_probs[i]).astype(low)
        hop_two(i).start()

    @pl.loop(0, images)
    def _(i):
        rows = rows_of(i)
        wait(hop(i))
        dh[rows] += got[rows].astype(full)
        place = (near_lanes == half + near_rows % half).astype(low)
        dprobs[rows] += dot_lt(got_gates[i], place)

    each = mine_one.shape[-1] // GROUPS
    homes = []

    def send_home(g):
        wait(eighths[2 * g])
        wait(eighths[2 * g + 1])
        add(sizes, mine_one, others_one, slice(None), slice(g * each, (g + 1) * each))
        copies = homeward(sizes, wide_part, mine_one, one_ref, home_one, g, g)
        start(copies)
        homes.extend(copies)

    send_home(0)
    send_home(1)
    for ref in (qkv_acc, proj_acc, router_acc, norm_acc):
        ref[...] = jnp.zeros_like(ref)

    @pl.loop(0, images)
    def _(i):
        attend_back(
            i, (w_ref, order_ref), (xs, qkvs, ctxs, rs, hs, ps, dys, dh, dprobs),
            (qkv_acc, proj_acc, router_acc, norm_acc), dqkv, dx_ref,
        )

    columns = norm_acc[...].T
    shifted = pltpu.roll(columns, EXPERTS, 1)
    tile = jnp.where(lanes_of(shifted.shape) < EXPERTS, router_acc[...], shifted)
    router_acc[...] = dot_rt(tile.astype(low), order_ref[...])
    depth = grads.shape[1]
    core = lax.axis_index("part") % 2
    blocks = replicas * parts // 2

    @pl.loop(0, 2 * blocks)
    def _(o):
        rows = pl.ds(pl.multiple_of(o * depth, depth), depth)
        grads[o, :, :QKV] = qkv_acc[rows].astype(low)
        grads[o, :, QKV : QKV + D] = proj_acc[rows].astype(low)
        grads[o, :, QKV + D :] = router_acc[rows].astype(low)

    to_core = [
        remote(grads.at[2 * i + 1 - core], first.at[i], core_sems.at[0, i], core_sems.at[1, i], CORE)
        for i in range(blocks)
    ]
    start(to_core)
    for i in range(blocks):
        to_core[i].wait()
        kept[i] = (grads[2 * i + core].astype(full) + first[i].astype(full)).astype(low)
    side = lax.axis_index("part") // 2 % 2
    to_row = [
        remote(kept.at[2 * i + 1 - side], second.at[i], row_sems.at[0, i], row_sems.at[1, i], ROW)
        for i in range(blocks // 2)
    ]
    start(to_row)
    for i in range(blocks // 2):
        to_row[i].wait()
        at = 2 * i + side
        kept[at] = (kept[at].astype(full) + second[i].astype(full)).astype(low)
    to_owner = [
        remote(kept.at[owner(parts, o) // 2], along.at[i], owner_sems.at[0, i], owner_sems.at[1, i], o)
        for i, o in enumerate(in_line(replicas, parts))
    ]
    start(to_owner)

    for g in range(2, GROUPS):
        send_home(g)
    wait(swaps[0])

    @pl.loop(0, images)
    def _(i):
        rows = rows_of(i)
        total = rs[i] + weighted(0, rows, ps[i].astype(low))
        hop_two(i).wait()
        out_ref[rows] = (total + got_two[rows].astype(full)).astype(low)

    total = kept[owner(parts) // 2].astype(full)
    for i, copy in enumerate(to_owner):
        copy.wait()
        total = total + along[i].astype(full)
    me = lax.axis_index("expert")
    third[me] = total.astype(low)
    to_others = [
        remote(third.at[me], third.at[me], expert_sems.at[0, i], expert_sems.at[1, i], o)
        for i, o in enumerate(sideways)
    ]
    start(to_others)
    wait(to_others)
    total = third[0].astype(full)
    for g in range(1, groups):
        total = total + third[g].astype(full)
    total_ref[...] = total
    wait(homes)


def close(keys, back, weights, order, x, qkv, ctx, r, h, probs, dy, theirs, y, dw_one, sizes, number):
    replicas, parts, groups = sizes
    images = x.shape[0]
    tokens = images * ROWS
    count = y.shape[0]
    owners = replicas * parts
    shard = weights.shape[1:]
    one = (parts, *dw_one.shape[1:])
    line = len(in_line(replicas, parts))
    inner = pl.BlockSpec(memory_space=pltpu.VMEM)
    outer = pl.BlockSpec(memory_space=pl.ANY)
    buffers = [
        (x.shape, low), (qkv.shape, low), (ctx.shape, low), (r.shape, full), (x.shape, low),
        (probs.shape, full), (dy.shape, low), (theirs.shape, low), (y.shape, low),
        ((tokens, D), full), ((tokens, LANES), full),
        ((tokens, D), low), ((tokens, D), low), ((images, EXPERTS, ROWS), low), ((images, EXPERTS, ROWS), low),
        ((tokens, D), low), ((tokens, D), low),
        (one, low), ((replicas - 1, *one), low),
        ((ROWS, QKV), low), ((D, QKV), full), ((D, D), full), ((D, LANES), full), ((LANES, D), full),
        ((owners, *shard), low), ((owners // 2, *shard), low), ((owners // 2, *shard), low),
        ((owners // 4, *shard), low), ((line, *shard), low), ((groups, *shard), low),
    ]
    semaphores = [
        (10,), (count, 2), (count, 2), (2, images), (2, images), (2, images), (2, 2 * GROUPS, replicas),
        (2, GROUPS, parts), (2, owners // 2), (2, owners // 4), (2, line), (2, groups - 1),
    ]
    arrays = (
        keys, back, weights, order, x, qkv, ctx, r, h, probs, dy, theirs, y, dw_one,
    )
    return pl.pallas_call(
        partial(close_kernel, sizes),
        in_specs=[inner] * 4 + [outer] * 10,
        out_specs=[inner] * 3 + [outer],
        out_shape=[
            jax.ShapeDtypeStruct((images, ROWS, D), full),
            jax.ShapeDtypeStruct((tokens, D), low),
            jax.ShapeDtypeStruct(shard, full),
            jax.ShapeDtypeStruct(one, low),
        ],
        scratch_shapes=[pltpu.VMEM(*b) for b in buffers]
        + [pltpu.SemaphoreType.DMA(n) for n in semaphores],
        compiler_params=pltpu.CompilerParams(
            vmem_limit_bytes=BIG, collective_id=number, has_side_effects=True
        ),
        cost_estimate=pl.CostEstimate(
            flops=60 * 10**9, bytes_accessed=30 * 10**6, transcendentals=2 * 10**6
        ),
        name="close",
    )(*arrays)


GELU = 0.7978845608028654
CUBE = 0.044715


def gelu_pair(u):
    square = u * u
    bent = jnp.tanh(u * (GELU * CUBE * square + GELU))
    half = 0.5 * bent + 0.5
    value = u * half
    return value, half + value * (1.0 - bent) * (3.0 * GELU * CUBE * square + GELU)


def first_kernel(
    sizes, h_ref, dy_ref, w_ref, wr_ref, sel_ref, master_ref, _, g_ref, slope_ref, dw_ref, second_ref,
    gates, dye_t, flow,
):
    sources = h_ref.shape[0]
    tile = w_ref.shape[3]
    at = pl.program_id(0) * pl.num_programs(1) + pl.program_id(1)

    def moved(g):
        return outward(sizes, small_part, master_ref, second_ref, flow, g, g - EARLY)

    @pl.when(at == 0)
    def _():
        greet(all_owners(*sizes[:2]))
        for g in range(EARLY, 2 * GROUPS):
            start(moved(g))

    @pl.when(pl.program_id(1) == 0)
    def _():
        for k in range(sources):
            rows = slice(k * CAP, (k + 1) * CAP)
            logits = dot(h_ref[k, 0], wr_ref[...])
            logits = jnp.where(lanes_of(logits.shape) < EXPERTS, logits, -1e30)
            grown = jnp.exp(logits - jnp.max(logits, axis=-1, keepdims=True))
            mine = jnp.sum(grown * sel_ref[0], axis=-1, keepdims=True)
            gate = mine / jnp.sum(grown, axis=-1, keepdims=True)
            gates[rows] = jnp.broadcast_to(gate, (CAP, LANES))
            dye_t[:, rows] = (dy_ref[k, 0].astype(full) * gate).T.astype(low)

    w = w_ref[:, 0].reshape(D, tile)
    for k in range(0, sources, 2):
        rows = slice(k * CAP, (k + 2) * CAP)
        value, slope = gelu_pair(dot(h_ref[k : k + 2, 0].reshape(2 * CAP, D), w))
        g_ref[0, rows] = value.astype(low)
        slope_ref[0, rows] = (slope * gates[rows, :1]).astype(low)
    grad = dot(dye_t[...], g_ref[0]).T
    dw_ref[:, 0] = grad.astype(low).reshape(dw_ref.shape[0], dw_ref.shape[2], D)

    @pl.when(at == pl.num_programs(0) * pl.num_programs(1) - 1)
    def _():
        for g in range(EARLY, 2 * GROUPS):
            wait(moved(g))


def slot_spec(sources):
    return pl.BlockSpec((sources, 1, CAP, D), lambda e, f: (0, e, 0, 0))


def expert_first(h, dy, w_in, w_router, select, master, second, sizes, tile, number):
    sources = h.shape[0]
    owners, own, depth, hidden = w_in.shape
    rows = sources * CAP
    per = hidden // owners
    hidden_spec = pl.BlockSpec((1, rows, tile), lambda e, f: (e, 0, f))
    return pl.pallas_call(
        partial(first_kernel, sizes),
        grid=(own, hidden // tile),
        in_specs=[
            slot_spec(sources),
            slot_spec(sources),
            pl.BlockSpec((owners, 1, depth, tile), lambda e, f: (0, e, 0, f)),
            whole_spec(w_router.shape),
            pl.BlockSpec((1, 1, LANES), lambda e, f: (e, 0, 0)),
            pl.BlockSpec(memory_space=pl.ANY),
            pl.BlockSpec(memory_space=pl.ANY),
        ],
        out_specs=[
            hidden_spec,
            hidden_spec,
            pl.BlockSpec((tile // per, 1, per, D), lambda e, f: (f, e, 0, 0)),
            pl.BlockSpec(memory_space=pl.ANY),
        ],
        out_shape=[
            jax.ShapeDtypeStruct((own, rows, hidden), low),
            jax.ShapeDtypeStruct((own, rows, hidden), low),
            jax.ShapeDtypeStruct((owners, own, per, D), low),
            jax.ShapeDtypeStruct(second.shape, low),
        ],
        input_output_aliases={6: 3},
        scratch_shapes=[
            pltpu.VMEM((rows, LANES), full), pltpu.VMEM((D, rows), low), flow_semaphores(sizes, 2 * GROUPS - EARLY),
        ],
        compiler_params=pltpu.CompilerParams(
            dimension_semantics=("arbitrary",) * 2,
            vmem_limit_bytes=BIG,
            collective_id=number,
            has_side_effects=True,
        ),
        cost_estimate=pl.CostEstimate(
            flops=4 * own * rows * D * hidden,
            bytes_accessed=50 * 10**6,
            transcendentals=own * rows * hidden,
        ),
        name="expert_first",
    )(h, dy, w_in, w_router, select, master, second)


def rest_kernel(
    sizes, own, steps, dy_ref, h_ref, g_ref, slope_ref, w_in_ref, w_out_ref, dw_two_ref,
    back_ref, dw_ref, y_ref, two_ref, du, acc, dgates, dgate_rows, h_t, staged, mine_two, others_two,
    sends, receives, local, flow, home, load,
):
    replicas, parts, groups = sizes

    def moved(g):
        return across(sizes, tall_part, dw_two_ref, others_two, flow, g, g)

    def homes(g):
        return homeward(sizes, tall_part, mine_two, two_ref, home, g, g)

    def send_home(g):
        wait(moved(g))
        depth = mine_two.shape[2] // GROUPS
        add(sizes, mine_two, others_two, slice(g * depth, (g + 1) * depth), slice(None))
        start(homes(g))

    loading = pltpu.make_async_copy(mine_of(sizes, dw_two_ref), mine_two, load)

    sources = dy_ref.shape[0]
    tile = slope_ref.shape[2]
    at = pl.program_id(0)
    phase, expert, step = at // (own * steps), at // steps % own, at % steps
    w_in = w_in_ref[:, 0].reshape(D, tile)
    w_out = w_out_ref[:, 0].reshape(tile, D)
    chunk = 2 * CAP

    def copy(k, e):
        return pltpu.make_async_remote_copy(
            src_ref=staged.at[k, e],
            dst_ref=back_ref.at[k, e],
            send_sem=sends.at[k, e],
            recv_sem=receives.at[k, e],
            device_id=device(near(groups, k // 2)),
            device_id_type=MESH,
        )

    def mine(k, e):
        return pltpu.make_async_copy(staged.at[k, e], back_ref.at[k, e], local.at[k, e])

    @pl.when(at == 0)
    def _():
        greet(sorted({near(groups, j) for j in range(1, sources // 2)} | partners(sizes)))
        loading.start()
        start(moved(0))
        start(moved(1))

    @pl.when((phase != 1) & (step == 0))
    def _():
        acc[...] = jnp.zeros_like(acc)

    @pl.when(phase == 0)
    def _():
        @pl.when(step == 0)
        def _():
            dgates[...] = jnp.zeros_like(dgates)

        for k in range(0, sources, 2):
            rows = slice(k * CAP, (k + 2) * CAP)
            dg = dot_rt(dy_ref[k : k + 2, 0].reshape(chunk, D), w_out)
            change = (dg * slope_ref[0, rows].astype(full)).astype(low)
            du[expert * steps + step, rows] = change
            acc[rows] += dot_rt(change, w_in)
            agreed = dg * g_ref[0, rows].astype(full)
            dgates[rows] += sum(agreed[:, i : i + LANES] for i in range(0, tile, LANES))

        @pl.when(step == steps - 1)
        def _():
            sums = dgates[...]
            high = sums.astype(low)
            rest = (sums - high.astype(full)).astype(low)
            ones = jnp.ones((16, LANES), low)
            dgate_rows[...] = dot_rt(ones, high) + dot_rt(ones, rest)
            for k in range(sources):
                rows = slice(k * CAP, (k + 1) * CAP)
                staged[k, expert, :CAP] = acc[rows].astype(low)
                row = dgate_rows[:, rows]
                high = row.astype(low)
                staged[k, expert, CAP:, :CAP] = high
                staged[k, expert, CAP:, CAP : 2 * CAP] = (row - high.astype(full)).astype(low)
                staged[k, expert, CAP:, 2 * CAP :] = jnp.zeros((16, D - 2 * CAP), low)

        for e in range(own):
            @pl.when((step == steps - 1) & (expert == e))
            def _():
                for k in range(2, sources):
                    copy(k, e).start()
                mine(0, e).start()
                mine(1, e).start()

    @pl.when(at == own * steps)
    def _():
        loading.wait()
        send_home(0)
        start(moved(2))

    @pl.when(at == 2 * own * steps)
    def _():
        send_home(1)
        start(moved(3))

    @pl.when(phase == 1)
    def _():
        @pl.when(step == 0)
        def _():
            for k in range(sources):
                h_t[:, k * CAP : (k + 1) * CAP] = h_ref[k, 0].T

        grad = dot(h_t[...], du[expert * steps + step]).astype(low)
        dw_ref[:, 0] = grad.reshape(dw_ref.shape[0], dw_ref.shape[2], tile)

    @pl.when(phase == 2)
    def _():
        for k in range(0, sources, 2):
            rows = slice(k * CAP, (k + 2) * CAP)
            acc[rows] += dot(g_ref[0, rows], w_out)

        @pl.when(step == steps - 1)
        def _():
            y_ref[:, 0] = acc[...].astype(low).reshape(sources, CAP, D)

    @pl.when(at == 3 * own * steps - 1)
    def _():
        send_home(2)
        send_home(3)
        for e in range(own):
            for k in range(2, sources):
                copy(k, e).wait()
            mine(0, e).wait()
            mine(1, e).wait()
        for g in range(GROUPS):
            wait(homes(g))


def expert_rest(dy, h, g, slope, w_in, w_out, dw_two, tile, sizes, number):
    sources, own, _, _ = dy.shape
    owners, _, depth, hidden = w_in.shape
    rows = sources * CAP
    per = hidden // owners
    steps = hidden // tile
    last = own * steps - 1

    def during(phases):
        def find(at):
            if 0 in phases and 2 in phases:
                inside = jnp.where(at // (last + 1) == 1, last, at % (last + 1))
            else:
                inside = jnp.clip(at - phases[0] * (last + 1), 0, last)
            return inside // steps, inside % steps

        return find

    def spec(shape, phases, index, buffers=2):
        return pl.BlockSpec(
            shape, lambda at: index(*during(phases)(at)), pipeline_mode=pl.Buffered(buffers)
        )

    token, hidden_at = (sources, 1, CAP, D), (1, rows, tile)
    whole_expert = lambda e, f: (0, e, 0, 0)
    in_tile = lambda e, f: (0, e, 0, f)
    return pl.pallas_call(
        partial(rest_kernel, sizes, own, steps),
        grid=(3 * own * steps,),
        in_specs=[
            spec(token, (0,), whole_expert, 1),
            spec(token, (1,), whole_expert, 1),
            spec(hidden_at, (0, 2), lambda e, f: (e, 0, f)),
            spec(hidden_at, (0,), lambda e, f: (e, 0, f)),
            spec((owners, 1, depth, tile), (0,), in_tile),
            spec((tile // per, 1, per, D), (0, 2), lambda e, f: (f, e, 0, 0)),
            pl.BlockSpec(memory_space=pl.ANY),
        ],
        out_specs=[
            pl.BlockSpec(memory_space=pl.ANY),
            spec((owners, 1, depth, tile), (1,), in_tile),
            spec(token, (2,), whole_expert, 1),
            pl.BlockSpec(memory_space=pl.ANY),
        ],
        out_shape=[
            jax.ShapeDtypeStruct((sources, own, CAP + 16, D), low),
            jax.ShapeDtypeStruct(w_in.shape, low),
            jax.ShapeDtypeStruct(dy.shape, low),
            jax.ShapeDtypeStruct((sizes[1], *dw_two.shape[1:]), low),
        ],
        scratch_shapes=[
            pltpu.VMEM((own * steps, rows, tile), low),
            pltpu.VMEM((rows, D), full),
            pltpu.VMEM((rows, LANES), full),
            pltpu.VMEM((16, rows), full),
            pltpu.VMEM((D, rows), low),
            pltpu.VMEM((sources, own, CAP + 16, D), low),
            pltpu.VMEM((sizes[1], *dw_two.shape[1:]), low),
            pltpu.VMEM((sizes[0] - 1, sizes[1], *dw_two.shape[1:]), low),
            pltpu.SemaphoreType.DMA((sources, own)),
            pltpu.SemaphoreType.DMA((sources, own)),
            pltpu.SemaphoreType.DMA((2, own)),
            pltpu.SemaphoreType.DMA((2, GROUPS, sizes[0])),
            pltpu.SemaphoreType.DMA((2, GROUPS, sizes[1])),
            pltpu.SemaphoreType.DMA,
        ],
        compiler_params=pltpu.CompilerParams(
            dimension_semantics=("arbitrary",),
            vmem_limit_bytes=BIG,
            collective_id=number,
            has_side_effects=True,
        ),
        cost_estimate=pl.CostEstimate(
            flops=8 * own * rows * D * hidden, bytes_accessed=60 * 10**6, transcendentals=0
        ),
        name="expert_rest",
    )(dy, h, g, slope, w_in, w_out, dw_two)


def experts_kernel(
    sizes, own, steps, h_ref, dy_ref, w_in_ref, wr_ref, sel_ref, master_ref, _,
    back_ref, dw_ref, y_ref, two_ref, second_ref,
    hidden, slopes, acc, column, dgate_rows, turned, staged, dw_two, others, w_tiles,
    sends, receives, local, flow, cross, home, tile_sems,
):
    replicas, parts, groups = sizes
    sources = dy_ref.shape[0]
    tile = hidden.shape[2]
    owners, _, per, _ = dw_two.shape
    span = tile // per
    chunk = 2 * CAP
    at = pl.program_id(0)
    total = own * steps
    phase, expert, step = at // total, at // steps % own, at % steps
    now = at % total
    first_of_mine = lax.axis_index("replica") * parts

    def weight_part(g):
        return outward(sizes, small_part, master_ref, second_ref, flow, g, g - EARLY)

    def tile_copy(t):
        rows = pl.ds(t % steps * span, span)
        return pltpu.make_async_copy(
            second_ref.at[rows, t // steps], w_tiles.at[t % 2], tile_sems.at[t % 2]
        )

    def rows_of(q, count):
        return pl.ds(q * (per // count), per // count)

    def crossing(e, q):
        return [
            remote(
                dw_two.at[pl.ds((lax.axis_index("replica") ^ r) * parts, parts), e, rows_of(q, 4)],
                others.at[r - 1, :, e, rows_of(q, 4)],
                cross.at[0, 4 * e + q, r], cross.at[1, 4 * e + q, r], (r, 0, 0),
            )
            for r in range(1, replicas)
        ]

    def homes(e, q):
        here = lax.axis_index("part")

        def source(p):
            return dw_two.at[first_of_mine + (here ^ p), e, rows_of(q, 2)]

        target = two_ref.at[here, e, rows_of(q, 2)]
        slot = 2 * e + q
        copies = [
            remote(source(p), target, home.at[0, slot, p], home.at[1, slot, p], (0, p, 0))
            for p in range(1, parts)
        ]
        return copies + [pltpu.make_async_copy(source(0), target, home.at[0, slot, 0])]

    def send_home(e, q):
        wait(crossing(e, 2 * q))
        wait(crossing(e, 2 * q + 1))
        rows = slice(q * (per // 2), (q + 1) * (per // 2))

        @pl.loop(0, parts)
        def _(p):
            value = dw_two[first_of_mine + p, e, rows].astype(full)
            for r in range(replicas - 1):
                value = value + others[r, p, e, rows].astype(full)
            dw_two[first_of_mine + p, e, rows] = value.astype(low)

        start(homes(e, q))

    def copy(k, e):
        if k < 2:
            return pltpu.make_async_copy(staged.at[k, e], back_ref.at[k, e], local.at[k, e])
        return remote(
            staged.at[k, e], back_ref.at[k, e], sends.at[k, e], receives.at[k, e], near(groups, k // 2)
        )

    @pl.when(at == 0)
    def _():
        greet(sorted({near(groups, j) for j in range(1, sources // 2)} | {*all_owners(replicas, parts)}))
        for g in range(EARLY, 2 * GROUPS):
            start(weight_part(g))

    @pl.when(phase == 0)
    def _():
        @pl.when(step == 0)
        def _():
            for k in range(sources):
                rows = slice(k * CAP, (k + 1) * CAP)
                logits = dot(h_ref[k, 0], wr_ref[...])
                logits = jnp.where(lanes_of(logits.shape) < EXPERTS, logits, -1e30)
                grown = jnp.exp(logits - jnp.max(logits, axis=-1, keepdims=True))
                mine = jnp.sum(grown * sel_ref[0], axis=-1, keepdims=True)
                gate = mine / jnp.sum(grown, axis=-1, keepdims=True)
                column[rows] = jnp.broadcast_to(gate, (CAP, LANES))
                turned[:, rows] = (dy_ref[k, 0].astype(full) * gate).T.astype(low)

        w_in = w_in_ref[:, 0].reshape(D, tile)
        for k in range(0, sources, 2):
            rows = slice(k * CAP, (k + 2) * CAP)
            value, slope = gelu_pair(dot(h_ref[k : k + 2, 0].reshape(chunk, D), w_in))
            hidden[now, rows] = value.astype(low)
            slopes[now, rows] = (slope * column[rows, :1]).astype(low)
        grad = dot(turned[...], hidden[now]).T.astype(low)
        dw_two[pl.ds(step * span, span), expert] = grad.reshape(span, per, D)

    for e in range(own):
        @pl.when(at == (e + 1) * steps - 1)
        def _():
            if e == 0:
                start(crossing(0, 0))
                start(crossing(0, 1))
            if e == own - 1:
                for g in range(EARLY, 2 * GROUPS):
                    wait(weight_part(g))
                tile_copy(0).start()
                start(crossing(0, 2))
                start(crossing(0, 3))

    @pl.when(phase % 2 == 1)
    def _():
        tile_copy(now).wait()

        @pl.when(now < total - 1)
        def _():
            tile_copy(now + 1).start()

        @pl.when(step == 0)
        def _():
            acc[...] = jnp.zeros_like(acc)

    @pl.when(phase == 1)
    def _():
        @pl.when(step == 0)
        def _():
            column[...] = jnp.zeros_like(column)

        w_in = w_in_ref[:, 0].reshape(D, tile)
        w_out = w_tiles[now % 2].reshape(tile, D)
        for k in range(0, sources, 2):
            rows = slice(k * CAP, (k + 2) * CAP)
            dg = dot_rt(dy_ref[k : k + 2, 0].reshape(chunk, D), w_out)
            change = (dg * slopes[now, rows].astype(full)).astype(low)
            slopes[now, rows] = change
            acc[rows] += dot_rt(change, w_in)
            agreed = dg * hidden[now, rows].astype(full)
            column[rows] += sum(agreed[:, i : i + LANES] for i in range(0, tile, LANES))

        @pl.when(step == steps - 1)
        def _():
            sums = column[...]
            high = sums.astype(low)
            rest = (sums - high.astype(full)).astype(low)
            ones = jnp.ones((16, LANES), low)
            dgate_rows[...] = dot_rt(ones, high) + dot_rt(ones, rest)
            for k in range(sources):
                rows = slice(k * CAP, (k + 1) * CAP)
                staged[k, expert, :CAP] = acc[rows].astype(low)
                row = dgate_rows[:, rows]
                high = row.astype(low)
                staged[k, expert, CAP:, :CAP] = high
                staged[k, expert, CAP:, CAP : 2 * CAP] = (row - high.astype(full)).astype(low)
                staged[k, expert, CAP:, 2 * CAP :] = jnp.zeros((16, D - 2 * CAP), low)

        for e in range(own):
            @pl.when((step == steps - 1) & (expert == e))
            def _():
                for k in range(sources):
                    copy(k, e).start()

    @pl.when(at == total + steps)
    def _():
        send_home(0, 0)
        start(crossing(1, 0))
        start(crossing(1, 1))

    @pl.when(phase == 2)
    def _():
        @pl.when(step == 0)
        def _():
            for k in range(sources):
                turned[:, k * CAP : (k + 1) * CAP] = h_ref[k, 0].T

        grad = dot(turned[...], slopes[now]).astype(low)
        dw_ref[:, 0] = grad.reshape(dw_ref.shape[0], dw_ref.shape[2], tile)

        @pl.when(now == total - 1)
        def _():
            tile_copy(0).start()

    @pl.when(at == 2 * total + 2)
    def _():
        send_home(0, 1)
        start(crossing(1, 2))
        start(crossing(1, 3))

    @pl.when(phase == 3)
    def _():
        w_out = w_tiles[now % 2].reshape(tile, D)
        for k in range(0, sources, 2):
            rows = slice(k * CAP, (k + 2) * CAP)
            acc[rows] += dot(hidden[now, rows], w_out)

        @pl.when(step == steps - 1)
        def _():
            y_ref[:, 0] = acc[...].astype(low).reshape(sources, CAP, D)

    @pl.when(at == 4 * total - 1)
    def _():
        for e in range(own):
            for k in range(sources):
                copy(k, e).wait()
        send_home(1, 0)
        send_home(1, 1)
        for e in range(own):
            for q in range(2):
                wait(homes(e, q))


def experts(h, dy, w_in, w_router, select, master, second, sizes, tile, number):
    sources = h.shape[0]
    owners, own, depth, width = w_in.shape
    rows = sources * CAP
    per = width // owners
    steps = width // tile
    total = own * steps

    def during(*phases):
        def find(at):
            inside = jnp.where(at // total < phases[0], 0, total - 1)
            for phase in phases:
                inside = jnp.where(at // total == phase, at % total, inside)
            return inside // steps, inside % steps

        return find

    def spec(shape, phases, index, buffers=2):
        return pl.BlockSpec(
            shape, lambda at: index(*during(*phases)(at)), pipeline_mode=pl.Buffered(buffers)
        )

    token = (sources, 1, CAP, D)
    whole_expert = lambda e, f: (0, e, 0, 0)
    in_tile = lambda e, f: (0, e, 0, f)
    outer = pl.BlockSpec(memory_space=pl.ANY)
    two = (sizes[1], own, per, D)
    return pl.pallas_call(
        partial(experts_kernel, sizes, own, steps),
        grid=(4 * total,),
        in_specs=[
            spec(token, (0, 2), whole_expert, 1),
            spec(token, (0, 1), whole_expert, 1),
            spec((owners, 1, depth, tile), (0, 1), in_tile),
            whole_spec(w_router.shape),
            spec((1, 1, LANES), (0,), lambda e, f: (e, 0, 0)),
            outer,
            outer,
        ],
        out_specs=[
            outer,
            spec((owners, 1, depth, tile), (2,), in_tile),
            spec(token, (3,), whole_expert, 1),
            outer,
            outer,
        ],
        out_shape=[
            jax.ShapeDtypeStruct((sources, own, CAP + 16, D), low),
            jax.ShapeDtypeStruct(w_in.shape, low),
            jax.ShapeDtypeStruct((sources, own, CAP, D), low),
            jax.ShapeDtypeStruct(two, low),
            jax.ShapeDtypeStruct(second.shape, low),
        ],
        input_output_aliases={6: 4},
        scratch_shapes=[
            pltpu.VMEM((total, rows, tile), low),
            pltpu.VMEM((total, rows, tile), low),
            pltpu.VMEM((rows, D), full),
            pltpu.VMEM((rows, LANES), full),
            pltpu.VMEM((16, rows), full),
            pltpu.VMEM((D, rows), low),
            pltpu.VMEM((sources, own, CAP + 16, D), low),
            pltpu.VMEM((owners, own, per, D), low),
            pltpu.VMEM((sizes[0] - 1, *two), low),
            pltpu.VMEM((2, tile // per, per, D), low),
            pltpu.SemaphoreType.DMA((sources, own)),
            pltpu.SemaphoreType.DMA((sources, own)),
            pltpu.SemaphoreType.DMA((2, own)),
            flow_semaphores(sizes, 2 * GROUPS - EARLY),
            pltpu.SemaphoreType.DMA((2, 4 * own, sizes[0])),
            pltpu.SemaphoreType.DMA((2, 2 * own, sizes[1])),
            pltpu.SemaphoreType.DMA((2,)),
        ],
        compiler_params=remote_params(1, number),
        cost_estimate=pl.CostEstimate(
            flops=12 * own * rows * D * width, bytes_accessed=40 * 10**6, transcendentals=own * rows * width
        ),
        name="experts",
    )(h, dy, w_in, w_router, select, master, second)


def finish_kernel(out_ref, dx_ref, dense_ref, one_ref, two_ref, output, input_grad, qkv, proj, one, two):
    one[...] = one_ref[...].astype(full)
    two[...] = two_ref[...].astype(full)
    images = dx_ref.shape[0]

    @pl.when(pl.program_id(0) == 0)
    def _():
        qkv[...] = dense_ref[:, :QKV]
        proj[...] = dense_ref[:, QKV : QKV + D]
        for i in range(images):
            input_grad[i * SEQ : (i + 1) * SEQ] = dx_ref[i, :SEQ]
            rows = out_ref[i * ROWS : i * ROWS + SEQ].astype(full)
            output[i * SEQ : (i + 1) * SEQ] = rows.astype(low)


def finish(output, dx, dense, one, two):
    images = dx.shape[0]
    tokens = (images * SEQ, D)
    steps = one.shape[0]
    widths = [(dense.shape[0], QKV), (dense.shape[0], D)]
    block = lambda a: pl.BlockSpec((1, *a.shape[1:]), lambda i: (i,) + (0,) * (a.ndim - 1))
    return pl.pallas_call(
        finish_kernel,
        grid=(steps,),
        in_specs=[whole_spec(a.shape) for a in (output, dx, dense)] + [block(one), block(two)],
        out_specs=[whole_spec(a) for a in (tokens, tokens, *widths)] + [block(one), block(two)],
        out_shape=[
            jax.ShapeDtypeStruct(tokens, low),
            jax.ShapeDtypeStruct(tokens, full),
            *(jax.ShapeDtypeStruct(a, full) for a in widths),
            jax.ShapeDtypeStruct(one.shape, full),
            jax.ShapeDtypeStruct(two.shape, full),
        ],
        compiler_params=pltpu.CompilerParams(
            dimension_semantics=("arbitrary",), vmem_limit_bytes=BIG
        ),
        cost_estimate=pl.CostEstimate(flops=0, bytes_accessed=19 * 10**6, transcendentals=0),
        name="finish",
    )(output, dx, dense, one, two)


ALL = ("replica", "part")


def body(
    tokens,
    choices,
    ln1_gain,
    ln1_bias,
    w_qkv,
    w_proj,
    ln2_gain,
    ln2_bias,
    w_router,
    w_expert_in,
    w_expert_out,
    cotangent,
):
    replicas, parts, groups = (lax.axis_size(name) for name in ("replica", "part", "expert"))
    owners = replicas * parts
    peers = parts * groups
    own = EXPERTS // peers
    images = tokens.shape[0] // SEQ
    count = images * ROWS
    tile = 512 * 16 // peers

    small_rows = w_router.shape[0]
    placed_router = (
        w_router.reshape(small_rows, groups, parts, own).transpose(0, 2, 1, 3).reshape(small_rows, EXPERTS)
    )
    vectors = jnp.concatenate([ln1_gain, ln1_bias, ln2_gain, ln2_bias]).reshape(4, small_rows).T
    packed = jnp.concatenate(
        [w_qkv, w_proj, placed_router, vectors, jnp.zeros((small_rows, LANES - EXPERTS - 4), full)],
        axis=1,
    ).astype(low)
    me = lax.axis_index("part") * groups + lax.axis_index("expert")
    sizes = (replicas, parts, groups)

    half = parts // 2
    flips = [(i, i ^ half) for i in range(parts)]
    picks = jnp.stack([choices, lax.ppermute(choices, "part", flips)]).reshape(2 * images, SEQ, 2)
    picks = jnp.pad(picks, ((0, 0), (0, ROWS - SEQ), (0, 0)), constant_values=-1)
    picks = picks.reshape(2, count, 2)
    column = jnp.arange(EXPERTS)
    place = (me ^ (column // own)) * own + column % own
    expert = (place // own % groups) * (parts * own) + place // (groups * own) * own + place % own
    lane = jnp.arange(LANES)
    order = jnp.where(lane < EXPERTS, jnp.pad(place, (0, LANES - EXPERTS)), lane)
    order = (lane[:, None] == order[None, :]).astype(low)
    expert = expert[: EXPERTS // 2]
    named = (picks[:, :, :, None] == expert).any(axis=2)
    row = jnp.arange(count)
    earlier = (row[None, :] < row[:, None]).astype(low)
    slots = jnp.einsum("tu,sue->ste", earlier, named.astype(low), preferred_element_type=full)
    keys = jnp.where(named, slots, -1.0)
    key_rows = keys.transpose(0, 2, 1).reshape(2, peers // 2, own, count)
    key_columns = jnp.pad(
        keys, ((0, 0), (0, 0), (0, LANES - EXPERTS // 2)), constant_values=-1
    ).astype(low)

    (
        x, dy, dy_slots, h_slots, weights, first_weight, second_weight, qkv, ctx, r, h, probs, theirs, second_master,
    ) = forward(key_rows, cotangent, tokens, order, packed, w_expert_in, w_expert_out, sizes, 0)
    dy_slots = dy_slots.reshape(peers, own, CAP, D)
    h_slots = h_slots.reshape(peers, own, CAP, D)
    select = ((me * own + jnp.arange(own))[:, None, None] == lane[None, None, :]).astype(full)
    routers = weights[:, :, QKV + D :].reshape(D, LANES)
    if own == 2:
        back, dw_first, y, second_grad, _ = experts(
            h_slots, dy_slots, first_weight, routers, select, second_master, second_weight, sizes, tile, 4,
        )
    else:
        g, slope, dw_second, second_weight = expert_first(
            h_slots, dy_slots, first_weight, routers, select, second_master, second_weight,
            sizes, tile, 5,
        )
        back, dw_first, y, second_grad = expert_rest(
            dy_slots, h_slots, g, slope, first_weight, second_weight, dw_second, tile, sizes, 2
        )
    back = back.reshape(peers // 2, 2, own, CAP + 16, D)
    y = y.reshape(peers // 2, 2, own, CAP, D)
    dx, output, grads, first_grad = close(
        key_columns, back, weights, order, x, qkv, ctx, r, h, probs, dy, theirs, y,
        dw_first, sizes, 3,
    )
    output, input_grad, qkv_grad, proj_grad, expert_in_grad, expert_out_grad = finish(
        output, dx, grads, first_grad, second_grad
    )
    router_grad = (
        grads[:, QKV + D : QKV + D + EXPERTS]
        .reshape(small_rows, parts, groups, own)
        .transpose(0, 2, 1, 3)
        .reshape(small_rows, EXPERTS)
    )
    norms = [grads[:, QKV + D + EXPERTS + i] for i in range(4)]

    return (
        output,
        input_grad,
        norms[0],
        norms[1],
        qkv_grad,
        proj_grad,
        norms[2],
        norms[3],
        router_grad,
        expert_in_grad.reshape(w_expert_in.shape),
        expert_out_grad.reshape(w_expert_out.shape),
    )


def solution(mesh):
    dp, groups = mesh.shape["dp"], mesh.shape["expert"]
    parts = min(EXPERTS // groups, dp // 2)
    mesh = Mesh(mesh.devices.reshape(dp // parts, parts, groups), ("replica", "part", "expert"))
    rows = P(("replica", "part", "expert"), None)
    vector, matrix = P(ALL), P(ALL, None)
    experts = P("expert", ALL, None)
    return jax.shard_map(
        body,
        mesh=mesh,
        in_specs=(
            rows, rows, vector, vector, matrix, matrix, vector, vector, matrix, experts, experts, rows,
        ),
        out_specs=(
            rows, rows, vector, vector, matrix, matrix, vector, vector, matrix, experts, experts,
        ),
        check_vma=False,
    )
```

```python
from functools import partial

import jax
import jax.numpy as jnp
from jax import lax
from jax.experimental import pallas as pl
from jax.experimental.pallas import tpu as pltpu
from jax.sharding import Mesh
from jax.sharding import PartitionSpec as P

D = 512
HEADS = 8
EXPERTS = 32
SEQ = 197
CAP = 128
ROWS = 208
HEAD = D // HEADS
LANES = 128
QKV = 3 * D
PACKED = QKV + D + LANES
epsilon = 1e-06
low = jnp.bfloat16
full = jnp.float32
MESH = pl.DeviceIdType.MESH
BIG = 63 * 1024 * 1024


def dot(left, right):
    return jnp.dot(left, right, preferred_element_type=full)


def dot_rt(left, right):
    return lax.dot_general(left, right, (((1,), (1,)), ((), ())), preferred_element_type=full)


def dot_lt(left, right):
    return lax.dot_general(left, right, (((0,), (0,)), ((), ())), preferred_element_type=full)


def lanes_of(shape):
    return lax.broadcasted_iota(jnp.int32, shape, len(shape) - 1)


def normed_rows(values):
    center = values - jnp.mean(values, axis=-1, keepdims=True)
    factor = lax.rsqrt(jnp.mean(center * center, axis=-1, keepdims=True) + epsilon)
    return center * factor, factor


def norm_back(normed, factor, gain_vec, upstream):
    scaled = upstream * gain_vec
    return factor * (
        scaled
        - jnp.mean(scaled, axis=-1, keepdims=True)
        - normed * jnp.mean(scaled * normed, axis=-1, keepdims=True)
    )


def columns_of(weights_ref, start_at, end):
    return weights_ref[:, :, start_at:end].reshape(D, end - start_at)


def norm_vectors(weights_ref):
    rows = columns_of(weights_ref, QKV + D, PACKED).astype(full).T
    return [rows[EXPERTS + i : EXPERTS + i + 1] for i in range(4)]


def halves(pair):
    first = lanes_of(pair.shape) < HEAD
    zero = jnp.zeros_like(pair)
    return jnp.where(first, pair, zero), jnp.where(first, zero, pair)


def head_probs(query, key_pair):
    scores = dot_rt(query, key_pair) * (HEAD**-0.5)
    scores = jnp.where(lanes_of(scores.shape) < SEQ, scores, -1e30)
    grown = jnp.exp(scores - jnp.max(scores, axis=-1, keepdims=True))
    return grown / jnp.sum(grown, axis=-1, keepdims=True)


def attend(i, weights, order, x_ref, qkv_ref, ctx_ref, r_ref, h_ref, probs_ref):
    gain_one, bias_one, gain_two, bias_two = norm_vectors(weights)
    x = x_ref[i].astype(full)
    normed, _ = normed_rows(x)
    attn_in = (normed * gain_one + bias_one).astype(low)
    qkv_ref[i] = dot(attn_in, columns_of(weights, 0, QKV)).astype(low)
    for pair in range(HEADS // 2):
        at = pair * LANES
        query = halves(qkv_ref[i, :, at : at + LANES])
        key = qkv_ref[i, :, D + at : D + at + LANES]
        value = halves(qkv_ref[i, :, 2 * D + at : 2 * D + at + LANES])
        total = None
        for e in range(2):
            part = dot(head_probs(query[e], key).astype(low), value[e])
            total = part if total is None else total + part
        ctx_ref[i, :, at : at + LANES] = total.astype(low)
    r = x + dot(ctx_ref[i], columns_of(weights, QKV, QKV + D))
    r_ref[i] = r
    normed, _ = normed_rows(r)
    h = (normed * gain_two + bias_two).astype(low)
    h_ref[i] = h
    probs_ref[i] = routed(h, weights, order)


def routed(h, weights, order):
    logits = dot(h, dot(columns_of(weights, QKV + D, PACKED), order).astype(low))
    logits = jnp.where(lanes_of(logits.shape) < EXPERTS, logits, -1e30)
    grown = jnp.exp(logits - jnp.max(logits, axis=-1, keepdims=True))
    return grown / jnp.sum(grown, axis=-1, keepdims=True)


def whole_spec(shape):
    return pl.BlockSpec(shape, lambda *_: (0,) * len(shape))


def remote_params(n, number):
    return pltpu.CompilerParams(
        dimension_semantics=("arbitrary",) * n,
        vmem_limit_bytes=BIG,
        collective_id=number,
        has_side_effects=True,
    )


def device(offset):
    names = ("replica", "part", "expert")
    return tuple(lax.axis_index(name) ^ o for name, o in zip(names, offset))


def near(groups, j):
    return (0, j // groups, j % groups)


def greet(offsets):
    barrier = pltpu.get_barrier_semaphore()
    for offset in offsets:
        pl.semaphore_signal(barrier, inc=1, device_id=device(offset), device_id_type=MESH)
    pl.semaphore_wait(barrier, len(offsets))


def remote(source, target, send, receive, offset):
    return pltpu.make_async_remote_copy(
        src_ref=source,
        dst_ref=target,
        send_sem=send,
        recv_sem=receive,
        device_id=device(offset),
        device_id_type=MESH,
    )


def owners_like(replicas, parts):
    return [(r, p, 0) for r in range(replicas) for p in range(0, parts, 2) if (r, p) != (0, 0)]


def owner(parts, offset=(0, 0, 0)):
    return (lax.axis_index("replica") ^ offset[0]) * parts + (lax.axis_index("part") ^ offset[1])


def in_line(replicas, parts):
    return [o for o in owners_like(replicas, parts) if o[1] % 4 == 0]


CORE = (0, 1, 0)
ROW = (0, 2, 0)
GROUPS = 4
EARLY = 5


def all_owners(replicas, parts):
    return [(r, p, 0) for r in range(replicas) for p in range(parts) if (r, p) != (0, 0)]


def wide_part(ref, at, g):
    width = ref.shape[-1] // GROUPS
    return ref.at[at, ..., pl.ds(g * width, width)]


def narrow_part(ref, at, g):
    width = ref.shape[-1] // (2 * GROUPS)
    return ref.at[at, ..., pl.ds(g * width, width)]


def tall_part(ref, at, g):
    depth = ref.shape[-2] // GROUPS
    return ref.at[at, ..., pl.ds(g * depth, depth), :]


def small_part(ref, at, g):
    depth, width = ref.shape[-2] // GROUPS, ref.shape[-1] // 2
    return ref.at[at, ..., pl.ds(g // 2 * depth, depth), pl.ds(g % 2 * width, width)]


def outward(sizes, part_of, source, target, semaphores, g, slot):
    _, parts, _ = sizes
    own = target.shape[1]
    here = owner(parts)

    def block(p):
        return part_of(source, pl.ds((lax.axis_index("part") ^ p) * own, own), g)

    copies = [
        remote(block(o[1]), part_of(target, here, g), semaphores.at[0, slot, i], semaphores.at[1, slot, i], o)
        for i, o in enumerate(all_owners(*sizes[:2]))
    ]
    last = semaphores.at[0, slot, len(copies)]
    return copies + [pltpu.make_async_copy(block(0), part_of(target, here, g), last)]


def across(sizes, part_of, source, target, semaphores, g, slot):
    replicas, parts, _ = sizes

    def rows(r):
        return pl.ds((lax.axis_index("replica") ^ r) * parts, parts)

    return [
        remote(
            part_of(source, rows(r), g), part_of(target, r - 1, g),
            semaphores.at[0, slot, r], semaphores.at[1, slot, r], (r, 0, 0),
        )
        for r in range(1, replicas)
    ]


def homeward(sizes, part_of, source, target, semaphores, g, slot):
    _, parts, _ = sizes
    here = lax.axis_index("part")
    copies = [
        remote(
            part_of(source, here ^ p, g), part_of(target, here, g),
            semaphores.at[0, slot, p], semaphores.at[1, slot, p], (0, p, 0),
        )
        for p in range(1, parts)
    ]
    last = semaphores.at[0, slot, 0]
    return copies + [pltpu.make_async_copy(part_of(source, here, g), part_of(target, here, g), last)]


def partners(sizes):
    replicas, parts, _ = sizes
    return {(0, p, 0) for p in range(1, parts)} | {(r, 0, 0) for r in range(1, replicas)}


def mine_of(sizes, dw_ref):
    return dw_ref.at[pl.ds(lax.axis_index("replica") * sizes[1], sizes[1])]


def add(sizes, mine, others, rows, columns):
    @pl.loop(0, sizes[1])
    def _(p):
        total = mine[p, :, rows, columns].astype(full)
        for r in range(sizes[0] - 1):
            total = total + others[r, p, :, rows, columns].astype(full)
        mine[p, :, rows, columns] = total.astype(low)


def start(copies):
    for copy in copies:
        copy.start()


def wait(copies):
    for copy in copies:
        copy.wait()


def flow_semaphores(sizes, slots):
    return pltpu.SemaphoreType.DMA((2, slots, sizes[0] * sizes[1]))


def swap_slots(groups, keys_ref, blocks, out_ref, sends, receives, local):
    _, count, own, tokens = keys_ref.shape
    slots = lax.broadcasted_iota(jnp.int32, (CAP, tokens), 0).astype(full)

    def build(s, source):
        copies = []
        for j in [*range(1, count), 0]:
            picks = [(keys_ref[s, j, i : i + 1] == slots).astype(low) for i in range(own)]
            picks = jnp.concatenate(picks, axis=0) if own > 1 else picks[0]
            rows = dot(picks, source).astype(low)
            blocks[j, s] = rows.reshape(own, CAP, D)
            if j:
                copy = remote(
                    blocks.at[j, s], out_ref.at[j, s], sends.at[j, s], receives.at[j, s],
                    near(groups, j),
                )
            else:
                copy = pltpu.make_async_copy(blocks.at[0, s], out_ref.at[0, s], local.at[s])
            copy.start()
            copies.append(copy)
        return copies

    return build


def open_kernel(
    sizes, keys_ref, cotangent_ref, tokens_ref, order_ref, shard_ref, raw_one_ref, raw_two_ref,
    x_out, dy_kept, dy_out, h_out, weights_out, first_ref, second_ref, qkv_out, ctx_out, r_out, h_kept, probs_out, theirs_out,
    master_out,
    x_ref, dy_ref, dy_blocks, h_blocks, weights, other_dy, other_h, qkv, ctx, r, h, probs, theirs,
    raw_one, raw_two, master_one, master_two,
    hop, hops, dy_sends, dy_receives, dy_local, h_sends, h_receives, h_local, early, middle, late, here, keeps,
    raws, flow,
):
    replicas, parts, groups = sizes
    count = keys_ref.shape[1]
    images = x_ref.shape[0]
    mirror = (0, parts // 2, 0)
    owners = owners_like(replicas, parts)
    reading = [
        pltpu.make_async_copy(raw_one_ref, raw_one, raws.at[0]),
        pltpu.make_async_copy(raw_two_ref, raw_two, raws.at[1]),
    ]
    start(reading)
    for padded, rows_ref in ((dy_ref, cotangent_ref), (x_ref, tokens_ref)):
        padded[...] = jnp.zeros_like(padded)
        for i in range(images):
            padded[i, :SEQ] = rows_ref[i * SEQ : (i + 1) * SEQ].astype(full).astype(low)
    greet(
        sorted({near(groups, j) for j in range(1, count)} | {mirror, *all_owners(replicas, parts)})
    )
    swap_dy = remote(dy_ref, other_dy, hop.at[0], hop.at[1], mirror)
    swap_dy.start()
    side = lax.axis_index("expert") % 2
    cut_at = (PACKED // LANES + 1) // 2 * LANES

    def half(ref, which):
        return ref.at[:, : PACKED - cut_at] if which == 0 else ref.at[:, PACKED - cut_at :]

    def halves_of(o, which):
        return half(weights.at[owner(parts, o)], which)

    kept = pltpu.make_async_copy(shard_ref, weights.at[owner(parts)], here)
    kept.start()
    to_core = remote(shard_ref, weights.at[owner(parts)], late.at[0, 0, 0], late.at[1, 0, 0], CORE)
    to_core.start()

    def gathers(which):
        return [
            remote(
                half(shard_ref, which), halves_of((0, 0, 0), which), early.at[0, i], early.at[1, i], o
            )
            for i, o in enumerate(owners)
        ]

    def beside(which):
        return [
            remote(
                halves_of(o, which), halves_of(o, which), middle.at[0, i], middle.at[1, i], (0, 0, 1)
            )
            for i, o in enumerate(owners)
        ]

    def onward(which, slot):
        return [
            remote(
                halves_of(o, which), halves_of(o, which), late.at[0, slot, i + 1], late.at[1, slot, i + 1], CORE
            )
            for i, o in enumerate(owners)
        ]

    for which in range(2):
        @pl.when(side == which)
        def _():
            start(gathers(which))

    one = [outward(sizes, wide_part, master_one, first_ref, flow, g, g) for g in range(GROUPS)]
    two = [
        outward(sizes, small_part, master_two, second_ref, flow, g, GROUPS + g)
        for g in range(EARLY)
    ]
    reading[0].wait()

    @pl.loop(0, raw_one.shape[0])
    def _(e):
        master_one[e] = raw_one[e].astype(low)

    start(one[0])
    build_dy = swap_slots(groups, keys_ref, dy_blocks, dy_out, dy_sends, dy_receives, dy_local)
    build_h = swap_slots(groups, keys_ref, h_blocks, h_out, h_sends, h_receives, h_local)
    copies = build_dy(0, dy_ref[...].reshape(images * ROWS, D))
    start(one[1])
    reading[1].wait()

    @pl.loop(0, raw_two.shape[0])
    def _(e):
        master_two[e] = raw_two[e].astype(low)

    for which in range(2):
        @pl.when(side == which)
        def _():
            for a, b, c in zip(gathers(which), beside(which), onward(which, 0)):
                a.wait_recv()
                b.start()
                c.start()

    swap_dy.wait()
    copies += build_dy(1, other_dy[...].reshape(images * ROWS, D))
    for which in range(2):
        @pl.when(side == which)
        def _():
            for b, c in zip(beside(1 - which), onward(1 - which, 1)):
                b.wait_recv()
                c.start()
            for a, b, c, d in zip(gathers(which), beside(which), onward(which, 0), onward(1 - which, 1)):
                a.wait_send()
                b.wait_send()
                c.wait()
                d.wait()

    to_core.wait()
    kept.wait()

    def hop_of(i):
        return remote(h.at[i], other_h.at[i], hops.at[0, i], hops.at[1, i], mirror)

    @pl.loop(0, images)
    def _(i):
        attend(i, weights, order_ref[...], x_ref, qkv, ctx, r, h, probs)
        hop_of(i).start()

    start(one[2])
    start(one[3])
    keeping = [
        pltpu.make_async_copy(source, target, keeps.at[i])
        for i, (source, target) in enumerate(
            [
                (weights, weights_out), (qkv, qkv_out), (ctx, ctx_out), (r, r_out), (h, h_kept),
                (probs, probs_out), (master_two, master_out), (x_ref, x_out), (dy_ref, dy_kept),
            ]
        )
    ]
    start(keeping)
    copies += build_h(0, h[...].reshape(images * ROWS, D))
    start(two[0])
    start(two[1])

    @pl.loop(0, images)
    def _(i):
        hop_of(i).wait()
        theirs[i] = routed(other_h[i], weights, order_ref[...]).astype(low)

    copies += build_h(1, other_h[...].reshape(images * ROWS, D))
    for group in two[2:]:
        start(group)
    last = pltpu.make_async_copy(theirs, theirs_out, keeps.at[9])
    last.start()
    wait(copies)
    wait(keeping)
    last.wait()
    for group in one + two:
        wait(group)


def forward(keys, cotangent, tokens, order, shard, raw_one, raw_two, sizes, number):
    replicas, parts, groups = sizes
    _, count, own, _ = keys.shape
    images = tokens.shape[0] // SEQ
    owners = replicas * parts
    slots = (count, 2, own, CAP, D)
    rows = lambda width: (images, ROWS, width)
    shapes = [
        (rows(D), low), (rows(D), low), (slots, low), (slots, low), ((owners, *shard.shape), low),
        ((owners, own, *raw_one.shape[1:]), low), ((owners, own, *raw_two.shape[1:]), low),
        (rows(QKV), low), (rows(D), low), (rows(D), full), (rows(D), low), (rows(LANES), full), (rows(LANES), low),
        (raw_two.shape, low),
    ]
    buffers = [
        (rows(D), low), (rows(D), low), (slots, low), (slots, low), ((owners, *shard.shape), low), (rows(D), low),
        (rows(D), low),
        (rows(QKV), low), (rows(D), low), (rows(D), full), (rows(D), low), (rows(LANES), full), (rows(LANES), low),
        (raw_one.shape, full), (raw_two.shape, full), (raw_one.shape, low), (raw_two.shape, low),
    ]
    semaphores = [
        (2,), (2, images), (count, 2), (count, 2), (2,), (count, 2), (count, 2), (2,),
        (2, owners // 2 - 1), (2, owners // 2 - 1), (2, 2, owners // 2), (), (10,), (2,),
        (2, GROUPS + EARLY, owners),
    ]
    inner = pl.BlockSpec(memory_space=pltpu.VMEM)
    outer = pl.BlockSpec(memory_space=pl.ANY)
    return pl.pallas_call(
        partial(open_kernel, sizes),
        in_specs=[inner] * 4 + [outer] * 3,
        out_specs=[outer] * len(shapes),
        out_shape=[jax.ShapeDtypeStruct(*shape) for shape in shapes],
        scratch_shapes=[pltpu.VMEM(*b) for b in buffers]
        + [pltpu.SemaphoreType.DMA(n) for n in semaphores],
        compiler_params=pltpu.CompilerParams(
            vmem_limit_bytes=BIG, collective_id=number, has_side_effects=True
        ),
        cost_estimate=pl.CostEstimate(
            flops=60 * 10**9, bytes_accessed=30 * 10**6, transcendentals=2 * 10**6
        ),
        name="forward",
    )(keys, cotangent, tokens, order, shard, raw_one, raw_two)


def chooser(own, j):
    shape = (LANES, own * CAP)
    expert = lax.broadcasted_iota(jnp.int32, shape, 0)
    slot = lax.broadcasted_iota(jnp.int32, shape, 1)
    return (expert == j * own + slot // CAP).astype(low)


def attend_back(i, weights, held, acc, dqkv, dx_ref):
    w_ref, order_ref = weights
    x_ref, qkv_ref, ctx_ref, r_ref, h_ref, probs_ref, dy_ref, dh_ref, dprobs_ref = held
    qkv_acc, proj_acc, router_acc, norm_acc = acc
    rows = pl.ds(pl.multiple_of(i * ROWS, ROWS), ROWS)
    gain_one, bias_one, gain_two, _ = norm_vectors(w_ref)
    probs, dprobs = probs_ref[i], dprobs_ref[rows]
    dlogits = (probs * (dprobs - jnp.sum(probs * dprobs, axis=-1, keepdims=True))).astype(low)
    router_acc[...] += dot_lt(h_ref[i], dlogits)
    router = dot(columns_of(w_ref, QKV + D, PACKED), order_ref[...]).astype(low)
    dh = dh_ref[rows] + dot_rt(dlogits, router)
    normed, factor = normed_rows(r_ref[i])
    norm_acc[2:3] += jnp.sum(dh * normed, axis=0, keepdims=True)
    norm_acc[3:4] += jnp.sum(dh, axis=0, keepdims=True)
    dr = dy_ref[i].astype(full) + norm_back(normed, factor, gain_two, dh)
    dattended = dr.astype(low)
    proj_acc[...] += dot_lt(ctx_ref[i], dattended)
    dctx = dot_rt(dattended, columns_of(w_ref, QKV, QKV + D)).astype(low)
    for pair in range(HEADS // 2):
        at = pair * LANES
        query = halves(qkv_ref[i, :, at : at + LANES])
        key = qkv_ref[i, :, D + at : D + at + LANES]
        keys = halves(key)
        value = qkv_ref[i, :, 2 * D + at : 2 * D + at + LANES]
        dhead = halves(dctx[:, at : at + LANES])
        dq = dk = dv = None
        for e in range(2):
            p = head_probs(query[e], key)
            dp = dot_rt(dhead[e], value)
            ds = (p * (dp - jnp.sum(p * dp, axis=-1, keepdims=True))).astype(low)
            terms = dot(ds, keys[e]), dot_lt(ds, query[e]), dot_lt(p.astype(low), dhead[e])
            dq, dk, dv = terms if dq is None else (dq + terms[0], dk + terms[1], dv + terms[2])
        dqkv[:, at : at + LANES] = (dq * HEAD**-0.5).astype(low)
        dqkv[:, D + at : D + at + LANES] = (dk * HEAD**-0.5).astype(low)
        dqkv[:, 2 * D + at : 2 * D + at + LANES] = dv.astype(low)
    normed, factor = normed_rows(x_ref[i].astype(full))
    attn_in = (normed * gain_one + bias_one).astype(low)
    qkv_acc[...] += dot_lt(attn_in, dqkv[...])
    da = dot_rt(dqkv[...], columns_of(w_ref, 0, QKV))
    norm_acc[0:1] += jnp.sum(da * normed, axis=0, keepdims=True)
    norm_acc[1:2] += jnp.sum(da, axis=0, keepdims=True)
    dx_ref[i] = dr + norm_back(normed, factor, gain_one, da)


def close_kernel(
    sizes, keys_ref, back_ref, w_ref, order_ref, x_ref, qkv_ref, ctx_ref, r_ref, h_ref, probs_ref, dy_ref,
    theirs_ref, y_ref, dw_one_ref,
    dx_ref, out_ref, total_ref, one_ref,
    xs, qkvs, ctxs, rs, hs, ps, dys, their_probs, ys, dh, dprobs, sent, got, sent_gates, got_gates, sent_two, got_two,
    mine_one, others_one,
    dqkv, qkv_acc, proj_acc, router_acc, norm_acc, grads, kept, first, second, along, third,
    loads, y_sends, y_receives, hops, gate_hops, hops_two, flow, home_one,
    core_sems, row_sems, owner_sems, expert_sems,
):
    replicas, parts, groups = sizes
    count, _, own, _, _ = y_ref.shape
    images = x_ref.shape[0]
    width = own * CAP
    half = count * own
    mirror = (0, parts // 2, 0)
    owners = owners_like(replicas, parts)
    sideways = [(0, 0, g) for g in range(1, groups)]
    peers = {near(groups, j) for j in range(1, count)} | {mirror, *sideways, *owners}
    greet(sorted(peers | partners(sizes)))

    pairs_of = [
        (r_ref, rs), (theirs_ref, their_probs), (x_ref, xs), (qkv_ref, qkvs), (ctx_ref, ctxs),
        (h_ref, hs), (probs_ref, ps), (dy_ref, dys),
        (mine_of(sizes, dw_one_ref), mine_one), (y_ref.at[0], ys.at[0]),
    ]
    loading = [
        pltpu.make_async_copy(source, target, loads.at[i])
        for i, (source, target) in enumerate(pairs_of)
    ]
    swaps = [
        [
            remote(y_ref.at[j, s], ys.at[j, s], y_sends.at[j, s], y_receives.at[j, s], near(groups, j))
            for j in range(1, count)
        ]
        for s in range(2)
    ]
    eighths = [
        across(sizes, narrow_part, dw_one_ref, others_one, flow, g, g) for g in range(2 * GROUPS)
    ]
    start(swaps[1])
    start(swaps[0])
    for g in range(GROUPS):
        start(eighths[g])
    start(loading)

    def rows_of(i):
        return pl.ds(pl.multiple_of(i * ROWS, ROWS), ROWS)

    def hop(i):
        rows = rows_of(i)
        return [
            remote(sent.at[rows], got.at[rows], hops.at[0, i], hops.at[1, i], mirror),
            remote(sent_gates.at[i], got_gates.at[i], gate_hops.at[0, i], gate_hops.at[1, i], mirror),
        ]

    near_lanes = lanes_of((2 * half, LANES))
    near_rows = lax.broadcasted_iota(jnp.int32, (2 * half, LANES), 0)

    def hop_two(i):
        rows = rows_of(i)
        return remote(sent_two.at[rows], got_two.at[rows], hops_two.at[0, i], hops_two.at[1, i], mirror)

    def gathered(s, rows):
        slot = (lanes_of((ROWS, width)) % CAP).astype(full)
        lane = lanes_of((ROWS, LANES))
        keys = keys_ref[s, rows]
        total = jnp.zeros((ROWS, D), full)
        change = jnp.zeros((ROWS, LANES), full)
        for j in range(count):
            here = dot(keys, chooser(own, j)) == slot
            total = total + dot(here.astype(low), back_ref[j, s, :, :CAP].reshape(width, D))
            dgate = back_ref[j, s, :, CAP : CAP + 1].astype(full)
            dgate = dgate[:, :, :CAP] + dgate[:, :, CAP : 2 * CAP]
            for e in range(own):
                agreed = jnp.where(here[:, e * CAP : (e + 1) * CAP], dgate[e], 0.0)
                column = jnp.sum(agreed, axis=-1, keepdims=True)
                change = jnp.where(lane == j * own + e, column, change)
        return total, change

    def weighted(s, rows, probs):
        slot = (lanes_of((ROWS, width)) % CAP).astype(full)
        keys = keys_ref[s, rows]
        total = jnp.zeros((ROWS, D), full)
        for j in range(count):
            spread = chooser(own, j)
            gate = jnp.where(dot(keys, spread) == slot, dot(probs, spread), 0.0)
            total = total + dot(gate.astype(low), ys[j, s].reshape(width, D))
        return total

    @pl.loop(0, images)
    def _(i):
        rows = rows_of(i)
        total, change = gathered(1, rows)
        sent[rows] = total.astype(low)
        high = change.astype(low)
        rest = pltpu.roll(change - high.astype(full), half, 1)
        both = (high.astype(full) + rest).astype(low)
        sent_gates[i] = dot_rt((near_lanes == near_rows).astype(low), both).astype(low)
        start(hop(i))

    for g in range(GROUPS, 2 * GROUPS):
        start(eighths[g])

    @pl.loop(0, images)
    def _(i):
        rows = rows_of(i)
        dh[rows], dprobs[rows] = gathered(0, rows)

    wait(loading)
    wait(swaps[1])

    @pl.loop(0, images)
    def _(i):
        rows = rows_of(i)
        sent_two[rows] = weighted(1, rows, their_probs[i]).astype(low)
        hop_two(i).start()

    @pl.loop(0, images)
    def _(i):
        rows = rows_of(i)
        wait(hop(i))
        dh[rows] += got[rows].astype(full)
        place = (near_lanes == half + near_rows % half).astype(low)
        dprobs[rows] += dot_lt(got_gates[i], place)

    each = mine_one.shape[-1] // GROUPS
    homes = []

    def send_home(g):
        wait(eighths[2 * g])
        wait(eighths[2 * g + 1])
        add(sizes, mine_one, others_one, slice(None), slice(g * each, (g + 1) * each))
        copies = homeward(sizes, wide_part, mine_one, one_ref, home_one, g, g)
        start(copies)
        homes.extend(copies)

    send_home(0)
    send_home(1)
    for ref in (qkv_acc, proj_acc, router_acc, norm_acc):
        ref[...] = jnp.zeros_like(ref)

    @pl.loop(0, images)
    def _(i):
        attend_back(
            i, (w_ref, order_ref), (xs, qkvs, ctxs, rs, hs, ps, dys, dh, dprobs),
            (qkv_acc, proj_acc, router_acc, norm_acc), dqkv, dx_ref,
        )

    columns = norm_acc[...].T
    shifted = pltpu.roll(columns, EXPERTS, 1)
    tile = jnp.where(lanes_of(shifted.shape) < EXPERTS, router_acc[...], shifted)
    router_acc[...] = dot_rt(tile.astype(low), order_ref[...])
    depth = grads.shape[1]
    core = lax.axis_index("part") % 2
    blocks = replicas * parts // 2

    @pl.loop(0, 2 * blocks)
    def _(o):
        rows = pl.ds(pl.multiple_of(o * depth, depth), depth)
        grads[o, :, :QKV] = qkv_acc[rows].astype(low)
        grads[o, :, QKV : QKV + D] = proj_acc[rows].astype(low)
        grads[o, :, QKV + D :] = router_acc[rows].astype(low)

    to_core = [
        remote(grads.at[2 * i + 1 - core], first.at[i], core_sems.at[0, i], core_sems.at[1, i], CORE)
        for i in range(blocks)
    ]
    start(to_core)
    for i in range(blocks):
        to_core[i].wait()
        kept[i] = (grads[2 * i + core].astype(full) + first[i].astype(full)).astype(low)
    side = lax.axis_index("part") // 2 % 2
    to_row = [
        remote(kept.at[2 * i + 1 - side], second.at[i], row_sems.at[0, i], row_sems.at[1, i], ROW)
        for i in range(blocks // 2)
    ]
    start(to_row)
    for i in range(blocks // 2):
        to_row[i].wait()
        at = 2 * i + side
        kept[at] = (kept[at].astype(full) + second[i].astype(full)).astype(low)
    to_owner = [
        remote(kept.at[owner(parts, o) // 2], along.at[i], owner_sems.at[0, i], owner_sems.at[1, i], o)
        for i, o in enumerate(in_line(replicas, parts))
    ]
    start(to_owner)

    for g in range(2, GROUPS):
        send_home(g)
    wait(swaps[0])

    @pl.loop(0, images)
    def _(i):
        rows = rows_of(i)
        total = rs[i] + weighted(0, rows, ps[i].astype(low))
        hop_two(i).wait()
        out_ref[rows] = (total + got_two[rows].astype(full)).astype(low)

    total = kept[owner(parts) // 2].astype(full)
    for i, copy in enumerate(to_owner):
        copy.wait()
        total = total + along[i].astype(full)
    me = lax.axis_index("expert")
    third[me] = total.astype(low)
    to_others = [
        remote(third.at[me], third.at[me], expert_sems.at[0, i], expert_sems.at[1, i], o)
        for i, o in enumerate(sideways)
    ]
    start(to_others)
    wait(to_others)
    total = third[0].astype(full)
    for g in range(1, groups):
        total = total + third[g].astype(full)
    total_ref[...] = total
    wait(homes)


def close(keys, back, weights, order, x, qkv, ctx, r, h, probs, dy, theirs, y, dw_one, sizes, number):
    replicas, parts, groups = sizes
    images = x.shape[0]
    tokens = images * ROWS
    count = y.shape[0]
    owners = replicas * parts
    shard = weights.shape[1:]
    one = (parts, *dw_one.shape[1:])
    line = len(in_line(replicas, parts))
    inner = pl.BlockSpec(memory_space=pltpu.VMEM)
    outer = pl.BlockSpec(memory_space=pl.ANY)
    buffers = [
        (x.shape, low), (qkv.shape, low), (ctx.shape, low), (r.shape, full), (x.shape, low),
        (probs.shape, full), (dy.shape, low), (theirs.shape, low), (y.shape, low),
        ((tokens, D), full), ((tokens, LANES), full),
        ((tokens, D), low), ((tokens, D), low), ((images, EXPERTS, ROWS), low), ((images, EXPERTS, ROWS), low),
        ((tokens, D), low), ((tokens, D), low),
        (one, low), ((replicas - 1, *one), low),
        ((ROWS, QKV), low), ((D, QKV), full), ((D, D), full), ((D, LANES), full), ((LANES, D), full),
        ((owners, *shard), low), ((owners // 2, *shard), low), ((owners // 2, *shard), low),
        ((owners // 4, *shard), low), ((line, *shard), low), ((groups, *shard), low),
    ]
    semaphores = [
        (10,), (count, 2), (count, 2), (2, images), (2, images), (2, images), (2, 2 * GROUPS, replicas),
        (2, GROUPS, parts), (2, owners // 2), (2, owners // 4), (2, line), (2, groups - 1),
    ]
    arrays = (
        keys, back, weights, order, x, qkv, ctx, r, h, probs, dy, theirs, y, dw_one,
    )
    return pl.pallas_call(
        partial(close_kernel, sizes),
        in_specs=[inner] * 4 + [outer] * 10,
        out_specs=[inner] * 3 + [outer],
        out_shape=[
            jax.ShapeDtypeStruct((images, ROWS, D), full),
            jax.ShapeDtypeStruct((tokens, D), low),
            jax.ShapeDtypeStruct(shard, full),
            jax.ShapeDtypeStruct(one, low),
        ],
        scratch_shapes=[pltpu.VMEM(*b) for b in buffers]
        + [pltpu.SemaphoreType.DMA(n) for n in semaphores],
        compiler_params=pltpu.CompilerParams(
            vmem_limit_bytes=BIG, collective_id=number, has_side_effects=True
        ),
        cost_estimate=pl.CostEstimate(
            flops=60 * 10**9, bytes_accessed=30 * 10**6, transcendentals=2 * 10**6
        ),
        name="close",
    )(*arrays)


GELU = 0.7978845608028654
CUBE = 0.044715


def gelu_pair(u):
    square = u * u
    bent = jnp.tanh(u * (GELU * CUBE * square + GELU))
    half = 0.5 * bent + 0.5
    value = u * half
    return value, half + value * (1.0 - bent) * (3.0 * GELU * CUBE * square + GELU)


def first_kernel(
    sizes, h_ref, dy_ref, w_ref, wr_ref, sel_ref, master_ref, _, g_ref, slope_ref, dw_ref, second_ref,
    gates, dye_t, flow,
):
    sources = h_ref.shape[0]
    tile = w_ref.shape[3]
    at = pl.program_id(0) * pl.num_programs(1) + pl.program_id(1)

    def moved(g):
        return outward(sizes, small_part, master_ref, second_ref, flow, g, g - EARLY)

    @pl.when(at == 0)
    def _():
        greet(all_owners(*sizes[:2]))
        for g in range(EARLY, 2 * GROUPS):
            start(moved(g))

    @pl.when(pl.program_id(1) == 0)
    def _():
        for k in range(sources):
            rows = slice(k * CAP, (k + 1) * CAP)
            logits = dot(h_ref[k, 0], wr_ref[...])
            logits = jnp.where(lanes_of(logits.shape) < EXPERTS, logits, -1e30)
            grown = jnp.exp(logits - jnp.max(logits, axis=-1, keepdims=True))
            mine = jnp.sum(grown * sel_ref[0], axis=-1, keepdims=True)
            gate = mine / jnp.sum(grown, axis=-1, keepdims=True)
            gates[rows] = jnp.broadcast_to(gate, (CAP, LANES))
            dye_t[:, rows] = (dy_ref[k, 0].astype(full) * gate).T.astype(low)

    w = w_ref[:, 0].reshape(D, tile)
    for k in range(0, sources, 2):
        rows = slice(k * CAP, (k + 2) * CAP)
        value, slope = gelu_pair(dot(h_ref[k : k + 2, 0].reshape(2 * CAP, D), w))
        g_ref[0, rows] = value.astype(low)
        slope_ref[0, rows] = (slope * gates[rows, :1]).astype(low)
    grad = dot(dye_t[...], g_ref[0]).T
    dw_ref[:, 0] = grad.astype(low).reshape(dw_ref.shape[0], dw_ref.shape[2], D)

    @pl.when(at == pl.num_programs(0) * pl.num_programs(1) - 1)
    def _():
        for g in range(EARLY, 2 * GROUPS):
            wait(moved(g))


def slot_spec(sources):
    return pl.BlockSpec((sources, 1, CAP, D), lambda e, f: (0, e, 0, 0))


def expert_first(h, dy, w_in, w_router, select, master, second, sizes, tile, number):
    sources = h.shape[0]
    owners, own, depth, hidden = w_in.shape
    rows = sources * CAP
    per = hidden // owners
    hidden_spec = pl.BlockSpec((1, rows, tile), lambda e, f: (e, 0, f))
    return pl.pallas_call(
        partial(first_kernel, sizes),
        grid=(own, hidden // tile),
        in_specs=[
            slot_spec(sources),
            slot_spec(sources),
            pl.BlockSpec((owners, 1, depth, tile), lambda e, f: (0, e, 0, f)),
            whole_spec(w_router.shape),
            pl.BlockSpec((1, 1, LANES), lambda e, f: (e, 0, 0)),
            pl.BlockSpec(memory_space=pl.ANY),
            pl.BlockSpec(memory_space=pl.ANY),
        ],
        out_specs=[
            hidden_spec,
            hidden_spec,
            pl.BlockSpec((tile // per, 1, per, D), lambda e, f: (f, e, 0, 0)),
            pl.BlockSpec(memory_space=pl.ANY),
        ],
        out_shape=[
            jax.ShapeDtypeStruct((own, rows, hidden), low),
            jax.ShapeDtypeStruct((own, rows, hidden), low),
            jax.ShapeDtypeStruct((owners, own, per, D), low),
            jax.ShapeDtypeStruct(second.shape, low),
        ],
        input_output_aliases={6: 3},
        scratch_shapes=[
            pltpu.VMEM((rows, LANES), full), pltpu.VMEM((D, rows), low), flow_semaphores(sizes, 2 * GROUPS - EARLY),
        ],
        compiler_params=pltpu.CompilerParams(
            dimension_semantics=("arbitrary",) * 2,
            vmem_limit_bytes=BIG,
            collective_id=number,
            has_side_effects=True,
        ),
        cost_estimate=pl.CostEstimate(
            flops=4 * own * rows * D * hidden,
            bytes_accessed=50 * 10**6,
            transcendentals=own * rows * hidden,
        ),
        name="expert_first",
    )(h, dy, w_in, w_router, select, master, second)


def rest_kernel(
    sizes, own, steps, dy_ref, h_ref, g_ref, slope_ref, w_in_ref, w_out_ref, dw_two_ref,
    back_ref, dw_ref, y_ref, two_ref, du, acc, dgates, dgate_rows, h_t, staged, mine_two, others_two,
    sends, receives, local, flow, home, load,
):
    replicas, parts, groups = sizes

    def moved(g):
        return across(sizes, tall_part, dw_two_ref, others_two, flow, g, g)

    def homes(g):
        return homeward(sizes, tall_part, mine_two, two_ref, home, g, g)

    def send_home(g):
        wait(moved(g))
        depth = mine_two.shape[2] // GROUPS
        add(sizes, mine_two, others_two, slice(g * depth, (g + 1) * depth), slice(None))
        start(homes(g))

    loading = pltpu.make_async_copy(mine_of(sizes, dw_two_ref), mine_two, load)

    sources = dy_ref.shape[0]
    tile = slope_ref.shape[2]
    at = pl.program_id(0)
    phase, expert, step = at // (own * steps), at // steps % own, at % steps
    w_in = w_in_ref[:, 0].reshape(D, tile)
    w_out = w_out_ref[:, 0].reshape(tile, D)
    chunk = 2 * CAP

    def copy(k, e):
        return pltpu.make_async_remote_copy(
            src_ref=staged.at[k, e],
            dst_ref=back_ref.at[k, e],
            send_sem=sends.at[k, e],
            recv_sem=receives.at[k, e],
            device_id=device(near(groups, k // 2)),
            device_id_type=MESH,
        )

    def mine(k, e):
        return pltpu.make_async_copy(staged.at[k, e], back_ref.at[k, e], local.at[k, e])

    @pl.when(at == 0)
    def _():
        greet(sorted({near(groups, j) for j in range(1, sources // 2)} | partners(sizes)))
        loading.start()
        start(moved(0))
        start(moved(1))

    @pl.when((phase != 1) & (step == 0))
    def _():
        acc[...] = jnp.zeros_like(acc)

    @pl.when(phase == 0)
    def _():
        @pl.when(step == 0)
        def _():
            dgates[...] = jnp.zeros_like(dgates)

        for k in range(0, sources, 2):
            rows = slice(k * CAP, (k + 2) * CAP)
            dg = dot_rt(dy_ref[k : k + 2, 0].reshape(chunk, D), w_out)
            change = (dg * slope_ref[0, rows].astype(full)).astype(low)
            du[expert * steps + step, rows] = change
            acc[rows] += dot_rt(change, w_in)
            agreed = dg * g_ref[0, rows].astype(full)
            dgates[rows] += sum(agreed[:, i : i + LANES] for i in range(0, tile, LANES))

        @pl.when(step == steps - 1)
        def _():
            sums = dgates[...]
            high = sums.astype(low)
            rest = (sums - high.astype(full)).astype(low)
            ones = jnp.ones((16, LANES), low)
            dgate_rows[...] = dot_rt(ones, high) + dot_rt(ones, rest)
            for k in range(sources):
                rows = slice(k * CAP, (k + 1) * CAP)
                staged[k, expert, :CAP] = acc[rows].astype(low)
                row = dgate_rows[:, rows]
                high = row.astype(low)
                staged[k, expert, CAP:, :CAP] = high
                staged[k, expert, CAP:, CAP : 2 * CAP] = (row - high.astype(full)).astype(low)
                staged[k, expert, CAP:, 2 * CAP :] = jnp.zeros((16, D - 2 * CAP), low)

        for e in range(own):
            @pl.when((step == steps - 1) & (expert == e))
            def _():
                for k in range(2, sources):
                    copy(k, e).start()
                mine(0, e).start()
                mine(1, e).start()

    @pl.when(at == own * steps)
    def _():
        loading.wait()
        send_home(0)
        start(moved(2))

    @pl.when(at == 2 * own * steps)
    def _():
        send_home(1)
        start(moved(3))

    @pl.when(phase == 1)
    def _():
        @pl.when(step == 0)
        def _():
            for k in range(sources):
                h_t[:, k * CAP : (k + 1) * CAP] = h_ref[k, 0].T

        grad = dot(h_t[...], du[expert * steps + step]).astype(low)
        dw_ref[:, 0] = grad.reshape(dw_ref.shape[0], dw_ref.shape[2], tile)

    @pl.when(phase == 2)
    def _():
        for k in range(0, sources, 2):
            rows = slice(k * CAP, (k + 2) * CAP)
            acc[rows] += dot(g_ref[0, rows], w_out)

        @pl.when(step == steps - 1)
        def _():
            y_ref[:, 0] = acc[...].astype(low).reshape(sources, CAP, D)

    @pl.when(at == 3 * own * steps - 1)
    def _():
        send_home(2)
        send_home(3)
        for e in range(own):
            for k in range(2, sources):
                copy(k, e).wait()
            mine(0, e).wait()
            mine(1, e).wait()
        for g in range(GROUPS):
            wait(homes(g))


def expert_rest(dy, h, g, slope, w_in, w_out, dw_two, tile, sizes, number):
    sources, own, _, _ = dy.shape
    owners, _, depth, hidden = w_in.shape
    rows = sources * CAP
    per = hidden // owners
    steps = hidden // tile
    last = own * steps - 1

    def during(phases):
        def find(at):
            if 0 in phases and 2 in phases:
                inside = jnp.where(at // (last + 1) == 1, last, at % (last + 1))
            else:
                inside = jnp.clip(at - phases[0] * (last + 1), 0, last)
            return inside // steps, inside % steps

        return find

    def spec(shape, phases, index, buffers=2):
        return pl.BlockSpec(
            shape, lambda at: index(*during(phases)(at)), pipeline_mode=pl.Buffered(buffers)
        )

    token, hidden_at = (sources, 1, CAP, D), (1, rows, tile)
    whole_expert = lambda e, f: (0, e, 0, 0)
    in_tile = lambda e, f: (0, e, 0, f)
    return pl.pallas_call(
        partial(rest_kernel, sizes, own, steps),
        grid=(3 * own * steps,),
        in_specs=[
            spec(token, (0,), whole_expert, 1),
            spec(token, (1,), whole_expert, 1),
            spec(hidden_at, (0, 2), lambda e, f: (e, 0, f)),
            spec(hidden_at, (0,), lambda e, f: (e, 0, f)),
            spec((owners, 1, depth, tile), (0,), in_tile),
            spec((tile // per, 1, per, D), (0, 2), lambda e, f: (f, e, 0, 0)),
            pl.BlockSpec(memory_space=pl.ANY),
        ],
        out_specs=[
            pl.BlockSpec(memory_space=pl.ANY),
            spec((owners, 1, depth, tile), (1,), in_tile),
            spec(token, (2,), whole_expert, 1),
            pl.BlockSpec(memory_space=pl.ANY),
        ],
        out_shape=[
            jax.ShapeDtypeStruct((sources, own, CAP + 16, D), low),
            jax.ShapeDtypeStruct(w_in.shape, low),
            jax.ShapeDtypeStruct(dy.shape, low),
            jax.ShapeDtypeStruct((sizes[1], *dw_two.shape[1:]), low),
        ],
        scratch_shapes=[
            pltpu.VMEM((own * steps, rows, tile), low),
            pltpu.VMEM((rows, D), full),
            pltpu.VMEM((rows, LANES), full),
            pltpu.VMEM((16, rows), full),
            pltpu.VMEM((D, rows), low),
            pltpu.VMEM((sources, own, CAP + 16, D), low),
            pltpu.VMEM((sizes[1], *dw_two.shape[1:]), low),
            pltpu.VMEM((sizes[0] - 1, sizes[1], *dw_two.shape[1:]), low),
            pltpu.SemaphoreType.DMA((sources, own)),
            pltpu.SemaphoreType.DMA((sources, own)),
            pltpu.SemaphoreType.DMA((2, own)),
            pltpu.SemaphoreType.DMA((2, GROUPS, sizes[0])),
            pltpu.SemaphoreType.DMA((2, GROUPS, sizes[1])),
            pltpu.SemaphoreType.DMA,
        ],
        compiler_params=pltpu.CompilerParams(
            dimension_semantics=("arbitrary",),
            vmem_limit_bytes=BIG,
            collective_id=number,
            has_side_effects=True,
        ),
        cost_estimate=pl.CostEstimate(
            flops=8 * own * rows * D * hidden, bytes_accessed=60 * 10**6, transcendentals=0
        ),
        name="expert_rest",
    )(dy, h, g, slope, w_in, w_out, dw_two)


def experts_kernel(
    sizes, own, steps, h_ref, dy_ref, w_in_ref, wr_ref, sel_ref, master_ref, _,
    back_ref, dw_ref, y_ref, two_ref, second_ref,
    hidden, slopes, acc, column, dgate_rows, turned, staged, dw_two, others, w_tiles,
    sends, receives, local, flow, cross, home, tile_sems,
):
    replicas, parts, groups = sizes
    sources = dy_ref.shape[0]
    tile = hidden.shape[2]
    owners, _, per, _ = dw_two.shape
    span = tile // per
    chunk = 2 * CAP
    at = pl.program_id(0)
    total = own * steps
    phase, expert, step = at // total, at // steps % own, at % steps
    now = at % total
    first_of_mine = lax.axis_index("replica") * parts

    def weight_part(g):
        return outward(sizes, small_part, master_ref, second_ref, flow, g, g - EARLY)

    def tile_copy(t):
        rows = pl.ds(t % steps * span, span)
        return pltpu.make_async_copy(
            second_ref.at[rows, t // steps], w_tiles.at[t % 2], tile_sems.at[t % 2]
        )

    def rows_of(q, count):
        return pl.ds(q * (per // count), per // count)

    def crossing(e, q):
        return [
            remote(
                dw_two.at[pl.ds((lax.axis_index("replica") ^ r) * parts, parts), e, rows_of(q, 4)],
                others.at[r - 1, :, e, rows_of(q, 4)],
                cross.at[0, 4 * e + q, r], cross.at[1, 4 * e + q, r], (r, 0, 0),
            )
            for r in range(1, replicas)
        ]

    def homes(e, q):
        here = lax.axis_index("part")

        def source(p):
            return dw_two.at[first_of_mine + (here ^ p), e, rows_of(q, 2)]

        target = two_ref.at[here, e, rows_of(q, 2)]
        slot = 2 * e + q
        copies = [
            remote(source(p), target, home.at[0, slot, p], home.at[1, slot, p], (0, p, 0))
            for p in range(1, parts)
        ]
        return copies + [pltpu.make_async_copy(source(0), target, home.at[0, slot, 0])]

    def send_home(e, q):
        wait(crossing(e, 2 * q))
        wait(crossing(e, 2 * q + 1))
        rows = slice(q * (per // 2), (q + 1) * (per // 2))

        @pl.loop(0, parts)
        def _(p):
            value = dw_two[first_of_mine + p, e, rows].astype(full)
            for r in range(replicas - 1):
                value = value + others[r, p, e, rows].astype(full)
            dw_two[first_of_mine + p, e, rows] = value.astype(low)

        start(homes(e, q))

    def copy(k, e):
        if k < 2:
            return pltpu.make_async_copy(staged.at[k, e], back_ref.at[k, e], local.at[k, e])
        return remote(
            staged.at[k, e], back_ref.at[k, e], sends.at[k, e], receives.at[k, e], near(groups, k // 2)
        )

    @pl.when(at == 0)
    def _():
        greet(sorted({near(groups, j) for j in range(1, sources // 2)} | {*all_owners(replicas, parts)}))
        for g in range(EARLY, 2 * GROUPS):
            start(weight_part(g))

    @pl.when(phase == 0)
    def _():
        @pl.when(step == 0)
        def _():
            for k in range(sources):
                rows = slice(k * CAP, (k + 1) * CAP)
                logits = dot(h_ref[k, 0], wr_ref[...])
                logits = jnp.where(lanes_of(logits.shape) < EXPERTS, logits, -1e30)
                grown = jnp.exp(logits - jnp.max(logits, axis=-1, keepdims=True))
                mine = jnp.sum(grown * sel_ref[0], axis=-1, keepdims=True)
                gate = mine / jnp.sum(grown, axis=-1, keepdims=True)
                column[rows] = jnp.broadcast_to(gate, (CAP, LANES))
                turned[:, rows] = (dy_ref[k, 0].astype(full) * gate).T.astype(low)

        w_in = w_in_ref[:, 0].reshape(D, tile)
        for k in range(0, sources, 2):
            rows = slice(k * CAP, (k + 2) * CAP)
            value, slope = gelu_pair(dot(h_ref[k : k + 2, 0].reshape(chunk, D), w_in))
            hidden[now, rows] = value.astype(low)
            slopes[now, rows] = (slope * column[rows, :1]).astype(low)
        grad = dot(turned[...], hidden[now]).T.astype(low)
        dw_two[pl.ds(step * span, span), expert] = grad.reshape(span, per, D)

    for e in range(own):
        @pl.when(at == (e + 1) * steps - 1)
        def _():
            if e == own - 1:
                for g in range(EARLY, 2 * GROUPS):
                    wait(weight_part(g))
                tile_copy(0).start()

    @pl.when(phase % 2 == 1)
    def _():
        tile_copy(now).wait()

        @pl.when(now < total - 1)
        def _():
            tile_copy(now + 1).start()

        @pl.when(step == 0)
        def _():
            acc[...] = jnp.zeros_like(acc)

    @pl.when(phase == 1)
    def _():
        @pl.when(step == 0)
        def _():
            column[...] = jnp.zeros_like(column)

        w_in = w_in_ref[:, 0].reshape(D, tile)
        w_out = w_tiles[now % 2].reshape(tile, D)
        for k in range(0, sources, 2):
            rows = slice(k * CAP, (k + 2) * CAP)
            dg = dot_rt(dy_ref[k : k + 2, 0].reshape(chunk, D), w_out)
            change = (dg * slopes[now, rows].astype(full)).astype(low)
            slopes[now, rows] = change
            acc[rows] += dot_rt(change, w_in)
            agreed = dg * hidden[now, rows].astype(full)
            column[rows] += sum(agreed[:, i : i + LANES] for i in range(0, tile, LANES))

        @pl.when(step == steps - 1)
        def _():
            sums = column[...]
            high = sums.astype(low)
            rest = (sums - high.astype(full)).astype(low)
            ones = jnp.ones((16, LANES), low)
            dgate_rows[...] = dot_rt(ones, high) + dot_rt(ones, rest)
            for k in range(sources):
                rows = slice(k * CAP, (k + 1) * CAP)
                staged[k, expert, :CAP] = acc[rows].astype(low)
                row = dgate_rows[:, rows]
                high = row.astype(low)
                staged[k, expert, CAP:, :CAP] = high
                staged[k, expert, CAP:, CAP : 2 * CAP] = (row - high.astype(full)).astype(low)
                staged[k, expert, CAP:, 2 * CAP :] = jnp.zeros((16, D - 2 * CAP), low)

        for e in range(own):
            @pl.when((step == steps - 1) & (expert == e))
            def _():
                for k in range(sources):
                    copy(k, e).start()

    @pl.when(phase == 2)
    def _():
        @pl.when(step == 0)
        def _():
            for k in range(sources):
                turned[:, k * CAP : (k + 1) * CAP] = h_ref[k, 0].T

        grad = dot(turned[...], slopes[now]).astype(low)
        dw_ref[:, 0] = grad.reshape(dw_ref.shape[0], dw_ref.shape[2], tile)

        @pl.when(now == total - 1)
        def _():
            tile_copy(0).start()

    @pl.when(phase == 3)
    def _():
        w_out = w_tiles[now % 2].reshape(tile, D)
        for k in range(0, sources, 2):
            rows = slice(k * CAP, (k + 2) * CAP)
            acc[rows] += dot(hidden[now, rows], w_out)

        @pl.when(step == steps - 1)
        def _():
            y_ref[:, 0] = acc[...].astype(low).reshape(sources, CAP, D)

    for number, turn in enumerate(
        (5, total - 1, total + 2, total + 4, total + 7, 2 * total + 3, 3 * total + 1, 4 * total - 1)
    ):
        @pl.when(at == turn)
        def _():
            start(crossing(number // 4, number % 4))

    for number, turn in enumerate((total + 6, 2 * total + 6)):
        @pl.when(at == turn)
        def _():
            send_home(0, number)

    @pl.when(at == 4 * total - 1)
    def _():
        for e in range(own):
            for k in range(sources):
                copy(k, e).wait()
        send_home(1, 0)
        send_home(1, 1)
        for e in range(own):
            for q in range(2):
                wait(homes(e, q))


def experts(h, dy, w_in, w_router, select, master, second, sizes, tile, number):
    sources = h.shape[0]
    owners, own, depth, width = w_in.shape
    rows = sources * CAP
    per = width // owners
    steps = width // tile
    total = own * steps

    def during(*phases):
        def find(at):
            inside = jnp.where(at // total < phases[0], 0, total - 1)
            for phase in phases:
                inside = jnp.where(at // total == phase, at % total, inside)
            return inside // steps, inside % steps

        return find

    def spec(shape, phases, index, buffers=2):
        return pl.BlockSpec(
            shape, lambda at: index(*during(*phases)(at)), pipeline_mode=pl.Buffered(buffers)
        )

    token = (sources, 1, CAP, D)
    whole_expert = lambda e, f: (0, e, 0, 0)
    in_tile = lambda e, f: (0, e, 0, f)
    outer = pl.BlockSpec(memory_space=pl.ANY)
    two = (sizes[1], own, per, D)
    return pl.pallas_call(
        partial(experts_kernel, sizes, own, steps),
        grid=(4 * total,),
        in_specs=[
            spec(token, (0, 2), whole_expert, 1),
            spec(token, (0, 1), whole_expert, 1),
            spec((owners, 1, depth, tile), (0, 1), in_tile),
            pl.BlockSpec((D, LANES), lambda at: (0, (QKV + D) // LANES)),
            spec((1, 1, LANES), (0,), lambda e, f: (e, 0, 0)),
            outer,
            outer,
        ],
        out_specs=[
            outer,
            spec((owners, 1, depth, tile), (2,), in_tile),
            spec(token, (3,), whole_expert, 1),
            outer,
            outer,
        ],
        out_shape=[
            jax.ShapeDtypeStruct((sources, own, CAP + 16, D), low),
            jax.ShapeDtypeStruct(w_in.shape, low),
            jax.ShapeDtypeStruct((sources, own, CAP, D), low),
            jax.ShapeDtypeStruct(two, low),
            jax.ShapeDtypeStruct(second.shape, low),
        ],
        input_output_aliases={6: 4},
        scratch_shapes=[
            pltpu.VMEM((total, rows, tile), low),
            pltpu.VMEM((total, rows, tile), low),
            pltpu.VMEM((rows, D), full),
            pltpu.VMEM((rows, LANES), full),
            pltpu.VMEM((16, rows), full),
            pltpu.VMEM((D, rows), low),
            pltpu.VMEM((sources, own, CAP + 16, D), low),
            pltpu.VMEM((owners, own, per, D), low),
            pltpu.VMEM((sizes[0] - 1, *two), low),
            pltpu.VMEM((2, tile // per, per, D), low),
            pltpu.SemaphoreType.DMA((sources, own)),
            pltpu.SemaphoreType.DMA((sources, own)),
            pltpu.SemaphoreType.DMA((2, own)),
            flow_semaphores(sizes, 2 * GROUPS - EARLY),
            pltpu.SemaphoreType.DMA((2, 4 * own, sizes[0])),
            pltpu.SemaphoreType.DMA((2, 2 * own, sizes[1])),
            pltpu.SemaphoreType.DMA((2,)),
        ],
        compiler_params=remote_params(1, number),
        cost_estimate=pl.CostEstimate(
            flops=12 * own * rows * D * width, bytes_accessed=40 * 10**6, transcendentals=own * rows * width
        ),
        name="experts",
    )(h, dy, w_in, w_router, select, master, second)


def finish_kernel(out_ref, dx_ref, dense_ref, one_ref, two_ref, output, input_grad, qkv, proj, one, two):
    one[...] = one_ref[...].astype(full)
    two[...] = two_ref[...].astype(full)
    images = dx_ref.shape[0]

    @pl.when(pl.program_id(0) == 0)
    def _():
        qkv[...] = dense_ref[:, :QKV]
        proj[...] = dense_ref[:, QKV : QKV + D]
        for i in range(images):
            input_grad[i * SEQ : (i + 1) * SEQ] = dx_ref[i, :SEQ]
            rows = out_ref[i * ROWS : i * ROWS + SEQ].astype(full)
            output[i * SEQ : (i + 1) * SEQ] = rows.astype(low)


def finish(output, dx, dense, one, two):
    images = dx.shape[0]
    tokens = (images * SEQ, D)
    steps = min(4, one.shape[0])
    widths = [(dense.shape[0], QKV), (dense.shape[0], D)]
    block = lambda a: pl.BlockSpec(
        (a.shape[0] // steps, *a.shape[1:]), lambda i: (i,) + (0,) * (a.ndim - 1)
    )
    return pl.pallas_call(
        finish_kernel,
        grid=(steps,),
        in_specs=[whole_spec(a.shape) for a in (output, dx, dense)] + [block(one), block(two)],
        out_specs=[whole_spec(a) for a in (tokens, tokens, *widths)] + [block(one), block(two)],
        out_shape=[
            jax.ShapeDtypeStruct(tokens, low),
            jax.ShapeDtypeStruct(tokens, full),
            *(jax.ShapeDtypeStruct(a, full) for a in widths),
            jax.ShapeDtypeStruct(one.shape, full),
            jax.ShapeDtypeStruct(two.shape, full),
        ],
        compiler_params=pltpu.CompilerParams(
            dimension_semantics=("arbitrary",), vmem_limit_bytes=BIG
        ),
        cost_estimate=pl.CostEstimate(flops=0, bytes_accessed=19 * 10**6, transcendentals=0),
        name="finish",
    )(output, dx, dense, one, two)


ALL = ("replica", "part")


def body(
    tokens,
    choices,
    ln1_gain,
    ln1_bias,
    w_qkv,
    w_proj,
    ln2_gain,
    ln2_bias,
    w_router,
    w_expert_in,
    w_expert_out,
    cotangent,
):
    replicas, parts, groups = (lax.axis_size(name) for name in ("replica", "part", "expert"))
    owners = replicas * parts
    peers = parts * groups
    own = EXPERTS // peers
    images = tokens.shape[0] // SEQ
    count = images * ROWS
    tile = 512 * 16 // peers

    small_rows = w_router.shape[0]
    placed_router = (
        w_router.reshape(small_rows, groups, parts, own).transpose(0, 2, 1, 3).reshape(small_rows, EXPERTS)
    )
    vectors = jnp.concatenate([ln1_gain, ln1_bias, ln2_gain, ln2_bias]).reshape(4, small_rows).T
    packed = jnp.concatenate(
        [w_qkv, w_proj, placed_router, vectors, jnp.zeros((small_rows, LANES - EXPERTS - 4), full)],
        axis=1,
    )
    packed = lax.optimization_barrier(packed).astype(low)
    me = lax.axis_index("part") * groups + lax.axis_index("expert")
    sizes = (replicas, parts, groups)

    half = parts // 2
    flips = [(i, i ^ half) for i in range(parts)]
    picks = jnp.stack([choices, lax.ppermute(choices, "part", flips)]).reshape(2 * images, SEQ, 2)
    picks = jnp.pad(picks, ((0, 0), (0, ROWS - SEQ), (0, 0)), constant_values=-1)
    picks = picks.reshape(2, count, 2)
    column = jnp.arange(EXPERTS)
    place = (me ^ (column // own)) * own + column % own
    expert = (place // own % groups) * (parts * own) + place // (groups * own) * own + place % own
    lane = jnp.arange(LANES)
    order = jnp.where(lane < EXPERTS, jnp.pad(place, (0, LANES - EXPERTS)), lane)
    order = (lane[:, None] == order[None, :]).astype(low)
    expert = expert[: EXPERTS // 2]
    named = (picks[:, :, :, None] == expert).any(axis=2)
    row = jnp.arange(count)
    earlier = (row[None, :] < row[:, None]).astype(low)
    slots = jnp.einsum("tu,sue->ste", earlier, named.astype(low), preferred_element_type=full)
    keys = jnp.where(named, slots, -1.0)
    key_rows = keys.transpose(0, 2, 1).reshape(2, peers // 2, own, count)
    key_columns = jnp.pad(
        keys, ((0, 0), (0, 0), (0, LANES - EXPERTS // 2)), constant_values=-1
    ).astype(low)

    (
        x, dy, dy_slots, h_slots, weights, first_weight, second_weight, qkv, ctx, r, h, probs, theirs, second_master,
    ) = forward(key_rows, cotangent, tokens, order, packed, w_expert_in, w_expert_out, sizes, 0)
    dy_slots = dy_slots.reshape(peers, own, CAP, D)
    h_slots = h_slots.reshape(peers, own, CAP, D)
    select = ((me * own + jnp.arange(own))[:, None, None] == lane[None, None, :]).astype(full)
    routers = weights.reshape(D, PACKED)
    if own == 2:
        back, dw_first, y, second_grad, _ = experts(
            h_slots, dy_slots, first_weight, routers, select, second_master, second_weight, sizes, tile, 4,
        )
    else:
        g, slope, dw_second, second_weight = expert_first(
            h_slots, dy_slots, first_weight, routers[:, QKV + D :], select, second_master, second_weight,
            sizes, tile, 5,
        )
        back, dw_first, y, second_grad = expert_rest(
            dy_slots, h_slots, g, slope, first_weight, second_weight, dw_second, tile, sizes, 2
        )
    back = back.reshape(peers // 2, 2, own, CAP + 16, D)
    y = y.reshape(peers // 2, 2, own, CAP, D)
    dx, output, grads, first_grad = close(
        key_columns, back, weights, order, x, qkv, ctx, r, h, probs, dy, theirs, y,
        dw_first, sizes, 3,
    )
    output, input_grad, qkv_grad, proj_grad, expert_in_grad, expert_out_grad = finish(
        output, dx, grads, first_grad, second_grad
    )
    router_grad = (
        grads[:, QKV + D : QKV + D + EXPERTS]
        .reshape(small_rows, parts, groups, own)
        .transpose(0, 2, 1, 3)
        .reshape(small_rows, EXPERTS)
    )
    norms = [grads[:, QKV + D + EXPERTS + i] for i in range(4)]

    return (
        output,
        input_grad,
        norms[0],
        norms[1],
        qkv_grad,
        proj_grad,
        norms[2],
        norms[3],
        router_grad,
        expert_in_grad.reshape(w_expert_in.shape),
        expert_out_grad.reshape(w_expert_out.shape),
    )


def solution(mesh):
    dp, groups = mesh.shape["dp"], mesh.shape["expert"]
    parts = min(EXPERTS // groups, dp // 2)
    mesh = Mesh(mesh.devices.reshape(dp // parts, parts, groups), ("replica", "part", "expert"))
    rows = P(("replica", "part", "expert"), None)
    vector, matrix = P(ALL), P(ALL, None)
    experts = P("expert", ALL, None)
    return jax.shard_map(
        body,
        mesh=mesh,
        in_specs=(
            rows, rows, vector, vector, matrix, matrix, vector, vector, matrix, experts, experts, rows,
        ),
        out_specs=(
            rows, rows, vector, vector, matrix, matrix, vector, vector, matrix, experts, experts,
        ),
        check_vma=False,
    )
```

```python
from functools import partial

import jax
import jax.numpy as jnp
from jax import lax
from jax.experimental import pallas as pl
from jax.experimental.pallas import tpu as pltpu
from jax.sharding import Mesh
from jax.sharding import PartitionSpec as P

D = 512
HEADS = 8
EXPERTS = 32
SEQ = 197
CAP = 128
ROWS = 208
HEAD = D // HEADS
LANES = 128
QKV = 3 * D
PACKED = QKV + D + LANES
epsilon = 1e-06
low = jnp.bfloat16
full = jnp.float32
MESH = pl.DeviceIdType.MESH
BIG = 63 * 1024 * 1024


def dot(left, right):
    return jnp.dot(left, right, preferred_element_type=full)


def dot_rt(left, right):
    return lax.dot_general(left, right, (((1,), (1,)), ((), ())), preferred_element_type=full)


def dot_lt(left, right):
    return lax.dot_general(left, right, (((0,), (0,)), ((), ())), preferred_element_type=full)


def lanes_of(shape):
    return lax.broadcasted_iota(jnp.int32, shape, len(shape) - 1)


def normed_rows(values):
    center = values - jnp.mean(values, axis=-1, keepdims=True)
    factor = lax.rsqrt(jnp.mean(center * center, axis=-1, keepdims=True) + epsilon)
    return center * factor, factor


def norm_back(normed, factor, gain_vec, upstream):
    scaled = upstream * gain_vec
    return factor * (
        scaled
        - jnp.mean(scaled, axis=-1, keepdims=True)
        - normed * jnp.mean(scaled * normed, axis=-1, keepdims=True)
    )


def columns_of(weights_ref, start_at, end):
    return weights_ref[:, :, start_at:end].reshape(D, end - start_at)


def norm_vectors(weights_ref):
    rows = columns_of(weights_ref, QKV + D, PACKED).astype(full).T
    return [rows[EXPERTS + i : EXPERTS + i + 1] for i in range(4)]


def halves(pair):
    first = lanes_of(pair.shape) < HEAD
    zero = jnp.zeros_like(pair)
    return jnp.where(first, pair, zero), jnp.where(first, zero, pair)


def head_probs(query, key_pair):
    scores = dot_rt(query, key_pair) * (HEAD**-0.5)
    scores = jnp.where(lanes_of(scores.shape) < SEQ, scores, -1e30)
    grown = jnp.exp(scores - jnp.max(scores, axis=-1, keepdims=True))
    return grown / jnp.sum(grown, axis=-1, keepdims=True)


def attend(i, weights, order, x_ref, qkv_ref, ctx_ref, r_ref, h_ref, probs_ref):
    gain_one, bias_one, gain_two, bias_two = norm_vectors(weights)
    x = x_ref[i].astype(full)
    normed, _ = normed_rows(x)
    attn_in = (normed * gain_one + bias_one).astype(low)
    qkv_ref[i] = dot(attn_in, columns_of(weights, 0, QKV)).astype(low)
    for pair in range(HEADS // 2):
        at = pair * LANES
        query = halves(qkv_ref[i, :, at : at + LANES])
        key = qkv_ref[i, :, D + at : D + at + LANES]
        value = halves(qkv_ref[i, :, 2 * D + at : 2 * D + at + LANES])
        total = None
        for e in range(2):
            part = dot(head_probs(query[e], key).astype(low), value[e])
            total = part if total is None else total + part
        ctx_ref[i, :, at : at + LANES] = total.astype(low)
    r = x + dot(ctx_ref[i], columns_of(weights, QKV, QKV + D))
    r_ref[i] = r
    normed, _ = normed_rows(r)
    h = (normed * gain_two + bias_two).astype(low)
    h_ref[i] = h
    probs_ref[i] = routed(h, weights, order)


def routed(h, weights, order):
    logits = dot(h, dot(columns_of(weights, QKV + D, PACKED), order).astype(low))
    logits = jnp.where(lanes_of(logits.shape) < EXPERTS, logits, -1e30)
    grown = jnp.exp(logits - jnp.max(logits, axis=-1, keepdims=True))
    return grown / jnp.sum(grown, axis=-1, keepdims=True)


def whole_spec(shape):
    return pl.BlockSpec(shape, lambda *_: (0,) * len(shape))


def remote_params(n, number):
    return pltpu.CompilerParams(
        dimension_semantics=("arbitrary",) * n,
        vmem_limit_bytes=BIG,
        collective_id=number,
        has_side_effects=True,
    )


def device(offset):
    names = ("replica", "part", "expert")
    return tuple(lax.axis_index(name) ^ o for name, o in zip(names, offset))


def near(groups, j):
    return (0, j // groups, j % groups)


def greet(offsets):
    barrier = pltpu.get_barrier_semaphore()
    for offset in offsets:
        pl.semaphore_signal(barrier, inc=1, device_id=device(offset), device_id_type=MESH)
    pl.semaphore_wait(barrier, len(offsets))


def remote(source, target, send, receive, offset):
    return pltpu.make_async_remote_copy(
        src_ref=source,
        dst_ref=target,
        send_sem=send,
        recv_sem=receive,
        device_id=device(offset),
        device_id_type=MESH,
    )


def owners_like(replicas, parts):
    return [(r, p, 0) for r in range(replicas) for p in range(0, parts, 2) if (r, p) != (0, 0)]


def owner(parts, offset=(0, 0, 0)):
    return (lax.axis_index("replica") ^ offset[0]) * parts + (lax.axis_index("part") ^ offset[1])


def in_line(replicas, parts):
    return [o for o in owners_like(replicas, parts) if o[1] % 4 == 0]


CORE = (0, 1, 0)
ROW = (0, 2, 0)
GROUPS = 4
EARLY = 5


def all_owners(replicas, parts):
    return [(r, p, 0) for r in range(replicas) for p in range(parts) if (r, p) != (0, 0)]


def wide_part(ref, at, g):
    width = ref.shape[-1] // GROUPS
    return ref.at[at, ..., pl.ds(g * width, width)]


def narrow_part(ref, at, g):
    width = ref.shape[-1] // (2 * GROUPS)
    return ref.at[at, ..., pl.ds(g * width, width)]


def tall_part(ref, at, g):
    depth = ref.shape[-2] // GROUPS
    return ref.at[at, ..., pl.ds(g * depth, depth), :]


def small_part(ref, at, g):
    depth, width = ref.shape[-2] // GROUPS, ref.shape[-1] // 2
    return ref.at[at, ..., pl.ds(g // 2 * depth, depth), pl.ds(g % 2 * width, width)]


def outward(sizes, part_of, source, target, semaphores, g, slot):
    _, parts, _ = sizes
    own = target.shape[1]
    here = owner(parts)

    def block(p):
        return part_of(source, pl.ds((lax.axis_index("part") ^ p) * own, own), g)

    copies = [
        remote(block(o[1]), part_of(target, here, g), semaphores.at[0, slot, i], semaphores.at[1, slot, i], o)
        for i, o in enumerate(all_owners(*sizes[:2]))
    ]
    last = semaphores.at[0, slot, len(copies)]
    return copies + [pltpu.make_async_copy(block(0), part_of(target, here, g), last)]


def across(sizes, part_of, source, target, semaphores, g, slot):
    replicas, parts, _ = sizes

    def rows(r):
        return pl.ds((lax.axis_index("replica") ^ r) * parts, parts)

    return [
        remote(
            part_of(source, rows(r), g), part_of(target, r - 1, g),
            semaphores.at[0, slot, r], semaphores.at[1, slot, r], (r, 0, 0),
        )
        for r in range(1, replicas)
    ]


def homeward(sizes, part_of, source, target, semaphores, g, slot):
    _, parts, _ = sizes
    here = lax.axis_index("part")
    copies = [
        remote(
            part_of(source, here ^ p, g), part_of(target, here, g),
            semaphores.at[0, slot, p], semaphores.at[1, slot, p], (0, p, 0),
        )
        for p in range(1, parts)
    ]
    last = semaphores.at[0, slot, 0]
    return copies + [pltpu.make_async_copy(part_of(source, here, g), part_of(target, here, g), last)]


def partners(sizes):
    replicas, parts, _ = sizes
    return {(0, p, 0) for p in range(1, parts)} | {(r, 0, 0) for r in range(1, replicas)}


def mine_of(sizes, dw_ref):
    return dw_ref.at[pl.ds(lax.axis_index("replica") * sizes[1], sizes[1])]


def add(sizes, mine, others, rows, columns):
    @pl.loop(0, sizes[1])
    def _(p):
        total = mine[p, :, rows, columns].astype(full)
        for r in range(sizes[0] - 1):
            total = total + others[r, p, :, rows, columns].astype(full)
        mine[p, :, rows, columns] = total.astype(low)


def start(copies):
    for copy in copies:
        copy.start()


def wait(copies):
    for copy in copies:
        copy.wait()


def flow_semaphores(sizes, slots):
    return pltpu.SemaphoreType.DMA((2, slots, sizes[0] * sizes[1]))


def swap_slots(groups, keys_ref, blocks, out_ref, sends, receives, local):
    _, count, own, tokens = keys_ref.shape
    slots = lax.broadcasted_iota(jnp.int32, (CAP, tokens), 0).astype(full)

    def build(s, source):
        copies = []
        for j in [*range(1, count), 0]:
            picks = [(keys_ref[s, j, i : i + 1] == slots).astype(low) for i in range(own)]
            picks = jnp.concatenate(picks, axis=0) if own > 1 else picks[0]
            rows = dot(picks, source).astype(low)
            blocks[j, s] = rows.reshape(own, CAP, D)
            if j:
                copy = remote(
                    blocks.at[j, s], out_ref.at[j, s], sends.at[j, s], receives.at[j, s],
                    near(groups, j),
                )
            else:
                copy = pltpu.make_async_copy(blocks.at[0, s], out_ref.at[0, s], local.at[s])
            copy.start()
            copies.append(copy)
        return copies

    return build


def open_kernel(
    sizes, keys_ref, cotangent_ref, tokens_ref, order_ref, shard_ref, raw_one_ref, raw_two_ref,
    x_out, dy_kept, dy_out, h_out, weights_out, first_ref, second_ref, qkv_out, ctx_out, r_out, h_kept, probs_out, theirs_out,
    master_out,
    x_ref, dy_ref, dy_blocks, h_blocks, weights, other_dy, other_h, qkv, ctx, r, h, probs, theirs,
    raw_one, raw_two, master_one, master_two,
    hop, hops, dy_sends, dy_receives, dy_local, h_sends, h_receives, h_local, early, middle, late, here, keeps,
    raws, flow,
):
    replicas, parts, groups = sizes
    count = keys_ref.shape[1]
    images = x_ref.shape[0]
    mirror = (0, parts // 2, 0)
    owners = owners_like(replicas, parts)
    reading = [
        pltpu.make_async_copy(raw_one_ref, raw_one, raws.at[0]),
        pltpu.make_async_copy(raw_two_ref, raw_two, raws.at[1]),
    ]
    start(reading)
    for padded, rows_ref in ((dy_ref, cotangent_ref), (x_ref, tokens_ref)):
        padded[...] = jnp.zeros_like(padded)
        for i in range(images):
            padded[i, :SEQ] = rows_ref[i * SEQ : (i + 1) * SEQ].astype(full).astype(low)
    greet(
        sorted({near(groups, j) for j in range(1, count)} | {mirror, *all_owners(replicas, parts)})
    )
    swap_dy = remote(dy_ref, other_dy, hop.at[0], hop.at[1], mirror)
    swap_dy.start()
    side = lax.axis_index("expert") % 2
    cut_at = (PACKED // LANES + 1) // 2 * LANES

    def half(ref, which):
        return ref.at[:, : PACKED - cut_at] if which == 0 else ref.at[:, PACKED - cut_at :]

    def halves_of(o, which):
        return half(weights.at[owner(parts, o)], which)

    kept = pltpu.make_async_copy(shard_ref, weights.at[owner(parts)], here)
    kept.start()
    to_core = remote(shard_ref, weights.at[owner(parts)], late.at[0, 0, 0], late.at[1, 0, 0], CORE)
    to_core.start()

    def gathers(which):
        return [
            remote(
                half(shard_ref, which), halves_of((0, 0, 0), which), early.at[0, i], early.at[1, i], o
            )
            for i, o in enumerate(owners)
        ]

    def beside(which):
        return [
            remote(
                halves_of(o, which), halves_of(o, which), middle.at[0, i], middle.at[1, i], (0, 0, 1)
            )
            for i, o in enumerate(owners)
        ]

    def onward(which, slot):
        return [
            remote(
                halves_of(o, which), halves_of(o, which), late.at[0, slot, i + 1], late.at[1, slot, i + 1], CORE
            )
            for i, o in enumerate(owners)
        ]

    for which in range(2):
        @pl.when(side == which)
        def _():
            start(gathers(which))

    one = [outward(sizes, wide_part, master_one, first_ref, flow, g, g) for g in range(GROUPS)]
    two = [
        outward(sizes, small_part, master_two, second_ref, flow, g, GROUPS + g)
        for g in range(EARLY)
    ]
    reading[0].wait()

    @pl.loop(0, raw_one.shape[0])
    def _(e):
        master_one[e] = raw_one[e].astype(low)

    start(one[0])
    build_dy = swap_slots(groups, keys_ref, dy_blocks, dy_out, dy_sends, dy_receives, dy_local)
    build_h = swap_slots(groups, keys_ref, h_blocks, h_out, h_sends, h_receives, h_local)
    copies = build_dy(0, dy_ref[...].reshape(images * ROWS, D))
    start(one[1])
    reading[1].wait()

    @pl.loop(0, raw_two.shape[0])
    def _(e):
        master_two[e] = raw_two[e].astype(low)

    for which in range(2):
        @pl.when(side == which)
        def _():
            for a, b, c in zip(gathers(which), beside(which), onward(which, 0)):
                a.wait_recv()
                b.start()
                c.start()

    swap_dy.wait()
    copies += build_dy(1, other_dy[...].reshape(images * ROWS, D))
    for which in range(2):
        @pl.when(side == which)
        def _():
            for b, c in zip(beside(1 - which), onward(1 - which, 1)):
                b.wait_recv()
                c.start()
            for a, b, c, d in zip(gathers(which), beside(which), onward(which, 0), onward(1 - which, 1)):
                a.wait_send()
                b.wait_send()
                c.wait()
                d.wait()

    to_core.wait()
    kept.wait()

    def hop_of(i):
        return remote(h.at[i], other_h.at[i], hops.at[0, i], hops.at[1, i], mirror)

    @pl.loop(0, images)
    def _(i):
        attend(i, weights, order_ref[...], x_ref, qkv, ctx, r, h, probs)
        hop_of(i).start()

    start(one[2])
    start(one[3])
    keeping = [
        pltpu.make_async_copy(source, target, keeps.at[i])
        for i, (source, target) in enumerate(
            [
                (weights, weights_out), (qkv, qkv_out), (ctx, ctx_out), (r, r_out), (h, h_kept),
                (probs, probs_out), (master_two, master_out), (x_ref, x_out), (dy_ref, dy_kept),
            ]
        )
    ]
    start(keeping)
    copies += build_h(0, h[...].reshape(images * ROWS, D))
    start(two[0])
    start(two[1])

    @pl.loop(0, images)
    def _(i):
        hop_of(i).wait()
        theirs[i] = routed(other_h[i], weights, order_ref[...]).astype(low)

    copies += build_h(1, other_h[...].reshape(images * ROWS, D))
    for group in two[2:]:
        start(group)
    last = pltpu.make_async_copy(theirs, theirs_out, keeps.at[9])
    last.start()
    wait(copies)
    wait(keeping)
    last.wait()
    for group in one + two:
        wait(group)


def forward(keys, cotangent, tokens, order, shard, raw_one, raw_two, sizes, number):
    replicas, parts, groups = sizes
    _, count, own, _ = keys.shape
    images = tokens.shape[0] // SEQ
    owners = replicas * parts
    slots = (count, 2, own, CAP, D)
    rows = lambda width: (images, ROWS, width)
    shapes = [
        (rows(D), low), (rows(D), low), (slots, low), (slots, low), ((owners, *shard.shape), low),
        ((owners, own, *raw_one.shape[1:]), low), ((owners, own, *raw_two.shape[1:]), low),
        (rows(QKV), low), (rows(D), low), (rows(D), full), (rows(D), low), (rows(LANES), full), (rows(LANES), low),
        (raw_two.shape, low),
    ]
    buffers = [
        (rows(D), low), (rows(D), low), (slots, low), (slots, low), ((owners, *shard.shape), low), (rows(D), low),
        (rows(D), low),
        (rows(QKV), low), (rows(D), low), (rows(D), full), (rows(D), low), (rows(LANES), full), (rows(LANES), low),
        (raw_one.shape, full), (raw_two.shape, full), (raw_one.shape, low), (raw_two.shape, low),
    ]
    semaphores = [
        (2,), (2, images), (count, 2), (count, 2), (2,), (count, 2), (count, 2), (2,),
        (2, owners // 2 - 1), (2, owners // 2 - 1), (2, 2, owners // 2), (), (10,), (2,),
        (2, GROUPS + EARLY, owners),
    ]
    inner = pl.BlockSpec(memory_space=pltpu.VMEM)
    outer = pl.BlockSpec(memory_space=pl.ANY)
    return pl.pallas_call(
        partial(open_kernel, sizes),
        in_specs=[inner] * 4 + [outer] * 3,
        out_specs=[outer] * len(shapes),
        out_shape=[jax.ShapeDtypeStruct(*shape) for shape in shapes],
        scratch_shapes=[pltpu.VMEM(*b) for b in buffers]
        + [pltpu.SemaphoreType.DMA(n) for n in semaphores],
        compiler_params=pltpu.CompilerParams(
            vmem_limit_bytes=BIG, collective_id=number, has_side_effects=True
        ),
        cost_estimate=pl.CostEstimate(
            flops=60 * 10**9, bytes_accessed=30 * 10**6, transcendentals=2 * 10**6
        ),
        name="forward",
    )(keys, cotangent, tokens, order, shard, raw_one, raw_two)


def chooser(own, j):
    shape = (LANES, own * CAP)
    expert = lax.broadcasted_iota(jnp.int32, shape, 0)
    slot = lax.broadcasted_iota(jnp.int32, shape, 1)
    return (expert == j * own + slot // CAP).astype(low)


def attend_back(i, weights, held, acc, dqkv, dx_ref):
    w_ref, order_ref = weights
    x_ref, qkv_ref, ctx_ref, r_ref, h_ref, probs_ref, dy_ref, dh_ref, dprobs_ref = held
    qkv_acc, proj_acc, router_acc, norm_acc = acc
    rows = pl.ds(pl.multiple_of(i * ROWS, ROWS), ROWS)
    gain_one, bias_one, gain_two, _ = norm_vectors(w_ref)
    probs, dprobs = probs_ref[i], dprobs_ref[rows]
    dlogits = (probs * (dprobs - jnp.sum(probs * dprobs, axis=-1, keepdims=True))).astype(low)
    router_acc[...] += dot_lt(h_ref[i], dlogits)
    router = dot(columns_of(w_ref, QKV + D, PACKED), order_ref[...]).astype(low)
    dh = dh_ref[rows] + dot_rt(dlogits, router)
    normed, factor = normed_rows(r_ref[i])
    norm_acc[2:3] += jnp.sum(dh * normed, axis=0, keepdims=True)
    norm_acc[3:4] += jnp.sum(dh, axis=0, keepdims=True)
    dr = dy_ref[i].astype(full) + norm_back(normed, factor, gain_two, dh)
    dattended = dr.astype(low)
    proj_acc[...] += dot_lt(ctx_ref[i], dattended)
    dctx = dot_rt(dattended, columns_of(w_ref, QKV, QKV + D)).astype(low)
    for pair in range(HEADS // 2):
        at = pair * LANES
        query = halves(qkv_ref[i, :, at : at + LANES])
        key = qkv_ref[i, :, D + at : D + at + LANES]
        keys = halves(key)
        value = qkv_ref[i, :, 2 * D + at : 2 * D + at + LANES]
        dhead = halves(dctx[:, at : at + LANES])
        dq = dk = dv = None
        for e in range(2):
            p = head_probs(query[e], key)
            dp = dot_rt(dhead[e], value)
            ds = (p * (dp - jnp.sum(p * dp, axis=-1, keepdims=True))).astype(low)
            terms = dot(ds, keys[e]), dot_lt(ds, query[e]), dot_lt(p.astype(low), dhead[e])
            dq, dk, dv = terms if dq is None else (dq + terms[0], dk + terms[1], dv + terms[2])
        dqkv[:, at : at + LANES] = (dq * HEAD**-0.5).astype(low)
        dqkv[:, D + at : D + at + LANES] = (dk * HEAD**-0.5).astype(low)
        dqkv[:, 2 * D + at : 2 * D + at + LANES] = dv.astype(low)
    normed, factor = normed_rows(x_ref[i].astype(full))
    attn_in = (normed * gain_one + bias_one).astype(low)
    qkv_acc[...] += dot_lt(attn_in, dqkv[...])
    da = dot_rt(dqkv[...], columns_of(w_ref, 0, QKV))
    norm_acc[0:1] += jnp.sum(da * normed, axis=0, keepdims=True)
    norm_acc[1:2] += jnp.sum(da, axis=0, keepdims=True)
    dx_ref[i] = dr + norm_back(normed, factor, gain_one, da)


def close_kernel(
    sizes, keys_ref, back_ref, w_ref, order_ref, x_ref, qkv_ref, ctx_ref, r_ref, h_ref, probs_ref, dy_ref,
    theirs_ref, y_ref, dw_one_ref,
    dx_ref, out_ref, total_ref, one_ref,
    xs, qkvs, ctxs, rs, hs, ps, dys, their_probs, ys, dh, dprobs, sent, got, sent_gates, got_gates, sent_two, got_two,
    mine_one, others_one,
    dqkv, qkv_acc, proj_acc, router_acc, norm_acc, grads, kept, first, second, along, third,
    loads, y_sends, y_receives, hops, gate_hops, hops_two, flow, home_one,
    core_sems, row_sems, owner_sems, expert_sems,
):
    replicas, parts, groups = sizes
    count, _, own, _, _ = y_ref.shape
    images = x_ref.shape[0]
    width = own * CAP
    half = count * own
    mirror = (0, parts // 2, 0)
    owners = owners_like(replicas, parts)
    sideways = [(0, 0, g) for g in range(1, groups)]
    peers = {near(groups, j) for j in range(1, count)} | {mirror, *sideways, *owners}
    greet(sorted(peers | partners(sizes)))

    pairs_of = [
        (r_ref, rs), (theirs_ref, their_probs), (x_ref, xs), (qkv_ref, qkvs), (ctx_ref, ctxs),
        (h_ref, hs), (probs_ref, ps), (dy_ref, dys),
        (mine_of(sizes, dw_one_ref), mine_one), (y_ref.at[0], ys.at[0]),
    ]
    loading = [
        pltpu.make_async_copy(source, target, loads.at[i])
        for i, (source, target) in enumerate(pairs_of)
    ]
    swaps = [
        [
            remote(y_ref.at[j, s], ys.at[j, s], y_sends.at[j, s], y_receives.at[j, s], near(groups, j))
            for j in range(1, count)
        ]
        for s in range(2)
    ]
    eighths = [
        across(sizes, narrow_part, dw_one_ref, others_one, flow, g, g) for g in range(2 * GROUPS)
    ]
    start(swaps[1])
    start(swaps[0])
    for g in range(GROUPS):
        start(eighths[g])
    start(loading)

    def rows_of(i):
        return pl.ds(pl.multiple_of(i * ROWS, ROWS), ROWS)

    def hop(i):
        rows = rows_of(i)
        return [
            remote(sent.at[rows], got.at[rows], hops.at[0, i], hops.at[1, i], mirror),
            remote(sent_gates.at[i], got_gates.at[i], gate_hops.at[0, i], gate_hops.at[1, i], mirror),
        ]

    near_lanes = lanes_of((2 * half, LANES))
    near_rows = lax.broadcasted_iota(jnp.int32, (2 * half, LANES), 0)

    def hop_two(i):
        rows = rows_of(i)
        return remote(sent_two.at[rows], got_two.at[rows], hops_two.at[0, i], hops_two.at[1, i], mirror)

    def gathered(s, rows):
        slot = (lanes_of((ROWS, width)) % CAP).astype(full)
        lane = lanes_of((ROWS, LANES))
        keys = keys_ref[s, rows]
        total = jnp.zeros((ROWS, D), full)
        change = jnp.zeros((ROWS, LANES), full)
        for j in range(count):
            here = dot(keys, chooser(own, j)) == slot
            total = total + dot(here.astype(low), back_ref[j, s, :, :CAP].reshape(width, D))
            dgate = back_ref[j, s, :, CAP : CAP + 1].astype(full)
            dgate = dgate[:, :, :CAP] + dgate[:, :, CAP : 2 * CAP]
            for e in range(own):
                agreed = jnp.where(here[:, e * CAP : (e + 1) * CAP], dgate[e], 0.0)
                column = jnp.sum(agreed, axis=-1, keepdims=True)
                change = jnp.where(lane == j * own + e, column, change)
        return total, change

    def weighted(s, rows, probs):
        slot = (lanes_of((ROWS, width)) % CAP).astype(full)
        keys = keys_ref[s, rows]
        total = jnp.zeros((ROWS, D), full)
        for j in range(count):
            spread = chooser(own, j)
            gate = jnp.where(dot(keys, spread) == slot, dot(probs, spread), 0.0)
            total = total + dot(gate.astype(low), ys[j, s].reshape(width, D))
        return total

    @pl.loop(0, images)
    def _(i):
        rows = rows_of(i)
        total, change = gathered(1, rows)
        sent[rows] = total.astype(low)
        high = change.astype(low)
        rest = pltpu.roll(change - high.astype(full), half, 1)
        both = (high.astype(full) + rest).astype(low)
        sent_gates[i] = dot_rt((near_lanes == near_rows).astype(low), both).astype(low)
        start(hop(i))

    for g in range(GROUPS, 2 * GROUPS):
        start(eighths[g])

    @pl.loop(0, images)
    def _(i):
        rows = rows_of(i)
        dh[rows], dprobs[rows] = gathered(0, rows)

    wait(loading)
    wait(swaps[1])

    @pl.loop(0, images)
    def _(i):
        rows = rows_of(i)
        sent_two[rows] = weighted(1, rows, their_probs[i]).astype(low)
        hop_two(i).start()

    @pl.loop(0, images)
    def _(i):
        rows = rows_of(i)
        wait(hop(i))
        dh[rows] += got[rows].astype(full)
        place = (near_lanes == half + near_rows % half).astype(low)
        dprobs[rows] += dot_lt(got_gates[i], place)

    each = mine_one.shape[-1] // GROUPS
    homes = []

    def send_home(g):
        wait(eighths[2 * g])
        wait(eighths[2 * g + 1])
        add(sizes, mine_one, others_one, slice(None), slice(g * each, (g + 1) * each))
        copies = homeward(sizes, wide_part, mine_one, one_ref, home_one, g, g)
        start(copies)
        homes.extend(copies)

    send_home(0)
    send_home(1)
    for ref in (qkv_acc, proj_acc, router_acc, norm_acc):
        ref[...] = jnp.zeros_like(ref)

    @pl.loop(0, images)
    def _(i):
        attend_back(
            i, (w_ref, order_ref), (xs, qkvs, ctxs, rs, hs, ps, dys, dh, dprobs),
            (qkv_acc, proj_acc, router_acc, norm_acc), dqkv, dx_ref,
        )

    columns = norm_acc[...].T
    shifted = pltpu.roll(columns, EXPERTS, 1)
    tile = jnp.where(lanes_of(shifted.shape) < EXPERTS, router_acc[...], shifted)
    router_acc[...] = dot_rt(tile.astype(low), order_ref[...])
    depth = grads.shape[1]
    core = lax.axis_index("part") % 2
    blocks = replicas * parts // 2

    @pl.loop(0, 2 * blocks)
    def _(o):
        rows = pl.ds(pl.multiple_of(o * depth, depth), depth)
        grads[o, :, :QKV] = qkv_acc[rows].astype(low)
        grads[o, :, QKV : QKV + D] = proj_acc[rows].astype(low)
        grads[o, :, QKV + D :] = router_acc[rows].astype(low)

    to_core = [
        remote(grads.at[2 * i + 1 - core], first.at[i], core_sems.at[0, i], core_sems.at[1, i], CORE)
        for i in range(blocks)
    ]
    start(to_core)
    for i in range(blocks):
        to_core[i].wait()
        kept[i] = (grads[2 * i + core].astype(full) + first[i].astype(full)).astype(low)
    side = lax.axis_index("part") // 2 % 2
    to_row = [
        remote(kept.at[2 * i + 1 - side], second.at[i], row_sems.at[0, i], row_sems.at[1, i], ROW)
        for i in range(blocks // 2)
    ]
    start(to_row)
    for i in range(blocks // 2):
        to_row[i].wait()
        at = 2 * i + side
        kept[at] = (kept[at].astype(full) + second[i].astype(full)).astype(low)
    to_owner = [
        remote(kept.at[owner(parts, o) // 2], along.at[i], owner_sems.at[0, i], owner_sems.at[1, i], o)
        for i, o in enumerate(in_line(replicas, parts))
    ]
    start(to_owner)

    for g in range(2, GROUPS):
        send_home(g)
    wait(swaps[0])

    @pl.loop(0, images)
    def _(i):
        rows = rows_of(i)
        total = rs[i] + weighted(0, rows, ps[i].astype(low))
        hop_two(i).wait()
        out_ref[rows] = (total + got_two[rows].astype(full)).astype(low)

    total = kept[owner(parts) // 2].astype(full)
    for i, copy in enumerate(to_owner):
        copy.wait()
        total = total + along[i].astype(full)
    me = lax.axis_index("expert")
    third[me] = total.astype(low)
    to_others = [
        remote(third.at[me], third.at[me], expert_sems.at[0, i], expert_sems.at[1, i], o)
        for i, o in enumerate(sideways)
    ]
    start(to_others)
    wait(to_others)
    total = third[0].astype(full)
    for g in range(1, groups):
        total = total + third[g].astype(full)
    total_ref[...] = total
    wait(homes)


def close(keys, back, weights, order, x, qkv, ctx, r, h, probs, dy, theirs, y, dw_one, sizes, number):
    replicas, parts, groups = sizes
    images = x.shape[0]
    tokens = images * ROWS
    count = y.shape[0]
    owners = replicas * parts
    shard = weights.shape[1:]
    one = (parts, *dw_one.shape[1:])
    line = len(in_line(replicas, parts))
    inner = pl.BlockSpec(memory_space=pltpu.VMEM)
    outer = pl.BlockSpec(memory_space=pl.ANY)
    buffers = [
        (x.shape, low), (qkv.shape, low), (ctx.shape, low), (r.shape, full), (x.shape, low),
        (probs.shape, full), (dy.shape, low), (theirs.shape, low), (y.shape, low),
        ((tokens, D), full), ((tokens, LANES), full),
        ((tokens, D), low), ((tokens, D), low), ((images, EXPERTS, ROWS), low), ((images, EXPERTS, ROWS), low),
        ((tokens, D), low), ((tokens, D), low),
        (one, low), ((replicas - 1, *one), low),
        ((ROWS, QKV), low), ((D, QKV), full), ((D, D), full), ((D, LANES), full), ((LANES, D), full),
        ((owners, *shard), low), ((owners // 2, *shard), low), ((owners // 2, *shard), low),
        ((owners // 4, *shard), low), ((line, *shard), low), ((groups, *shard), low),
    ]
    semaphores = [
        (10,), (count, 2), (count, 2), (2, images), (2, images), (2, images), (2, 2 * GROUPS, replicas),
        (2, GROUPS, parts), (2, owners // 2), (2, owners // 4), (2, line), (2, groups - 1),
    ]
    arrays = (
        keys, back, weights, order, x, qkv, ctx, r, h, probs, dy, theirs, y, dw_one,
    )
    return pl.pallas_call(
        partial(close_kernel, sizes),
        in_specs=[inner] * 4 + [outer] * 10,
        out_specs=[inner] * 3 + [outer],
        out_shape=[
            jax.ShapeDtypeStruct((images, ROWS, D), full),
            jax.ShapeDtypeStruct((tokens, D), low),
            jax.ShapeDtypeStruct(shard, full),
            jax.ShapeDtypeStruct(one, low),
        ],
        scratch_shapes=[pltpu.VMEM(*b) for b in buffers]
        + [pltpu.SemaphoreType.DMA(n) for n in semaphores],
        compiler_params=pltpu.CompilerParams(
            vmem_limit_bytes=BIG, collective_id=number, has_side_effects=True
        ),
        cost_estimate=pl.CostEstimate(
            flops=60 * 10**9, bytes_accessed=30 * 10**6, transcendentals=2 * 10**6
        ),
        name="close",
    )(*arrays)


GELU = 0.7978845608028654
CUBE = 0.044715


def gelu_pair(u):
    square = u * u
    bent = jnp.tanh(u * (GELU * CUBE * square + GELU))
    half = 0.5 * bent + 0.5
    value = u * half
    return value, half + value * (1.0 - bent) * (3.0 * GELU * CUBE * square + GELU)


def first_kernel(
    sizes, h_ref, dy_ref, w_ref, wr_ref, sel_ref, master_ref, _, g_ref, slope_ref, dw_ref, second_ref,
    gates, dye_t, flow,
):
    sources = h_ref.shape[0]
    tile = w_ref.shape[3]
    at = pl.program_id(0) * pl.num_programs(1) + pl.program_id(1)

    def moved(g):
        return outward(sizes, small_part, master_ref, second_ref, flow, g, g - EARLY)

    @pl.when(at == 0)
    def _():
        greet(all_owners(*sizes[:2]))
        for g in range(EARLY, 2 * GROUPS):
            start(moved(g))

    @pl.when(pl.program_id(1) == 0)
    def _():
        for k in range(sources):
            rows = slice(k * CAP, (k + 1) * CAP)
            logits = dot(h_ref[k, 0], wr_ref[...])
            logits = jnp.where(lanes_of(logits.shape) < EXPERTS, logits, -1e30)
            grown = jnp.exp(logits - jnp.max(logits, axis=-1, keepdims=True))
            mine = jnp.sum(grown * sel_ref[0], axis=-1, keepdims=True)
            gate = mine / jnp.sum(grown, axis=-1, keepdims=True)
            gates[rows] = jnp.broadcast_to(gate, (CAP, LANES))
            dye_t[:, rows] = (dy_ref[k, 0].astype(full) * gate).T.astype(low)

    w = w_ref[:, 0].reshape(D, tile)
    for k in range(0, sources, 2):
        rows = slice(k * CAP, (k + 2) * CAP)
        value, slope = gelu_pair(dot(h_ref[k : k + 2, 0].reshape(2 * CAP, D), w))
        g_ref[0, rows] = value.astype(low)
        slope_ref[0, rows] = (slope * gates[rows, :1]).astype(low)
    grad = dot(dye_t[...], g_ref[0]).T
    dw_ref[:, 0] = grad.astype(low).reshape(dw_ref.shape[0], dw_ref.shape[2], D)

    @pl.when(at == pl.num_programs(0) * pl.num_programs(1) - 1)
    def _():
        for g in range(EARLY, 2 * GROUPS):
            wait(moved(g))


def slot_spec(sources):
    return pl.BlockSpec((sources, 1, CAP, D), lambda e, f: (0, e, 0, 0))


def expert_first(h, dy, w_in, w_router, select, master, second, sizes, tile, number):
    sources = h.shape[0]
    owners, own, depth, hidden = w_in.shape
    rows = sources * CAP
    per = hidden // owners
    hidden_spec = pl.BlockSpec((1, rows, tile), lambda e, f: (e, 0, f))
    return pl.pallas_call(
        partial(first_kernel, sizes),
        grid=(own, hidden // tile),
        in_specs=[
            slot_spec(sources),
            slot_spec(sources),
            pl.BlockSpec((owners, 1, depth, tile), lambda e, f: (0, e, 0, f)),
            whole_spec(w_router.shape),
            pl.BlockSpec((1, 1, LANES), lambda e, f: (e, 0, 0)),
            pl.BlockSpec(memory_space=pl.ANY),
            pl.BlockSpec(memory_space=pl.ANY),
        ],
        out_specs=[
            hidden_spec,
            hidden_spec,
            pl.BlockSpec((tile // per, 1, per, D), lambda e, f: (f, e, 0, 0)),
            pl.BlockSpec(memory_space=pl.ANY),
        ],
        out_shape=[
            jax.ShapeDtypeStruct((own, rows, hidden), low),
            jax.ShapeDtypeStruct((own, rows, hidden), low),
            jax.ShapeDtypeStruct((owners, own, per, D), low),
            jax.ShapeDtypeStruct(second.shape, low),
        ],
        input_output_aliases={6: 3},
        scratch_shapes=[
            pltpu.VMEM((rows, LANES), full), pltpu.VMEM((D, rows), low), flow_semaphores(sizes, 2 * GROUPS - EARLY),
        ],
        compiler_params=pltpu.CompilerParams(
            dimension_semantics=("arbitrary",) * 2,
            vmem_limit_bytes=BIG,
            collective_id=number,
            has_side_effects=True,
        ),
        cost_estimate=pl.CostEstimate(
            flops=4 * own * rows * D * hidden,
            bytes_accessed=50 * 10**6,
            transcendentals=own * rows * hidden,
        ),
        name="expert_first",
    )(h, dy, w_in, w_router, select, master, second)


def rest_kernel(
    sizes, own, steps, dy_ref, h_ref, g_ref, slope_ref, w_in_ref, w_out_ref, dw_two_ref,
    back_ref, dw_ref, y_ref, two_ref, du, acc, dgates, dgate_rows, h_t, staged, mine_two, others_two,
    sends, receives, local, flow, home, load,
):
    replicas, parts, groups = sizes

    def moved(g):
        return across(sizes, tall_part, dw_two_ref, others_two, flow, g, g)

    def homes(g):
        return homeward(sizes, tall_part, mine_two, two_ref, home, g, g)

    def send_home(g):
        wait(moved(g))
        depth = mine_two.shape[2] // GROUPS
        add(sizes, mine_two, others_two, slice(g * depth, (g + 1) * depth), slice(None))
        start(homes(g))

    loading = pltpu.make_async_copy(mine_of(sizes, dw_two_ref), mine_two, load)

    sources = dy_ref.shape[0]
    tile = slope_ref.shape[2]
    at = pl.program_id(0)
    phase, expert, step = at // (own * steps), at // steps % own, at % steps
    w_in = w_in_ref[:, 0].reshape(D, tile)
    w_out = w_out_ref[:, 0].reshape(tile, D)
    chunk = 2 * CAP

    def copy(k, e):
        return pltpu.make_async_remote_copy(
            src_ref=staged.at[k, e],
            dst_ref=back_ref.at[k, e],
            send_sem=sends.at[k, e],
            recv_sem=receives.at[k, e],
            device_id=device(near(groups, k // 2)),
            device_id_type=MESH,
        )

    def mine(k, e):
        return pltpu.make_async_copy(staged.at[k, e], back_ref.at[k, e], local.at[k, e])

    @pl.when(at == 0)
    def _():
        greet(sorted({near(groups, j) for j in range(1, sources // 2)} | partners(sizes)))
        loading.start()
        start(moved(0))
        start(moved(1))

    @pl.when((phase != 1) & (step == 0))
    def _():
        acc[...] = jnp.zeros_like(acc)

    @pl.when(phase == 0)
    def _():
        @pl.when(step == 0)
        def _():
            dgates[...] = jnp.zeros_like(dgates)

        for k in range(0, sources, 2):
            rows = slice(k * CAP, (k + 2) * CAP)
            dg = dot_rt(dy_ref[k : k + 2, 0].reshape(chunk, D), w_out)
            change = (dg * slope_ref[0, rows].astype(full)).astype(low)
            du[expert * steps + step, rows] = change
            acc[rows] += dot_rt(change, w_in)
            agreed = dg * g_ref[0, rows].astype(full)
            dgates[rows] += sum(agreed[:, i : i + LANES] for i in range(0, tile, LANES))

        @pl.when(step == steps - 1)
        def _():
            sums = dgates[...]
            high = sums.astype(low)
            rest = (sums - high.astype(full)).astype(low)
            ones = jnp.ones((16, LANES), low)
            dgate_rows[...] = dot_rt(ones, high) + dot_rt(ones, rest)
            for k in range(sources):
                rows = slice(k * CAP, (k + 1) * CAP)
                staged[k, expert, :CAP] = acc[rows].astype(low)
                row = dgate_rows[:, rows]
                high = row.astype(low)
                staged[k, expert, CAP:, :CAP] = high
                staged[k, expert, CAP:, CAP : 2 * CAP] = (row - high.astype(full)).astype(low)
                staged[k, expert, CAP:, 2 * CAP :] = jnp.zeros((16, D - 2 * CAP), low)

        for e in range(own):
            @pl.when((step == steps - 1) & (expert == e))
            def _():
                for k in range(2, sources):
                    copy(k, e).start()
                mine(0, e).start()
                mine(1, e).start()

    @pl.when(at == own * steps)
    def _():
        loading.wait()
        send_home(0)
        start(moved(2))

    @pl.when(at == 2 * own * steps)
    def _():
        send_home(1)
        start(moved(3))

    @pl.when(phase == 1)
    def _():
        @pl.when(step == 0)
        def _():
            for k in range(sources):
                h_t[:, k * CAP : (k + 1) * CAP] = h_ref[k, 0].T

        grad = dot(h_t[...], du[expert * steps + step]).astype(low)
        dw_ref[:, 0] = grad.reshape(dw_ref.shape[0], dw_ref.shape[2], tile)

    @pl.when(phase == 2)
    def _():
        for k in range(0, sources, 2):
            rows = slice(k * CAP, (k + 2) * CAP)
            acc[rows] += dot(g_ref[0, rows], w_out)

        @pl.when(step == steps - 1)
        def _():
            y_ref[:, 0] = acc[...].astype(low).reshape(sources, CAP, D)

    @pl.when(at == 3 * own * steps - 1)
    def _():
        send_home(2)
        send_home(3)
        for e in range(own):
            for k in range(2, sources):
                copy(k, e).wait()
            mine(0, e).wait()
            mine(1, e).wait()
        for g in range(GROUPS):
            wait(homes(g))


def expert_rest(dy, h, g, slope, w_in, w_out, dw_two, tile, sizes, number):
    sources, own, _, _ = dy.shape
    owners, _, depth, hidden = w_in.shape
    rows = sources * CAP
    per = hidden // owners
    steps = hidden // tile
    last = own * steps - 1

    def during(phases):
        def find(at):
            if 0 in phases and 2 in phases:
                inside = jnp.where(at // (last + 1) == 1, last, at % (last + 1))
            else:
                inside = jnp.clip(at - phases[0] * (last + 1), 0, last)
            return inside // steps, inside % steps

        return find

    def spec(shape, phases, index, buffers=2):
        return pl.BlockSpec(
            shape, lambda at: index(*during(phases)(at)), pipeline_mode=pl.Buffered(buffers)
        )

    token, hidden_at = (sources, 1, CAP, D), (1, rows, tile)
    whole_expert = lambda e, f: (0, e, 0, 0)
    in_tile = lambda e, f: (0, e, 0, f)
    return pl.pallas_call(
        partial(rest_kernel, sizes, own, steps),
        grid=(3 * own * steps,),
        in_specs=[
            spec(token, (0,), whole_expert, 1),
            spec(token, (1,), whole_expert, 1),
            spec(hidden_at, (0, 2), lambda e, f: (e, 0, f)),
            spec(hidden_at, (0,), lambda e, f: (e, 0, f)),
            spec((owners, 1, depth, tile), (0,), in_tile),
            spec((tile // per, 1, per, D), (0, 2), lambda e, f: (f, e, 0, 0)),
            pl.BlockSpec(memory_space=pl.ANY),
        ],
        out_specs=[
            pl.BlockSpec(memory_space=pl.ANY),
            spec((owners, 1, depth, tile), (1,), in_tile),
            spec(token, (2,), whole_expert, 1),
            pl.BlockSpec(memory_space=pl.ANY),
        ],
        out_shape=[
            jax.ShapeDtypeStruct((sources, own, CAP + 16, D), low),
            jax.ShapeDtypeStruct(w_in.shape, low),
            jax.ShapeDtypeStruct(dy.shape, low),
            jax.ShapeDtypeStruct((sizes[1], *dw_two.shape[1:]), low),
        ],
        scratch_shapes=[
            pltpu.VMEM((own * steps, rows, tile), low),
            pltpu.VMEM((rows, D), full),
            pltpu.VMEM((rows, LANES), full),
            pltpu.VMEM((16, rows), full),
            pltpu.VMEM((D, rows), low),
            pltpu.VMEM((sources, own, CAP + 16, D), low),
            pltpu.VMEM((sizes[1], *dw_two.shape[1:]), low),
            pltpu.VMEM((sizes[0] - 1, sizes[1], *dw_two.shape[1:]), low),
            pltpu.SemaphoreType.DMA((sources, own)),
            pltpu.SemaphoreType.DMA((sources, own)),
            pltpu.SemaphoreType.DMA((2, own)),
            pltpu.SemaphoreType.DMA((2, GROUPS, sizes[0])),
            pltpu.SemaphoreType.DMA((2, GROUPS, sizes[1])),
            pltpu.SemaphoreType.DMA,
        ],
        compiler_params=pltpu.CompilerParams(
            dimension_semantics=("arbitrary",),
            vmem_limit_bytes=BIG,
            collective_id=number,
            has_side_effects=True,
        ),
        cost_estimate=pl.CostEstimate(
            flops=8 * own * rows * D * hidden, bytes_accessed=60 * 10**6, transcendentals=0
        ),
        name="expert_rest",
    )(dy, h, g, slope, w_in, w_out, dw_two)


def experts_kernel(
    sizes, own, steps, h_ref, dy_ref, w_in_ref, wr_ref, sel_ref, master_ref, _,
    back_ref, dw_ref, y_ref, two_ref, second_ref,
    hidden, slopes, acc, column, dgate_rows, turned, staged, dw_two, others, w_tiles,
    sends, receives, local, flow, cross, home, tile_sems,
):
    replicas, parts, groups = sizes
    sources = dy_ref.shape[0]
    tile = hidden.shape[2]
    owners, _, per, _ = dw_two.shape
    span = tile // per
    chunk = 2 * CAP
    at = pl.program_id(0)
    total = own * steps
    phase, expert, step = at // total, at // steps % own, at % steps
    now = at % total
    first_of_mine = lax.axis_index("replica") * parts

    def weight_part(g):
        return outward(sizes, small_part, master_ref, second_ref, flow, g, g - EARLY)

    def tile_copy(t):
        rows = pl.ds(t % steps * span, span)
        return pltpu.make_async_copy(
            second_ref.at[rows, t // steps], w_tiles.at[t % 2], tile_sems.at[t % 2]
        )

    def rows_of(q, count):
        return pl.ds(q * (per // count), per // count)

    def crossing(e, q):
        return [
            remote(
                dw_two.at[pl.ds((lax.axis_index("replica") ^ r) * parts, parts), e, rows_of(q, 4)],
                others.at[r - 1, :, e, rows_of(q, 4)],
                cross.at[0, 4 * e + q, r], cross.at[1, 4 * e + q, r], (r, 0, 0),
            )
            for r in range(1, replicas)
        ]

    def homes(e, q):
        here = lax.axis_index("part")

        def source(p):
            return dw_two.at[first_of_mine + (here ^ p), e, rows_of(q, 2)]

        target = two_ref.at[here, e, rows_of(q, 2)]
        slot = 2 * e + q
        copies = [
            remote(source(p), target, home.at[0, slot, p], home.at[1, slot, p], (0, p, 0))
            for p in range(1, parts)
        ]
        return copies + [pltpu.make_async_copy(source(0), target, home.at[0, slot, 0])]

    def send_home(e, q):
        wait(crossing(e, 2 * q))
        wait(crossing(e, 2 * q + 1))
        rows = slice(q * (per // 2), (q + 1) * (per // 2))

        @pl.loop(0, parts)
        def _(p):
            value = dw_two[first_of_mine + p, e, rows].astype(full)
            for r in range(replicas - 1):
                value = value + others[r, p, e, rows].astype(full)
            dw_two[first_of_mine + p, e, rows] = value.astype(low)

        start(homes(e, q))

    def copy(k, e):
        if k < 2:
            return pltpu.make_async_copy(staged.at[k, e], back_ref.at[k, e], local.at[k, e])
        return remote(
            staged.at[k, e], back_ref.at[k, e], sends.at[k, e], receives.at[k, e], near(groups, k // 2)
        )

    @pl.when(at == 0)
    def _():
        greet(sorted({near(groups, j) for j in range(1, sources // 2)} | {*all_owners(replicas, parts)}))
        for g in range(EARLY, 2 * GROUPS):
            start(weight_part(g))

    @pl.when(phase == 0)
    def _():
        @pl.when(step == 0)
        def _():
            for k in range(sources):
                rows = slice(k * CAP, (k + 1) * CAP)
                logits = dot(h_ref[k, 0], wr_ref[...])
                logits = jnp.where(lanes_of(logits.shape) < EXPERTS, logits, -1e30)
                grown = jnp.exp(logits - jnp.max(logits, axis=-1, keepdims=True))
                mine = jnp.sum(grown * sel_ref[0], axis=-1, keepdims=True)
                gate = mine / jnp.sum(grown, axis=-1, keepdims=True)
                column[rows] = jnp.broadcast_to(gate, (CAP, LANES))
                turned[:, rows] = (dy_ref[k, 0].astype(full) * gate).T.astype(low)

        w_in = w_in_ref[:, 0].reshape(D, tile)
        for k in range(0, sources, 2):
            rows = slice(k * CAP, (k + 2) * CAP)
            value, slope = gelu_pair(dot(h_ref[k : k + 2, 0].reshape(chunk, D), w_in))
            hidden[now, rows] = value.astype(low)
            slopes[now, rows] = (slope * column[rows, :1]).astype(low)
        grad = dot(turned[...], hidden[now]).T.astype(low)
        dw_two[pl.ds(step * span, span), expert] = grad.reshape(span, per, D)

    for e in range(own):
        @pl.when(at == (e + 1) * steps - 1)
        def _():
            if e == own - 1:
                for g in range(EARLY, 2 * GROUPS):
                    wait(weight_part(g))
                tile_copy(0).start()

    @pl.when(phase % 2 == 1)
    def _():
        tile_copy(now).wait()

        @pl.when(now < total - 1)
        def _():
            tile_copy(now + 1).start()

        @pl.when(step == 0)
        def _():
            acc[...] = jnp.zeros_like(acc)

    @pl.when(phase == 1)
    def _():
        @pl.when(step == 0)
        def _():
            column[...] = jnp.zeros_like(column)

        w_in = w_in_ref[:, 0].reshape(D, tile)
        w_out = w_tiles[now % 2].reshape(tile, D)
        for k in range(0, sources, 2):
            rows = slice(k * CAP, (k + 2) * CAP)
            dg = dot_rt(dy_ref[k : k + 2, 0].reshape(chunk, D), w_out)
            change = (dg * slopes[now, rows].astype(full)).astype(low)
            slopes[now, rows] = change
            acc[rows] += dot_rt(change, w_in)
            agreed = dg * hidden[now, rows].astype(full)
            column[rows] += sum(agreed[:, i : i + LANES] for i in range(0, tile, LANES))

        @pl.when(step == steps - 1)
        def _():
            sums = column[...]
            high = sums.astype(low)
            rest = (sums - high.astype(full)).astype(low)
            ones = jnp.ones((16, LANES), low)
            dgate_rows[...] = dot_rt(ones, high) + dot_rt(ones, rest)
            for k in range(sources):
                rows = slice(k * CAP, (k + 1) * CAP)
                staged[k, expert, :CAP] = acc[rows].astype(low)
                row = dgate_rows[:, rows]
                high = row.astype(low)
                staged[k, expert, CAP:, :CAP] = high
                staged[k, expert, CAP:, CAP : 2 * CAP] = (row - high.astype(full)).astype(low)
                staged[k, expert, CAP:, 2 * CAP :] = jnp.zeros((16, D - 2 * CAP), low)

        for e in range(own):
            @pl.when((step == steps - 1) & (expert == e))
            def _():
                for k in range(sources):
                    copy(k, e).start()

    @pl.when(phase == 2)
    def _():
        @pl.when(step == 0)
        def _():
            for k in range(sources):
                turned[:, k * CAP : (k + 1) * CAP] = h_ref[k, 0].T

        grad = dot(turned[...], slopes[now]).astype(low)
        dw_ref[:, 0] = grad.reshape(dw_ref.shape[0], dw_ref.shape[2], tile)

        @pl.when(now == total - 1)
        def _():
            tile_copy(0).start()

    @pl.when(phase == 3)
    def _():
        w_out = w_tiles[now % 2].reshape(tile, D)
        for k in range(0, sources, 2):
            rows = slice(k * CAP, (k + 2) * CAP)
            acc[rows] += dot(hidden[now, rows], w_out)

        @pl.when(step == steps - 1)
        def _():
            y_ref[:, 0] = acc[...].astype(low).reshape(sources, CAP, D)

    for number, turn in enumerate(
        (5, total - 1, total + 2, total + 4, total + 7, 2 * total + 3, 3 * total + 1, 4 * total - 1)
    ):
        @pl.when(at == turn)
        def _():
            start(crossing(number // 4, number % 4))

    for number, turn in enumerate((total + 6, 2 * total + 6)):
        @pl.when(at == turn)
        def _():
            send_home(0, number)

    @pl.when(at == 4 * total - 1)
    def _():
        for e in range(own):
            for k in range(sources):
                copy(k, e).wait()
        send_home(1, 0)
        send_home(1, 1)
        for e in range(own):
            for q in range(2):
                wait(homes(e, q))


def experts(h, dy, w_in, w_router, select, master, second, sizes, tile, number):
    sources = h.shape[0]
    owners, own, depth, width = w_in.shape
    rows = sources * CAP
    per = width // owners
    steps = width // tile
    total = own * steps

    def during(*phases):
        def find(at):
            inside = jnp.where(at // total < phases[0], 0, total - 1)
            for phase in phases:
                inside = jnp.where(at // total == phase, at % total, inside)
            return inside // steps, inside % steps

        return find

    def spec(shape, phases, index, buffers=2):
        return pl.BlockSpec(
            shape, lambda at: index(*during(*phases)(at)), pipeline_mode=pl.Buffered(buffers)
        )

    token = (sources, 1, CAP, D)
    whole_expert = lambda e, f: (0, e, 0, 0)
    in_tile = lambda e, f: (0, e, 0, f)
    outer = pl.BlockSpec(memory_space=pl.ANY)
    two = (sizes[1], own, per, D)
    return pl.pallas_call(
        partial(experts_kernel, sizes, own, steps),
        grid=(4 * total,),
        in_specs=[
            spec(token, (0, 2), whole_expert, 1),
            spec(token, (0, 1), whole_expert, 1),
            spec((owners, 1, depth, tile), (0, 1), in_tile),
            pl.BlockSpec((D, LANES), lambda at: (0, (QKV + D) // LANES)),
            spec((1, 1, LANES), (0,), lambda e, f: (e, 0, 0)),
            outer,
            outer,
        ],
        out_specs=[
            outer,
            spec((owners, 1, depth, tile), (2,), in_tile),
            spec(token, (3,), whole_expert, 1),
            outer,
            outer,
        ],
        out_shape=[
            jax.ShapeDtypeStruct((sources, own, CAP + 16, D), low),
            jax.ShapeDtypeStruct(w_in.shape, low),
            jax.ShapeDtypeStruct((sources, own, CAP, D), low),
            jax.ShapeDtypeStruct(two, low),
            jax.ShapeDtypeStruct(second.shape, low),
        ],
        input_output_aliases={6: 4},
        scratch_shapes=[
            pltpu.VMEM((total, rows, tile), low),
            pltpu.VMEM((total, rows, tile), low),
            pltpu.VMEM((rows, D), full),
            pltpu.VMEM((rows, LANES), full),
            pltpu.VMEM((16, rows), full),
            pltpu.VMEM((D, rows), low),
            pltpu.VMEM((sources, own, CAP + 16, D), low),
            pltpu.VMEM((owners, own, per, D), low),
            pltpu.VMEM((sizes[0] - 1, *two), low),
            pltpu.VMEM((2, tile // per, per, D), low),
            pltpu.SemaphoreType.DMA((sources, own)),
            pltpu.SemaphoreType.DMA((sources, own)),
            pltpu.SemaphoreType.DMA((2, own)),
            flow_semaphores(sizes, 2 * GROUPS - EARLY),
            pltpu.SemaphoreType.DMA((2, 4 * own, sizes[0])),
            pltpu.SemaphoreType.DMA((2, 2 * own, sizes[1])),
            pltpu.SemaphoreType.DMA((2,)),
        ],
        compiler_params=remote_params(1, number),
        cost_estimate=pl.CostEstimate(
            flops=12 * own * rows * D * width, bytes_accessed=40 * 10**6, transcendentals=own * rows * width
        ),
        name="experts",
    )(h, dy, w_in, w_router, select, master, second)


def finish_kernel(
    sizes, out_ref, dx_ref, dense_ref, one_ref, two_ref,
    output, input_grad, qkv, proj, router, norms, one, two,
):
    one[...] = one_ref[...].astype(full)
    two[...] = two_ref[...].astype(full)
    images = dx_ref.shape[0]

    @pl.when(pl.program_id(0) == 0)
    def _():
        qkv[...] = dense_ref[:, :QKV]
        proj[...] = dense_ref[:, QKV : QKV + D]
        _, parts, groups = sizes
        own = EXPERTS // (parts * groups)
        tile = dense_ref[:, QKV + D :]
        place = lax.broadcasted_iota(jnp.int32, (LANES, EXPERTS), 0)
        expert = lanes_of((LANES, EXPERTS))
        group, part = expert // (parts * own), expert // own % parts
        moved = place == (part * groups + group) * own + expert % own
        router[...] = jnp.dot(
            tile, moved.astype(full), preferred_element_type=full, precision=lax.Precision.HIGHEST
        )
        norms[...] = tile.T[EXPERTS : EXPERTS + 8]
        for i in range(images):
            input_grad[i * SEQ : (i + 1) * SEQ] = dx_ref[i, :SEQ]
            rows = out_ref[i * ROWS : i * ROWS + SEQ].astype(full)
            output[i * SEQ : (i + 1) * SEQ] = rows.astype(low)


def finish(output, dx, dense, one, two, sizes):
    images = dx.shape[0]
    tokens = (images * SEQ, D)
    steps = min(4, one.shape[0])
    depth = dense.shape[0]
    widths = [(depth, QKV), (depth, D), (depth, EXPERTS), (8, depth)]
    block = lambda a: pl.BlockSpec(
        (a.shape[0] // steps, *a.shape[1:]), lambda i: (i,) + (0,) * (a.ndim - 1)
    )
    return pl.pallas_call(
        partial(finish_kernel, sizes),
        grid=(steps,),
        in_specs=[whole_spec(a.shape) for a in (output, dx, dense)] + [block(one), block(two)],
        out_specs=[whole_spec(a) for a in (tokens, tokens, *widths)] + [block(one), block(two)],
        out_shape=[
            jax.ShapeDtypeStruct(tokens, low),
            jax.ShapeDtypeStruct(tokens, full),
            *(jax.ShapeDtypeStruct(a, full) for a in widths),
            jax.ShapeDtypeStruct(one.shape, full),
            jax.ShapeDtypeStruct(two.shape, full),
        ],
        compiler_params=pltpu.CompilerParams(
            dimension_semantics=("arbitrary",), vmem_limit_bytes=BIG
        ),
        cost_estimate=pl.CostEstimate(flops=0, bytes_accessed=19 * 10**6, transcendentals=0),
        name="finish",
    )(output, dx, dense, one, two)


ALL = ("replica", "part")


def body(
    tokens,
    choices,
    ln1_gain,
    ln1_bias,
    w_qkv,
    w_proj,
    ln2_gain,
    ln2_bias,
    w_router,
    w_expert_in,
    w_expert_out,
    cotangent,
):
    replicas, parts, groups = (lax.axis_size(name) for name in ("replica", "part", "expert"))
    owners = replicas * parts
    peers = parts * groups
    own = EXPERTS // peers
    images = tokens.shape[0] // SEQ
    count = images * ROWS
    tile = 512 * 16 // peers

    small_rows = w_router.shape[0]
    placed_router = (
        w_router.reshape(small_rows, groups, parts, own).transpose(0, 2, 1, 3).reshape(small_rows, EXPERTS)
    )
    vectors = jnp.concatenate([ln1_gain, ln1_bias, ln2_gain, ln2_bias]).reshape(4, small_rows).T
    packed = jnp.concatenate(
        [w_qkv, w_proj, placed_router, vectors, jnp.zeros((small_rows, LANES - EXPERTS - 4), full)],
        axis=1,
    )
    packed = lax.optimization_barrier(packed).astype(low)
    me = lax.axis_index("part") * groups + lax.axis_index("expert")
    sizes = (replicas, parts, groups)

    half = parts // 2
    flips = [(i, i ^ half) for i in range(parts)]
    picks = jnp.stack([choices, lax.ppermute(choices, "part", flips)]).reshape(2 * images, SEQ, 2)
    picks = jnp.pad(picks, ((0, 0), (0, ROWS - SEQ), (0, 0)), constant_values=-1)
    picks = picks.reshape(2, count, 2)
    column = jnp.arange(EXPERTS)
    place = (me ^ (column // own)) * own + column % own
    expert = (place // own % groups) * (parts * own) + place // (groups * own) * own + place % own
    lane = jnp.arange(LANES)
    order = jnp.where(lane < EXPERTS, jnp.pad(place, (0, LANES - EXPERTS)), lane)
    order = (lane[:, None] == order[None, :]).astype(low)
    expert = expert[: EXPERTS // 2]
    named = (picks[:, :, :, None] == expert).any(axis=2)
    row = jnp.arange(count)
    earlier = (row[None, :] < row[:, None]).astype(low)
    slots = jnp.einsum("tu,sue->ste", earlier, named.astype(low), preferred_element_type=full)
    keys = jnp.where(named, slots, -1.0)
    key_rows = keys.transpose(0, 2, 1).reshape(2, peers // 2, own, count)
    key_columns = jnp.pad(
        keys, ((0, 0), (0, 0), (0, LANES - EXPERTS // 2)), constant_values=-1
    ).astype(low)

    (
        x, dy, dy_slots, h_slots, weights, first_weight, second_weight, qkv, ctx, r, h, probs, theirs, second_master,
    ) = forward(key_rows, cotangent, tokens, order, packed, w_expert_in, w_expert_out, sizes, 0)
    dy_slots = dy_slots.reshape(peers, own, CAP, D)
    h_slots = h_slots.reshape(peers, own, CAP, D)
    select = ((me * own + jnp.arange(own))[:, None, None] == lane[None, None, :]).astype(full)
    routers = weights.reshape(D, PACKED)
    if own == 2:
        back, dw_first, y, second_grad, _ = experts(
            h_slots, dy_slots, first_weight, routers, select, second_master, second_weight, sizes, tile, 4,
        )
    else:
        g, slope, dw_second, second_weight = expert_first(
            h_slots, dy_slots, first_weight, routers[:, QKV + D :], select, second_master, second_weight,
            sizes, tile, 5,
        )
        back, dw_first, y, second_grad = expert_rest(
            dy_slots, h_slots, g, slope, first_weight, second_weight, dw_second, tile, sizes, 2
        )
    back = back.reshape(peers // 2, 2, own, CAP + 16, D)
    y = y.reshape(peers // 2, 2, own, CAP, D)
    dx, output, grads, first_grad = close(
        key_columns, back, weights, order, x, qkv, ctx, r, h, probs, dy, theirs, y,
        dw_first, sizes, 3,
    )
    output, input_grad, qkv_grad, proj_grad, router_grad, norms, expert_in_grad, expert_out_grad = finish(
        output, dx, grads, first_grad, second_grad, sizes
    )
    return (
        output,
        input_grad,
        norms[0],
        norms[1],
        qkv_grad,
        proj_grad,
        norms[2],
        norms[3],
        router_grad,
        expert_in_grad.reshape(w_expert_in.shape),
        expert_out_grad.reshape(w_expert_out.shape),
    )


def solution(mesh):
    dp, groups = mesh.shape["dp"], mesh.shape["expert"]
    parts = min(EXPERTS // groups, dp // 2)
    mesh = Mesh(mesh.devices.reshape(dp // parts, parts, groups), ("replica", "part", "expert"))
    rows = P(("replica", "part", "expert"), None)
    vector, matrix = P(ALL), P(ALL, None)
    experts = P("expert", ALL, None)
    return jax.shard_map(
        body,
        mesh=mesh,
        in_specs=(
            rows, rows, vector, vector, matrix, matrix, vector, vector, matrix, experts, experts, rows,
        ),
        out_specs=(
            rows, rows, vector, vector, matrix, matrix, vector, vector, matrix, experts, experts,
        ),
        check_vma=False,
    )
```
